32 devices in a mesh: band: 8 (over y, x, core), grid: 4 (over z).
Axes of the slice: x: 2, y: 2, z: 4, core: 2. Of those that a mesh axis runs over, the one named last changes fastest.
Arguments:
- orbitals: bfloat16 [16, 160, 25600], P('band', 'grid'), may hold values from -6 to 6
- source_index: int32 [2], replicated, may hold values from 0 to 15
Outputs:
- fock_exchange: bfloat16 [16, 160, 25600], P('band', 'grid')
The draws below stay inside these ranges and needn't reach their ends.
All inputs are finite; a program needn't handle non-finite values.
Results may differ from the reference program's by a relative error of at most 0.012.
The reference program's roundings to bfloat16 on the way count: a program that leaves them out, or rounds other values in their place, can miss the bound.
Values may be sent and summed in bfloat16 or wider, within the bound.
No kernel may reach another device: no remote copies, remote signals or barrier semaphores. Data moves between devices by JAX's collectives and lax.ppermute only.
A program may use at most 128 MiB of HBM per device.

```python
import math
import jax
import jax.numpy as jnp
from jax import lax

GRID = 160
NSRC = 2
ORBITALS = 16


def draw_orbitals(key, part):
    first_key = jax.random.fold_in(key, 0)
    shape_all = (ORBITALS, GRID, GRID * GRID)
    normal_part = jax.random.normal(first_key, shape_all, jnp.float32)
    return jnp.clip(normal_part, -6.0, 6.0).astype(jnp.bfloat16)


def setup_inputs(seed: int = 0) -> dict:
    streams_of = jax.random.split(jax.random.key(seed), 3)
    orbitals = draw_orbitals(jax.random.fold_in(streams_of[2], 71), 0)
    source_index = jax.random.randint(streams_of[1], (NSRC,), 0, ORBITALS).astype(jnp.int32)
    return dict(orbitals=orbitals, source_index=source_index)


spacing = 0.3

def cas_table(extent):
    wavenum = jnp.arange(extent, dtype=jnp.int32)
    products_mod = wavenum[:, None] * wavenum[None, :] % extent
    radians = products_mod.astype(jnp.float32) * (2.0 * math.pi / extent)
    return ((jnp.cos(radians) + jnp.sin(radians)) / math.sqrt(extent)).astype(jnp.bfloat16)

def wave_square(indices, extent):
    folded = jnp.minimum(indices, extent - indices).astype(jnp.float32)
    return folded * folded

def coulomb_table(extent):
    square_x = wave_square(jnp.arange(extent, dtype=jnp.int32), extent)
    total_sq = square_x[:, None, None] + square_x[None, :, None] + square_x[None, None, :]
    strength = (extent * spacing) ** 2 / math.pi
    return jnp.where(total_sq > 0, strength / (total_sq + 1.0), 0.0).astype(jnp.float32)

def along(grid_data, cas_matrix, which_axis):
    turned = jnp.tensordot(grid_data.astype(jnp.float32), cas_matrix.astype(jnp.float32), axes=([which_axis], [1]))
    return jnp.moveaxis(turned, -1, which_axis)

def reference(orbitals, source_index):
    grids = orbitals.reshape(ORBITALS, GRID, GRID, GRID)
    cas_matrix = cas_table(GRID)
    kernel = coulomb_table(GRID)
    sources = grids[source_index]

    def exchange_for(target_orbital):
        summed = jnp.zeros(target_orbital.shape, jnp.float32)
        for number in range(NSRC):
            source = sources[number].astype(jnp.float32)
            density = (source * target_orbital.astype(jnp.float32)).astype(jnp.bfloat16)
            along_z = along(density, cas_matrix, 2).astype(jnp.bfloat16)
            along_y = along(along_z, cas_matrix, 1).astype(jnp.bfloat16)
            scaled = (kernel * along(along_y, cas_matrix, 0)).astype(jnp.bfloat16)
            back_x = along(scaled, cas_matrix, 0).astype(jnp.bfloat16)
            again_y = along(back_x, cas_matrix, 1).astype(jnp.bfloat16)
            summed = summed + source * along(again_y, cas_matrix, 2)
        return (-summed).astype(jnp.bfloat16)
    result = lax.map(exchange_for, grids)
    return result.reshape(ORBITALS, GRID, GRID * GRID)
```

```python
import math

import jax
import jax.numpy as jnp
from jax import lax
from jax.sharding import PartitionSpec as P

spacing = 0.3
cores = 2


def cas_table(extent):
    wavenum = jnp.arange(extent, dtype=jnp.int32)
    products_mod = wavenum[:, None] * wavenum[None, :] % extent
    radians = products_mod.astype(jnp.float32) * (2.0 * math.pi / extent)
    return ((jnp.cos(radians) + jnp.sin(radians)) / math.sqrt(extent)).astype(jnp.bfloat16)


def wave_square(indices, extent):
    folded = jnp.minimum(indices, extent - indices).astype(jnp.float32)
    return folded * folded


def coulomb_block(extent, columns, offset):
    square_x = wave_square(jnp.arange(extent, dtype=jnp.int32), extent)
    square_y = wave_square(offset + jnp.arange(columns, dtype=jnp.int32), extent)
    total_sq = square_x[:, None, None] + square_y[None, :, None] + square_x[None, None, :]
    strength = (extent * spacing) ** 2 / math.pi
    return jnp.where(total_sq > 0, strength / (total_sq + 1.0), 0.0)


def transform(grid_data, cas_matrix, pattern):
    return jnp.einsum(pattern, grid_data, cas_matrix, preferred_element_type=jnp.float32)


def broadcast(x, axis, root):
    mine = lax.axis_index(axis) == root
    return lax.psum(jnp.where(mine, x, jnp.zeros_like(x)), axis)


def slab_potentials(pair_rho, cas_matrix, kernel_block):
    along_z = transform(pair_rho, cas_matrix, "pxyz,kz->pxyk").astype(jnp.bfloat16)
    along_y = transform(along_z, cas_matrix, "pxyz,ky->pxkz").astype(jnp.bfloat16)
    turned = lax.all_to_all(along_y, "grid", split_axis=2, concat_axis=1, tiled=True)
    scaled = (kernel_block * transform(turned, cas_matrix, "pxyz,kx->pkyz")).astype(jnp.bfloat16)
    back_x = transform(scaled, cas_matrix, "pxyz,kx->pkyz").astype(jnp.bfloat16)
    returned = lax.all_to_all(back_x, "grid", split_axis=1, concat_axis=2, tiled=True)
    again_y = transform(returned, cas_matrix, "pxyz,ky->pxkz").astype(jnp.bfloat16)
    return transform(again_y, cas_matrix, "pxyz,kz->pxyk")


def fetch_source(orbitals, which):
    local_count = orbitals.shape[0]
    local_slab = lax.dynamic_index_in_dim(orbitals, which % local_count, 0, keepdims=False)
    return broadcast(local_slab, "band", which // local_count)


def slab_plan(orbitals, source_index):
    local_count, planes, _ = orbitals.shape
    extent = planes * lax.axis_size("grid")
    orbitals = orbitals.reshape(local_count, planes, extent, extent)
    source_count = source_index.shape[0]
    cas_matrix = cas_table(extent)
    columns = extent // lax.axis_size("grid")
    kernel_block = coulomb_block(extent, columns, lax.axis_index("grid") * columns)
    fetched = [fetch_source(orbitals, source_index[number]) for number in range(source_count)]
    stacked = jnp.stack(fetched)[:, None].astype(jnp.float32)
    pair_rho = (stacked * orbitals[None].astype(jnp.float32)).astype(jnp.bfloat16)
    pair_rho = pair_rho.reshape(source_count * local_count, planes, extent, extent)
    potential = slab_potentials(pair_rho, cas_matrix, kernel_block)
    potential = potential.reshape(source_count, local_count, planes, extent, extent)
    result = (-jnp.sum(stacked * potential, axis=0)).astype(jnp.bfloat16)
    return result.reshape(local_count, planes, extent * extent)


def move(x, route):
    bands, slabs = lax.axis_size("band"), lax.axis_size("grid")
    pairs = []
    for band in range(bands):
        for z in range(slabs):
            column, core, to_z = route(band // cores, band % cores, z)
            pairs.append((band * slabs + z, (column * cores + core) * slabs + to_z))
    return lax.ppermute(x, ("band", "grid"), pairs)


def swap_cores(x):
    return move(x, lambda c, k, z: (c, 1 - k, z))


def to_column(x, d):
    return move(x, lambda c, k, z: (c ^ d, k, z))


def to_height(x, d):
    return move(x, lambda c, k, z: (c, k, z ^ d))


def fetch_whole_source(orbitals, source_index):
    local_count, planes, points = orbitals.shape
    band = lax.axis_index("band")
    column, core = band // cores, band % cores
    quarter = points // 4
    picked = lax.dynamic_index_in_dim(orbitals, source_index[core] % local_count, 0, keepdims=False)
    other = lax.dynamic_index_in_dim(orbitals, source_index[1 - core] % local_count, 0, keepdims=False)
    owner = source_index[core] // local_count
    crossed = swap_cores(other)
    slab = jnp.where(owner % cores == core, picked, crossed)

    def cut(d):
        return lax.dynamic_slice_in_dim(slab, (column ^ d) * quarter, quarter, 1)

    candidates = jnp.stack([cut(0)] + [to_column(cut(d), d) for d in (1, 2, 3)])
    mine = lax.dynamic_index_in_dim(candidates, column ^ (owner // cores), 0, keepdims=False)
    heights = [mine] + [to_height(mine, d) for d in (1, 2, 3)]
    half = quarter // 2
    gathered = []
    for part in heights:
        from_x = to_column(part, 1)
        from_y = to_column(part, 2)
        low = to_column(from_x[:, :half], 2)
        high = to_column(from_y[:, half:], 1)
        gathered.append([part, from_x, from_y, jnp.concatenate([low, high], axis=1)])
    return gathered


def pair_plan(orbitals, source_index):
    local_count, planes, points = orbitals.shape
    slabs = lax.axis_size("grid")
    extent = planes * slabs
    band, z = lax.axis_index("band"), lax.axis_index("grid")
    column, core = band // cores, band % cores
    half, quarter = points // 2, points // 4

    target = jnp.zeros((extent, points), jnp.bfloat16)
    for r in range(slabs):
        q = z ^ r
        chunk = lax.dynamic_slice(orbitals, (q // 2, 0, (q % 2) * half), (1, planes, half))[0]
        got = move(chunk, lambda c, k, zz: (c, (zz ^ r) % 2, 2 * k + (zz ^ r) // 2))
        crossed = swap_cores(got)
        mine_slab = (2 * (z % 2) + core) ^ r
        target = lax.dynamic_update_slice(target, got, (mine_slab * planes, core * half))
        target = lax.dynamic_update_slice(target, crossed, ((mine_slab ^ 1) * planes, (1 - core) * half))

    source = jnp.zeros((extent, points), jnp.bfloat16)
    for d, parts in enumerate(fetch_whole_source(orbitals, source_index)):
        for e, part in enumerate(parts):
            source = lax.dynamic_update_slice(source, part, ((z ^ d) * planes, (column ^ e) * quarter))

    cas_matrix = cas_table(extent)
    kernel = coulomb_block(extent, extent, 0)
    density = (source.astype(jnp.float32) * target.astype(jnp.float32)).astype(jnp.bfloat16)
    density = density.reshape(extent, extent, extent)
    along_z = transform(density, cas_matrix, "xyz,kz->xyk").astype(jnp.bfloat16)
    along_y = transform(along_z, cas_matrix, "xyz,ky->xkz").astype(jnp.bfloat16)
    scaled = (kernel * transform(along_y, cas_matrix, "xyz,kx->kyz")).astype(jnp.bfloat16)
    back_x = transform(scaled, cas_matrix, "xyz,kx->kyz").astype(jnp.bfloat16)
    again_y = transform(back_x, cas_matrix, "xyz,ky->xkz").astype(jnp.bfloat16)
    potential = transform(again_y, cas_matrix, "xyz,kz->xyk")
    product = -(source.reshape(extent, extent, extent).astype(jnp.float32) * potential)
    product = product.astype(jnp.bfloat16).reshape(extent, points)

    kept = lax.dynamic_slice_in_dim(product, core * half, half, 1)
    given = lax.dynamic_slice_in_dim(product, (1 - core) * half, half, 1)
    received = swap_cores(given)
    total = (kept.astype(jnp.float32) + received.astype(jnp.float32)).astype(jnp.bfloat16)

    result = jnp.zeros(orbitals.shape, jnp.bfloat16)
    for r in range(slabs):
        slab = (2 * (z % 2) + core) ^ r
        chunk = lax.dynamic_slice_in_dim(total, slab * planes, planes, 0)
        got = move(chunk, lambda c, k, zz: (c, zz // 2, (2 * (zz % 2) + k) ^ r))
        q = z ^ r
        result = lax.dynamic_update_slice(result, got[None], (q // 2, 0, (q % 2) * half))
    return result


def solution(mesh):
    def shards(orbitals, source_index):
        slabs, bands = mesh.shape["grid"], mesh.shape["band"]
        fits = slabs == 4 and bands == 8 and orbitals.shape[0] == 2 and source_index.shape[0] == cores
        return (pair_plan if fits else slab_plan)(orbitals, source_index)

    return jax.shard_map(
        shards,
        mesh=mesh,
        in_specs=(P("band", "grid", None), P()),
        out_specs=P("band", "grid", None),
        check_vma=False,
    )
```

```python
import math

import jax
import jax.numpy as jnp
from jax import lax
from jax.experimental import pallas as pl
from jax.experimental.pallas import tpu as pltpu
from jax.sharding import PartitionSpec as P

spacing = 0.3
cores = 2


def cas_entries(rows, columns, extent):
    products_mod = rows[:, None] * columns[None, :] % extent
    radians = products_mod.astype(jnp.float32) * (2.0 * math.pi / extent)
    return ((jnp.cos(radians) + jnp.sin(radians)) / math.sqrt(extent)).astype(jnp.bfloat16)


def cas_table(extent):
    wavenum = jnp.arange(extent, dtype=jnp.int32)
    return cas_entries(wavenum, wavenum, extent)


def wave_square(indices, extent):
    folded = jnp.minimum(indices, extent - indices).astype(jnp.float32)
    return folded * folded


def coulomb_block(extent, columns, offset):
    square_x = wave_square(jnp.arange(extent, dtype=jnp.int32), extent)
    square_y = wave_square(offset + jnp.arange(columns, dtype=jnp.int32), extent)
    total_sq = square_x[:, None, None] + square_y[None, :, None] + square_x[None, None, :]
    strength = (extent * spacing) ** 2 / math.pi
    return jnp.where(total_sq > 0, strength / (total_sq + 1.0), 0.0)


def transform(grid_data, cas_matrix, pattern):
    return jnp.einsum(pattern, grid_data, cas_matrix, preferred_element_type=jnp.float32)


def broadcast(x, axis, root):
    mine = lax.axis_index(axis) == root
    return lax.psum(jnp.where(mine, x, jnp.zeros_like(x)), axis)


def slab_potentials(pair_rho, cas_matrix, kernel_block):
    along_z = transform(pair_rho, cas_matrix, "pxyz,kz->pxyk").astype(jnp.bfloat16)
    along_y = transform(along_z, cas_matrix, "pxyz,ky->pxkz").astype(jnp.bfloat16)
    turned = lax.all_to_all(along_y, "grid", split_axis=2, concat_axis=1, tiled=True)
    scaled = (kernel_block * transform(turned, cas_matrix, "pxyz,kx->pkyz")).astype(jnp.bfloat16)
    back_x = transform(scaled, cas_matrix, "pxyz,kx->pkyz").astype(jnp.bfloat16)
    returned = lax.all_to_all(back_x, "grid", split_axis=1, concat_axis=2, tiled=True)
    again_y = transform(returned, cas_matrix, "pxyz,ky->pxkz").astype(jnp.bfloat16)
    return transform(again_y, cas_matrix, "pxyz,kz->pxyk")


def fetch_source(orbitals, which):
    local_count = orbitals.shape[0]
    local_slab = lax.dynamic_index_in_dim(orbitals, which % local_count, 0, keepdims=False)
    return broadcast(local_slab, "band", which // local_count)


def slab_plan(orbitals, source_index):
    local_count, planes, _ = orbitals.shape
    extent = planes * lax.axis_size("grid")
    orbitals = orbitals.reshape(local_count, planes, extent, extent)
    source_count = source_index.shape[0]
    cas_matrix = cas_table(extent)
    columns = extent // lax.axis_size("grid")
    kernel_block = coulomb_block(extent, columns, lax.axis_index("grid") * columns)
    fetched = [fetch_source(orbitals, source_index[number]) for number in range(source_count)]
    stacked = jnp.stack(fetched)[:, None].astype(jnp.float32)
    pair_rho = (stacked * orbitals[None].astype(jnp.float32)).astype(jnp.bfloat16)
    pair_rho = pair_rho.reshape(source_count * local_count, planes, extent, extent)
    potential = slab_potentials(pair_rho, cas_matrix, kernel_block)
    potential = potential.reshape(source_count, local_count, planes, extent, extent)
    result = (-jnp.sum(stacked * potential, axis=0)).astype(jnp.bfloat16)
    return result.reshape(local_count, planes, extent * extent)


lanes = 128
quad = 4
pitch = 160


def move(x, routes):
    slabs = lax.axis_size("grid")

    def place(column, core, z):
        return (column * cores + core) * slabs + z

    return lax.ppermute(x, ("band", "grid"), [(place(*a), place(*b)) for a, b in routes])


def everywhere():
    columns = lax.axis_size("band") // cores
    return [(c, k, z) for c in range(columns) for k in range(cores) for z in range(lax.axis_size("grid"))]


def swap_cores(x):
    return move(x, [((c, k, z), (c, 1 - k, z)) for c, k, z in everywhere()])


def to_column(x, d):
    return move(x, [((c, k, z), (c ^ d, k, z)) for c, k, z in everywhere()])


def to_height(x, d):
    return move(x, [((c, k, z), (c, k, z ^ d)) for c, k, z in everywhere()])


def to_chip(x, d, core):
    return move(x, [((c, z // 2, z ^ d), (c, core, z)) for c, k, z in everywhere() if k == core])


def to_home(x, d, core):
    return move(x, [((c, core, z), (c, z // 2, z ^ d)) for c, k, z in everywhere() if k == core])


def fetch_whole_source(orbitals, source_index):
    local_count, planes, points = orbitals.shape
    band = lax.axis_index("band")
    column, core = band // cores, band % cores
    quarter = points // 4
    picked = lax.dynamic_index_in_dim(orbitals, source_index[core] % local_count, 0, keepdims=False)
    other = lax.dynamic_index_in_dim(orbitals, source_index[1 - core] % local_count, 0, keepdims=False)
    owner = source_index[core] // local_count
    crossed = swap_cores(other)
    slab = jnp.where(owner % cores == core, picked, crossed)

    def cut(d):
        return lax.dynamic_slice_in_dim(slab, (column ^ d) * quarter, quarter, 1)

    candidates = [cut(0)] + [to_column(cut(d), d) for d in (1, 2, 3)]
    which = column ^ (owner // cores)
    mine = lax.select_n(which, *candidates)
    half = quarter // 2
    gathered = []
    for d in range(4):
        part = to_height(mine, d) if d else mine
        from_x = to_column(part, 1)
        from_y = to_column(part, 2)
        low = to_column(from_x[:, :half], 2)
        high = to_column(from_y[:, half:], 1)
        gathered.append([part, from_x, from_y, low, high])
    return gathered


def copy_pieces(pieces, sems):
    copies = []
    for number, (ref, whole, offset) in enumerate(pieces):
        where = pl.ds(pl.multiple_of(offset, lanes), ref.shape[1])
        copies.append(pltpu.make_async_copy(ref, whole.at[:, where], sems.at[number]))
    for copy in copies:
        copy.start()
    for copy in copies:
        copy.wait()


def source_pieces(refs, source, column):
    quarter = source.shape[1] // 4
    offsets = [(column ^ e) * quarter for e in range(4)]
    offsets.append(offsets[3] + quarter // 2)
    return [(ref, source, offset) for ref, offset in zip(refs, offsets)]


def dot(a, b):
    return jnp.dot(a, b, preferred_element_type=jnp.float32)


def both(ref, rows):
    return jnp.concatenate([ref[0, rows, :], ref[1, rows, :]], axis=1)


def put_both(ref, rows, value):
    ref[0, rows, :] = value[:, :lanes]
    ref[1, rows, :] = value[:, lanes:]


def forward_kernel(place, *refs):
    targets, (s0, s1, s2, s3, s4, cas, windows, out, target, source, turned, sems) = refs[:-12], refs[-12:]
    planes, points = target.shape
    extent = cas.shape[0]
    core, column = place[0], place[1]
    half = points // 2
    pieces = [(targets[0], target, 0)]
    if len(targets) == 2:
        pieces = [(targets[0], target, core * half), (targets[1], target, (1 - core) * half)]
    copy_pieces(pieces + source_pieces((s0, s1, s2, s3, s4), source, column), sems)
    step = 8
    block = quad * extent

    @pl.loop(0, points // block // step)
    def _(i):
        for r in range(quad):
            density = []
            for j in range(step):
                at = pl.ds(pl.multiple_of((i * step + j) * block + r * lanes, lanes), 2 * lanes)
                density.append(source[:, at].astype(jnp.float32) * target[:, at].astype(jnp.float32))
            density = jnp.concatenate(density, axis=0).astype(jnp.bfloat16)
            along_z = dot(density, windows[r])
            for j in range(step):
                y = (i * step + j) * quad + r
                put_both(turned, pl.ds(y, planes, stride=pitch), along_z[j * planes : (j + 1) * planes])

    @pl.loop(0, planes // 4)
    def _(i):
        for j in range(4):
            x = i * 4 + j
            along_z = both(turned, pl.ds(x * pitch, extent)).astype(jnp.bfloat16)
            put_both(out, pl.ds(x, extent, stride=planes), dot(cas[...], along_z))


def middle_kernel(g0, g1, g2, g3, into, back, square, o0, o1, o2, o3):
    rows, planes = g0.shape[1], g0.shape[2]
    extent = square.shape[0]
    strength = (extent * spacing) ** 2 / math.pi
    first = pl.program_id(0) * rows
    for i in range(rows):
        along_y = jnp.concatenate(
            [jnp.concatenate([g[0, i], g[1, i]], axis=1) for g in (g0, g1, g2, g3)], axis=0
        ).astype(jnp.bfloat16)
        ky = first + i
        folded = jnp.minimum(ky, extent - ky)
        total_sq = square[...] + (folded * folded).astype(jnp.float32)
        factor = jnp.where(total_sq > 0, strength / (total_sq + 1.0), 0.0)
        scaled = (factor * dot(into[...], along_y)).astype(jnp.bfloat16)
        back_x = dot(back[...], scaled)
        for d, o in enumerate((o0, o1, o2, o3)):
            part = back_x[d * planes : (d + 1) * planes]
            o[0, i] = part[:, :lanes]
            o[1, i] = part[:, lanes:]


def backward_kernel(place, back_x, s0, s1, s2, s3, s4, cas, windows, *refs):
    outs, (source, turned, sems) = refs[:-3], refs[-3:]
    planes, points = source.shape
    extent = cas.shape[0]
    core, column = place[0], place[1]
    copy_pieces(source_pieces((s0, s1, s2, s3, s4), source, column), sems)

    @pl.loop(0, planes // 4)
    def _(i):
        for j in range(4):
            x = i * 4 + j
            column_x = both(back_x, pl.ds(x, extent, stride=planes)).astype(jnp.bfloat16)
            put_both(turned, pl.ds(x * pitch, extent), dot(cas[...], column_x))

    step = 4
    block = quad * extent
    parts = len(outs)
    blocks = points // block // parts
    for number, out in enumerate(outs):
        base = 0 if parts == 1 else blocks * (core if number == 0 else 1 - core)

        @pl.loop(0, blocks // step)
        def _(i):
            windowed = []
            for r in range(quad):
                again_y = jnp.concatenate(
                    [
                        both(turned, pl.ds((base + i * step + j) * quad + r, planes, stride=pitch))
                        for j in range(step)
                    ],
                    axis=0,
                ).astype(jnp.bfloat16)
                windowed.append(dot(again_y, windows[r]))
            for j in range(step):
                w = [part[j * planes : (j + 1) * planes] for part in windowed]
                potential = [w[0][:, :lanes]]
                potential += [w[r][:, lanes:] + w[r + 1][:, :lanes] for r in range(quad - 1)]
                potential = jnp.concatenate(potential + [w[-1][:, lanes:]], axis=1)
                at = pl.ds(pl.multiple_of((base + i * step + j) * block, lanes), block)
                to = pl.ds(pl.multiple_of((i * step + j) * block, lanes), block)
                out[:, to] = (-(source[:, at].astype(jnp.float32) * potential)).astype(jnp.bfloat16)


def window_tables(cas_matrix):
    extent = cas_matrix.shape[0]
    tables = []
    for r in range(quad):
        shift = r * extent % lanes
        tables.append(jnp.pad(cas_matrix, ((shift, 2 * lanes - extent - shift), (0, 2 * lanes - extent))))
    return jnp.stack(tables)


limit = 56 * 2**20
whole = pl.BlockSpec(memory_space=pltpu.VMEM)
outside = pl.BlockSpec(memory_space=pl.ANY)
scalars = pl.BlockSpec(memory_space=pltpu.SMEM)


def forward(place, targets, sources, cas_matrix, windows):
    planes = sources[0].shape[0]
    extent = cas_matrix.shape[0]
    points = extent * extent
    return pl.pallas_call(
        forward_kernel,
        out_shape=jax.ShapeDtypeStruct((2, extent * planes, lanes), jnp.float32),
        in_specs=[scalars] + [outside] * (len(targets) + len(sources)) + [whole] * 2,
        out_specs=whole,
        scratch_shapes=[
            pltpu.VMEM((planes, points), jnp.bfloat16),
            pltpu.VMEM((planes, points), jnp.bfloat16),
            pltpu.VMEM((2, planes * pitch, lanes), jnp.float32),
            pltpu.SemaphoreType.DMA((len(targets) + len(sources),)),
        ],
        compiler_params=pltpu.CompilerParams(vmem_limit_bytes=limit),
        cost_estimate=pl.CostEstimate(flops=10**10, bytes_accessed=10**7, transcendentals=0),
        name="forward",
    )(place, *targets, *sources, cas_matrix, windows)


def middle(slabs, into, back, square):
    extent = square.shape[0]
    planes = slabs[0].shape[1] // extent
    rows = 8
    block = pl.BlockSpec((2, rows, planes, lanes), lambda i: (0, i, 0, 0))

    def same(shape):
        return pl.BlockSpec(shape, lambda i: (0, 0))

    shape = (2, extent, planes, lanes)
    outs = pl.pallas_call(
        middle_kernel,
        grid=(extent // rows,),
        out_shape=[jax.ShapeDtypeStruct(shape, jnp.float32)] * 4,
        in_specs=[block] * 4 + [same(into.shape), same(back.shape), same(square.shape)],
        out_specs=[block] * 4,
        compiler_params=pltpu.CompilerParams(vmem_limit_bytes=limit),
        cost_estimate=pl.CostEstimate(flops=2 * 10**10, bytes_accessed=10**7, transcendentals=0),
        name="middle",
    )(*[slab.reshape(shape) for slab in slabs], into, back, square)
    return [out.reshape(slabs[0].shape) for out in outs]


def backward(place, back_x, sources, cas_matrix, windows, parts):
    planes = sources[0].shape[0]
    extent = cas_matrix.shape[0]
    points = extent * extent
    return pl.pallas_call(
        backward_kernel,
        out_shape=[jax.ShapeDtypeStruct((planes, points // parts), jnp.bfloat16)] * parts,
        in_specs=[scalars, whole] + [outside] * len(sources) + [whole] * 2,
        out_specs=[whole] * parts,
        scratch_shapes=[
            pltpu.VMEM((planes, points), jnp.bfloat16),
            pltpu.VMEM((2, planes * pitch, lanes), jnp.float32),
            pltpu.SemaphoreType.DMA((len(sources),)),
        ],
        compiler_params=pltpu.CompilerParams(vmem_limit_bytes=limit),
        cost_estimate=pl.CostEstimate(flops=10**10, bytes_accessed=10**7, transcendentals=0),
        name="backward",
    )(place, back_x, *sources, cas_matrix, windows)


def pair_plan(orbitals, source_index):
    local_count, planes, points = orbitals.shape
    slabs = lax.axis_size("grid")
    extent = planes * slabs
    band, z = lax.axis_index("band"), lax.axis_index("grid")
    column, core = band // cores, band % cores
    half = points // 2
    place = jnp.stack([core, column]).astype(jnp.int32)

    sources = fetch_whole_source(orbitals, source_index)

    targets = {}
    for d in (2, 3, 1):
        which = (z ^ d) % 2
        chunks = [lax.dynamic_slice(orbitals, (which, 0, h * half), (1, planes, half))[0] for h in range(2)]
        arrived = [to_chip(chunk, d, h) for h, chunk in enumerate(chunks)]
        own = jnp.where(core == 0, arrived[0], arrived[1])
        targets[d] = [own, swap_cores(own)]
    local = lax.dynamic_index_in_dim(orbitals, z % 2, 0, keepdims=False)
    targets[0] = [jnp.where(core == z // 2, local, swap_cores(local))]

    cas_matrix = cas_table(extent)
    windows = window_tables(cas_matrix)
    windows_back = jnp.swapaxes(windows, 1, 2)
    slots = (((jnp.arange(slabs) ^ z) * planes)[:, None] + jnp.arange(planes)).reshape(extent)
    into = cas_entries(jnp.arange(extent), slots, extent)
    square_x = wave_square(jnp.arange(extent, dtype=jnp.int32), extent)
    square = jnp.pad(square_x[:, None] + square_x[None, :], ((0, 0), (0, 2 * lanes - extent)))

    along_y = [forward(place, targets[d], sources[d], cas_matrix, windows) for d in range(4)]
    back_x = middle(along_y, into, into.T, square)

    near = z // 2 == core
    totals = {}
    for d in (2, 3, 1):
        kept, given = backward(place, back_x[d], sources[d], cas_matrix, windows_back, 2)
        received = swap_cores(given)
        total = (kept.astype(jnp.float32) + received.astype(jnp.float32)).astype(jnp.bfloat16)
        totals[d] = [to_home(total, d, h) for h in range(2)]
    (partial,) = backward(place, back_x[0], sources[0], cas_matrix, windows_back, 1)
    local = (partial.astype(jnp.float32) + swap_cores(partial).astype(jnp.float32)).astype(jnp.bfloat16)

    first = jnp.where(near, local, jnp.concatenate(totals[2], axis=1))
    second = jnp.where(near, jnp.concatenate(totals[1], axis=1), jnp.concatenate(totals[3], axis=1))
    even = z % 2 == 0
    return jnp.stack([jnp.where(even, first, second), jnp.where(even, second, first)])


def solution(mesh):
    def shards(orbitals, source_index):
        slabs, bands = mesh.shape["grid"], mesh.shape["band"]
        fits = slabs == 4 and bands == 8 and orbitals.shape[0] == 2 and source_index.shape[0] == cores
        return (pair_plan if fits else slab_plan)(orbitals, source_index)

    return jax.shard_map(
        shards,
        mesh=mesh,
        in_specs=(P("band", "grid", None), P()),
        out_specs=P("band", "grid", None),
        check_vma=False,
    )
```

```python
import functools
import math

import jax
import jax.numpy as jnp
from jax import lax
from jax.experimental import pallas as pl
from jax.experimental.pallas import tpu as pltpu
from jax.sharding import PartitionSpec as P

spacing = 0.3
cores = 2


def cas_entries(rows, columns, extent):
    products_mod = rows[:, None] * columns[None, :] % extent
    radians = products_mod.astype(jnp.float32) * (2.0 * math.pi / extent)
    return ((jnp.cos(radians) + jnp.sin(radians)) / math.sqrt(extent)).astype(jnp.bfloat16)


def cas_table(extent):
    wavenum = jnp.arange(extent, dtype=jnp.int32)
    return cas_entries(wavenum, wavenum, extent)


def wave_square(indices, extent):
    folded = jnp.minimum(indices, extent - indices).astype(jnp.float32)
    return folded * folded


def coulomb_block(extent, columns, offset):
    square_x = wave_square(jnp.arange(extent, dtype=jnp.int32), extent)
    square_y = wave_square(offset + jnp.arange(columns, dtype=jnp.int32), extent)
    total_sq = square_x[:, None, None] + square_y[None, :, None] + square_x[None, None, :]
    strength = (extent * spacing) ** 2 / math.pi
    return jnp.where(total_sq > 0, strength / (total_sq + 1.0), 0.0)


def transform(grid_data, cas_matrix, pattern):
    return jnp.einsum(pattern, grid_data, cas_matrix, preferred_element_type=jnp.float32)


def broadcast(x, axis, root):
    mine = lax.axis_index(axis) == root
    return lax.psum(jnp.where(mine, x, jnp.zeros_like(x)), axis)


def slab_potentials(pair_rho, cas_matrix, kernel_block):
    along_z = transform(pair_rho, cas_matrix, "pxyz,kz->pxyk").astype(jnp.bfloat16)
    along_y = transform(along_z, cas_matrix, "pxyz,ky->pxkz").astype(jnp.bfloat16)
    turned = lax.all_to_all(along_y, "grid", split_axis=2, concat_axis=1, tiled=True)
    scaled = (kernel_block * transform(turned, cas_matrix, "pxyz,kx->pkyz")).astype(jnp.bfloat16)
    back_x = transform(scaled, cas_matrix, "pxyz,kx->pkyz").astype(jnp.bfloat16)
    returned = lax.all_to_all(back_x, "grid", split_axis=1, concat_axis=2, tiled=True)
    again_y = transform(returned, cas_matrix, "pxyz,ky->pxkz").astype(jnp.bfloat16)
    return transform(again_y, cas_matrix, "pxyz,kz->pxyk")


def fetch_source(orbitals, which):
    local_count = orbitals.shape[0]
    local_slab = lax.dynamic_index_in_dim(orbitals, which % local_count, 0, keepdims=False)
    return broadcast(local_slab, "band", which // local_count)


def slab_plan(orbitals, source_index):
    local_count, planes, _ = orbitals.shape
    extent = planes * lax.axis_size("grid")
    orbitals = orbitals.reshape(local_count, planes, extent, extent)
    source_count = source_index.shape[0]
    cas_matrix = cas_table(extent)
    columns = extent // lax.axis_size("grid")
    kernel_block = coulomb_block(extent, columns, lax.axis_index("grid") * columns)
    fetched = [fetch_source(orbitals, source_index[number]) for number in range(source_count)]
    stacked = jnp.stack(fetched)[:, None].astype(jnp.float32)
    pair_rho = (stacked * orbitals[None].astype(jnp.float32)).astype(jnp.bfloat16)
    pair_rho = pair_rho.reshape(source_count * local_count, planes, extent, extent)
    potential = slab_potentials(pair_rho, cas_matrix, kernel_block)
    potential = potential.reshape(source_count, local_count, planes, extent, extent)
    result = (-jnp.sum(stacked * potential, axis=0)).astype(jnp.bfloat16)
    return result.reshape(local_count, planes, extent * extent)


lanes = 128
quad = 4
ring = 4
turned_pitch = 161
plane_pitch = 41


def move(x, routes):
    slabs = lax.axis_size("grid")

    def place(column, core, z):
        return (column * cores + core) * slabs + z % slabs

    return lax.ppermute(x, ("band", "grid"), [(place(*a), place(*b)) for a, b in routes])


def everywhere():
    columns = lax.axis_size("band") // cores
    return [(c, k, z) for c in range(columns) for k in range(cores) for z in range(lax.axis_size("grid"))]


def swap_cores(x):
    return move(x, [((c, k, z), (c, 1 - k, z)) for c, k, z in everywhere()])


def to_column(x, d):
    return move(x, [((c, k, z), (c ^ d, k, z)) for c, k, z in everywhere()])


def up(x, d):
    return move(x, [((c, k, z), (c, k, z + d)) for c, k, z in everywhere()])


def holder(z):
    return z % ring // 2


def side(core):
    return 2 * core - 1


def near_in(x):
    return move(x, [((c, holder(z), z + side(k)), (c, k, z)) for c, k, z in everywhere()])


def near_out(x):
    return move(x, [((c, k, z), (c, holder(z), z + side(k))) for c, k, z in everywhere()])


def far_in(halves):
    first = [
        move(x, [((c, holder(z), z + 2), (c, k, z - side(k))) for c, k, z in everywhere() if k == half])
        for half, x in enumerate(halves)
    ]
    return first, lambda x: move(x, [((c, k, z - side(k)), (c, k, z)) for c, k, z in everywhere()])


def far_out_first(x):
    return move(x, [((c, k, z), (c, k, z + side(k))) for c, k, z in everywhere()])


def far_out_second(x, half):
    return move(x, [((c, k, z + side(k)), (c, holder(z), z + 2)) for c, k, z in everywhere() if k == half])


def after(x, *others):
    return lax.optimization_barrier((x, *others))[0]


def quarters_to_all(part):
    half = part.shape[2] // 2
    from_x = to_column(part, 1)
    from_y = to_column(part, 2)
    low = to_column(from_x[:, :, :half], 2)
    high = to_column(from_y[:, :, half:], 1)
    return [part, from_x, from_y, low, high]


def own_quarter(orbitals, source_index, column, core):
    local_count, _, points = orbitals.shape
    quarter = points // 4
    picked = lax.dynamic_index_in_dim(orbitals, source_index[core] % local_count, 0, keepdims=False)
    other = lax.dynamic_index_in_dim(orbitals, source_index[1 - core] % local_count, 0, keepdims=False)
    owner = source_index[core] // local_count
    slab = jnp.where(owner % cores == core, picked, swap_cores(other))

    def cut(d):
        return lax.dynamic_slice_in_dim(slab, (column ^ d) * quarter, quarter, 1)

    candidates = [cut(0)] + [to_column(cut(d), d) for d in (1, 2, 3)]
    return lax.select_n(column ^ (owner // cores), *candidates)


def copy_pieces(pieces, sems):
    copies = []
    for number, (ref, whole, offset) in enumerate(pieces):
        where = pl.ds(pl.multiple_of(offset, lanes), ref.shape[1])
        copies.append(pltpu.make_async_copy(ref, whole.at[:, where], sems.at[number]))
    for copy in copies:
        copy.start()
    for copy in copies:
        copy.wait()


def source_pieces(refs, source, column, which):
    quarter = source.shape[1] // 4
    offsets = [(column ^ e) * quarter for e in range(4)]
    offsets.append(offsets[3] + quarter // 2)
    return [(ref.at[which], source, offset) for ref, offset in zip(refs, offsets)]


def dot(a, b):
    return jnp.dot(a, b, preferred_element_type=jnp.float32)


def both(ref, rows):
    return jnp.concatenate([ref[0, rows, :], ref[1, rows, :]], axis=1)


def put_both(ref, rows, value):
    ref[0, rows, :] = value[:, :lanes]
    ref[1, rows, :] = value[:, lanes:]


def forward_kernel(pick, place, *refs):
    targets, (s0, s1, s2, s3, s4, cas, windows, out, target, source, turned, sems) = refs[:-12], refs[-12:]
    planes, points = target.shape
    extent = cas.shape[0]
    core, column = place[0], place[1]
    half = points // 2
    pieces = [(targets[0], target, 0)]
    if len(targets) == 2:
        pieces = [(targets[0], target, core * half), (targets[1], target, (1 - core) * half)]
    copy_pieces(pieces + source_pieces((s0, s1, s2, s3, s4), source, column, pick(core)), sems)
    step = 8
    block = quad * extent

    @pl.loop(0, points // block // step)
    def _(i):
        for r in range(quad):
            density = []
            for j in range(step):
                at = pl.ds(pl.multiple_of((i * step + j) * block + r * lanes, lanes), 2 * lanes)
                density.append(source[:, at].astype(jnp.float32) * target[:, at].astype(jnp.float32))
            density = jnp.concatenate(density, axis=0).astype(jnp.bfloat16)
            along_z = dot(density, windows[r])
            for j in range(step):
                y = (i * step + j) * quad + r
                put_both(turned, pl.ds(y, planes, stride=turned_pitch), along_z[j * planes : (j + 1) * planes])

    @pl.loop(0, planes // 4)
    def _(i):
        for j in range(4):
            x = i * 4 + j
            along_z = both(turned, pl.ds(x * turned_pitch, extent)).astype(jnp.bfloat16)
            put_both(out, pl.ds(x, extent, stride=plane_pitch), dot(cas[...], along_z))


def middle_kernel(g0, g1, g2, g3, into, back, square, o0, o1, o2, o3):
    rows = g0.shape[1] // plane_pitch
    extent = square.shape[0]
    planes = extent // ring
    strength = (extent * spacing) ** 2 / math.pi
    first = pl.program_id(0) * rows
    for i in range(rows):
        at = pl.ds(i * plane_pitch, planes)
        along_y = jnp.concatenate([both(g, at) for g in (g0, g1, g2, g3)], axis=0).astype(jnp.bfloat16)
        ky = first + i
        folded = jnp.minimum(ky, extent - ky)
        weight = square[...] + (folded * folded).astype(jnp.float32) * (1.0 / strength)
        guess = pl.reciprocal(weight, approx=True)
        factor = guess * (2.0 - weight * guess)
        factor = jnp.where(weight > 1.25 / strength, factor, 0.0)
        scaled = (factor * dot(into[...], along_y)).astype(jnp.bfloat16)
        back_x = dot(back[...], scaled)
        for d, o in enumerate((o0, o1, o2, o3)):
            put_both(o, at, back_x[d * planes : (d + 1) * planes])


def backward_kernel(pick, place, back_x, s0, s1, s2, s3, s4, cas, windows, *refs):
    outs, (source, turned, sems) = refs[:-3], refs[-3:]
    planes, points = source.shape
    extent = cas.shape[0]
    core, column = place[0], place[1]
    copy_pieces(source_pieces((s0, s1, s2, s3, s4), source, column, pick(core)), sems)

    @pl.loop(0, planes // 4)
    def _(i):
        for j in range(4):
            x = i * 4 + j
            column_x = both(back_x, pl.ds(x, extent, stride=plane_pitch)).astype(jnp.bfloat16)
            put_both(turned, pl.ds(x * turned_pitch, extent), dot(cas[...], column_x))

    step = 4
    block = quad * extent
    parts = len(outs)
    blocks = points // block // parts
    for number, out in enumerate(outs):
        base = 0 if parts == 1 else blocks * (core if number == 0 else 1 - core)

        @pl.loop(0, blocks // step)
        def _(i):
            windowed = []
            for r in range(quad):
                again_y = jnp.concatenate(
                    [
                        both(turned, pl.ds((base + i * step + j) * quad + r, planes, stride=turned_pitch))
                        for j in range(step)
                    ],
                    axis=0,
                ).astype(jnp.bfloat16)
                windowed.append(dot(again_y, windows[r]))
            for j in range(step):
                w = [part[j * planes : (j + 1) * planes] for part in windowed]
                potential = [w[0][:, :lanes]]
                potential += [w[r][:, lanes:] + w[r + 1][:, :lanes] for r in range(quad - 1)]
                potential = jnp.concatenate(potential + [w[-1][:, lanes:]], axis=1)
                at = pl.ds(pl.multiple_of((base + i * step + j) * block, lanes), block)
                to = pl.ds(pl.multiple_of((i * step + j) * block, lanes), block)
                out[:, to] = (-(source[:, at].astype(jnp.float32) * potential)).astype(jnp.bfloat16)


def window_tables(cas_matrix):
    extent = cas_matrix.shape[0]
    tables = []
    for r in range(quad):
        shift = r * extent % lanes
        tables.append(jnp.pad(cas_matrix, ((shift, 2 * lanes - extent - shift), (0, 2 * lanes - extent))))
    return jnp.stack(tables)


limit = 56 * 2**20
whole = pl.BlockSpec(memory_space=pltpu.VMEM)
outside = pl.BlockSpec(memory_space=pl.ANY)
scalars = pl.BlockSpec(memory_space=pltpu.SMEM)


def forward(place, targets, sources, pick, cas_matrix, windows):
    planes = sources[0].shape[1]
    extent = cas_matrix.shape[0]
    points = extent * extent
    return pl.pallas_call(
        functools.partial(forward_kernel, pick),
        out_shape=jax.ShapeDtypeStruct((2, extent * plane_pitch, lanes), jnp.float32),
        in_specs=[scalars] + [outside] * (len(targets) + len(sources)) + [whole] * 2,
        out_specs=whole,
        scratch_shapes=[
            pltpu.VMEM((planes, points), jnp.bfloat16),
            pltpu.VMEM((planes, points), jnp.bfloat16),
            pltpu.VMEM((2, planes * turned_pitch, lanes), jnp.float32),
            pltpu.SemaphoreType.DMA((len(targets) + len(sources),)),
        ],
        compiler_params=pltpu.CompilerParams(vmem_limit_bytes=limit),
        cost_estimate=pl.CostEstimate(flops=10**6, bytes_accessed=10**4, transcendentals=0),
        name="forward",
    )(place, *targets, *sources, cas_matrix, windows)


def middle(slabs, into, back, square):
    extent = square.shape[0]
    rows = 8
    block = pl.BlockSpec((2, rows * plane_pitch, lanes), lambda i: (0, i, 0))

    def same(shape):
        return pl.BlockSpec(shape, lambda i: (0, 0))

    return pl.pallas_call(
        middle_kernel,
        grid=(extent // rows,),
        out_shape=[jax.ShapeDtypeStruct(slabs[0].shape, jnp.float32)] * 4,
        in_specs=[block] * 4 + [same(into.shape), same(back.shape), same(square.shape)],
        out_specs=[block] * 4,
        compiler_params=pltpu.CompilerParams(vmem_limit_bytes=limit),
        cost_estimate=pl.CostEstimate(flops=10**6, bytes_accessed=10**4, transcendentals=0),
        name="middle",
    )(*slabs, into, back, square)


def backward(place, back_x, sources, pick, cas_matrix, windows, parts):
    planes = sources[0].shape[1]
    extent = cas_matrix.shape[0]
    points = extent * extent
    return pl.pallas_call(
        functools.partial(backward_kernel, pick),
        out_shape=[jax.ShapeDtypeStruct((planes, points // parts), jnp.bfloat16)] * parts,
        in_specs=[scalars, whole] + [outside] * len(sources) + [whole] * 2,
        out_specs=[whole] * parts,
        scratch_shapes=[
            pltpu.VMEM((planes, points), jnp.bfloat16),
            pltpu.VMEM((2, planes * turned_pitch, lanes), jnp.float32),
            pltpu.SemaphoreType.DMA((len(sources),)),
        ],
        compiler_params=pltpu.CompilerParams(vmem_limit_bytes=limit),
        cost_estimate=pl.CostEstimate(flops=10**6, bytes_accessed=10**4, transcendentals=0),
        name="backward",
    )(place, back_x, *sources, cas_matrix, windows)


def add(a, b):
    return (a.astype(jnp.float32) + b.astype(jnp.float32)).astype(jnp.bfloat16)


def pair_plan(orbitals, source_index):
    _, planes, points = orbitals.shape
    slabs = lax.axis_size("grid")
    extent = planes * slabs
    band, z = lax.axis_index("band"), lax.axis_index("grid")
    column, core = band // cores, band % cores
    half = points // 2
    place = jnp.stack([core, column]).astype(jnp.int32)
    at_home = core == holder(z)

    def only(core):
        return 0

    def same(core):
        return core

    def opposite(core):
        return 1 - core

    own_parity = lax.dynamic_index_in_dim(orbitals, z % 2, 0, keepdims=False)
    relayed, far_second = far_in([own_parity[:, :half], own_parity[:, half:]])
    mine = own_quarter(orbitals, source_index, column, core)
    near = near_in(lax.dynamic_index_in_dim(orbitals, 1 - z % 2, 0, keepdims=False))

    sources_0 = quarters_to_all(mine[None])
    mine_near = jnp.stack([up(mine, 1), up(mine, -1)])
    sources_near = quarters_to_all(mine_near)
    mine_far = up(mine, 2)
    sources_2 = quarters_to_all(mine_far[None])
    sources = [sources_0, sources_near, sources_2, sources_near]
    picks = [only, same, only, opposite]

    far = far_second(jnp.where(core == 0, relayed[0], relayed[1]))
    targets = [
        [jnp.where(at_home, own_parity, swap_cores(own_parity))],
        [near],
        [far, swap_cores(far)],
        [swap_cores(near)],
    ]

    cas_matrix = cas_table(extent)
    windows = window_tables(cas_matrix)
    windows_back = jnp.swapaxes(windows, 1, 2)
    slab_of = jnp.stack([z, z + side(core), z + 2, z - side(core)]) % slabs
    places = ((slab_of * planes)[:, None] + jnp.arange(planes)).reshape(extent)
    into = cas_entries(jnp.arange(extent), places, extent)
    square_x = wave_square(jnp.arange(extent, dtype=jnp.int32), extent)
    strength = (extent * spacing) ** 2 / math.pi
    square = (square_x[:, None] + square_x[None, :] + 1.0) * (1.0 / strength)
    square = jnp.pad(square, ((0, 0), (0, 2 * lanes - extent)), constant_values=1.0)

    along_y = [forward(place, targets[p], sources[p], picks[p], cas_matrix, windows) for p in range(4)]
    back_x = middle(along_y, into, into.T, square)

    def partials(p, parts, *earlier):
        return backward(place, after(back_x[p], *earlier), sources[p], picks[p], cas_matrix, windows_back, parts)

    kept, given = partials(2, 2)
    total = add(kept, swap_cores(given))
    first = far_out_first(total)
    (given,) = partials(3, 1, total)
    far = [far_out_second(first, h) for h in range(2)]
    (kept,) = partials(1, 1, first)
    total = add(kept, swap_cores(given))
    near = near_out(total)
    (kept,) = partials(0, 1, total)
    local = add(kept, swap_cores(kept))
    own_parity = jnp.where(at_home, local, jnp.concatenate(far, axis=1))
    even = z % 2 == 0
    return jnp.stack([jnp.where(even, own_parity, near), jnp.where(even, near, own_parity)])


def solution(mesh):
    def shards(orbitals, source_index):
        slabs, bands = mesh.shape["grid"], mesh.shape["band"]
        fits = slabs == 4 and bands == 8 and orbitals.shape[0] == 2 and source_index.shape[0] == cores
        return (pair_plan if fits else slab_plan)(orbitals, source_index)

    return jax.shard_map(
        shards,
        mesh=mesh,
        in_specs=(P("band", "grid", None), P()),
        out_specs=P("band", "grid", None),
        check_vma=False,
    )
```

```python
import functools
import math

import jax
import jax.numpy as jnp
from jax import lax
from jax.experimental import pallas as pl
from jax.experimental.pallas import tpu as pltpu
from jax.sharding import PartitionSpec as P

spacing = 0.3
cores = 2


def cas_entries(rows, columns, extent):
    products_mod = rows[:, None] * columns[None, :] % extent
    radians = products_mod.astype(jnp.float32) * (2.0 * math.pi / extent)
    return ((jnp.cos(radians) + jnp.sin(radians)) / math.sqrt(extent)).astype(jnp.bfloat16)


def cas_table(extent):
    wavenum = jnp.arange(extent, dtype=jnp.int32)
    return cas_entries(wavenum, wavenum, extent)


def wave_square(indices, extent):
    folded = jnp.minimum(indices, extent - indices).astype(jnp.float32)
    return folded * folded


def coulomb_block(extent, columns, offset):
    square_x = wave_square(jnp.arange(extent, dtype=jnp.int32), extent)
    square_y = wave_square(offset + jnp.arange(columns, dtype=jnp.int32), extent)
    total_sq = square_x[:, None, None] + square_y[None, :, None] + square_x[None, None, :]
    strength = (extent * spacing) ** 2 / math.pi
    return jnp.where(total_sq > 0, strength / (total_sq + 1.0), 0.0)


def transform(grid_data, cas_matrix, pattern):
    return jnp.einsum(pattern, grid_data, cas_matrix, preferred_element_type=jnp.float32)


def broadcast(x, axis, root):
    mine = lax.axis_index(axis) == root
    return lax.psum(jnp.where(mine, x, jnp.zeros_like(x)), axis)


def slab_potentials(pair_rho, cas_matrix, kernel_block):
    along_z = transform(pair_rho, cas_matrix, "pxyz,kz->pxyk").astype(jnp.bfloat16)
    along_y = transform(along_z, cas_matrix, "pxyz,ky->pxkz").astype(jnp.bfloat16)
    turned = lax.all_to_all(along_y, "grid", split_axis=2, concat_axis=1, tiled=True)
    scaled = (kernel_block * transform(turned, cas_matrix, "pxyz,kx->pkyz")).astype(jnp.bfloat16)
    back_x = transform(scaled, cas_matrix, "pxyz,kx->pkyz").astype(jnp.bfloat16)
    returned = lax.all_to_all(back_x, "grid", split_axis=1, concat_axis=2, tiled=True)
    again_y = transform(returned, cas_matrix, "pxyz,ky->pxkz").astype(jnp.bfloat16)
    return transform(again_y, cas_matrix, "pxyz,kz->pxyk")


def fetch_source(orbitals, which):
    local_count = orbitals.shape[0]
    local_slab = lax.dynamic_index_in_dim(orbitals, which % local_count, 0, keepdims=False)
    return broadcast(local_slab, "band", which // local_count)


def slab_plan(orbitals, source_index):
    local_count, planes, _ = orbitals.shape
    extent = planes * lax.axis_size("grid")
    orbitals = orbitals.reshape(local_count, planes, extent, extent)
    source_count = source_index.shape[0]
    cas_matrix = cas_table(extent)
    columns = extent // lax.axis_size("grid")
    kernel_block = coulomb_block(extent, columns, lax.axis_index("grid") * columns)
    fetched = [fetch_source(orbitals, source_index[number]) for number in range(source_count)]
    stacked = jnp.stack(fetched)[:, None].astype(jnp.float32)
    pair_rho = (stacked * orbitals[None].astype(jnp.float32)).astype(jnp.bfloat16)
    pair_rho = pair_rho.reshape(source_count * local_count, planes, extent, extent)
    potential = slab_potentials(pair_rho, cas_matrix, kernel_block)
    potential = potential.reshape(source_count, local_count, planes, extent, extent)
    result = (-jnp.sum(stacked * potential, axis=0)).astype(jnp.bfloat16)
    return result.reshape(local_count, planes, extent * extent)


lanes = 128
quad = 4
ring = 4
turned_pitch = 161
plane_pitch = 41


def move(x, routes):
    slabs = lax.axis_size("grid")

    def place(column, core, z):
        return (column * cores + core) * slabs + z % slabs

    return lax.ppermute(x, ("band", "grid"), [(place(*a), place(*b)) for a, b in routes])


def everywhere():
    columns = lax.axis_size("band") // cores
    return [(c, k, z) for c in range(columns) for k in range(cores) for z in range(lax.axis_size("grid"))]


def swap_cores(x):
    return move(x, [((c, k, z), (c, 1 - k, z)) for c, k, z in everywhere()])


def to_column(x, d):
    return move(x, [((c, k, z), (c ^ d, k, z)) for c, k, z in everywhere()])


def up(x, d):
    return move(x, [((c, k, z), (c, k, z + d)) for c, k, z in everywhere()])


def holder(z):
    return z % ring // 2


def side(core):
    return 2 * core - 1


def near_routes():
    return [((c, holder(z), z + side(k)), (c, k, z)) for c, k, z in everywhere()]


def far_routes():
    return [((c, holder(z), z + 2), (c, k, z)) for c, k, z in everywhere() if k != holder(z)]


def back(routes):
    return [(b, a) for a, b in routes]


def after(x, *others):
    return lax.optimization_barrier((x, *others))[0]


def quarters_to_all(part):
    half = part.shape[2] // 2
    from_x = to_column(part, 1)
    from_y = to_column(part, 2)
    low = to_column(from_x[:, :, :half], 2)
    high = to_column(from_y[:, :, half:], 1)
    return [part, from_x, from_y, low, high]


def own_quarter(picked, other, owner, column, core, earlier):
    quarter = picked.shape[1] // 4
    slab = after(jnp.where(owner % cores == core, picked, swap_cores(other)), earlier)

    def cut(d):
        return lax.dynamic_slice_in_dim(slab, (column ^ d) * quarter, quarter, 1)

    candidates = [cut(0)] + [to_column(cut(d), d) for d in (1, 2, 3)]
    return lax.select_n(column ^ (owner // cores), *candidates)


def choose(first, refs, start):
    if len(refs) == 1:
        start(refs[0])
    else:
        pl.when(first)(lambda: start(refs[0]))
        pl.when(jnp.logical_not(first))(lambda: start(refs[1]))


def start_pieces(pieces, sems):
    for number, (refs, first, to) in enumerate(pieces):
        choose(first, refs, lambda ref, to=to, number=number: pltpu.make_async_copy(ref, to, sems.at[number]).start())


def wait_pieces(pieces, sems):
    for number, (refs, _, to) in enumerate(pieces):
        pltpu.make_async_copy(refs[0], to, sems.at[number]).wait()


def source_pieces(groups, first, source, column):
    quarter = source.shape[1] // 4
    offsets = [(column ^ e) * quarter for e in range(4)]
    offsets.append(offsets[3] + quarter // 2)
    pieces = []
    for number, offset in enumerate(offsets):
        refs = [five[number].at[which] for five, which in groups]
        to = source.at[:, pl.ds(pl.multiple_of(offset, lanes), refs[0].shape[1])]
        pieces.append((refs, first, to))
    return pieces


def split(refs, *counts):
    taken = []
    for count in counts:
        taken.append(refs[:count])
        refs = refs[count:]
    return taken


def place_of(flags):
    return flags[0], flags[1], flags[2] == 1


def dot(a, b):
    return jnp.dot(a, b, preferred_element_type=jnp.float32)


def both(ref, rows):
    return jnp.concatenate([ref[0, rows, :], ref[1, rows, :]], axis=1)


def put_both(ref, rows, value):
    ref[0, rows, :] = value[:, :lanes]
    ref[1, rows, :] = value[:, lanes:]


def lane_ranges(pieces):
    ranges = []
    start = 0
    for piece in pieces:
        ranges.append((start, piece.shape[1]))
        start += piece.shape[1]
    return ranges


def pick_kernel(flags, orbitals, *refs):
    outs, sems = refs[:-1], refs[-1]
    parts = len(outs) // flags.shape[0]
    ranges = lane_ranges(outs[:parts])
    copies = []
    for n, out in enumerate(outs):
        lane = pl.ds(*ranges[n % parts])
        copies.append(pltpu.make_async_copy(orbitals.at[flags[n // parts], :, lane], out, sems.at[n]))
    for copy in copies:
        copy.start()
    for copy in copies:
        copy.wait()


def put_kernel(flags, *refs):
    choices, out, sems = refs[1:-2], refs[-2], refs[-1]
    count = sems.shape[0]
    ranges = lane_ranges(choices[:count])
    pieces = [
        (choices[n::count], flags[0] == 1, out.at[flags[1], :, pl.ds(*lane)]) for n, lane in enumerate(ranges)
    ]
    start_pieces(pieces, sems)
    wait_pieces(pieces, sems)


def forward_kernel(pick, choices, count, flags, *refs):
    targets, five, (cas, windows, out, target, source, turned, sems) = split(refs, choices * count, 5, 7)
    planes, points = target.shape
    extent = cas.shape[0]
    core, column, at_home = place_of(flags)
    ranges = lane_ranges(targets[:count])
    pieces = [(targets[n::count], at_home, target.at[:, pl.ds(*lane)]) for n, lane in enumerate(ranges)]
    pieces += source_pieces([(five, pick(core))], None, source, column)
    start_pieces(pieces, sems)
    wait_pieces(pieces, sems)
    step = 8
    block = quad * extent

    @pl.loop(0, points // block // step)
    def _(i):
        for r in range(quad):
            density = []
            for j in range(step):
                at = pl.ds(pl.multiple_of((i * step + j) * block + r * lanes, lanes), 2 * lanes)
                density.append(source[:, at].astype(jnp.float32) * target[:, at].astype(jnp.float32))
            density = jnp.concatenate(density, axis=0).astype(jnp.bfloat16)
            along_z = dot(density, windows[r])
            for j in range(step):
                y = (i * step + j) * quad + r
                put_both(turned, pl.ds(y, planes, stride=turned_pitch), along_z[j * planes : (j + 1) * planes])

    @pl.loop(0, planes // 4)
    def _(i):
        for j in range(4):
            x = i * 4 + j
            along_z = both(turned, pl.ds(x * turned_pitch, extent)).astype(jnp.bfloat16)
            put_both(out, pl.ds(x, extent, stride=plane_pitch), dot(cas[...], along_z))


def middle_kernel(g0, g1, g2, g3, into, back, square, o0, o1, o2, o3):
    rows = g0.shape[1] // plane_pitch
    extent = square.shape[0]
    planes = extent // ring
    strength = (extent * spacing) ** 2 / math.pi
    first = pl.program_id(0) * rows
    for i in range(rows):
        at = pl.ds(i * plane_pitch, planes)
        along_y = jnp.concatenate([both(g, at) for g in (g0, g1, g2, g3)], axis=0).astype(jnp.bfloat16)
        ky = first + i
        folded = jnp.minimum(ky, extent - ky)
        weight = square[...] + (folded * folded).astype(jnp.float32) * (1.0 / strength)
        guess = pl.reciprocal(weight, approx=True)
        factor = guess * (2.0 - weight * guess)
        factor = jnp.where(weight > 1.25 / strength, factor, 0.0)
        scaled = (factor * dot(into[...], along_y)).astype(jnp.bfloat16)
        back_x = dot(back[...], scaled)
        for d, o in enumerate((o0, o1, o2, o3)):
            put_both(o, at, back_x[d * planes : (d + 1) * planes])


def backward_kernel(picks, parts, flags, *refs):
    slabs, groups, rest, outs, (back_x, source, turned, sems) = split(
        refs, len(picks), 5 * len(picks), 2, parts, 4
    )
    cas, windows = rest
    planes, points = source.shape
    extent = cas.shape[0]
    core, column, at_home = place_of(flags)
    groups = [(groups[5 * n : 5 * n + 5], pick(core)) for n, pick in enumerate(picks)]
    pieces = [(slabs, at_home, back_x)] + source_pieces(groups, at_home, source, column)
    start_pieces(pieces, sems)
    wait_pieces(pieces, sems)

    @pl.loop(0, planes // 4)
    def _(i):
        for j in range(4):
            x = i * 4 + j
            column_x = both(back_x, pl.ds(x, extent, stride=plane_pitch)).astype(jnp.bfloat16)
            put_both(turned, pl.ds(x * turned_pitch, extent), dot(cas[...], column_x))

    step = 5
    block = quad * extent
    blocks = points // block // parts
    for number, out in enumerate(outs):

        @pl.loop(0, blocks // step)
        def _(i):
            first = number * blocks + i * step
            windowed = []
            for r in range(quad):
                again_y = jnp.concatenate(
                    [both(turned, pl.ds((first + j) * quad + r, planes, stride=turned_pitch)) for j in range(step)],
                    axis=0,
                ).astype(jnp.bfloat16)
                windowed.append(dot(again_y, windows[r]))
            for j in range(step):
                w = [part[j * planes : (j + 1) * planes] for part in windowed]
                potential = [w[0][:, :lanes]]
                potential += [w[r][:, lanes:] + w[r + 1][:, :lanes] for r in range(quad - 1)]
                potential = jnp.concatenate(potential + [w[-1][:, lanes:]], axis=1)
                at = pl.ds(pl.multiple_of((first + j) * block, lanes), block)
                to = pl.ds(pl.multiple_of((i * step + j) * block, lanes), block)
                out[:, to] = (-(source[:, at].astype(jnp.float32) * potential)).astype(jnp.bfloat16)


def window_tables(cas_matrix):
    extent = cas_matrix.shape[0]
    tables = []
    for r in range(quad):
        shift = r * extent % lanes
        tables.append(jnp.pad(cas_matrix, ((shift, 2 * lanes - extent - shift), (0, 2 * lanes - extent))))
    return jnp.stack(tables)


limit = 56 * 2**20
whole = pl.BlockSpec(memory_space=pltpu.VMEM)
outside = pl.BlockSpec(memory_space=pl.ANY)
scalars = pl.BlockSpec(memory_space=pltpu.SMEM)
small = pl.CostEstimate(flops=10**6, bytes_accessed=10**4, transcendentals=0)


def pick(orbitals, which, shares=(1,)):
    _, planes, points = orbitals.shape
    unit = points // sum(shares)
    outs = [jax.ShapeDtypeStruct((planes, share * unit), orbitals.dtype) for share in shares] * len(which)
    count = len(outs)
    return pl.pallas_call(
        pick_kernel,
        out_shape=outs,
        in_specs=[scalars, outside],
        out_specs=[outside] * count,
        scratch_shapes=[pltpu.SemaphoreType.DMA((count,))],
        cost_estimate=small,
        name="pick",
    )(jnp.stack(which).astype(jnp.int32), orbitals)


def put(out, first, which, *choices):
    return pl.pallas_call(
        put_kernel,
        out_shape=jax.ShapeDtypeStruct(out.shape, out.dtype),
        in_specs=[scalars] + [outside] * (1 + len(choices) * len(choices[0])),
        out_specs=outside,
        scratch_shapes=[pltpu.SemaphoreType.DMA((len(choices[0]),))],
        input_output_aliases={1: 0},
        cost_estimate=small,
        name="put",
    )(jnp.stack([first, which]).astype(jnp.int32), out, *[piece for choice in choices for piece in choice])


def forward(flags, targets, group, which, cas_matrix, windows):
    planes = group[0].shape[1]
    extent = cas_matrix.shape[0]
    points = extent * extent
    return pl.pallas_call(
        functools.partial(forward_kernel, which, len(targets), len(targets[0])),
        out_shape=jax.ShapeDtypeStruct((2, extent * plane_pitch, lanes), jnp.float32),
        in_specs=[scalars] + [outside] * (len(targets) * len(targets[0]) + 5) + [whole] * 2,
        out_specs=whole,
        scratch_shapes=[
            pltpu.VMEM((planes, points), jnp.bfloat16),
            pltpu.VMEM((planes, points), jnp.bfloat16),
            pltpu.VMEM((2, planes * turned_pitch, lanes), jnp.float32),
            pltpu.SemaphoreType.DMA((len(targets[0]) + 5,)),
        ],
        compiler_params=pltpu.CompilerParams(vmem_limit_bytes=limit),
        cost_estimate=small,
        name="forward",
    )(flags, *[piece for choice in targets for piece in choice], *group, cas_matrix, windows)


def middle(slabs, into, back, square):
    extent = square.shape[0]
    rows = 8
    block = pl.BlockSpec((2, rows * plane_pitch, lanes), lambda i: (0, i, 0))

    def same(shape):
        return pl.BlockSpec(shape, lambda i: (0, 0))

    return pl.pallas_call(
        middle_kernel,
        grid=(extent // rows,),
        out_shape=[jax.ShapeDtypeStruct(slabs[0].shape, jnp.float32)] * 4,
        in_specs=[block] * 4 + [same(into.shape), same(back.shape), same(square.shape)],
        out_specs=[block] * 4,
        compiler_params=pltpu.CompilerParams(vmem_limit_bytes=limit),
        cost_estimate=small,
        name="middle",
    )(*slabs, into, back, square)


def backward(flags, slabs, groups, picks, cas_matrix, windows, parts):
    planes = groups[0][0].shape[1]
    extent = cas_matrix.shape[0]
    points = extent * extent
    pieces = [piece for group in groups for piece in group]
    return pl.pallas_call(
        functools.partial(backward_kernel, picks, parts),
        out_shape=[jax.ShapeDtypeStruct((planes, points // parts), jnp.bfloat16)] * parts,
        in_specs=[scalars] + [outside] * (len(slabs) + len(pieces)) + [whole] * 2,
        out_specs=[whole] * parts,
        scratch_shapes=[
            pltpu.VMEM(slabs[0].shape, jnp.float32),
            pltpu.VMEM((planes, points), jnp.bfloat16),
            pltpu.VMEM((2, planes * turned_pitch, lanes), jnp.float32),
            pltpu.SemaphoreType.DMA((6,)),
        ],
        compiler_params=pltpu.CompilerParams(vmem_limit_bytes=limit),
        cost_estimate=small,
        name="backward",
    )(flags, *slabs, *pieces, cas_matrix, windows)


def add(a, b):
    return (a.astype(jnp.float32) + b.astype(jnp.float32)).astype(jnp.bfloat16)


def pair_plan(orbitals, source_index):
    local_count, planes, points = orbitals.shape
    slabs = lax.axis_size("grid")
    extent = planes * slabs
    band, z = lax.axis_index("band"), lax.axis_index("grid")
    column, core = band // cores, band % cores
    at_home = core == holder(z)
    flags = jnp.stack([core, column, at_home.astype(jnp.int32)]).astype(jnp.int32)
    parity = z % 2

    to_near = pick(orbitals, [1 - parity], (1, 2, 1))
    near = [move(part, near_routes()) for part in to_near]
    chosen = [source_index[core] % local_count, source_index[1 - core] % local_count]
    picked, other = pick(after(orbitals, to_near[0]), chosen)
    mine = own_quarter(picked, other, source_index[core] // local_count, column, core, near[0])
    (own_parity,) = pick(after(orbitals, mine), [parity])

    source_0 = quarters_to_all(mine[None])
    sent = after(mine, near[1])
    others = jnp.stack([up(sent, 1), up(sent, -1), up(sent, 2)])
    source_others = quarters_to_all(after(others, source_0[1], source_0[2]))
    far = move(after(own_parity, others), far_routes())

    near_swapped = [swap_cores(after(half, source_others[0])) for half in near]
    swapped = swap_cores(jnp.where(at_home, own_parity, far))
    targets = [[[own_parity], [swapped]], [near], [[swapped], [far]], [near_swapped]]
    sources = [source_0, source_others, source_others, source_others]
    which = [lambda core: 0, lambda core: core, lambda core: 2, lambda core: 1 - core]

    cas_matrix = cas_table(extent)
    windows = window_tables(cas_matrix)
    windows_back = jnp.swapaxes(windows, 1, 2)
    slab_of = jnp.stack([z, z + side(core), z + 2, z - side(core)]) % slabs
    places = ((slab_of * planes)[:, None] + jnp.arange(planes)).reshape(extent)
    into = cas_entries(jnp.arange(extent), places, extent)
    square_x = wave_square(jnp.arange(extent, dtype=jnp.int32), extent)
    strength = (extent * spacing) ** 2 / math.pi
    square = (square_x[:, None] + square_x[None, :] + 1.0) * (1.0 / strength)
    square = jnp.pad(square, ((0, 0), (0, 2 * lanes - extent)), constant_values=1.0)

    along_y = [forward(flags, targets[p], sources[p], which[p], cas_matrix, windows) for p in range(4)]
    back_x = middle(along_y, into, into.T, square)

    def partials(places, parts, *earlier):
        return backward(
            flags,
            [after(back_x[p], *earlier) for p in places],
            [sources[p] for p in places],
            [which[p] for p in places],
            cas_matrix,
            windows_back,
            parts,
        )

    def total(kept, given):
        return jnp.concatenate([add(k, swap_cores(g)) for k, g in zip(kept, given)], axis=1)

    near = total(partials([1], 2), partials([3], 2))
    near_home = move(near, back(near_routes()))
    given = partials([2, 0], 4, near)
    kept = partials([0, 2], 4, given[0])
    far = [total(kept[n : n + 2], given[n : n + 2]) for n in (0, 2)]
    far_home = [move(half, back(far_routes())) for half in far]
    result = put(jnp.zeros(orbitals.shape, orbitals.dtype), at_home, parity, far, far_home)
    return put(result, at_home, 1 - parity, [near_home])


def solution(mesh):
    def shards(orbitals, source_index):
        slabs, bands = mesh.shape["grid"], mesh.shape["band"]
        fits = slabs == 4 and bands == 8 and orbitals.shape[0] == 2 and source_index.shape[0] == cores
        return (pair_plan if fits else slab_plan)(orbitals, source_index)

    return jax.shard_map(
        shards,
        mesh=mesh,
        in_specs=(P("band", "grid", None), P()),
        out_specs=P("band", "grid", None),
        check_vma=False,
    )
```

```python
import functools
import math

import jax
import jax.numpy as jnp
from jax import lax
from jax.experimental import pallas as pl
from jax.experimental.pallas import tpu as pltpu
from jax.sharding import PartitionSpec as P

spacing = 0.3
cores = 2


def cas_entries(rows, columns, extent):
    products_mod = rows[:, None] * columns[None, :] % extent
    radians = products_mod.astype(jnp.float32) * (2.0 * math.pi / extent)
    return ((jnp.cos(radians) + jnp.sin(radians)) / math.sqrt(extent)).astype(jnp.bfloat16)


def cas_table(extent):
    wavenum = jnp.arange(extent, dtype=jnp.int32)
    return cas_entries(wavenum, wavenum, extent)


def wave_square(indices, extent):
    folded = jnp.minimum(indices, extent - indices).astype(jnp.float32)
    return folded * folded


def coulomb_block(extent, columns, offset):
    square_x = wave_square(jnp.arange(extent, dtype=jnp.int32), extent)
    square_y = wave_square(offset + jnp.arange(columns, dtype=jnp.int32), extent)
    total_sq = square_x[:, None, None] + square_y[None, :, None] + square_x[None, None, :]
    strength = (extent * spacing) ** 2 / math.pi
    return jnp.where(total_sq > 0, strength / (total_sq + 1.0), 0.0)


def transform(grid_data, cas_matrix, pattern):
    return jnp.einsum(pattern, grid_data, cas_matrix, preferred_element_type=jnp.float32)


def broadcast(x, axis, root):
    mine = lax.axis_index(axis) == root
    return lax.psum(jnp.where(mine, x, jnp.zeros_like(x)), axis)


def slab_potentials(pair_rho, cas_matrix, kernel_block):
    along_z = transform(pair_rho, cas_matrix, "pxyz,kz->pxyk").astype(jnp.bfloat16)
    along_y = transform(along_z, cas_matrix, "pxyz,ky->pxkz").astype(jnp.bfloat16)
    turned = lax.all_to_all(along_y, "grid", split_axis=2, concat_axis=1, tiled=True)
    scaled = (kernel_block * transform(turned, cas_matrix, "pxyz,kx->pkyz")).astype(jnp.bfloat16)
    back_x = transform(scaled, cas_matrix, "pxyz,kx->pkyz").astype(jnp.bfloat16)
    returned = lax.all_to_all(back_x, "grid", split_axis=1, concat_axis=2, tiled=True)
    again_y = transform(returned, cas_matrix, "pxyz,ky->pxkz").astype(jnp.bfloat16)
    return transform(again_y, cas_matrix, "pxyz,kz->pxyk")


def fetch_source(orbitals, which):
    local_count = orbitals.shape[0]
    local_slab = lax.dynamic_index_in_dim(orbitals, which % local_count, 0, keepdims=False)
    return broadcast(local_slab, "band", which // local_count)


def slab_plan(orbitals, source_index):
    local_count, planes, _ = orbitals.shape
    extent = planes * lax.axis_size("grid")
    orbitals = orbitals.reshape(local_count, planes, extent, extent)
    source_count = source_index.shape[0]
    cas_matrix = cas_table(extent)
    columns = extent // lax.axis_size("grid")
    kernel_block = coulomb_block(extent, columns, lax.axis_index("grid") * columns)
    fetched = [fetch_source(orbitals, source_index[number]) for number in range(source_count)]
    stacked = jnp.stack(fetched)[:, None].astype(jnp.float32)
    pair_rho = (stacked * orbitals[None].astype(jnp.float32)).astype(jnp.bfloat16)
    pair_rho = pair_rho.reshape(source_count * local_count, planes, extent, extent)
    potential = slab_potentials(pair_rho, cas_matrix, kernel_block)
    potential = potential.reshape(source_count, local_count, planes, extent, extent)
    result = (-jnp.sum(stacked * potential, axis=0)).astype(jnp.bfloat16)
    return result.reshape(local_count, planes, extent * extent)


lanes = 128
quad = 4
ring = 4
turned_pitch = 161
plane_pitch = 41


def move(x, routes):
    slabs = lax.axis_size("grid")

    def place(column, core, z):
        return (column * cores + core) * slabs + z % slabs

    return lax.ppermute(x, ("band", "grid"), [(place(*a), place(*b)) for a, b in routes])


def everywhere():
    columns = lax.axis_size("band") // cores
    return [(c, k, z) for c in range(columns) for k in range(cores) for z in range(lax.axis_size("grid"))]


def swap_cores(x):
    return move(x, [((c, k, z), (c, 1 - k, z)) for c, k, z in everywhere()])


def to_column(x, d):
    return move(x, [((c, k, z), (c ^ d, k, z)) for c, k, z in everywhere()])


def up(x, d):
    return move(x, [((c, k, z), (c, k, z + d)) for c, k, z in everywhere()])


def holder(z):
    return z % ring // 2


def side(core):
    return 2 * core - 1


def near_routes():
    return [((c, holder(z), z + side(k)), (c, k, z)) for c, k, z in everywhere()]


def far_routes():
    return [((c, holder(z), z + 2), (c, k, z)) for c, k, z in everywhere() if k != holder(z)]


def back(routes):
    return [(b, a) for a, b in routes]


def after(x, *others):
    return lax.optimization_barrier((x, *others))[0]


def quarters_to_all(part):
    half = part.shape[2] // 2
    from_x = to_column(part, 1)
    from_y = to_column(part, 2)
    low = to_column(from_x[:, :, :half], 2)
    high = to_column(from_y[:, :, half:], 1)
    return [part, from_x, from_y, low, high]


def own_quarter(picked, other, owner, column, core, earlier):
    quarter = picked.shape[1] // 4
    slab = after(jnp.where(owner % cores == core, picked, swap_cores(other)), earlier)

    def cut(d):
        return lax.dynamic_slice_in_dim(slab, (column ^ d) * quarter, quarter, 1)

    candidates = [cut(0)] + [to_column(cut(d), d) for d in (1, 2, 3)]
    return lax.select_n(column ^ (owner // cores), *candidates)


def choose(first, refs, start):
    if len(refs) == 1:
        start(refs[0])
    else:
        pl.when(first)(lambda: start(refs[0]))
        pl.when(jnp.logical_not(first))(lambda: start(refs[1]))


def start_pieces(pieces, sems):
    for number, (refs, first, to) in enumerate(pieces):
        choose(first, refs, lambda ref, to=to, number=number: pltpu.make_async_copy(ref, to, sems.at[number]).start())


def wait_pieces(pieces, sems):
    for number, (refs, _, to) in enumerate(pieces):
        pltpu.make_async_copy(refs[0], to, sems.at[number]).wait()


def source_pieces(groups, first, source, column):
    quarter = source.shape[1] // 4
    offsets = [(column ^ e) * quarter for e in range(4)]
    offsets.append(offsets[3] + quarter // 2)
    pieces = []
    for number, offset in enumerate(offsets):
        refs = [five[number].at[which] for five, which in groups]
        to = source.at[:, pl.ds(pl.multiple_of(offset, lanes), refs[0].shape[1])]
        pieces.append((refs, first, to))
    return pieces


def split(refs, *counts):
    taken = []
    for count in counts:
        taken.append(refs[:count])
        refs = refs[count:]
    return taken


def place_of(flags):
    return flags[0], flags[1], flags[2] == 1


def dot(a, b):
    return jnp.dot(a, b, preferred_element_type=jnp.float32)


def both(ref, rows):
    return jnp.concatenate([ref[0, rows, :], ref[1, rows, :]], axis=1)


def put_both(ref, rows, value):
    ref[0, rows, :] = value[:, :lanes]
    ref[1, rows, :] = value[:, lanes:]


def lane_ranges(pieces):
    ranges = []
    start = 0
    for piece in pieces:
        ranges.append((start, piece.shape[1]))
        start += piece.shape[1]
    return ranges


def pick_kernel(flags, orbitals, *refs):
    outs, sems = refs[:-1], refs[-1]
    parts = len(outs) // flags.shape[0]
    ranges = lane_ranges(outs[:parts])
    copies = []
    for n, out in enumerate(outs):
        lane = pl.ds(*ranges[n % parts])
        copies.append(pltpu.make_async_copy(orbitals.at[flags[n // parts], :, lane], out, sems.at[n]))
    for copy in copies:
        copy.start()
    for copy in copies:
        copy.wait()


def put_kernel(flags, *refs):
    choices, (out, staged, sems, out_sem) = refs[1:-4], refs[-4:]
    count = sems.shape[0]
    ranges = lane_ranges(choices[:count])
    pieces = [
        (choices[n::count], flags[0] == 1, staged.at[:, pl.ds(*lane)]) for n, lane in enumerate(ranges)
    ]
    start_pieces(pieces, sems)
    wait_pieces(pieces, sems)
    copy = pltpu.make_async_copy(staged, out.at[flags[1]], out_sem)
    copy.start()
    copy.wait()


def forward_kernel(pick, choices, count, flags, *refs):
    targets, five, (cas, windows, out, target, source, turned, sems) = split(refs, choices * count, 5, 7)
    planes, points = target.shape
    extent = cas.shape[0]
    core, column, at_home = place_of(flags)
    ranges = lane_ranges(targets[:count])
    pieces = [(targets[n::count], at_home, target.at[:, pl.ds(*lane)]) for n, lane in enumerate(ranges)]
    pieces += source_pieces([(five, pick(core))], None, source, column)
    start_pieces(pieces, sems)
    wait_pieces(pieces, sems)
    step = 8
    block = quad * extent

    @pl.loop(0, points // block // step)
    def _(i):
        for r in range(quad):
            density = []
            for j in range(step):
                at = pl.ds(pl.multiple_of((i * step + j) * block + r * lanes, lanes), 2 * lanes)
                density.append(source[:, at].astype(jnp.float32) * target[:, at].astype(jnp.float32))
            density = jnp.concatenate(density, axis=0).astype(jnp.bfloat16)
            along_z = dot(density, windows[r])
            for j in range(step):
                y = (i * step + j) * quad + r
                put_both(turned, pl.ds(y, planes, stride=turned_pitch), along_z[j * planes : (j + 1) * planes])

    @pl.loop(0, planes // 4)
    def _(i):
        for j in range(4):
            x = i * 4 + j
            along_z = both(turned, pl.ds(x * turned_pitch, extent)).astype(jnp.bfloat16)
            put_both(out, pl.ds(x, extent, stride=plane_pitch), dot(cas[...], along_z))


def middle_kernel(g0, g1, g2, g3, into, back, square, o0, o1, o2, o3):
    rows = g0.shape[1] // plane_pitch
    extent = square.shape[0]
    planes = extent // ring
    strength = (extent * spacing) ** 2 / math.pi
    first = pl.program_id(0) * rows
    for i in range(rows):
        at = pl.ds(i * plane_pitch, planes)
        along_y = jnp.concatenate([both(g, at) for g in (g0, g1, g2, g3)], axis=0).astype(jnp.bfloat16)
        ky = first + i
        folded = jnp.minimum(ky, extent - ky)
        weight = square[...] + (folded * folded).astype(jnp.float32) * (1.0 / strength)
        guess = pl.reciprocal(weight, approx=True)
        factor = guess * (2.0 - weight * guess)
        factor = jnp.where(weight > 1.25 / strength, factor, 0.0)
        scaled = (factor * dot(into[...], along_y)).astype(jnp.bfloat16)
        back_x = dot(back[...], scaled)
        for d, o in enumerate((o0, o1, o2, o3)):
            put_both(o, at, back_x[d * planes : (d + 1) * planes])


def backward_kernel(picks, parts, flags, *refs):
    slabs, groups, rest, outs, (back_x, source, turned, sems) = split(
        refs, len(picks), 5 * len(picks), 2, parts, 4
    )
    cas, windows = rest
    planes, points = source.shape
    extent = cas.shape[0]
    core, column, at_home = place_of(flags)
    groups = [(groups[5 * n : 5 * n + 5], pick(core)) for n, pick in enumerate(picks)]
    pieces = [(slabs, at_home, back_x)] + source_pieces(groups, at_home, source, column)
    start_pieces(pieces, sems)
    wait_pieces(pieces, sems)

    @pl.loop(0, planes // 4)
    def _(i):
        for j in range(4):
            x = i * 4 + j
            column_x = both(back_x, pl.ds(x, extent, stride=plane_pitch)).astype(jnp.bfloat16)
            put_both(turned, pl.ds(x * turned_pitch, extent), dot(cas[...], column_x))

    step = 5
    block = quad * extent
    blocks = points // block // parts
    for number, out in enumerate(outs):

        @pl.loop(0, blocks // step)
        def _(i):
            first = number * blocks + i * step
            windowed = []
            for r in range(quad):
                again_y = jnp.concatenate(
                    [both(turned, pl.ds((first + j) * quad + r, planes, stride=turned_pitch)) for j in range(step)],
                    axis=0,
                ).astype(jnp.bfloat16)
                windowed.append(dot(again_y, windows[r]))
            for j in range(step):
                w = [part[j * planes : (j + 1) * planes] for part in windowed]
                potential = [w[0][:, :lanes]]
                potential += [w[r][:, lanes:] + w[r + 1][:, :lanes] for r in range(quad - 1)]
                potential = jnp.concatenate(potential + [w[-1][:, lanes:]], axis=1)
                at = pl.ds(pl.multiple_of((first + j) * block, lanes), block)
                to = pl.ds(pl.multiple_of((i * step + j) * block, lanes), block)
                out[:, to] = (-(source[:, at].astype(jnp.float32) * potential)).astype(jnp.bfloat16)


def window_tables(cas_matrix):
    extent = cas_matrix.shape[0]
    tables = []
    for r in range(quad):
        shift = r * extent % lanes
        tables.append(jnp.pad(cas_matrix, ((shift, 2 * lanes - extent - shift), (0, 2 * lanes - extent))))
    return jnp.stack(tables)


limit = 56 * 2**20
whole = pl.BlockSpec(memory_space=pltpu.VMEM)
outside = pl.BlockSpec(memory_space=pl.ANY)
scalars = pl.BlockSpec(memory_space=pltpu.SMEM)
small = pl.CostEstimate(flops=10**6, bytes_accessed=10**4, transcendentals=0)


def pick(orbitals, which, shares=(1,)):
    _, planes, points = orbitals.shape
    unit = points // sum(shares)
    outs = [jax.ShapeDtypeStruct((planes, share * unit), orbitals.dtype) for share in shares] * len(which)
    count = len(outs)
    return pl.pallas_call(
        pick_kernel,
        out_shape=outs,
        in_specs=[scalars, outside],
        out_specs=[whole] * count,
        scratch_shapes=[pltpu.SemaphoreType.DMA((count,))],
        compiler_params=pltpu.CompilerParams(vmem_limit_bytes=limit),
        cost_estimate=small,
        name="pick",
    )(jnp.stack(which).astype(jnp.int32), orbitals)


def put(out, first, which, *choices):
    return pl.pallas_call(
        put_kernel,
        out_shape=jax.ShapeDtypeStruct(out.shape, out.dtype),
        in_specs=[scalars] + [outside] * (1 + len(choices) * len(choices[0])),
        out_specs=outside,
        scratch_shapes=[
            pltpu.VMEM(out.shape[1:], out.dtype),
            pltpu.SemaphoreType.DMA((len(choices[0]),)),
            pltpu.SemaphoreType.DMA,
        ],
        input_output_aliases={1: 0},
        compiler_params=pltpu.CompilerParams(vmem_limit_bytes=limit),
        cost_estimate=small,
        name="put",
    )(jnp.stack([first, which]).astype(jnp.int32), out, *[piece for choice in choices for piece in choice])


def forward(flags, targets, group, which, cas_matrix, windows):
    planes = group[0].shape[1]
    extent = cas_matrix.shape[0]
    points = extent * extent
    return pl.pallas_call(
        functools.partial(forward_kernel, which, len(targets), len(targets[0])),
        out_shape=jax.ShapeDtypeStruct((2, extent * plane_pitch, lanes), jnp.float32),
        in_specs=[scalars] + [outside] * (len(targets) * len(targets[0]) + 5) + [whole] * 2,
        out_specs=whole,
        scratch_shapes=[
            pltpu.VMEM((planes, points), jnp.bfloat16),
            pltpu.VMEM((planes, points), jnp.bfloat16),
            pltpu.VMEM((2, planes * turned_pitch, lanes), jnp.float32),
            pltpu.SemaphoreType.DMA((len(targets[0]) + 5,)),
        ],
        compiler_params=pltpu.CompilerParams(vmem_limit_bytes=limit),
        cost_estimate=small,
        name="forward",
    )(flags, *[piece for choice in targets for piece in choice], *group, cas_matrix, windows)


def middle(slabs, into, back, square):
    extent = square.shape[0]
    rows = 8
    block = pl.BlockSpec((2, rows * plane_pitch, lanes), lambda i: (0, i, 0))

    def same(shape):
        return pl.BlockSpec(shape, lambda i: (0, 0))

    return pl.pallas_call(
        middle_kernel,
        grid=(extent // rows,),
        out_shape=[jax.ShapeDtypeStruct(slabs[0].shape, jnp.float32)] * 4,
        in_specs=[block] * 4 + [same(into.shape), same(back.shape), same(square.shape)],
        out_specs=[block] * 4,
        compiler_params=pltpu.CompilerParams(vmem_limit_bytes=limit),
        cost_estimate=small,
        name="middle",
    )(*slabs, into, back, square)


def backward(flags, slabs, groups, picks, cas_matrix, windows, parts):
    planes = groups[0][0].shape[1]
    extent = cas_matrix.shape[0]
    points = extent * extent
    pieces = [piece for group in groups for piece in group]
    return pl.pallas_call(
        functools.partial(backward_kernel, picks, parts),
        out_shape=[jax.ShapeDtypeStruct((planes, points // parts), jnp.bfloat16)] * parts,
        in_specs=[scalars] + [outside] * (len(slabs) + len(pieces)) + [whole] * 2,
        out_specs=[whole] * parts,
        scratch_shapes=[
            pltpu.VMEM(slabs[0].shape, jnp.float32),
            pltpu.VMEM((planes, points), jnp.bfloat16),
            pltpu.VMEM((2, planes * turned_pitch, lanes), jnp.float32),
            pltpu.SemaphoreType.DMA((6,)),
        ],
        compiler_params=pltpu.CompilerParams(vmem_limit_bytes=limit),
        cost_estimate=small,
        name="backward",
    )(flags, *slabs, *pieces, cas_matrix, windows)


def add(a, b):
    return (a.astype(jnp.float32) + b.astype(jnp.float32)).astype(jnp.bfloat16)


def pair_plan(orbitals, source_index):
    local_count, planes, points = orbitals.shape
    slabs = lax.axis_size("grid")
    extent = planes * slabs
    band, z = lax.axis_index("band"), lax.axis_index("grid")
    column, core = band // cores, band % cores
    at_home = core == holder(z)
    flags = jnp.stack([core, column, at_home.astype(jnp.int32)]).astype(jnp.int32)
    parity = z % 2

    to_near = pick(orbitals, [1 - parity], (1, 2, 1))
    near = [move(part, near_routes()) for part in to_near]
    chosen = [source_index[core] % local_count, source_index[1 - core] % local_count]
    picked, other = pick(after(orbitals, to_near[0]), chosen)
    mine = own_quarter(picked, other, source_index[core] // local_count, column, core, near[0])
    (own_parity,) = pick(after(orbitals, mine), [parity])

    source_0 = quarters_to_all(mine[None])
    sent = after(mine, near[1])
    others = jnp.stack([up(sent, 1), up(sent, -1), up(sent, 2)])
    source_others = quarters_to_all(after(others, source_0[1], source_0[2]))
    far = move(after(own_parity, others), far_routes())

    near_swapped = [swap_cores(after(half, source_others[0])) for half in near]
    swapped = swap_cores(jnp.where(at_home, own_parity, far))
    targets = [[[own_parity], [swapped]], [near], [[swapped], [far]], [near_swapped]]
    sources = [source_0, source_others, source_others, source_others]
    which = [lambda core: 0, lambda core: core, lambda core: 2, lambda core: 1 - core]

    cas_matrix = cas_table(extent)
    windows = window_tables(cas_matrix)
    windows_back = jnp.swapaxes(windows, 1, 2)
    slab_of = jnp.stack([z, z + side(core), z + 2, z - side(core)]) % slabs
    places = ((slab_of * planes)[:, None] + jnp.arange(planes)).reshape(extent)
    into = cas_entries(jnp.arange(extent), places, extent)
    square_x = wave_square(jnp.arange(extent, dtype=jnp.int32), extent)
    strength = (extent * spacing) ** 2 / math.pi
    square = (square_x[:, None] + square_x[None, :] + 1.0) * (1.0 / strength)
    square = jnp.pad(square, ((0, 0), (0, 2 * lanes - extent)), constant_values=1.0)

    along_y = [forward(flags, targets[p], sources[p], which[p], cas_matrix, windows) for p in range(4)]
    back_x = middle(along_y, into, into.T, square)

    def partials(places, parts, *earlier):
        return backward(
            flags,
            [after(back_x[p], *earlier) for p in places],
            [sources[p] for p in places],
            [which[p] for p in places],
            cas_matrix,
            windows_back,
            parts,
        )

    def total(kept, given):
        return jnp.concatenate([add(k, swap_cores(g)) for k, g in zip(kept, given)], axis=1)

    near = total(partials([1], 2), partials([3], 2))
    near_home = move(near, back(near_routes()))
    given = partials([2, 0], 4, near)
    kept = partials([0, 2], 4, given[0])
    far = [total(kept[n : n + 2], given[n : n + 2]) for n in (0, 2)]
    far_home = [move(half, back(far_routes())) for half in far]
    result = put(jnp.zeros(orbitals.shape, orbitals.dtype), at_home, parity, far, far_home)
    return put(result, at_home, 1 - parity, [near_home])


def solution(mesh):
    def shards(orbitals, source_index):
        slabs, bands = mesh.shape["grid"], mesh.shape["band"]
        fits = slabs == 4 and bands == 8 and orbitals.shape[0] == 2 and source_index.shape[0] == cores
        return (pair_plan if fits else slab_plan)(orbitals, source_index)

    return jax.shard_map(
        shards,
        mesh=mesh,
        in_specs=(P("band", "grid", None), P()),
        out_specs=P("band", "grid", None),
        check_vma=False,
    )
```

```python
import functools
import math

import jax
import jax.numpy as jnp
from jax import lax
from jax.experimental import pallas as pl
from jax.experimental.pallas import tpu as pltpu
from jax.sharding import PartitionSpec as P

spacing = 0.3
cores = 2


def cas_entries(rows, columns, extent):
    products_mod = rows[:, None] * columns[None, :] % extent
    radians = products_mod.astype(jnp.float32) * (2.0 * math.pi / extent)
    return ((jnp.cos(radians) + jnp.sin(radians)) / math.sqrt(extent)).astype(jnp.bfloat16)


def cas_table(extent):
    wavenum = jnp.arange(extent, dtype=jnp.int32)
    return cas_entries(wavenum, wavenum, extent)


def wave_square(indices, extent):
    folded = jnp.minimum(indices, extent - indices).astype(jnp.float32)
    return folded * folded


def coulomb_block(extent, columns, offset):
    square_x = wave_square(jnp.arange(extent, dtype=jnp.int32), extent)
    square_y = wave_square(offset + jnp.arange(columns, dtype=jnp.int32), extent)
    total_sq = square_x[:, None, None] + square_y[None, :, None] + square_x[None, None, :]
    strength = (extent * spacing) ** 2 / math.pi
    return jnp.where(total_sq > 0, strength / (total_sq + 1.0), 0.0)


def transform(grid_data, cas_matrix, pattern):
    return jnp.einsum(pattern, grid_data, cas_matrix, preferred_element_type=jnp.float32)


def broadcast(x, axis, root):
    mine = lax.axis_index(axis) == root
    return lax.psum(jnp.where(mine, x, jnp.zeros_like(x)), axis)


def slab_potentials(pair_rho, cas_matrix, kernel_block):
    along_z = transform(pair_rho, cas_matrix, "pxyz,kz->pxyk").astype(jnp.bfloat16)
    along_y = transform(along_z, cas_matrix, "pxyz,ky->pxkz").astype(jnp.bfloat16)
    turned = lax.all_to_all(along_y, "grid", split_axis=2, concat_axis=1, tiled=True)
    scaled = (kernel_block * transform(turned, cas_matrix, "pxyz,kx->pkyz")).astype(jnp.bfloat16)
    back_x = transform(scaled, cas_matrix, "pxyz,kx->pkyz").astype(jnp.bfloat16)
    returned = lax.all_to_all(back_x, "grid", split_axis=1, concat_axis=2, tiled=True)
    again_y = transform(returned, cas_matrix, "pxyz,ky->pxkz").astype(jnp.bfloat16)
    return transform(again_y, cas_matrix, "pxyz,kz->pxyk")


def fetch_source(orbitals, which):
    local_count = orbitals.shape[0]
    local_slab = lax.dynamic_index_in_dim(orbitals, which % local_count, 0, keepdims=False)
    return broadcast(local_slab, "band", which // local_count)


def slab_plan(orbitals, source_index):
    local_count, planes, _ = orbitals.shape
    extent = planes * lax.axis_size("grid")
    orbitals = orbitals.reshape(local_count, planes, extent, extent)
    source_count = source_index.shape[0]
    cas_matrix = cas_table(extent)
    columns = extent // lax.axis_size("grid")
    kernel_block = coulomb_block(extent, columns, lax.axis_index("grid") * columns)
    fetched = [fetch_source(orbitals, source_index[number]) for number in range(source_count)]
    stacked = jnp.stack(fetched)[:, None].astype(jnp.float32)
    pair_rho = (stacked * orbitals[None].astype(jnp.float32)).astype(jnp.bfloat16)
    pair_rho = pair_rho.reshape(source_count * local_count, planes, extent, extent)
    potential = slab_potentials(pair_rho, cas_matrix, kernel_block)
    potential = potential.reshape(source_count, local_count, planes, extent, extent)
    result = (-jnp.sum(stacked * potential, axis=0)).astype(jnp.bfloat16)
    return result.reshape(local_count, planes, extent * extent)


lanes = 128
quad = 4
ring = 4
turned_pitch = 161
plane_pitch = 41


def move(x, routes):
    slabs = lax.axis_size("grid")

    def place(column, core, z):
        return (column * cores + core) * slabs + z % slabs

    return lax.ppermute(x, ("band", "grid"), [(place(*a), place(*b)) for a, b in routes])


def everywhere():
    columns = lax.axis_size("band") // cores
    return [(c, k, z) for c in range(columns) for k in range(cores) for z in range(lax.axis_size("grid"))]


def swap_cores(x):
    return move(x, [((c, k, z), (c, 1 - k, z)) for c, k, z in everywhere()])


def to_column(x, d):
    return move(x, [((c, k, z), (c ^ d, k, z)) for c, k, z in everywhere()])


def to_height(x, to):
    return move(x, [((c, k, z), (c, k, to[z])) for c, k, z in everywhere() if z in to])


def holder(z):
    return z % ring // 2


def side(core):
    return 2 * core - 1


def near_routes():
    return [((c, holder(z), z + side(k)), (c, k, z)) for c, k, z in everywhere()]


def far_routes():
    return [((c, holder(z), z + 2), (c, k, z)) for c, k, z in everywhere() if k != holder(z)]


def back(routes):
    return [(b, a) for a, b in routes]


def after(x, *others):
    return lax.optimization_barrier((x, *others))[0]


def quarters_to_all(part):
    half = part.shape[2] // 2
    from_x = to_column(part, 1)
    from_y = to_column(part, 2)
    low = to_column(from_x[:, :, :half], 2)
    high = to_column(from_y[:, :, half:], 1)
    return [part, from_x, from_y, low, high]


def own_quarter(picked, other, owner, column, core, earlier):
    quarter = picked.shape[1] // 4
    slab = after(jnp.where(owner % cores == core, picked, swap_cores(other)), earlier)

    def cut(d):
        return lax.dynamic_slice_in_dim(slab, (column ^ d) * quarter, quarter, 1)

    candidates = [cut(0)] + [to_column(cut(d), d) for d in (1, 2, 3)]
    return lax.select_n(column ^ (owner // cores), *candidates)


def choose(first, refs, start):
    if len(refs) == 1:
        start(refs[0])
    else:
        pl.when(first)(lambda: start(refs[0]))
        pl.when(jnp.logical_not(first))(lambda: start(refs[1]))


def start_pieces(pieces, sems):
    for number, (refs, first, to) in enumerate(pieces):
        choose(first, refs, lambda ref, to=to, number=number: pltpu.make_async_copy(ref, to, sems.at[number]).start())


def wait_pieces(pieces, sems):
    for number, (refs, _, to) in enumerate(pieces):
        pltpu.make_async_copy(refs[0], to, sems.at[number]).wait()


def source_of(refs, flags, place):
    across = flags[7 + place] if place else 0
    if len(refs) == 5:
        return [(refs, across)], None
    return [(refs[:5], 0), (refs[5:], across)], flags[3 + place] == 1


def source_pieces(groups, first, source, column):
    quarter = source.shape[1] // 4
    offsets = [(column ^ e) * quarter for e in range(4)]
    offsets.append(offsets[3] + quarter // 2)
    pieces = []
    for number, offset in enumerate(offsets):
        refs = [five[number].at[which] for five, which in groups]
        to = source.at[:, pl.ds(pl.multiple_of(offset, lanes), refs[0].shape[1])]
        pieces.append((refs, first, to))
    return pieces


def split(refs, *counts):
    taken = []
    for count in counts:
        taken.append(refs[:count])
        refs = refs[count:]
    return taken


def place_of(flags):
    return flags[0], flags[1], flags[2] == 1


def dot(a, b):
    return jnp.dot(a, b, preferred_element_type=jnp.float32)


def both(ref, rows):
    return jnp.concatenate([ref[0, rows, :], ref[1, rows, :]], axis=1)


def beside(values):
    return jnp.concatenate(values, axis=1)


def apart(value):
    return [value[:, n : n + 2 * lanes] for n in range(0, value.shape[1], 2 * lanes)]


def put_both(ref, rows, value):
    ref[0, rows, :] = value[:, :lanes]
    ref[1, rows, :] = value[:, lanes:]


def lane_ranges(pieces):
    ranges = []
    start = 0
    for piece in pieces:
        ranges.append((start, piece.shape[1]))
        start += piece.shape[1]
    return ranges


def pick_kernel(flags, orbitals, *refs):
    outs, sems = refs[:-1], refs[-1]
    parts = len(outs) // flags.shape[0]
    ranges = lane_ranges(outs[:parts])
    copies = []
    for n, out in enumerate(outs):
        lane = pl.ds(*ranges[n % parts])
        copies.append(pltpu.make_async_copy(orbitals.at[flags[n // parts], :, lane], out, sems.at[n]))
    for copy in copies:
        copy.start()
    for copy in copies:
        copy.wait()


def put_kernel(count, flags, *refs):
    (out, sems), refs = refs[-2:], refs[:-2]
    near, choices = refs[:-count], refs[-count:]
    half = count // 2
    pieces = [((ref,), None, out.at[1 - flags[0], :, pl.ds(*lane)]) for ref, lane in zip(near, lane_ranges(near))]
    for n, lane in enumerate(lane_ranges(choices[:half])):
        pieces.append((choices[n::half], flags[1] == 1, out.at[flags[0], :, pl.ds(*lane)]))
    start_pieces(pieces, sems)
    wait_pieces(pieces, sems)


def forward_kernel(place, choices, count, groups, flags, *refs):
    targets, five, (cas, windows, out, target, source, turned, sems) = split(
        refs, choices * count, 5 * groups, 7
    )
    planes, points = target.shape
    extent = cas.shape[0]
    core, column, at_home = place_of(flags)
    ranges = lane_ranges(targets[:count])
    pieces = [(targets[n::count], at_home, target.at[:, pl.ds(*lane)]) for n, lane in enumerate(ranges)]
    pieces += source_pieces(*source_of(five, flags, place), source, column)
    start_pieces(pieces, sems)
    wait_pieces(pieces, sems)
    step = 8
    block = quad * extent

    @pl.loop(0, points // block // step)
    def _(i):
        for r in range(quad):
            density = []
            for j in range(step):
                at = pl.ds(pl.multiple_of((i * step + j) * block + r * lanes, lanes), 2 * lanes)
                density.append(source[:, at].astype(jnp.float32) * target[:, at].astype(jnp.float32))
            density = jnp.concatenate(density, axis=0).astype(jnp.bfloat16)
            along_z = dot(density, windows[r])
            for j in range(step):
                y = (i * step + j) * quad + r
                put_both(turned, pl.ds(y, planes, stride=turned_pitch), along_z[j * planes : (j + 1) * planes])

    @pl.loop(0, planes // 4)
    def _(i):
        for j in range(0, 4, 2):
            x = [i * 4 + j, i * 4 + j + 1]
            along_z = beside([both(turned, pl.ds(n * turned_pitch, extent)) for n in x]).astype(jnp.bfloat16)
            along_y = dot(cas[...], along_z)
            for n, part in zip(x, apart(along_y)):
                put_both(out, pl.ds(n, extent, stride=plane_pitch), part)


def middle_kernel(g0, g1, g2, g3, into, back, square, o0, o1, o2, o3):
    rows = g0.shape[1] // plane_pitch
    extent = square.shape[0]
    planes = extent // ring
    strength = (extent * spacing) ** 2 / math.pi
    first = pl.program_id(0) * rows
    for i in range(0, rows, 2):
        ats = [pl.ds(n * plane_pitch, planes) for n in (i, i + 1)]
        along_y = jnp.concatenate(
            [beside([both(g, at) for at in ats]) for g in (g0, g1, g2, g3)], axis=0
        ).astype(jnp.bfloat16)
        along_x = dot(into[...], along_y)
        scaled = []
        for n, part in enumerate(apart(along_x)):
            ky = first + i + n
            folded = jnp.minimum(ky, extent - ky)
            weight = square[...] + (folded * folded).astype(jnp.float32) * (1.0 / strength)
            guess = pl.reciprocal(weight, approx=True)
            factor = guess * (2.0 - weight * guess)
            factor = jnp.where(weight > 1.25 / strength, factor, 0.0)
            scaled.append((factor * part).astype(jnp.bfloat16))
        back_x = dot(back[...], beside(scaled))
        for at, part in zip(ats, apart(back_x)):
            for d, o in enumerate((o0, o1, o2, o3)):
                put_both(o, at, part[d * planes : (d + 1) * planes])


def backward_kernel(places, parts, counts, flags, *refs):
    slabs, groups, (cas, windows), outs, (back_x, source, turned, sems) = split(
        refs, len(places), sum(counts), 2, parts, 4
    )
    planes, points = source.shape
    extent = cas.shape[0]
    core, column, at_home = place_of(flags)
    chosen, first = [], at_home
    if len(places) == 1:
        chosen, first = source_of(groups, flags, places[0])
    else:
        for refs, place in zip(split(groups, *counts), places):
            chosen += source_of(refs, flags, place)[0]
    pieces = [(slabs, at_home, back_x)] + source_pieces(chosen, first, source, column)
    start_pieces(pieces, sems)
    wait_pieces(pieces, sems)

    @pl.loop(0, planes // 4)
    def _(i):
        for j in range(0, 4, 2):
            x = [i * 4 + j, i * 4 + j + 1]
            column_x = beside([both(back_x, pl.ds(n, extent, stride=plane_pitch)) for n in x]).astype(jnp.bfloat16)
            again_y = dot(cas[...], column_x)
            for n, part in zip(x, apart(again_y)):
                put_both(turned, pl.ds(n * turned_pitch, extent), part)

    step = 5
    block = quad * extent
    blocks = points // block // parts
    for number, out in enumerate(outs):

        @pl.loop(0, blocks // step)
        def _(i):
            first = number * blocks + i * step
            windowed = []
            for r in range(quad):
                again_y = jnp.concatenate(
                    [both(turned, pl.ds((first + j) * quad + r, planes, stride=turned_pitch)) for j in range(step)],
                    axis=0,
                ).astype(jnp.bfloat16)
                windowed.append(dot(again_y, windows[r]))
            for j in range(step):
                w = [part[j * planes : (j + 1) * planes] for part in windowed]
                potential = [w[0][:, :lanes]]
                potential += [w[r][:, lanes:] + w[r + 1][:, :lanes] for r in range(quad - 1)]
                potential = jnp.concatenate(potential + [w[-1][:, lanes:]], axis=1)
                at = pl.ds(pl.multiple_of((first + j) * block, lanes), block)
                to = pl.ds(pl.multiple_of((i * step + j) * block, lanes), block)
                out[:, to] = (-(source[:, at].astype(jnp.float32) * potential)).astype(jnp.bfloat16)


def window_tables(cas_matrix):
    extent = cas_matrix.shape[0]
    tables = []
    for r in range(quad):
        shift = r * extent % lanes
        tables.append(jnp.pad(cas_matrix, ((shift, 2 * lanes - extent - shift), (0, 2 * lanes - extent))))
    return jnp.stack(tables)


limit = 56 * 2**20
whole = pl.BlockSpec(memory_space=pltpu.VMEM)
outside = pl.BlockSpec(memory_space=pl.ANY)
scalars = pl.BlockSpec(memory_space=pltpu.SMEM)
small = pl.CostEstimate(flops=10**6, bytes_accessed=10**4, transcendentals=0)


def pick(orbitals, which, shares=(1,)):
    _, planes, points = orbitals.shape
    unit = points // sum(shares)
    outs = [jax.ShapeDtypeStruct((planes, share * unit), orbitals.dtype) for share in shares] * len(which)
    count = len(outs)
    return pl.pallas_call(
        pick_kernel,
        out_shape=outs,
        in_specs=[scalars, outside],
        out_specs=[whole] * count,
        scratch_shapes=[pltpu.SemaphoreType.DMA((count,))],
        compiler_params=pltpu.CompilerParams(vmem_limit_bytes=limit),
        cost_estimate=small,
        name="pick",
    )(jnp.stack(which).astype(jnp.int32), orbitals)


def put(parity, first, near, *choices):
    pieces = near + [piece for choice in choices for piece in choice]
    planes, points = near[0].shape[0], sum(piece.shape[1] for piece in near)
    return pl.pallas_call(
        functools.partial(put_kernel, 2 * len(choices[0])),
        out_shape=jax.ShapeDtypeStruct((2, planes, points), near[0].dtype),
        in_specs=[scalars] + [outside] * len(pieces),
        out_specs=whole,
        scratch_shapes=[pltpu.SemaphoreType.DMA((len(near) + len(choices[0]),))],
        compiler_params=pltpu.CompilerParams(vmem_limit_bytes=limit),
        cost_estimate=small,
        name="put",
    )(jnp.stack([parity, first.astype(parity.dtype)]).astype(jnp.int32), *pieces)


def forward(flags, place, targets, groups, cas_matrix, windows):
    planes = groups[0][0].shape[1]
    group = [piece for five in groups for piece in five]
    extent = cas_matrix.shape[0]
    points = extent * extent
    return pl.pallas_call(
        functools.partial(forward_kernel, place, len(targets), len(targets[0]), len(groups)),
        out_shape=jax.ShapeDtypeStruct((2, extent * plane_pitch, lanes), jnp.float32),
        in_specs=[scalars] + [outside] * (len(targets) * len(targets[0]) + len(group)) + [whole] * 2,
        out_specs=whole,
        scratch_shapes=[
            pltpu.VMEM((planes, points), jnp.bfloat16),
            pltpu.VMEM((planes, points), jnp.bfloat16),
            pltpu.VMEM((2, planes * turned_pitch, lanes), jnp.float32),
            pltpu.SemaphoreType.DMA((len(targets[0]) + 5,)),
        ],
        compiler_params=pltpu.CompilerParams(vmem_limit_bytes=limit),
        cost_estimate=small,
        name="forward",
    )(flags, *[piece for choice in targets for piece in choice], *group, cas_matrix, windows)


def middle(slabs, into, back, square):
    extent = square.shape[0]
    rows = 8
    block = pl.BlockSpec((2, rows * plane_pitch, lanes), lambda i: (0, i, 0))

    def same(shape):
        return pl.BlockSpec(shape, lambda i: (0, 0))

    return pl.pallas_call(
        middle_kernel,
        grid=(extent // rows,),
        out_shape=[jax.ShapeDtypeStruct(slabs[0].shape, jnp.float32)] * 4,
        in_specs=[block] * 4 + [same(into.shape), same(back.shape), same(square.shape)],
        out_specs=[block] * 4,
        compiler_params=pltpu.CompilerParams(vmem_limit_bytes=limit),
        cost_estimate=small,
        name="middle",
    )(*slabs, into, back, square)


def backward(flags, places, slabs, groups, cas_matrix, windows, parts):
    planes = groups[0][0][0].shape[1]
    extent = cas_matrix.shape[0]
    points = extent * extent
    groups = [[piece for five in group for piece in five] for group in groups]
    pieces = [piece for group in groups for piece in group]
    return pl.pallas_call(
        functools.partial(backward_kernel, places, parts, [len(group) for group in groups]),
        out_shape=[jax.ShapeDtypeStruct((planes, points // parts), jnp.bfloat16)] * parts,
        in_specs=[scalars] + [outside] * (len(slabs) + len(pieces)) + [whole] * 2,
        out_specs=[whole] * parts,
        scratch_shapes=[
            pltpu.VMEM(slabs[0].shape, jnp.float32),
            pltpu.VMEM((planes, points), jnp.bfloat16),
            pltpu.VMEM((2, planes * turned_pitch, lanes), jnp.float32),
            pltpu.SemaphoreType.DMA((6,)),
        ],
        compiler_params=pltpu.CompilerParams(vmem_limit_bytes=limit),
        cost_estimate=small,
        name="backward",
    )(flags, *slabs, *pieces, cas_matrix, windows)


def add(a, b):
    return (a.astype(jnp.float32) + b.astype(jnp.float32)).astype(jnp.bfloat16)


def pair_plan(orbitals, source_index):
    local_count, planes, points = orbitals.shape
    slabs = lax.axis_size("grid")
    extent = planes * slabs
    band, z = lax.axis_index("band"), lax.axis_index("grid")
    column, core = band // cores, band % cores
    at_home = core == holder(z)
    flags = jnp.stack([core, column, at_home.astype(jnp.int32)]).astype(jnp.int32)
    parity = z % 2

    to_near = pick(orbitals, [1 - parity], (1, 4, 3))
    near = [move(part, near_routes()) for part in to_near]
    chosen = [source_index[core] % local_count, source_index[1 - core] % local_count]
    picked, other = pick(after(orbitals, to_near[0]), chosen)
    mine = own_quarter(picked, other, source_index[core] // local_count, column, core, near[0])
    (own_parity,) = pick(after(orbitals, mine), [parity])

    mine = after(mine, near[1])
    inner = (z == 1) | (z == 2)
    neighbour = to_height(mine, {0: 1, 1: 0, 2: 3, 3: 2})
    crossed = [to_height(mine, {1: 2, 2: 1})]
    crossed.append(to_height(neighbour, {1: 2, 2: 1}))
    handed = [to_height(part, {1: 0, 2: 3}) for part in crossed]
    across = [jnp.where(inner, a, b) for a, b in zip(crossed, handed)]
    far = move(after(own_parity, *crossed), far_routes())

    own_source = quarters_to_all(mine[None])
    neighbour_source = quarters_to_all(after(neighbour, own_source[1])[None])
    across_source = quarters_to_all(after(jnp.stack(across), neighbour_source[1]))

    own_swapped = swap_cores(after(own_parity, own_source[1]))
    near_swapped = [swap_cores(after(part, neighbour_source[1])) for part in near]
    far_swapped = swap_cores(far)
    targets = [[[own_parity], [own_swapped]], [near], [[far_swapped], [far]], [near_swapped]]
    slab_of = jnp.stack([z, z + side(core), z + 2, z - side(core)]) % slabs
    is_neighbour = (slab_of == (z ^ 1)).astype(jnp.int32)
    second = jnp.logical_or(slab_of == 0, slab_of == 3).astype(jnp.int32)
    flags = jnp.concatenate([flags, is_neighbour, second])
    sources = [[own_source], [neighbour_source, across_source], [across_source], [neighbour_source, across_source]]

    cas_matrix = cas_table(extent)
    windows = window_tables(cas_matrix)
    windows_back = jnp.swapaxes(windows, 1, 2)
    places = ((slab_of * planes)[:, None] + jnp.arange(planes)).reshape(extent)
    into = cas_entries(jnp.arange(extent), places, extent)
    square_x = wave_square(jnp.arange(extent, dtype=jnp.int32), extent)
    strength = (extent * spacing) ** 2 / math.pi
    square = (square_x[:, None] + square_x[None, :] + 1.0) * (1.0 / strength)
    square = jnp.pad(square, ((0, 0), (0, 2 * lanes - extent)), constant_values=1.0)

    along_y = [forward(flags, p, targets[p], sources[p], cas_matrix, windows) for p in range(4)]
    back_x = middle(along_y, into, into.T, square)

    def partials(places, parts, *earlier):
        slabs = [after(back_x[p], *earlier) for p in places]
        return backward(flags, places, slabs, [sources[p] for p in places], cas_matrix, windows_back, parts)

    near = [add(k, swap_cores(g)) for g, k in zip(partials([3], 4), partials([1], 4))]
    near = [near[0], jnp.concatenate(near[1:], axis=1)]
    near_home = [move(part, back(near_routes())) for part in near]
    given = partials([2, 0], 4, near[0])
    kept = partials([0, 2], 4, given[0], near_home[0])
    far = [add(k, swap_cores(g)) for k, g in zip(kept, given)]
    far_home = [move(part, back(far_routes())) for part in far]
    return put(parity, at_home, near_home, far, far_home)


def solution(mesh):
    def shards(orbitals, source_index):
        slabs, bands = mesh.shape["grid"], mesh.shape["band"]
        fits = slabs == 4 and bands == 8 and orbitals.shape[0] == 2 and source_index.shape[0] == cores
        return (pair_plan if fits else slab_plan)(orbitals, source_index)

    return jax.shard_map(
        shards,
        mesh=mesh,
        in_specs=(P("band", "grid", None), P()),
        out_specs=P("band", "grid", None),
        check_vma=False,
    )
```

```python
import functools
import math

import jax
import jax.numpy as jnp
from jax import lax
from jax.experimental import pallas as pl
from jax.experimental.pallas import tpu as pltpu
from jax.sharding import PartitionSpec as P

spacing = 0.3
cores = 2


def cas_entries(rows, columns, extent):
    products_mod = rows[:, None] * columns[None, :] % extent
    radians = products_mod.astype(jnp.float32) * (2.0 * math.pi / extent)
    return ((jnp.cos(radians) + jnp.sin(radians)) / math.sqrt(extent)).astype(jnp.bfloat16)


def cas_table(extent):
    wavenum = jnp.arange(extent, dtype=jnp.int32)
    return cas_entries(wavenum, wavenum, extent)


def wave_square(indices, extent):
    folded = jnp.minimum(indices, extent - indices).astype(jnp.float32)
    return folded * folded


def coulomb_block(extent, columns, offset):
    square_x = wave_square(jnp.arange(extent, dtype=jnp.int32), extent)
    square_y = wave_square(offset + jnp.arange(columns, dtype=jnp.int32), extent)
    total_sq = square_x[:, None, None] + square_y[None, :, None] + square_x[None, None, :]
    strength = (extent * spacing) ** 2 / math.pi
    return jnp.where(total_sq > 0, strength / (total_sq + 1.0), 0.0)


def transform(grid_data, cas_matrix, pattern):
    return jnp.einsum(pattern, grid_data, cas_matrix, preferred_element_type=jnp.float32)


def broadcast(x, axis, root):
    mine = lax.axis_index(axis) == root
    return lax.psum(jnp.where(mine, x, jnp.zeros_like(x)), axis)


def slab_potentials(pair_rho, cas_matrix, kernel_block):
    along_z = transform(pair_rho, cas_matrix, "pxyz,kz->pxyk").astype(jnp.bfloat16)
    along_y = transform(along_z, cas_matrix, "pxyz,ky->pxkz").astype(jnp.bfloat16)
    turned = lax.all_to_all(along_y, "grid", split_axis=2, concat_axis=1, tiled=True)
    scaled = (kernel_block * transform(turned, cas_matrix, "pxyz,kx->pkyz")).astype(jnp.bfloat16)
    back_x = transform(scaled, cas_matrix, "pxyz,kx->pkyz").astype(jnp.bfloat16)
    returned = lax.all_to_all(back_x, "grid", split_axis=1, concat_axis=2, tiled=True)
    again_y = transform(returned, cas_matrix, "pxyz,ky->pxkz").astype(jnp.bfloat16)
    return transform(again_y, cas_matrix, "pxyz,kz->pxyk")


def fetch_source(orbitals, which):
    local_count = orbitals.shape[0]
    local_slab = lax.dynamic_index_in_dim(orbitals, which % local_count, 0, keepdims=False)
    return broadcast(local_slab, "band", which // local_count)


def slab_plan(orbitals, source_index):
    local_count, planes, _ = orbitals.shape
    extent = planes * lax.axis_size("grid")
    orbitals = orbitals.reshape(local_count, planes, extent, extent)
    source_count = source_index.shape[0]
    cas_matrix = cas_table(extent)
    columns = extent // lax.axis_size("grid")
    kernel_block = coulomb_block(extent, columns, lax.axis_index("grid") * columns)
    fetched = [fetch_source(orbitals, source_index[number]) for number in range(source_count)]
    stacked = jnp.stack(fetched)[:, None].astype(jnp.float32)
    pair_rho = (stacked * orbitals[None].astype(jnp.float32)).astype(jnp.bfloat16)
    pair_rho = pair_rho.reshape(source_count * local_count, planes, extent, extent)
    potential = slab_potentials(pair_rho, cas_matrix, kernel_block)
    potential = potential.reshape(source_count, local_count, planes, extent, extent)
    result = (-jnp.sum(stacked * potential, axis=0)).astype(jnp.bfloat16)
    return result.reshape(local_count, planes, extent * extent)


lanes = 128
quad = 4
ring = 4
turned_pitch = 161
plane_pitch = 41


def move(x, routes):
    slabs = lax.axis_size("grid")

    def place(column, core, z):
        return (column * cores + core) * slabs + z % slabs

    return lax.ppermute(x, ("band", "grid"), [(place(*a), place(*b)) for a, b in routes])


def everywhere():
    columns = lax.axis_size("band") // cores
    return [(c, k, z) for c in range(columns) for k in range(cores) for z in range(lax.axis_size("grid"))]


def swap_cores(x):
    return move(x, [((c, k, z), (c, 1 - k, z)) for c, k, z in everywhere()])


def to_column(x, d):
    return move(x, [((c, k, z), (c ^ d, k, z)) for c, k, z in everywhere()])


def to_height(x, to):
    return move(x, [((c, k, z), (c, k, to[z])) for c, k, z in everywhere() if z in to])


def holder(z):
    return z % ring // 2


def side(core):
    return 2 * core - 1


def near_routes():
    return [((c, holder(z), z + side(k)), (c, k, z)) for c, k, z in everywhere()]


def far_routes():
    return [((c, holder(z), z + 2), (c, k, z)) for c, k, z in everywhere() if k != holder(z)]


def back(routes):
    return [(b, a) for a, b in routes]


def stage(values, *earlier):
    return lax.optimization_barrier((values, earlier))[0]


def choose(first, refs, start):
    if len(refs) == 1:
        start(refs[0])
    else:
        pl.when(first)(lambda: start(refs[0]))
        pl.when(jnp.logical_not(first))(lambda: start(refs[1]))


def start_pieces(pieces, sems):
    for number, (refs, first, to) in enumerate(pieces):
        choose(first, refs, lambda ref, to=to, number=number: pltpu.make_async_copy(ref, to, sems.at[number]).start())


def wait_pieces(pieces, sems):
    for number, (refs, _, to) in enumerate(pieces):
        pltpu.make_async_copy(refs[0], to, sems.at[number]).wait()


def source_of(refs, flags, place):
    return refs, flags[2 + place] if place > 1 else 0


def source_pieces(groups, first, source, column):
    quarter = source.shape[1] // 4
    offsets = [(column ^ e) * quarter for e in range(4)]
    offsets.append(offsets[3] + quarter // 2)
    pieces = []
    for number, offset in enumerate(offsets):
        refs = [five[number].at[which] for five, which in groups]
        to = source.at[:, pl.ds(pl.multiple_of(offset, lanes), refs[0].shape[1])]
        pieces.append((refs, first, to))
    return pieces


def split(refs, *counts):
    taken = []
    for count in counts:
        taken.append(refs[:count])
        refs = refs[count:]
    return taken


def dot(a, b):
    return jnp.dot(a, b, preferred_element_type=jnp.float32)


def both(ref, rows):
    return jnp.concatenate([ref[0, rows, :], ref[1, rows, :]], axis=1)


def beside(values):
    return jnp.concatenate(values, axis=1)


def apart(value):
    return [value[:, n : n + 2 * lanes] for n in range(0, value.shape[1], 2 * lanes)]


def put_both(ref, rows, value):
    ref[0, rows, :] = value[:, :lanes]
    ref[1, rows, :] = value[:, lanes:]


def lane_ranges(pieces):
    ranges = []
    start = 0
    for piece in pieces:
        ranges.append((start, piece.shape[1]))
        start += piece.shape[1]
    return ranges


def pick_kernel(flags, orbitals, *refs):
    outs, sems = refs[:-1], refs[-1]
    parts = len(outs) // flags.shape[0]
    ranges = lane_ranges(outs[:parts])
    copies = []
    for n, out in enumerate(outs):
        lane = pl.ds(*ranges[n % parts])
        copies.append(pltpu.make_async_copy(orbitals.at[flags[n // parts], :, lane], out, sems.at[n]))
    for copy in copies:
        copy.start()
    for copy in copies:
        copy.wait()


def put_kernel(count, flags, *refs):
    (out, sems), refs = refs[-2:], refs[:-2]
    near, choices = refs[:-count], refs[-count:]
    half = count // 2
    pieces = [((ref,), None, out.at[1 - flags[0], :, pl.ds(*lane)]) for ref, lane in zip(near, lane_ranges(near))]
    for n, lane in enumerate(lane_ranges(choices[:half])):
        pieces.append((choices[n::half], flags[1] == 1, out.at[flags[0], :, pl.ds(*lane)]))
    start_pieces(pieces, sems)
    wait_pieces(pieces, sems)


def forward_kernel(place, first, choices, count, flags, *refs):
    targets, five, (cas, windows, out, target, source, turned, sems) = split(refs, choices * count, 5, 7)
    planes, points = target.shape
    extent = cas.shape[0]
    ranges = lane_ranges(targets[:count])
    pieces = [(targets[n::count], flags[first] == 1, target.at[:, pl.ds(*lane)]) for n, lane in enumerate(ranges)]
    pieces += source_pieces([source_of(five, flags, place)], None, source, flags[1])
    start_pieces(pieces, sems)
    wait_pieces(pieces, sems)
    step = 8
    block = quad * extent

    @pl.loop(0, points // block // step)
    def _(i):
        for r in range(quad):
            density = []
            for j in range(step):
                at = pl.ds(pl.multiple_of((i * step + j) * block + r * lanes, lanes), 2 * lanes)
                density.append(source[:, at].astype(jnp.float32) * target[:, at].astype(jnp.float32))
            density = jnp.concatenate(density, axis=0).astype(jnp.bfloat16)
            along_z = dot(density, windows[r])
            for j in range(step):
                y = (i * step + j) * quad + r
                put_both(turned, pl.ds(y, planes, stride=turned_pitch), along_z[j * planes : (j + 1) * planes])

    @pl.loop(0, planes // 4)
    def _(i):
        for j in range(0, 4, 2):
            x = [i * 4 + j, i * 4 + j + 1]
            along_z = beside([both(turned, pl.ds(n * turned_pitch, extent)) for n in x]).astype(jnp.bfloat16)
            along_y = dot(cas[...], along_z)
            for n, part in zip(x, apart(along_y)):
                put_both(out, pl.ds(n, extent, stride=plane_pitch), part)


def middle_kernel(g0, g1, g2, g3, into, back, square, o0, o1, o2, o3):
    rows = g0.shape[1] // plane_pitch
    extent = square.shape[0]
    planes = extent // ring
    strength = (extent * spacing) ** 2 / math.pi
    first = pl.program_id(0) * rows
    for i in range(0, rows, 2):
        ats = [pl.ds(n * plane_pitch, planes) for n in (i, i + 1)]
        along_y = jnp.concatenate(
            [beside([both(g, at) for at in ats]) for g in (g0, g1, g2, g3)], axis=0
        ).astype(jnp.bfloat16)
        along_x = dot(into[...], along_y)
        scaled = []
        for n, part in enumerate(apart(along_x)):
            ky = first + i + n
            folded = jnp.minimum(ky, extent - ky)
            weight = square[...] + (folded * folded).astype(jnp.float32) * (1.0 / strength)
            guess = pl.reciprocal(weight, approx=True)
            factor = guess * (2.0 - weight * guess)
            factor = jnp.where(weight > 1.25 / strength, factor, 0.0)
            scaled.append((factor * part).astype(jnp.bfloat16))
        back_x = dot(back[...], beside(scaled))
        for at, part in zip(ats, apart(back_x)):
            for d, o in enumerate((o0, o1, o2, o3)):
                put_both(o, at, part[d * planes : (d + 1) * planes])


def backward_kernel(places, first, parts, flags, *refs):
    slabs, groups, (cas, windows), outs, (back_x, source, turned, sems) = split(
        refs, len(places), 5 * len(places), 2, parts, 4
    )
    planes, points = source.shape
    extent = cas.shape[0]
    chosen = [source_of(five, flags, place) for five, place in zip(split(groups, *[5] * len(places)), places)]
    pieces = [(slabs, flags[first] == 1, back_x)] + source_pieces(chosen, flags[first] == 1, source, flags[1])
    start_pieces(pieces, sems)
    wait_pieces(pieces, sems)

    @pl.loop(0, planes // 4)
    def _(i):
        for j in range(0, 4, 2):
            x = [i * 4 + j, i * 4 + j + 1]
            column_x = beside([both(back_x, pl.ds(n, extent, stride=plane_pitch)) for n in x]).astype(jnp.bfloat16)
            again_y = dot(cas[...], column_x)
            for n, part in zip(x, apart(again_y)):
                put_both(turned, pl.ds(n * turned_pitch, extent), part)

    step = 5
    block = quad * extent
    blocks = points // block // parts
    for number, out in enumerate(outs):

        @pl.loop(0, blocks // step)
        def _(i):
            first = number * blocks + i * step
            windowed = []
            for r in range(quad):
                again_y = jnp.concatenate(
                    [both(turned, pl.ds((first + j) * quad + r, planes, stride=turned_pitch)) for j in range(step)],
                    axis=0,
                ).astype(jnp.bfloat16)
                windowed.append(dot(again_y, windows[r]))
            for j in range(step):
                w = [part[j * planes : (j + 1) * planes] for part in windowed]
                potential = [w[0][:, :lanes]]
                potential += [w[r][:, lanes:] + w[r + 1][:, :lanes] for r in range(quad - 1)]
                potential = jnp.concatenate(potential + [w[-1][:, lanes:]], axis=1)
                at = pl.ds(pl.multiple_of((first + j) * block, lanes), block)
                to = pl.ds(pl.multiple_of((i * step + j) * block, lanes), block)
                out[:, to] = (-(source[:, at].astype(jnp.float32) * potential)).astype(jnp.bfloat16)


def window_tables(cas_matrix):
    extent = cas_matrix.shape[0]
    tables = []
    for r in range(quad):
        shift = r * extent % lanes
        tables.append(jnp.pad(cas_matrix, ((shift, 2 * lanes - extent - shift), (0, 2 * lanes - extent))))
    return jnp.stack(tables)


limit = 56 * 2**20
whole = pl.BlockSpec(memory_space=pltpu.VMEM)
outside = pl.BlockSpec(memory_space=pl.ANY)
scalars = pl.BlockSpec(memory_space=pltpu.SMEM)
small = pl.CostEstimate(flops=10**6, bytes_accessed=10**4, transcendentals=0)


def pick(orbitals, which, shares=(1,)):
    _, planes, points = orbitals.shape
    unit = points // sum(shares)
    outs = [jax.ShapeDtypeStruct((planes, share * unit), orbitals.dtype) for share in shares] * len(which)
    count = len(outs)
    return pl.pallas_call(
        pick_kernel,
        out_shape=outs,
        in_specs=[scalars, outside],
        out_specs=[whole] * count,
        scratch_shapes=[pltpu.SemaphoreType.DMA((count,))],
        compiler_params=pltpu.CompilerParams(vmem_limit_bytes=limit),
        cost_estimate=small,
        name="pick",
    )(jnp.stack(which).astype(jnp.int32), orbitals)


def put(parity, first, near, *choices):
    pieces = near + [piece for choice in choices for piece in choice]
    planes, points = near[0].shape[0], sum(piece.shape[1] for piece in near)
    return pl.pallas_call(
        functools.partial(put_kernel, 2 * len(choices[0])),
        out_shape=jax.ShapeDtypeStruct((2, planes, points), near[0].dtype),
        in_specs=[scalars] + [outside] * len(pieces),
        out_specs=whole,
        scratch_shapes=[pltpu.SemaphoreType.DMA((len(near) + len(choices[0]),))],
        compiler_params=pltpu.CompilerParams(vmem_limit_bytes=limit),
        cost_estimate=small,
        name="put",
    )(jnp.stack([parity, first.astype(parity.dtype)]).astype(jnp.int32), *pieces)


def forward(flags, place, first, targets, group, cas_matrix, windows):
    planes = group[0].shape[1]
    extent = cas_matrix.shape[0]
    points = extent * extent
    return pl.pallas_call(
        functools.partial(forward_kernel, place, first, len(targets), len(targets[0])),
        out_shape=jax.ShapeDtypeStruct((2, extent * plane_pitch, lanes), jnp.float32),
        in_specs=[scalars] + [outside] * (len(targets) * len(targets[0]) + len(group)) + [whole] * 2,
        out_specs=whole,
        scratch_shapes=[
            pltpu.VMEM((planes, points), jnp.bfloat16),
            pltpu.VMEM((planes, points), jnp.bfloat16),
            pltpu.VMEM((2, planes * turned_pitch, lanes), jnp.float32),
            pltpu.SemaphoreType.DMA((len(targets[0]) + 5,)),
        ],
        compiler_params=pltpu.CompilerParams(vmem_limit_bytes=limit),
        cost_estimate=small,
        name="forward",
    )(flags, *[piece for choice in targets for piece in choice], *group, cas_matrix, windows)


def middle(slabs, into, back, square):
    extent = square.shape[0]
    rows = 8
    block = pl.BlockSpec((2, rows * plane_pitch, lanes), lambda i: (0, i, 0))

    def same(shape):
        return pl.BlockSpec(shape, lambda i: (0, 0))

    return pl.pallas_call(
        middle_kernel,
        grid=(extent // rows,),
        out_shape=[jax.ShapeDtypeStruct(slabs[0].shape, jnp.float32)] * 4,
        in_specs=[block] * 4 + [same(into.shape), same(back.shape), same(square.shape)],
        out_specs=[block] * 4,
        compiler_params=pltpu.CompilerParams(vmem_limit_bytes=limit),
        cost_estimate=small,
        name="middle",
    )(*slabs, into, back, square)


def backward(flags, places, first, slabs, groups, cas_matrix, windows, parts):
    planes = groups[0][0].shape[1]
    extent = cas_matrix.shape[0]
    points = extent * extent
    pieces = [piece for group in groups for piece in group]
    return pl.pallas_call(
        functools.partial(backward_kernel, places, first, parts),
        out_shape=[jax.ShapeDtypeStruct((planes, points // parts), jnp.bfloat16)] * parts,
        in_specs=[scalars] + [outside] * (len(slabs) + len(pieces)) + [whole] * 2,
        out_specs=[whole] * parts,
        scratch_shapes=[
            pltpu.VMEM(slabs[0].shape, jnp.float32),
            pltpu.VMEM((planes, points), jnp.bfloat16),
            pltpu.VMEM((2, planes * turned_pitch, lanes), jnp.float32),
            pltpu.SemaphoreType.DMA((6,)),
        ],
        compiler_params=pltpu.CompilerParams(vmem_limit_bytes=limit),
        cost_estimate=small,
        name="backward",
    )(flags, *slabs, *pieces, cas_matrix, windows)


def add(a, b):
    return (a.astype(jnp.float32) + b.astype(jnp.float32)).astype(jnp.bfloat16)


def pair_plan(orbitals, source_index):
    local_count, planes, points = orbitals.shape
    slabs = lax.axis_size("grid")
    extent = planes * slabs
    band, z = lax.axis_index("band"), lax.axis_index("grid")
    column, core = band // cores, band % cores
    quarter = points // 4
    at_home = core == holder(z)
    direct_neighbour = core == 1 - z % 2
    parity = z % 2
    inner = (z == 1) | (z == 2)
    second = inner.astype(jnp.int32)
    flags = jnp.stack([core, column, at_home, direct_neighbour, second, 1 - second]).astype(jnp.int32)
    home, direct = 2, 3

    to_near = pick(orbitals, [1 - parity], (1, 5, 1, 1))
    near = [move(to_near[0], near_routes())]
    chosen = [source_index[core] % local_count, source_index[1 - core] % local_count]
    picked, other = pick(stage(orbitals, to_near), chosen)
    owner = source_index[core] // local_count
    slab = jnp.where(owner % cores == core, picked, swap_cores(other))

    def cut(d):
        return lax.dynamic_slice_in_dim(slab, (column ^ d) * quarter, quarter, 1)

    cuts = stage([cut(d) for d in range(4)], near)
    near.append(move(stage(to_near[1], cuts), near_routes()))
    candidates = [cuts[0]] + [to_column(cuts[d], d) for d in (1, 2, 3)]
    (own_parity,) = pick(stage(orbitals, cuts), [parity])
    cas_matrix = cas_table(extent)
    windows = window_tables(cas_matrix)
    windows_back = jnp.swapaxes(windows, 1, 2)
    places = (((z ^ jnp.arange(slabs)) * planes)[:, None] + jnp.arange(planes)).reshape(extent)
    into = cas_entries(jnp.arange(extent), places, extent)
    square_x = wave_square(jnp.arange(extent, dtype=jnp.int32), extent)
    strength = (extent * spacing) ** 2 / math.pi
    square = (square_x[:, None] + square_x[None, :] + 1.0) * (1.0 / strength)
    square = jnp.pad(square, ((0, 0), (0, 2 * lanes - extent)), constant_values=1.0)
    tables = [cas_matrix, windows, windows_back, into, into.T, square]

    candidates, tables, own_parity, flags = stage((candidates, tables, own_parity, flags), near)
    cas_matrix, windows, windows_back, into, outof, square = tables
    own = lax.select_n(column ^ (owner // cores), *candidates)
    own, to_near = stage((own, to_near), near, tables)
    own_x, own_y = to_column(own, 1), to_column(own, 2)
    neighbour = to_height(own, {0: 1, 1: 0, 2: 3, 3: 2})
    crossed = to_height(own, {1: 2, 2: 1})
    near.append(move(to_near[2], near_routes()))

    neighbour, crossed, own_x, own_y, last = stage((neighbour, crossed, own_x, own_y, to_near[3]), near)
    neighbour_x, neighbour_y = to_column(neighbour, 1), to_column(neighbour, 2)
    crossed_2 = to_height(neighbour, {1: 2, 2: 1})
    handed = to_height(crossed, {1: 0, 2: 3})
    near.append(move(last, near_routes()))

    far_parts = [own_parity[:, : points // 4], own_parity[:, points // 4 : 3 * points // 4], own_parity[:, 3 * points // 4 :]]
    low = jnp.stack([own_x[:, : quarter // 2], neighbour_x[:, : quarter // 2]])
    high = jnp.stack([own_y[:, quarter // 2 :], neighbour_y[:, quarter // 2 :]])
    low, high, crossed_2, far_parts, near = stage((low, high, crossed_2, far_parts, near), handed)
    low, high = to_column(low, 2), to_column(high, 1)
    handed_2 = to_height(crossed_2, {1: 0, 2: 3})
    far = [move(far_parts[0], far_routes())]
    own_swapped = swap_cores(own_parity)

    across = jnp.stack([jnp.where(inner, crossed, handed), jnp.where(inner, crossed_2, handed_2)])
    across, low, high, far, far_parts, own_swapped = stage((across, low, high, far, far_parts, own_swapped), near)
    sources = [
        [own[None], own_x[None], own_y[None], low[:1], high[:1]],
        [neighbour[None], neighbour_x[None], neighbour_y[None], low[1:], high[1:]],
    ]
    across_x, across_y = to_column(across, 1), to_column(across, 2)
    far.append(move(far_parts[1], far_routes()))
    rest = jnp.concatenate([near[0], near[2], near[3]], axis=1)
    swapped = [swap_cores(near[1]), swap_cores(rest)]
    along_y = [forward(flags, 0, home, [[own_parity], [own_swapped]], sources[0], cas_matrix, windows)]

    direct_pieces = [near[0], near[1], near[2], near[3]]
    unit = points // 8
    near_swapped = [swapped[1][:, :unit], swapped[0], swapped[1][:, unit : 2 * unit], swapped[1][:, 2 * unit :]]
    low, high = across_x[:, :, : quarter // 2], across_y[:, :, quarter // 2 :]
    low, high, near_swapped, far, last = stage((low, high, near_swapped, far, far_parts[2]), along_y)
    low, high = to_column(low, 2), to_column(high, 1)
    far.append(move(last, far_routes()))
    far_swapped = [swap_cores(part) for part in far[:2]]
    along_y.append(forward(flags, 1, direct, [direct_pieces, near_swapped], sources[1], cas_matrix, windows))

    low, high, far, far_swapped = stage((low, high, far, far_swapped), along_y)
    across_source = [across, across_x, across_y, low, high]
    sources += [across_source, across_source]
    far_swapped.append(swap_cores(far[2]))
    along_y_3 = forward(flags, 3, direct, [near_swapped, direct_pieces], across_source, cas_matrix, windows)
    far_swapped = stage(far_swapped, along_y_3)
    along_y_2 = forward(flags, 2, home, [far_swapped, far], across_source, cas_matrix, windows)
    back_x = middle([*along_y, along_y_2, along_y_3], into, outof, square)

    def partials(places, first, *earlier):
        groups = [sources[p] for p in places]
        return backward(flags, places, first, stage([back_x[p] for p in places], *earlier), groups, cas_matrix, windows_back, 4)

    given = partials([3, 1], direct)
    kept = partials([1, 3], direct)
    near = [add(k, swap_cores(g)) for g, k in zip(given, kept)]
    near = [near[0], jnp.concatenate(near[1:], axis=1)]
    near_home = [move(part, back(near_routes())) for part in near]
    given = partials([2, 0], home, near[0])
    kept = partials([0, 2], home, given[0], near_home[0])
    far = [add(k, swap_cores(g)) for k, g in zip(kept, given)]
    far_home = [move(part, back(far_routes())) for part in far]
    return put(parity, at_home, near_home, far, far_home)


def solution(mesh):
    def shards(orbitals, source_index):
        slabs, bands = mesh.shape["grid"], mesh.shape["band"]
        fits = slabs == 4 and bands == 8 and orbitals.shape[0] == 2 and source_index.shape[0] == cores
        return (pair_plan if fits else slab_plan)(orbitals, source_index)

    return jax.shard_map(
        shards,
        mesh=mesh,
        in_specs=(P("band", "grid", None), P()),
        out_specs=P("band", "grid", None),
        check_vma=False,
    )
```

```python
import functools
import math

import jax
import jax.numpy as jnp
from jax import lax
from jax.experimental import pallas as pl
from jax.experimental.pallas import tpu as pltpu
from jax.sharding import PartitionSpec as P

spacing = 0.3
cores = 2


def cas_entries(rows, columns, extent):
    products_mod = rows[:, None] * columns[None, :] % extent
    radians = products_mod.astype(jnp.float32) * (2.0 * math.pi / extent)
    return ((jnp.cos(radians) + jnp.sin(radians)) / math.sqrt(extent)).astype(jnp.bfloat16)


def cas_table(extent):
    wavenum = jnp.arange(extent, dtype=jnp.int32)
    return cas_entries(wavenum, wavenum, extent)


def wave_square(indices, extent):
    folded = jnp.minimum(indices, extent - indices).astype(jnp.float32)
    return folded * folded


def coulomb_block(extent, columns, offset):
    square_x = wave_square(jnp.arange(extent, dtype=jnp.int32), extent)
    square_y = wave_square(offset + jnp.arange(columns, dtype=jnp.int32), extent)
    total_sq = square_x[:, None, None] + square_y[None, :, None] + square_x[None, None, :]
    strength = (extent * spacing) ** 2 / math.pi
    return jnp.where(total_sq > 0, strength / (total_sq + 1.0), 0.0)


def transform(grid_data, cas_matrix, pattern):
    return jnp.einsum(pattern, grid_data, cas_matrix, preferred_element_type=jnp.float32)


def broadcast(x, axis, root):
    mine = lax.axis_index(axis) == root
    return lax.psum(jnp.where(mine, x, jnp.zeros_like(x)), axis)


def slab_potentials(pair_rho, cas_matrix, kernel_block):
    along_z = transform(pair_rho, cas_matrix, "pxyz,kz->pxyk").astype(jnp.bfloat16)
    along_y = transform(along_z, cas_matrix, "pxyz,ky->pxkz").astype(jnp.bfloat16)
    turned = lax.all_to_all(along_y, "grid", split_axis=2, concat_axis=1, tiled=True)
    scaled = (kernel_block * transform(turned, cas_matrix, "pxyz,kx->pkyz")).astype(jnp.bfloat16)
    back_x = transform(scaled, cas_matrix, "pxyz,kx->pkyz").astype(jnp.bfloat16)
    returned = lax.all_to_all(back_x, "grid", split_axis=1, concat_axis=2, tiled=True)
    again_y = transform(returned, cas_matrix, "pxyz,ky->pxkz").astype(jnp.bfloat16)
    return transform(again_y, cas_matrix, "pxyz,kz->pxyk")


def fetch_source(orbitals, which):
    local_count = orbitals.shape[0]
    local_slab = lax.dynamic_index_in_dim(orbitals, which % local_count, 0, keepdims=False)
    return broadcast(local_slab, "band", which // local_count)


def slab_plan(orbitals, source_index):
    local_count, planes, _ = orbitals.shape
    extent = planes * lax.axis_size("grid")
    orbitals = orbitals.reshape(local_count, planes, extent, extent)
    source_count = source_index.shape[0]
    cas_matrix = cas_table(extent)
    columns = extent // lax.axis_size("grid")
    kernel_block = coulomb_block(extent, columns, lax.axis_index("grid") * columns)
    fetched = [fetch_source(orbitals, source_index[number]) for number in range(source_count)]
    stacked = jnp.stack(fetched)[:, None].astype(jnp.float32)
    pair_rho = (stacked * orbitals[None].astype(jnp.float32)).astype(jnp.bfloat16)
    pair_rho = pair_rho.reshape(source_count * local_count, planes, extent, extent)
    potential = slab_potentials(pair_rho, cas_matrix, kernel_block)
    potential = potential.reshape(source_count, local_count, planes, extent, extent)
    result = (-jnp.sum(stacked * potential, axis=0)).astype(jnp.bfloat16)
    return result.reshape(local_count, planes, extent * extent)


lanes = 128
quad = 4
ring = 4
turned_pitch = 161
plane_pitch = 41


def move(x, routes):
    slabs = lax.axis_size("grid")

    def place(column, core, z):
        return (column * cores + core) * slabs + z % slabs

    return lax.ppermute(x, ("band", "grid"), [(place(*a), place(*b)) for a, b in routes])


def everywhere():
    columns = lax.axis_size("band") // cores
    return [(c, k, z) for c in range(columns) for k in range(cores) for z in range(lax.axis_size("grid"))]


def swap_cores(x):
    return move(x, [((c, k, z), (c, 1 - k, z)) for c, k, z in everywhere()])


def to_column(x, d):
    return move(x, [((c, k, z), (c ^ d, k, z)) for c, k, z in everywhere()])


def to_height(x, to):
    return move(x, [((c, k, z), (c, k, to[z])) for c, k, z in everywhere() if z in to])


def holder(z):
    return z % ring // 2


def side(core):
    return 2 * core - 1


def near_routes():
    return [((c, holder(z), z + side(k)), (c, k, z)) for c, k, z in everywhere()]


def far_routes():
    return [((c, holder(z), z + 2), (c, k, z)) for c, k, z in everywhere() if k != holder(z)]


def back(routes):
    return [(b, a) for a, b in routes]


def stage(values, *earlier):
    return lax.optimization_barrier((values, earlier))[0]


def choose(first, refs, start):
    if len(refs) == 1:
        start(refs[0])
    else:
        pl.when(first)(lambda: start(refs[0]))
        pl.when(jnp.logical_not(first))(lambda: start(refs[1]))


def start_pieces(pieces, sems):
    for number, (refs, first, to) in enumerate(pieces):
        choose(first, refs, lambda ref, to=to, number=number: pltpu.make_async_copy(ref, to, sems.at[number]).start())


def wait_pieces(pieces, sems):
    for number, (refs, _, to) in enumerate(pieces):
        pltpu.make_async_copy(refs[0], to, sems.at[number]).wait()


def source_of(refs, flags, place):
    return refs, flags[2 + place] if place > 1 else 0


def source_pieces(groups, first, source, column):
    quarter = source.shape[1] // 4
    offsets = [(column ^ e) * quarter for e in range(4)]
    offsets.append(offsets[3] + quarter // 2)
    pieces = []
    for number, offset in enumerate(offsets):
        refs = [five[number].at[which] for five, which in groups]
        to = source.at[:, pl.ds(pl.multiple_of(offset, lanes), refs[0].shape[1])]
        pieces.append((refs, first, to))
    return pieces


def split(refs, *counts):
    taken = []
    for count in counts:
        taken.append(refs[:count])
        refs = refs[count:]
    return taken


def dot(a, b):
    return jnp.dot(a, b, preferred_element_type=jnp.float32)


def both(ref, rows):
    return jnp.concatenate([ref[0, rows, :], ref[1, rows, :]], axis=1)


def beside(values):
    return jnp.concatenate(values, axis=1)


def apart(value):
    return [value[:, n : n + 2 * lanes] for n in range(0, value.shape[1], 2 * lanes)]


def put_both(ref, rows, value):
    ref[0, rows, :] = value[:, :lanes]
    ref[1, rows, :] = value[:, lanes:]


def lane_ranges(pieces):
    ranges = []
    start = 0
    for piece in pieces:
        ranges.append((start, piece.shape[1]))
        start += piece.shape[1]
    return ranges


def pick_kernel(flags, orbitals, *refs):
    outs, sems = refs[:-1], refs[-1]
    parts = len(outs) // flags.shape[0]
    ranges = lane_ranges(outs[:parts])
    copies = []
    for n, out in enumerate(outs):
        lane = pl.ds(*ranges[n % parts])
        copies.append(pltpu.make_async_copy(orbitals.at[flags[n // parts], :, lane], out, sems.at[n]))
    for copy in copies:
        copy.start()
    for copy in copies:
        copy.wait()


def put_kernel(count, flags, *refs):
    (out, sems), refs = refs[-2:], refs[:-2]
    near, choices = refs[:-count], refs[-count:]
    half = count // 2
    pieces = [((ref,), None, out.at[1 - flags[0], :, pl.ds(*lane)]) for ref, lane in zip(near, lane_ranges(near))]
    for n, lane in enumerate(lane_ranges(choices[:half])):
        pieces.append((choices[n::half], flags[1] == 1, out.at[flags[0], :, pl.ds(*lane)]))
    start_pieces(pieces, sems)
    wait_pieces(pieces, sems)


def forward_kernel(place, first, choices, count, flags, *refs):
    targets, five, (cas, windows, out, target, source, turned, sems) = split(refs, choices * count, 5, 7)
    planes, points = target.shape
    extent = cas.shape[0]
    ranges = lane_ranges(targets[:count])
    pieces = [(targets[n::count], flags[first] == 1, target.at[:, pl.ds(*lane)]) for n, lane in enumerate(ranges)]
    pieces += source_pieces([source_of(five, flags, place)], None, source, flags[1])
    start_pieces(pieces, sems)
    wait_pieces(pieces, sems)
    step = 8
    block = quad * extent

    @pl.loop(0, points // block // step)
    def _(i):
        for r in range(quad):
            density = []
            for j in range(step):
                at = pl.ds(pl.multiple_of((i * step + j) * block + r * lanes, lanes), 2 * lanes)
                density.append(source[:, at].astype(jnp.float32) * target[:, at].astype(jnp.float32))
            density = jnp.concatenate(density, axis=0).astype(jnp.bfloat16)
            along_z = dot(density, windows[r])
            for j in range(step):
                y = (i * step + j) * quad + r
                put_both(turned, pl.ds(y, planes, stride=turned_pitch), along_z[j * planes : (j + 1) * planes])

    @pl.loop(0, planes // 4)
    def _(i):
        for j in range(0, 4, 2):
            x = [i * 4 + j, i * 4 + j + 1]
            along_z = beside([both(turned, pl.ds(n * turned_pitch, extent)) for n in x]).astype(jnp.bfloat16)
            along_y = dot(cas[...], along_z)
            for n, part in zip(x, apart(along_y)):
                put_both(out, pl.ds(n, extent, stride=plane_pitch), part)


def middle_kernel(g0, g1, g2, g3, into, back, square, o0, o1, o2, o3):
    rows = g0.shape[1] // plane_pitch
    extent = square.shape[0]
    planes = extent // ring
    strength = (extent * spacing) ** 2 / math.pi
    first = pl.program_id(0) * rows
    for i in range(0, rows, 2):
        ats = [pl.ds(n * plane_pitch, planes) for n in (i, i + 1)]
        along_y = jnp.concatenate(
            [beside([both(g, at) for at in ats]) for g in (g0, g1, g2, g3)], axis=0
        ).astype(jnp.bfloat16)
        along_x = dot(into[...], along_y)
        scaled = []
        for n, part in enumerate(apart(along_x)):
            ky = first + i + n
            folded = jnp.minimum(ky, extent - ky)
            weight = square[...] + (folded * folded).astype(jnp.float32) * (1.0 / strength)
            guess = pl.reciprocal(weight, approx=True)
            factor = guess * (2.0 - weight * guess)
            factor = jnp.where(weight > 1.25 / strength, factor, 0.0)
            scaled.append((factor * part).astype(jnp.bfloat16))
        back_x = dot(back[...], beside(scaled))
        for at, part in zip(ats, apart(back_x)):
            for d, o in enumerate((o0, o1, o2, o3)):
                put_both(o, at, part[d * planes : (d + 1) * planes])


def backward_kernel(places, first, parts, flags, *refs):
    slabs, groups, (cas, windows), outs, (back_x, source, turned, sems) = split(
        refs, len(places), 5 * len(places), 2, parts, 4
    )
    planes, points = source.shape
    extent = cas.shape[0]
    chosen = [source_of(five, flags, place) for five, place in zip(split(groups, *[5] * len(places)), places)]
    pieces = [(slabs, flags[first] == 1, back_x)] + source_pieces(chosen, flags[first] == 1, source, flags[1])
    start_pieces(pieces, sems)
    wait_pieces(pieces, sems)

    @pl.loop(0, planes // 4)
    def _(i):
        for j in range(0, 4, 2):
            x = [i * 4 + j, i * 4 + j + 1]
            column_x = beside([both(back_x, pl.ds(n, extent, stride=plane_pitch)) for n in x]).astype(jnp.bfloat16)
            again_y = dot(cas[...], column_x)
            for n, part in zip(x, apart(again_y)):
                put_both(turned, pl.ds(n * turned_pitch, extent), part)

    step = 5
    block = quad * extent
    blocks = points // block // parts
    for number, out in enumerate(outs):

        @pl.loop(0, blocks // step)
        def _(i):
            first = number * blocks + i * step
            windowed = []
            for r in range(quad):
                again_y = jnp.concatenate(
                    [both(turned, pl.ds((first + j) * quad + r, planes, stride=turned_pitch)) for j in range(step)],
                    axis=0,
                ).astype(jnp.bfloat16)
                windowed.append(dot(again_y, windows[r]))
            for j in range(step):
                w = [part[j * planes : (j + 1) * planes] for part in windowed]
                potential = [w[0][:, :lanes]]
                potential += [w[r][:, lanes:] + w[r + 1][:, :lanes] for r in range(quad - 1)]
                potential = jnp.concatenate(potential + [w[-1][:, lanes:]], axis=1)
                at = pl.ds(pl.multiple_of((first + j) * block, lanes), block)
                to = pl.ds(pl.multiple_of((i * step + j) * block, lanes), block)
                out[:, to] = (-(source[:, at].astype(jnp.float32) * potential)).astype(jnp.bfloat16)


def window_tables(cas_matrix):
    extent = cas_matrix.shape[0]
    tables = []
    for r in range(quad):
        shift = r * extent % lanes
        tables.append(jnp.pad(cas_matrix, ((shift, 2 * lanes - extent - shift), (0, 2 * lanes - extent))))
    return jnp.stack(tables)


limit = 56 * 2**20
whole = pl.BlockSpec(memory_space=pltpu.VMEM)
outside = pl.BlockSpec(memory_space=pl.ANY)
scalars = pl.BlockSpec(memory_space=pltpu.SMEM)
small = pl.CostEstimate(flops=10**6, bytes_accessed=10**4, transcendentals=0)


def pick(orbitals, which, shares=(1,)):
    _, planes, points = orbitals.shape
    unit = points // sum(shares)
    outs = [jax.ShapeDtypeStruct((planes, share * unit), orbitals.dtype) for share in shares] * len(which)
    count = len(outs)
    return pl.pallas_call(
        pick_kernel,
        out_shape=outs,
        in_specs=[scalars, outside],
        out_specs=[whole] * count,
        scratch_shapes=[pltpu.SemaphoreType.DMA((count,))],
        compiler_params=pltpu.CompilerParams(vmem_limit_bytes=limit),
        cost_estimate=small,
        name="pick",
    )(jnp.stack(which).astype(jnp.int32), orbitals)


def put(parity, first, near, *choices):
    pieces = near + [piece for choice in choices for piece in choice]
    planes, points = near[0].shape[0], sum(piece.shape[1] for piece in near)
    return pl.pallas_call(
        functools.partial(put_kernel, 2 * len(choices[0])),
        out_shape=jax.ShapeDtypeStruct((2, planes, points), near[0].dtype),
        in_specs=[scalars] + [outside] * len(pieces),
        out_specs=whole,
        scratch_shapes=[pltpu.SemaphoreType.DMA((len(near) + len(choices[0]),))],
        compiler_params=pltpu.CompilerParams(vmem_limit_bytes=limit),
        cost_estimate=small,
        name="put",
    )(jnp.stack([parity, first.astype(parity.dtype)]).astype(jnp.int32), *pieces)


def forward(flags, place, first, targets, group, cas_matrix, windows):
    planes = group[0].shape[1]
    extent = cas_matrix.shape[0]
    points = extent * extent
    return pl.pallas_call(
        functools.partial(forward_kernel, place, first, len(targets), len(targets[0])),
        out_shape=jax.ShapeDtypeStruct((2, extent * plane_pitch, lanes), jnp.float32),
        in_specs=[scalars] + [outside] * (len(targets) * len(targets[0]) + len(group)) + [whole] * 2,
        out_specs=whole,
        scratch_shapes=[
            pltpu.VMEM((planes, points), jnp.bfloat16),
            pltpu.VMEM((planes, points), jnp.bfloat16),
            pltpu.VMEM((2, planes * turned_pitch, lanes), jnp.float32),
            pltpu.SemaphoreType.DMA((len(targets[0]) + 5,)),
        ],
        compiler_params=pltpu.CompilerParams(vmem_limit_bytes=limit),
        cost_estimate=small,
        name="forward",
    )(flags, *[piece for choice in targets for piece in choice], *group, cas_matrix, windows)


def middle(slabs, into, back, square):
    extent = square.shape[0]
    rows = 8
    block = pl.BlockSpec((2, rows * plane_pitch, lanes), lambda i: (0, i, 0))

    def same(shape):
        return pl.BlockSpec(shape, lambda i: (0, 0))

    return pl.pallas_call(
        middle_kernel,
        grid=(extent // rows,),
        out_shape=[jax.ShapeDtypeStruct(slabs[0].shape, jnp.float32)] * 4,
        in_specs=[block] * 4 + [same(into.shape), same(back.shape), same(square.shape)],
        out_specs=[block] * 4,
        compiler_params=pltpu.CompilerParams(vmem_limit_bytes=limit),
        cost_estimate=small,
        name="middle",
    )(*slabs, into, back, square)


def backward(flags, places, first, slabs, groups, cas_matrix, windows, parts):
    planes = groups[0][0].shape[1]
    extent = cas_matrix.shape[0]
    points = extent * extent
    pieces = [piece for group in groups for piece in group]
    return pl.pallas_call(
        functools.partial(backward_kernel, places, first, parts),
        out_shape=[jax.ShapeDtypeStruct((planes, points // parts), jnp.bfloat16)] * parts,
        in_specs=[scalars] + [outside] * (len(slabs) + len(pieces)) + [whole] * 2,
        out_specs=[whole] * parts,
        scratch_shapes=[
            pltpu.VMEM(slabs[0].shape, jnp.float32),
            pltpu.VMEM((planes, points), jnp.bfloat16),
            pltpu.VMEM((2, planes * turned_pitch, lanes), jnp.float32),
            pltpu.SemaphoreType.DMA((6,)),
        ],
        compiler_params=pltpu.CompilerParams(vmem_limit_bytes=limit),
        cost_estimate=small,
        name="backward",
    )(flags, *slabs, *pieces, cas_matrix, windows)


def add(a, b):
    return (a.astype(jnp.float32) + b.astype(jnp.float32)).astype(jnp.bfloat16)


def pair_plan(orbitals, source_index):
    local_count, planes, points = orbitals.shape
    slabs = lax.axis_size("grid")
    extent = planes * slabs
    band, z = lax.axis_index("band"), lax.axis_index("grid")
    column, core = band // cores, band % cores
    quarter = points // 4
    at_home = core == holder(z)
    direct_neighbour = core == 1 - z % 2
    parity = z % 2
    inner = (z == 1) | (z == 2)
    second = inner.astype(jnp.int32)
    flags = jnp.stack([core, column, at_home, direct_neighbour, second, 1 - second]).astype(jnp.int32)
    home, direct = 2, 3

    to_near = pick(orbitals, [1 - parity], (1, 5, 2))
    near = [move(to_near[0], near_routes())]
    chosen = [source_index[core] % local_count, source_index[1 - core] % local_count]
    picked, other = pick(stage(orbitals, to_near), chosen)
    owner = source_index[core] // local_count
    slab = jnp.where(owner % cores == core, picked, swap_cores(other))

    def cut(d):
        return lax.dynamic_slice_in_dim(slab, (column ^ d) * quarter, quarter, 1)

    cuts = stage([cut(d) for d in range(4)], near)
    near.append(move(stage(to_near[1], cuts), near_routes()))
    candidates = [cuts[0]] + [to_column(cuts[d], d) for d in (1, 2, 3)]
    (own_parity,) = pick(stage(orbitals, cuts), [parity])
    cas_matrix = cas_table(extent)
    windows = window_tables(cas_matrix)
    windows_back = jnp.swapaxes(windows, 1, 2)
    places = (((z ^ jnp.arange(slabs)) * planes)[:, None] + jnp.arange(planes)).reshape(extent)
    into = cas_entries(jnp.arange(extent), places, extent)
    square_x = wave_square(jnp.arange(extent, dtype=jnp.int32), extent)
    strength = (extent * spacing) ** 2 / math.pi
    square = (square_x[:, None] + square_x[None, :] + 1.0) * (1.0 / strength)
    square = jnp.pad(square, ((0, 0), (0, 2 * lanes - extent)), constant_values=1.0)
    tables = [cas_matrix, windows, windows_back, into, into.T, square]

    candidates, tables, own_parity, flags = stage((candidates, tables, own_parity, flags), near)
    cas_matrix, windows, windows_back, into, outof, square = tables
    own = lax.select_n(column ^ (owner // cores), *candidates)
    own, last = stage((own, to_near[2]), near, tables)
    near.append(move(last, near_routes()))
    own_x, own_y = to_column(own, 1), to_column(own, 2)
    neighbour = to_height(own, {0: 1, 1: 0, 2: 3, 3: 2})
    crossed = to_height(own, {1: 2, 2: 1})

    neighbour, crossed, own_x, own_y = stage((neighbour, crossed, own_x, own_y))
    neighbour_x, neighbour_y = to_column(neighbour, 1), to_column(neighbour, 2)
    crossed_2 = to_height(neighbour, {1: 2, 2: 1})
    handed = to_height(crossed, {1: 0, 2: 3})

    low = jnp.stack([own_x[:, : quarter // 2], neighbour_x[:, : quarter // 2]])
    high = jnp.stack([own_y[:, quarter // 2 :], neighbour_y[:, quarter // 2 :]])
    low, high, crossed_2, own_parity, near = stage((low, high, crossed_2, own_parity, near), handed)
    low, high = to_column(low, 2), to_column(high, 1)
    handed_2 = to_height(crossed_2, {1: 0, 2: 3})
    far = move(own_parity, far_routes())
    own_swapped = swap_cores(own_parity)

    across = jnp.stack([jnp.where(inner, crossed, handed), jnp.where(inner, crossed_2, handed_2)])
    across, low, high, own_swapped, near = stage((across, low, high, own_swapped, near))
    sources = [
        [own[None], own_x[None], own_y[None], low[:1], high[:1]],
        [neighbour[None], neighbour_x[None], neighbour_y[None], low[1:], high[1:]],
    ]
    across_x, across_y = to_column(across, 1), to_column(across, 2)
    swapped = [swap_cores(near[1]), swap_cores(jnp.concatenate([near[0], near[2]], axis=1))]
    along_y = [forward(flags, 0, home, [[own_parity], [own_swapped]], sources[0], cas_matrix, windows)]

    low, high = across_x[:, :, : quarter // 2], across_y[:, :, quarter // 2 :]
    low, high, swapped = stage((low, high, swapped), along_y)
    unit = points // 8
    near_swapped = [swapped[1][:, :unit], swapped[0], swapped[1][:, unit:]]
    low, high = to_column(low, 2), to_column(high, 1)
    along_y.append(forward(flags, 1, direct, [near, near_swapped], sources[1], cas_matrix, windows))

    low, high, far = stage((low, high, far), along_y)
    across_source = [across, across_x, across_y, low, high]
    sources += [across_source, across_source]
    far_swapped = swap_cores(far)
    along_y_3 = forward(flags, 3, direct, [near_swapped, near], across_source, cas_matrix, windows)
    far_swapped = stage(far_swapped, along_y_3)
    along_y_2 = forward(flags, 2, home, [[far_swapped], [far]], across_source, cas_matrix, windows)
    back_x = middle([*along_y, along_y_2, along_y_3], into, outof, square)

    def partials(places, first, *earlier):
        groups = [sources[p] for p in places]
        return backward(flags, places, first, stage([back_x[p] for p in places], *earlier), groups, cas_matrix, windows_back, 4)

    given = partials([3, 1], direct)
    kept = partials([1, 3], direct)
    near = [add(k, swap_cores(g)) for g, k in zip(given, kept)]
    near = [near[0], jnp.concatenate(near[1:], axis=1)]
    near_home = [move(part, back(near_routes())) for part in near]
    given = partials([2, 0], home, near[0])
    kept = partials([0, 2], home, given[0], near_home[0])
    far = [add(k, swap_cores(g)) for k, g in zip(kept, given)]
    far_home = [move(part, back(far_routes())) for part in far]
    return put(parity, at_home, near_home, far, far_home)


def solution(mesh):
    def shards(orbitals, source_index):
        slabs, bands = mesh.shape["grid"], mesh.shape["band"]
        fits = slabs == 4 and bands == 8 and orbitals.shape[0] == 2 and source_index.shape[0] == cores
        return (pair_plan if fits else slab_plan)(orbitals, source_index)

    return jax.shard_map(
        shards,
        mesh=mesh,
        in_specs=(P("band", "grid", None), P()),
        out_specs=P("band", "grid", None),
        check_vma=False,
    )
```

```python
import functools
import math

import jax
import jax.numpy as jnp
from jax import lax
from jax.experimental import pallas as pl
from jax.experimental.pallas import tpu as pltpu
from jax.sharding import PartitionSpec as P

spacing = 0.3
cores = 2


def cas_entries(rows, columns, extent):
    products_mod = rows[:, None] * columns[None, :] % extent
    radians = products_mod.astype(jnp.float32) * (2.0 * math.pi / extent)
    return ((jnp.cos(radians) + jnp.sin(radians)) / math.sqrt(extent)).astype(jnp.bfloat16)


def cas_table(extent):
    wavenum = jnp.arange(extent, dtype=jnp.int32)
    return cas_entries(wavenum, wavenum, extent)


def wave_square(indices, extent):
    folded = jnp.minimum(indices, extent - indices).astype(jnp.float32)
    return folded * folded


def coulomb_block(extent, columns, offset):
    square_x = wave_square(jnp.arange(extent, dtype=jnp.int32), extent)
    square_y = wave_square(offset + jnp.arange(columns, dtype=jnp.int32), extent)
    total_sq = square_x[:, None, None] + square_y[None, :, None] + square_x[None, None, :]
    strength = (extent * spacing) ** 2 / math.pi
    return jnp.where(total_sq > 0, strength / (total_sq + 1.0), 0.0)


def transform(grid_data, cas_matrix, pattern):
    return jnp.einsum(pattern, grid_data, cas_matrix, preferred_element_type=jnp.float32)


def broadcast(x, axis, root):
    mine = lax.axis_index(axis) == root
    return lax.psum(jnp.where(mine, x, jnp.zeros_like(x)), axis)


def slab_potentials(pair_rho, cas_matrix, kernel_block):
    along_z = transform(pair_rho, cas_matrix, "pxyz,kz->pxyk").astype(jnp.bfloat16)
    along_y = transform(along_z, cas_matrix, "pxyz,ky->pxkz").astype(jnp.bfloat16)
    turned = lax.all_to_all(along_y, "grid", split_axis=2, concat_axis=1, tiled=True)
    scaled = (kernel_block * transform(turned, cas_matrix, "pxyz,kx->pkyz")).astype(jnp.bfloat16)
    back_x = transform(scaled, cas_matrix, "pxyz,kx->pkyz").astype(jnp.bfloat16)
    returned = lax.all_to_all(back_x, "grid", split_axis=1, concat_axis=2, tiled=True)
    again_y = transform(returned, cas_matrix, "pxyz,ky->pxkz").astype(jnp.bfloat16)
    return transform(again_y, cas_matrix, "pxyz,kz->pxyk")


def fetch_source(orbitals, which):
    local_count = orbitals.shape[0]
    local_slab = lax.dynamic_index_in_dim(orbitals, which % local_count, 0, keepdims=False)
    return broadcast(local_slab, "band", which // local_count)


def slab_plan(orbitals, source_index):
    local_count, planes, _ = orbitals.shape
    extent = planes * lax.axis_size("grid")
    orbitals = orbitals.reshape(local_count, planes, extent, extent)
    source_count = source_index.shape[0]
    cas_matrix = cas_table(extent)
    columns = extent // lax.axis_size("grid")
    kernel_block = coulomb_block(extent, columns, lax.axis_index("grid") * columns)
    fetched = [fetch_source(orbitals, source_index[number]) for number in range(source_count)]
    stacked = jnp.stack(fetched)[:, None].astype(jnp.float32)
    pair_rho = (stacked * orbitals[None].astype(jnp.float32)).astype(jnp.bfloat16)
    pair_rho = pair_rho.reshape(source_count * local_count, planes, extent, extent)
    potential = slab_potentials(pair_rho, cas_matrix, kernel_block)
    potential = potential.reshape(source_count, local_count, planes, extent, extent)
    result = (-jnp.sum(stacked * potential, axis=0)).astype(jnp.bfloat16)
    return result.reshape(local_count, planes, extent * extent)


lanes = 128
quad = 4
ring = 4
turned_pitch = 161
plane_pitch = 41


def move(x, routes):
    slabs = lax.axis_size("grid")

    def place(column, core, z):
        return (column * cores + core) * slabs + z % slabs

    return lax.ppermute(x, ("band", "grid"), [(place(*a), place(*b)) for a, b in routes])


def everywhere():
    columns = lax.axis_size("band") // cores
    return [(c, k, z) for c in range(columns) for k in range(cores) for z in range(lax.axis_size("grid"))]


def swap_cores(x):
    return move(x, [((c, k, z), (c, 1 - k, z)) for c, k, z in everywhere()])


def to_column(x, d):
    return move(x, [((c, k, z), (c ^ d, k, z)) for c, k, z in everywhere()])


def to_height(x, to):
    return move(x, [((c, k, z), (c, k, to[z])) for c, k, z in everywhere() if z in to])


def holder(z):
    return z % ring // 2


def side(core):
    return 2 * core - 1


def near_routes():
    return [((c, holder(z), z + side(k)), (c, k, z)) for c, k, z in everywhere()]


def far_routes():
    return [((c, holder(z), z + 2), (c, k, z)) for c, k, z in everywhere() if k != holder(z)]


def back(routes):
    return [(b, a) for a, b in routes]


def stage(values, *earlier):
    return lax.optimization_barrier((values, earlier))[0]


def choose(first, refs, start):
    if len(refs) == 1:
        start(refs[0])
    else:
        pl.when(first)(lambda: start(refs[0]))
        pl.when(jnp.logical_not(first))(lambda: start(refs[1]))


def start_pieces(pieces, sems):
    for number, (refs, first, to) in enumerate(pieces):
        choose(first, refs, lambda ref, to=to, number=number: pltpu.make_async_copy(ref, to, sems.at[number]).start())


def wait_pieces(pieces, sems):
    for number, (refs, _, to) in enumerate(pieces):
        pltpu.make_async_copy(refs[0], to, sems.at[number]).wait()


def source_of(refs, flags, place):
    return refs, flags[2 + place] if place > 1 else 0


def source_pieces(groups, first, source, column):
    quarter = source.shape[1] // 4
    offsets = [(column ^ e) * quarter for e in range(4)]
    offsets.append(offsets[3] + quarter // 2)
    pieces = []
    for number, offset in enumerate(offsets):
        refs = [five[number].at[which] for five, which in groups]
        to = source.at[:, pl.ds(pl.multiple_of(offset, lanes), refs[0].shape[1])]
        pieces.append((refs, first, to))
    return pieces


def split(refs, *counts):
    taken = []
    for count in counts:
        taken.append(refs[:count])
        refs = refs[count:]
    return taken


def dot(a, b):
    return jnp.dot(a, b, preferred_element_type=jnp.float32)


def both(ref, rows):
    return jnp.concatenate([ref[0, rows, :], ref[1, rows, :]], axis=1)


def beside(values):
    return jnp.concatenate(values, axis=1)


def apart(value):
    return [value[:, n : n + 2 * lanes] for n in range(0, value.shape[1], 2 * lanes)]


def put_both(ref, rows, value):
    ref[0, rows, :] = value[:, :lanes]
    ref[1, rows, :] = value[:, lanes:]


def lane_ranges(pieces):
    ranges = []
    start = 0
    for piece in pieces:
        ranges.append((start, piece.shape[1]))
        start += piece.shape[1]
    return ranges


def pick_kernel(flags, orbitals, *refs):
    outs, sems = refs[:-1], refs[-1]
    parts = len(outs) // flags.shape[0]
    ranges = lane_ranges(outs[:parts])
    copies = []
    for n, out in enumerate(outs):
        lane = pl.ds(*ranges[n % parts])
        copies.append(pltpu.make_async_copy(orbitals.at[flags[n // parts], :, lane], out, sems.at[n]))
    for copy in copies:
        copy.start()
    for copy in copies:
        copy.wait()


def put_kernel(count, flags, *refs):
    (out, sems), refs = refs[-2:], refs[:-2]
    near, choices = refs[:-count], refs[-count:]
    half = count // 2
    pieces = [((ref,), None, out.at[1 - flags[0], :, pl.ds(*lane)]) for ref, lane in zip(near, lane_ranges(near))]
    for n, lane in enumerate(lane_ranges(choices[:half])):
        pieces.append((choices[n::half], flags[1] == 1, out.at[flags[0], :, pl.ds(*lane)]))
    start_pieces(pieces, sems)
    wait_pieces(pieces, sems)


def transform_in(source, target, windows, cas, turned, out):
    planes, points = target.shape
    extent = cas.shape[0]
    step = 8
    block = quad * extent

    @pl.loop(0, points // block // step)
    def _(i):
        for r in range(quad):
            density = []
            for j in range(step):
                at = pl.ds(pl.multiple_of((i * step + j) * block + r * lanes, lanes), 2 * lanes)
                density.append(source[:, at].astype(jnp.float32) * target[:, at].astype(jnp.float32))
            density = jnp.concatenate(density, axis=0).astype(jnp.bfloat16)
            along_z = dot(density, windows[r])
            for j in range(step):
                y = (i * step + j) * quad + r
                put_both(turned, pl.ds(y, planes, stride=turned_pitch), along_z[j * planes : (j + 1) * planes])

    @pl.loop(0, planes // 4)
    def _(i):
        for j in range(4):
            x = i * 4 + j
            along_z = both(turned, pl.ds(x * turned_pitch, extent)).astype(jnp.bfloat16)
            put_both(out, pl.ds(x, extent, stride=plane_pitch), dot(cas[...], along_z))


def transform_x(slabs, into, outof, square):
    extent = square.shape[0]
    planes = extent // ring
    strength = (extent * spacing) ** 2 / math.pi
    rows = 8

    @pl.loop(0, extent // rows)
    def _(step):
        base = pl.multiple_of(step * rows * plane_pitch, 8)
        for i in range(rows):
            at = pl.ds(base + i * plane_pitch, planes)
            along_y = jnp.concatenate([both(slab, at) for slab in slabs], axis=0).astype(jnp.bfloat16)
            ky = step * rows + i
            folded = jnp.minimum(ky, extent - ky)
            weight = square[...] + (folded * folded).astype(jnp.float32) * (1.0 / strength)
            guess = pl.reciprocal(weight, approx=True)
            factor = guess * (2.0 - weight * guess)
            factor = jnp.where(weight > 1.25 / strength, factor, 0.0)
            scaled = (factor * dot(into[...], along_y)).astype(jnp.bfloat16)
            back_x = dot(outof[...], scaled)
            for n, slab in enumerate(slabs):
                put_both(slab, at, back_x[n * planes : (n + 1) * planes])


def transform_out(back_x, source, windows, cas, turned, outs):
    planes, points = source.shape
    extent = cas.shape[0]

    @pl.loop(0, planes // 4)
    def _(i):
        for j in range(4):
            x = i * 4 + j
            column_x = both(back_x, pl.ds(x, extent, stride=plane_pitch)).astype(jnp.bfloat16)
            put_both(turned, pl.ds(x * turned_pitch, extent), dot(cas[...], column_x))

    step = 5
    block = quad * extent
    blocks = points // block // len(outs)
    for number, out in enumerate(outs):

        @pl.loop(0, blocks // step)
        def _(i):
            first = number * blocks + i * step
            windowed = []
            for r in range(quad):
                again_y = jnp.concatenate(
                    [both(turned, pl.ds((first + j) * quad + r, planes, stride=turned_pitch)) for j in range(step)],
                    axis=0,
                ).astype(jnp.bfloat16)
                windowed.append(dot(again_y, windows[r]))
            for j in range(step):
                w = [part[j * planes : (j + 1) * planes] for part in windowed]
                potential = [w[0][:, :lanes]]
                potential += [w[r][:, lanes:] + w[r + 1][:, :lanes] for r in range(quad - 1)]
                potential = jnp.concatenate(potential + [w[-1][:, lanes:]], axis=1)
                at = pl.ds(pl.multiple_of((first + j) * block, lanes), block)
                to = pl.ds(pl.multiple_of((i * step + j) * block, lanes), block)
                out[:, to] = (-(source[:, at].astype(jnp.float32) * potential)).astype(jnp.bfloat16)


def forward_kernel(place, first, choices, count, flags, *refs):
    targets, five, (cas, windows, out, target, source, turned, sems) = split(refs, choices * count, 5, 7)
    ranges = lane_ranges(targets[:count])
    pieces = [(targets[n::count], flags[first] == 1, target.at[:, pl.ds(*lane)]) for n, lane in enumerate(ranges)]
    pieces += source_pieces([source_of(five, flags, place)], None, source, flags[1])
    start_pieces(pieces, sems)
    wait_pieces(pieces, sems)
    transform_in(source, target, windows, cas, turned, out)


def backward_kernel(places, first, parts, flags, *refs):
    slabs, groups, (cas, windows), outs, (back_x, source, turned, sems) = split(
        refs, len(places), 5 * len(places), 2, parts, 4
    )
    chosen = [source_of(five, flags, place) for five, place in zip(split(groups, *[5] * len(places)), places)]
    pieces = [(slabs, flags[first] == 1, back_x)] + source_pieces(chosen, flags[first] == 1, source, flags[1])
    start_pieces(pieces, sems)
    wait_pieces(pieces, sems)
    transform_out(back_x, source, windows, cas, turned, outs)


def central_kernel(home, direct, parts, flags, *refs):
    ready, targets, neighbour_source, across_source, tables, outs, scratch = split(refs, 3, 2, 5, 5, 6, 2 * parts + 2, 9)
    cas, windows, windows_back, into, outof, square = tables
    given, kept, (own_out, far_out) = split(outs, parts, parts, 2)
    slabs, target, source, given_source, kept_source, turned, first_sems, later_sems, out_sems = scratch
    at_direct = flags[direct] == 1
    column = flags[1]

    first = [(targets, flags[home] == 1, target)]
    first += source_pieces([source_of(across_source, flags, 2)], None, source, column)
    start_pieces(first, first_sems)
    later = [((ref,), None, slabs.at[place]) for ref, place in zip(ready, (0, 1, 3))]
    near_sources = [source_of(across_source, flags, 3), source_of(neighbour_source, flags, 1)]
    later += source_pieces(near_sources, at_direct, given_source, column)
    later += source_pieces(near_sources[::-1], at_direct, kept_source, column)
    start_pieces(later, later_sems)
    wait_pieces(first, first_sems)
    transform_in(source, target, windows, cas, turned, slabs.at[2])
    wait_pieces(later, later_sems)

    transform_x([slabs.at[place] for place in range(4)], into, outof, square)

    leave = [((slabs.at[0],), None, own_out), ((slabs.at[2],), None, far_out)]
    start_pieces(leave, out_sems)
    kept_place = jnp.where(at_direct, 1, 3)
    transform_out(slabs.at[4 - kept_place], given_source, windows_back, cas, turned, given)
    transform_out(slabs.at[kept_place], kept_source, windows_back, cas, turned, kept)
    wait_pieces(leave, out_sems)


def window_tables(cas_matrix):
    extent = cas_matrix.shape[0]
    tables = []
    for r in range(quad):
        shift = r * extent % lanes
        tables.append(jnp.pad(cas_matrix, ((shift, 2 * lanes - extent - shift), (0, 2 * lanes - extent))))
    return jnp.stack(tables)


limit = 40 * 2**20
central_limit = 60 * 2**20
whole = pl.BlockSpec(memory_space=pltpu.VMEM)
outside = pl.BlockSpec(memory_space=pl.ANY)
scalars = pl.BlockSpec(memory_space=pltpu.SMEM)
small = pl.CostEstimate(flops=10**6, bytes_accessed=10**4, transcendentals=0)


def pick(orbitals, which, shares=(1,)):
    _, planes, points = orbitals.shape
    unit = points // sum(shares)
    outs = [jax.ShapeDtypeStruct((planes, share * unit), orbitals.dtype) for share in shares] * len(which)
    count = len(outs)
    return pl.pallas_call(
        pick_kernel,
        out_shape=outs,
        in_specs=[scalars, outside],
        out_specs=[whole] * count,
        scratch_shapes=[pltpu.SemaphoreType.DMA((count,))],
        compiler_params=pltpu.CompilerParams(vmem_limit_bytes=limit),
        cost_estimate=small,
        name="pick",
    )(jnp.stack(which).astype(jnp.int32), orbitals)


def put(parity, first, near, *choices):
    pieces = near + [piece for choice in choices for piece in choice]
    planes, points = near[0].shape[0], sum(piece.shape[1] for piece in near)
    return pl.pallas_call(
        functools.partial(put_kernel, 2 * len(choices[0])),
        out_shape=jax.ShapeDtypeStruct((2, planes, points), near[0].dtype),
        in_specs=[scalars] + [outside] * len(pieces),
        out_specs=whole,
        scratch_shapes=[pltpu.SemaphoreType.DMA((len(near) + len(choices[0]),))],
        compiler_params=pltpu.CompilerParams(vmem_limit_bytes=limit),
        cost_estimate=small,
        name="put",
    )(jnp.stack([parity, first.astype(parity.dtype)]).astype(jnp.int32), *pieces)


def forward(flags, place, first, targets, group, cas_matrix, windows):
    planes = group[0].shape[1]
    extent = cas_matrix.shape[0]
    points = extent * extent
    return pl.pallas_call(
        functools.partial(forward_kernel, place, first, len(targets), len(targets[0])),
        out_shape=jax.ShapeDtypeStruct((2, extent * plane_pitch, lanes), jnp.float32),
        in_specs=[scalars] + [outside] * (len(targets) * len(targets[0]) + len(group)) + [whole] * 2,
        out_specs=whole,
        scratch_shapes=[
            pltpu.VMEM((planes, points), jnp.bfloat16),
            pltpu.VMEM((planes, points), jnp.bfloat16),
            pltpu.VMEM((2, planes * turned_pitch, lanes), jnp.float32),
            pltpu.SemaphoreType.DMA((len(targets[0]) + 5,)),
        ],
        compiler_params=pltpu.CompilerParams(vmem_limit_bytes=limit),
        cost_estimate=small,
        name="forward",
    )(flags, *[piece for choice in targets for piece in choice], *group, cas_matrix, windows)


def central(flags, home, direct, ready, targets, neighbour_source, across_source, tables, parts):
    planes = across_source[0].shape[1]
    extent = tables[0].shape[0]
    points = extent * extent
    pieces = [*ready, *targets, *neighbour_source, *across_source]
    part = jax.ShapeDtypeStruct((planes, points // parts), jnp.bfloat16)
    slab = jax.ShapeDtypeStruct(ready[0].shape, jnp.float32)
    outs = pl.pallas_call(
        functools.partial(central_kernel, home, direct, parts),
        out_shape=[part] * (2 * parts) + [slab] * 2,
        in_specs=[scalars] + [outside] * len(pieces) + [whole] * len(tables),
        out_specs=[whole] * (2 * parts) + [outside] * 2,
        scratch_shapes=[
            pltpu.VMEM((ring, *slab.shape), jnp.float32),
            *[pltpu.VMEM((planes, points), jnp.bfloat16)] * 4,
            pltpu.VMEM((2, planes * turned_pitch, lanes), jnp.float32),
            pltpu.SemaphoreType.DMA((6,)),
            pltpu.SemaphoreType.DMA((13,)),
            pltpu.SemaphoreType.DMA((2,)),
        ],
        compiler_params=pltpu.CompilerParams(vmem_limit_bytes=central_limit),
        cost_estimate=small,
        name="central",
    )(flags, *pieces, *tables)
    return split(outs, parts, parts, 2)


def backward(flags, places, first, slabs, groups, cas_matrix, windows, parts):
    planes = groups[0][0].shape[1]
    extent = cas_matrix.shape[0]
    points = extent * extent
    pieces = [piece for group in groups for piece in group]
    return pl.pallas_call(
        functools.partial(backward_kernel, places, first, parts),
        out_shape=[jax.ShapeDtypeStruct((planes, points // parts), jnp.bfloat16)] * parts,
        in_specs=[scalars] + [outside] * (len(slabs) + len(pieces)) + [whole] * 2,
        out_specs=[whole] * parts,
        scratch_shapes=[
            pltpu.VMEM(slabs[0].shape, jnp.float32),
            pltpu.VMEM((planes, points), jnp.bfloat16),
            pltpu.VMEM((2, planes * turned_pitch, lanes), jnp.float32),
            pltpu.SemaphoreType.DMA((6,)),
        ],
        compiler_params=pltpu.CompilerParams(vmem_limit_bytes=limit),
        cost_estimate=small,
        name="backward",
    )(flags, *slabs, *pieces, cas_matrix, windows)


def add(a, b):
    return (a.astype(jnp.float32) + b.astype(jnp.float32)).astype(jnp.bfloat16)


def pair_plan(orbitals, source_index):
    local_count, planes, points = orbitals.shape
    slabs = lax.axis_size("grid")
    extent = planes * slabs
    band, z = lax.axis_index("band"), lax.axis_index("grid")
    column, core = band // cores, band % cores
    quarter = points // 4
    at_home = core == holder(z)
    direct_neighbour = core == 1 - z % 2
    parity = z % 2
    inner = (z == 1) | (z == 2)
    second = inner.astype(jnp.int32)
    flags = jnp.stack([core, column, at_home, direct_neighbour, second, 1 - second]).astype(jnp.int32)
    home, direct = 2, 3

    to_near = pick(orbitals, [1 - parity], (1, 5, 2))
    near = [move(to_near[0], near_routes())]
    chosen = [source_index[core] % local_count, source_index[1 - core] % local_count]
    picked, other = pick(stage(orbitals, to_near), chosen)
    owner = source_index[core] // local_count
    slab = jnp.where(owner % cores == core, picked, swap_cores(other))

    def cut(d):
        return lax.dynamic_slice_in_dim(slab, (column ^ d) * quarter, quarter, 1)

    cuts = stage([cut(d) for d in range(4)], near)
    near.append(move(stage(to_near[1], cuts), near_routes()))
    candidates = [cuts[0]] + [to_column(cuts[d], d) for d in (1, 2, 3)]
    (own_parity,) = pick(stage(orbitals, cuts), [parity])
    cas_matrix = cas_table(extent)
    windows = window_tables(cas_matrix)
    windows_back = jnp.swapaxes(windows, 1, 2)
    places = (((z ^ jnp.arange(slabs)) * planes)[:, None] + jnp.arange(planes)).reshape(extent)
    into = cas_entries(jnp.arange(extent), places, extent)
    square_x = wave_square(jnp.arange(extent, dtype=jnp.int32), extent)
    strength = (extent * spacing) ** 2 / math.pi
    square = (square_x[:, None] + square_x[None, :] + 1.0) * (1.0 / strength)
    square = jnp.pad(square, ((0, 0), (0, 2 * lanes - extent)), constant_values=1.0)
    tables = [cas_matrix, windows, windows_back, into, into.T, square]

    candidates, tables, own_parity, flags = stage((candidates, tables, own_parity, flags), near)
    cas_matrix, windows, windows_back, into, outof, square = tables
    own = lax.select_n(column ^ (owner // cores), *candidates)
    own, last = stage((own, to_near[2]), near, tables)
    near.append(move(last, near_routes()))
    own_x, own_y = to_column(own, 1), to_column(own, 2)
    neighbour = to_height(own, {0: 1, 1: 0, 2: 3, 3: 2})
    crossed = to_height(own, {1: 2, 2: 1})

    neighbour, crossed, own_x, own_y = stage((neighbour, crossed, own_x, own_y))
    neighbour_x, neighbour_y = to_column(neighbour, 1), to_column(neighbour, 2)
    crossed_2 = to_height(neighbour, {1: 2, 2: 1})
    handed = to_height(crossed, {1: 0, 2: 3})

    low = jnp.stack([own_x[:, : quarter // 2], neighbour_x[:, : quarter // 2]])
    high = jnp.stack([own_y[:, quarter // 2 :], neighbour_y[:, quarter // 2 :]])
    low, high, crossed_2, own_parity, near = stage((low, high, crossed_2, own_parity, near), handed)
    low, high = to_column(low, 2), to_column(high, 1)
    handed_2 = to_height(crossed_2, {1: 0, 2: 3})
    far = move(own_parity, far_routes())
    own_swapped = swap_cores(own_parity)

    across = jnp.stack([jnp.where(inner, crossed, handed), jnp.where(inner, crossed_2, handed_2)])
    across, low, high, own_swapped, near = stage((across, low, high, own_swapped, near))
    sources = [
        [own[None], own_x[None], own_y[None], low[:1], high[:1]],
        [neighbour[None], neighbour_x[None], neighbour_y[None], low[1:], high[1:]],
    ]
    across_x, across_y = to_column(across, 1), to_column(across, 2)
    swapped = [swap_cores(near[1]), swap_cores(jnp.concatenate([near[0], near[2]], axis=1))]
    along_y = [forward(flags, 0, home, [[own_parity], [own_swapped]], sources[0], cas_matrix, windows)]

    low, high = across_x[:, :, : quarter // 2], across_y[:, :, quarter // 2 :]
    low, high, swapped = stage((low, high, swapped), along_y)
    unit = points // 8
    near_swapped = [swapped[1][:, :unit], swapped[0], swapped[1][:, unit:]]
    low, high = to_column(low, 2), to_column(high, 1)
    along_y.append(forward(flags, 1, direct, [near, near_swapped], sources[1], cas_matrix, windows))

    low, high, far = stage((low, high, far), along_y)
    across_source = [across, across_x, across_y, low, high]
    sources += [across_source, across_source]
    far_swapped = swap_cores(far)
    along_y_3 = forward(flags, 3, direct, [near_swapped, near], across_source, cas_matrix, windows)
    far_swapped = stage(far_swapped, along_y_3)
    given, kept, back_x = central(
        flags,
        home,
        direct,
        [*along_y, along_y_3],
        [far_swapped, far],
        sources[1],
        across_source,
        [cas_matrix, windows, windows_back, into, outof, square],
        4,
    )

    def partials(places, first, *earlier):
        slabs = stage([back_x[place // 2] for place in places], *earlier)
        groups = [sources[place] for place in places]
        return backward(flags, places, first, slabs, groups, cas_matrix, windows_back, 4)

    near = [add(k, swap_cores(g)) for g, k in zip(given, kept)]
    near = [near[0], jnp.concatenate(near[1:], axis=1)]
    near_home = [move(part, back(near_routes())) for part in near]
    given = partials([2, 0], home, near[0])
    kept = partials([0, 2], home, given[0], near_home[0])
    far = [add(k, swap_cores(g)) for k, g in zip(kept, given)]
    far_home = [move(part, back(far_routes())) for part in far]
    return put(parity, at_home, near_home, far, far_home)


def solution(mesh):
    def shards(orbitals, source_index):
        slabs, bands = mesh.shape["grid"], mesh.shape["band"]
        fits = slabs == 4 and bands == 8 and orbitals.shape[0] == 2 and source_index.shape[0] == cores
        return (pair_plan if fits else slab_plan)(orbitals, source_index)

    return jax.shard_map(
        shards,
        mesh=mesh,
        in_specs=(P("band", "grid", None), P()),
        out_specs=P("band", "grid", None),
        check_vma=False,
    )
```

```python
import functools
import math

import jax
import jax.numpy as jnp
from jax import lax
from jax.experimental import pallas as pl
from jax.experimental.pallas import tpu as pltpu
from jax.sharding import PartitionSpec as P

spacing = 0.3
cores = 2


def cas_entries(rows, columns, extent):
    products_mod = rows[:, None] * columns[None, :] % extent
    radians = products_mod.astype(jnp.float32) * (2.0 * math.pi / extent)
    return ((jnp.cos(radians) + jnp.sin(radians)) / math.sqrt(extent)).astype(jnp.bfloat16)


def cas_table(extent):
    wavenum = jnp.arange(extent, dtype=jnp.int32)
    return cas_entries(wavenum, wavenum, extent)


def wave_square(indices, extent):
    folded = jnp.minimum(indices, extent - indices).astype(jnp.float32)
    return folded * folded


def coulomb_block(extent, columns, offset):
    square_x = wave_square(jnp.arange(extent, dtype=jnp.int32), extent)
    square_y = wave_square(offset + jnp.arange(columns, dtype=jnp.int32), extent)
    total_sq = square_x[:, None, None] + square_y[None, :, None] + square_x[None, None, :]
    strength = (extent * spacing) ** 2 / math.pi
    return jnp.where(total_sq > 0, strength / (total_sq + 1.0), 0.0)


def transform(grid_data, cas_matrix, pattern):
    return jnp.einsum(pattern, grid_data, cas_matrix, preferred_element_type=jnp.float32)


def broadcast(x, axis, root):
    mine = lax.axis_index(axis) == root
    return lax.psum(jnp.where(mine, x, jnp.zeros_like(x)), axis)


def slab_potentials(pair_rho, cas_matrix, kernel_block):
    along_z = transform(pair_rho, cas_matrix, "pxyz,kz->pxyk").astype(jnp.bfloat16)
    along_y = transform(along_z, cas_matrix, "pxyz,ky->pxkz").astype(jnp.bfloat16)
    turned = lax.all_to_all(along_y, "grid", split_axis=2, concat_axis=1, tiled=True)
    scaled = (kernel_block * transform(turned, cas_matrix, "pxyz,kx->pkyz")).astype(jnp.bfloat16)
    back_x = transform(scaled, cas_matrix, "pxyz,kx->pkyz").astype(jnp.bfloat16)
    returned = lax.all_to_all(back_x, "grid", split_axis=1, concat_axis=2, tiled=True)
    again_y = transform(returned, cas_matrix, "pxyz,ky->pxkz").astype(jnp.bfloat16)
    return transform(again_y, cas_matrix, "pxyz,kz->pxyk")


def fetch_source(orbitals, which):
    local_count = orbitals.shape[0]
    local_slab = lax.dynamic_index_in_dim(orbitals, which % local_count, 0, keepdims=False)
    return broadcast(local_slab, "band", which // local_count)


def slab_plan(orbitals, source_index):
    local_count, planes, _ = orbitals.shape
    extent = planes * lax.axis_size("grid")
    orbitals = orbitals.reshape(local_count, planes, extent, extent)
    source_count = source_index.shape[0]
    cas_matrix = cas_table(extent)
    columns = extent // lax.axis_size("grid")
    kernel_block = coulomb_block(extent, columns, lax.axis_index("grid") * columns)
    fetched = [fetch_source(orbitals, source_index[number]) for number in range(source_count)]
    stacked = jnp.stack(fetched)[:, None].astype(jnp.float32)
    pair_rho = (stacked * orbitals[None].astype(jnp.float32)).astype(jnp.bfloat16)
    pair_rho = pair_rho.reshape(source_count * local_count, planes, extent, extent)
    potential = slab_potentials(pair_rho, cas_matrix, kernel_block)
    potential = potential.reshape(source_count, local_count, planes, extent, extent)
    result = (-jnp.sum(stacked * potential, axis=0)).astype(jnp.bfloat16)
    return result.reshape(local_count, planes, extent * extent)


lanes = 128
quad = 4
ring = 4
turned_pitch = 161
plane_pitch = 41


def move(x, routes):
    slabs = lax.axis_size("grid")

    def place(column, core, z):
        return (column * cores + core) * slabs + z % slabs

    return lax.ppermute(x, ("band", "grid"), [(place(*a), place(*b)) for a, b in routes])


def everywhere():
    columns = lax.axis_size("band") // cores
    return [(c, k, z) for c in range(columns) for k in range(cores) for z in range(lax.axis_size("grid"))]


def swap_cores(x):
    return move(x, [((c, k, z), (c, 1 - k, z)) for c, k, z in everywhere()])


def to_column(x, d):
    return move(x, [((c, k, z), (c ^ d, k, z)) for c, k, z in everywhere()])


def to_height(x, to):
    return move(x, [((c, k, z), (c, k, to[z])) for c, k, z in everywhere() if z in to])


def holder(z):
    return z % ring // 2


def side(core):
    return 2 * core - 1


def near_routes():
    return [((c, holder(z), z + side(k)), (c, k, z)) for c, k, z in everywhere()]


def far_routes():
    return [((c, holder(z), z + 2), (c, k, z)) for c, k, z in everywhere() if k != holder(z)]


def back(routes):
    return [(b, a) for a, b in routes]


def stage(values, *earlier):
    return lax.optimization_barrier((values, earlier))[0]


def choose(first, refs, start):
    if len(refs) == 1:
        start(refs[0])
    else:
        pl.when(first)(lambda: start(refs[0]))
        pl.when(jnp.logical_not(first))(lambda: start(refs[1]))


def start_pieces(pieces, sems):
    for number, (refs, first, to) in enumerate(pieces):
        choose(first, refs, lambda ref, to=to, number=number: pltpu.make_async_copy(ref, to, sems.at[number]).start())


def wait_pieces(pieces, sems):
    for number, (refs, _, to) in enumerate(pieces):
        pltpu.make_async_copy(refs[0], to, sems.at[number]).wait()


def source_of(refs, flags, place):
    return refs, flags[2 + place] if place > 1 else 0


def source_pieces(groups, first, source, column):
    quarter = source.shape[1] // 4
    offsets = [(column ^ e) * quarter for e in range(4)]
    offsets.append(offsets[3] + quarter // 2)
    pieces = []
    for number, offset in enumerate(offsets):
        refs = [five[number].at[which] for five, which in groups]
        to = source.at[:, pl.ds(pl.multiple_of(offset, lanes), refs[0].shape[1])]
        pieces.append((refs, first, to))
    return pieces


def split(refs, *counts):
    taken = []
    for count in counts:
        taken.append(refs[:count])
        refs = refs[count:]
    return taken


def dot(a, b):
    return jnp.dot(a, b, preferred_element_type=jnp.float32)


def both(ref, rows):
    return jnp.concatenate([ref[0, rows, :], ref[1, rows, :]], axis=1)


def beside(values):
    return jnp.concatenate(values, axis=1)


def apart(value):
    return [value[:, n : n + 2 * lanes] for n in range(0, value.shape[1], 2 * lanes)]


def put_both(ref, rows, value):
    ref[0, rows, :] = value[:, :lanes]
    ref[1, rows, :] = value[:, lanes:]


def lane_ranges(pieces):
    ranges = []
    start = 0
    for piece in pieces:
        ranges.append((start, piece.shape[1]))
        start += piece.shape[1]
    return ranges


def pick_kernel(flags, orbitals, *refs):
    outs, sems = refs[:-1], refs[-1]
    parts = len(outs) // flags.shape[0]
    ranges = lane_ranges(outs[:parts])
    copies = []
    for n, out in enumerate(outs):
        lane = pl.ds(*ranges[n % parts])
        copies.append(pltpu.make_async_copy(orbitals.at[flags[n // parts], :, lane], out, sems.at[n]))
    for copy in copies:
        copy.start()
    for copy in copies:
        copy.wait()


def put_kernel(count, flags, *refs):
    (out, sems), refs = refs[-2:], refs[:-2]
    near, choices = refs[:-count], refs[-count:]
    half = count // 2
    pieces = [((ref,), None, out.at[1 - flags[0], :, pl.ds(*lane)]) for ref, lane in zip(near, lane_ranges(near))]
    for n, lane in enumerate(lane_ranges(choices[:half])):
        pieces.append((choices[n::half], flags[1] == 1, out.at[flags[0], :, pl.ds(*lane)]))
    start_pieces(pieces, sems)
    wait_pieces(pieces, sems)


def transform_in(source, target, windows, cas, turned, out):
    planes, points = target.shape
    extent = cas.shape[0]
    step = 8
    block = quad * extent

    @pl.loop(0, points // block // step)
    def _(i):
        for r in range(quad):
            density = []
            for j in range(step):
                at = pl.ds(pl.multiple_of((i * step + j) * block + r * lanes, lanes), 2 * lanes)
                density.append(source[:, at].astype(jnp.float32) * target[:, at].astype(jnp.float32))
            density = jnp.concatenate(density, axis=0).astype(jnp.bfloat16)
            along_z = dot(density, windows[r])
            for j in range(step):
                y = (i * step + j) * quad + r
                put_both(turned, pl.ds(y, planes, stride=turned_pitch), along_z[j * planes : (j + 1) * planes])

    @pl.loop(0, planes // 4)
    def _(i):
        for j in range(4):
            x = i * 4 + j
            along_z = both(turned, pl.ds(x * turned_pitch, extent)).astype(jnp.bfloat16)
            put_both(out, pl.ds(x, extent, stride=plane_pitch), dot(cas[...], along_z))


def transform_x(slabs, into, outof, square):
    extent = square.shape[0]
    planes = extent // ring
    strength = (extent * spacing) ** 2 / math.pi
    rows = 8

    @pl.loop(0, extent // rows)
    def _(step):
        base = pl.multiple_of(step * rows * plane_pitch, 8)
        for i in range(rows):
            at = pl.ds(base + i * plane_pitch, planes)
            along_y = jnp.concatenate([both(slab, at) for slab in slabs], axis=0).astype(jnp.bfloat16)
            ky = step * rows + i
            folded = jnp.minimum(ky, extent - ky)
            weight = square[...] + (folded * folded).astype(jnp.float32) * (1.0 / strength)
            guess = pl.reciprocal(weight, approx=True)
            factor = guess * (2.0 - weight * guess)
            factor = jnp.where(weight > 1.25 / strength, factor, 0.0)
            scaled = (factor * dot(into[...], along_y)).astype(jnp.bfloat16)
            back_x = dot(outof[...], scaled)
            for n, slab in enumerate(slabs):
                put_both(slab, at, back_x[n * planes : (n + 1) * planes])


def transform_out(back_x, source, windows, cas, turned, outs):
    planes, points = source.shape
    extent = cas.shape[0]

    @pl.loop(0, planes // 4)
    def _(i):
        for j in range(4):
            x = i * 4 + j
            column_x = both(back_x, pl.ds(x, extent, stride=plane_pitch)).astype(jnp.bfloat16)
            put_both(turned, pl.ds(x * turned_pitch, extent), dot(cas[...], column_x))

    step = 5
    block = quad * extent
    blocks = points // block // len(outs)
    for number, out in enumerate(outs):

        @pl.loop(0, blocks // step)
        def _(i):
            first = number * blocks + i * step
            windowed = []
            for r in range(quad):
                again_y = jnp.concatenate(
                    [both(turned, pl.ds((first + j) * quad + r, planes, stride=turned_pitch)) for j in range(step)],
                    axis=0,
                ).astype(jnp.bfloat16)
                windowed.append(dot(again_y, windows[r]))
            for j in range(step):
                w = [part[j * planes : (j + 1) * planes] for part in windowed]
                potential = [w[0][:, :lanes]]
                potential += [w[r][:, lanes:] + w[r + 1][:, :lanes] for r in range(quad - 1)]
                potential = jnp.concatenate(potential + [w[-1][:, lanes:]], axis=1)
                at = pl.ds(pl.multiple_of((first + j) * block, lanes), block)
                to = pl.ds(pl.multiple_of((i * step + j) * block, lanes), block)
                out[:, to] = (-(source[:, at].astype(jnp.float32) * potential)).astype(jnp.bfloat16)


def forward_kernel(place, first, choices, count, flags, *refs):
    targets, five, (cas, windows, out, target, source, turned, sems) = split(refs, choices * count, 5, 7)
    ranges = lane_ranges(targets[:count])
    pieces = [(targets[n::count], flags[first] == 1, target.at[:, pl.ds(*lane)]) for n, lane in enumerate(ranges)]
    pieces += source_pieces([source_of(five, flags, place)], None, source, flags[1])
    start_pieces(pieces, sems)
    wait_pieces(pieces, sems)
    transform_in(source, target, windows, cas, turned, out)


def backward_kernel(places, first, parts, flags, *refs):
    slabs, groups, (cas, windows), outs, (back_x, source, turned, sems) = split(
        refs, len(places), 5 * len(places), 2, parts, 4
    )
    chosen = [source_of(five, flags, place) for five, place in zip(split(groups, *[5] * len(places)), places)]
    pieces = [(slabs, flags[first] == 1, back_x)] + source_pieces(chosen, flags[first] == 1, source, flags[1])
    start_pieces(pieces, sems)
    wait_pieces(pieces, sems)
    transform_out(back_x, source, windows, cas, turned, outs)


def central_kernel(home, direct, parts, flags, *refs):
    ready, targets, neighbour_source, across_source, tables, outs, scratch = split(refs, 3, 2, 5, 5, 6, 2 * parts + 2, 9)
    cas, windows, windows_back, into, outof, square = tables
    given, kept, (own_out, far_out) = split(outs, parts, parts, 2)
    slabs, target, source, given_source, kept_source, turned, first_sems, later_sems, out_sems = scratch
    at_direct = flags[direct] == 1
    column = flags[1]

    first = [(targets, flags[home] == 1, target)]
    first += source_pieces([source_of(across_source, flags, 2)], None, source, column)
    start_pieces(first, first_sems)
    later = [((ref,), None, slabs.at[place]) for ref, place in zip(ready, (0, 1, 3))]
    near_sources = [source_of(across_source, flags, 3), source_of(neighbour_source, flags, 1)]
    later += source_pieces(near_sources, at_direct, given_source, column)
    later += source_pieces(near_sources[::-1], at_direct, kept_source, column)
    start_pieces(later, later_sems)
    wait_pieces(first, first_sems)
    transform_in(source, target, windows, cas, turned, slabs.at[2])
    wait_pieces(later, later_sems)

    transform_x([slabs.at[place] for place in range(4)], into, outof, square)

    leave = [((slabs.at[0],), None, own_out), ((slabs.at[2],), None, far_out)]
    start_pieces(leave, out_sems)
    kept_place = jnp.where(at_direct, 1, 3)
    transform_out(slabs.at[4 - kept_place], given_source, windows_back, cas, turned, given)
    transform_out(slabs.at[kept_place], kept_source, windows_back, cas, turned, kept)
    wait_pieces(leave, out_sems)


def window_tables(cas_matrix):
    extent = cas_matrix.shape[0]
    tables = []
    for r in range(quad):
        shift = r * extent % lanes
        tables.append(jnp.pad(cas_matrix, ((shift, 2 * lanes - extent - shift), (0, 2 * lanes - extent))))
    return jnp.stack(tables)


limit = 60 * 2**20
whole = pl.BlockSpec(memory_space=pltpu.VMEM)
outside = pl.BlockSpec(memory_space=pl.ANY)
scalars = pl.BlockSpec(memory_space=pltpu.SMEM)
small = pl.CostEstimate(flops=10**6, bytes_accessed=10**4, transcendentals=0)


def pick(orbitals, which, shares=(1,)):
    _, planes, points = orbitals.shape
    unit = points // sum(shares)
    outs = [jax.ShapeDtypeStruct((planes, share * unit), orbitals.dtype) for share in shares] * len(which)
    count = len(outs)
    return pl.pallas_call(
        pick_kernel,
        out_shape=outs,
        in_specs=[scalars, outside],
        out_specs=[whole] * count,
        scratch_shapes=[pltpu.SemaphoreType.DMA((count,))],
        compiler_params=pltpu.CompilerParams(vmem_limit_bytes=limit),
        cost_estimate=small,
        name="pick",
    )(jnp.stack(which).astype(jnp.int32), orbitals)


def put(parity, first, near, *choices):
    pieces = near + [piece for choice in choices for piece in choice]
    planes, points = near[0].shape[0], sum(piece.shape[1] for piece in near)
    return pl.pallas_call(
        functools.partial(put_kernel, 2 * len(choices[0])),
        out_shape=jax.ShapeDtypeStruct((2, planes, points), near[0].dtype),
        in_specs=[scalars] + [outside] * len(pieces),
        out_specs=whole,
        scratch_shapes=[pltpu.SemaphoreType.DMA((len(near) + len(choices[0]),))],
        compiler_params=pltpu.CompilerParams(vmem_limit_bytes=limit),
        cost_estimate=small,
        name="put",
    )(jnp.stack([parity, first.astype(parity.dtype)]).astype(jnp.int32), *pieces)


def forward(flags, place, first, targets, group, cas_matrix, windows):
    planes = group[0].shape[1]
    extent = cas_matrix.shape[0]
    points = extent * extent
    return pl.pallas_call(
        functools.partial(forward_kernel, place, first, len(targets), len(targets[0])),
        out_shape=jax.ShapeDtypeStruct((2, extent * plane_pitch, lanes), jnp.float32),
        in_specs=[scalars] + [outside] * (len(targets) * len(targets[0]) + len(group)) + [whole] * 2,
        out_specs=whole,
        scratch_shapes=[
            pltpu.VMEM((planes, points), jnp.bfloat16),
            pltpu.VMEM((planes, points), jnp.bfloat16),
            pltpu.VMEM((2, planes * turned_pitch, lanes), jnp.float32),
            pltpu.SemaphoreType.DMA((len(targets[0]) + 5,)),
        ],
        compiler_params=pltpu.CompilerParams(vmem_limit_bytes=limit),
        cost_estimate=small,
        name="forward",
    )(flags, *[piece for choice in targets for piece in choice], *group, cas_matrix, windows)


def central(flags, home, direct, ready, targets, neighbour_source, across_source, tables, parts):
    planes = across_source[0].shape[1]
    extent = tables[0].shape[0]
    points = extent * extent
    pieces = [*ready, *targets, *neighbour_source, *across_source]
    part = jax.ShapeDtypeStruct((planes, points // parts), jnp.bfloat16)
    slab = jax.ShapeDtypeStruct(ready[0].shape, jnp.float32)
    outs = pl.pallas_call(
        functools.partial(central_kernel, home, direct, parts),
        out_shape=[part] * (2 * parts) + [slab] * 2,
        in_specs=[scalars] + [outside] * len(pieces) + [whole] * len(tables),
        out_specs=[whole] * (2 * parts) + [outside] * 2,
        scratch_shapes=[
            pltpu.VMEM((ring, *slab.shape), jnp.float32),
            *[pltpu.VMEM((planes, points), jnp.bfloat16)] * 4,
            pltpu.VMEM((2, planes * turned_pitch, lanes), jnp.float32),
            pltpu.SemaphoreType.DMA((6,)),
            pltpu.SemaphoreType.DMA((13,)),
            pltpu.SemaphoreType.DMA((2,)),
        ],
        compiler_params=pltpu.CompilerParams(vmem_limit_bytes=limit),
        cost_estimate=small,
        name="central",
    )(flags, *pieces, *tables)
    return split(outs, parts, parts, 2)


def backward(flags, places, first, slabs, groups, cas_matrix, windows, parts):
    planes = groups[0][0].shape[1]
    extent = cas_matrix.shape[0]
    points = extent * extent
    pieces = [piece for group in groups for piece in group]
    return pl.pallas_call(
        functools.partial(backward_kernel, places, first, parts),
        out_shape=[jax.ShapeDtypeStruct((planes, points // parts), jnp.bfloat16)] * parts,
        in_specs=[scalars] + [outside] * (len(slabs) + len(pieces)) + [whole] * 2,
        out_specs=[whole] * parts,
        scratch_shapes=[
            pltpu.VMEM(slabs[0].shape, jnp.float32),
            pltpu.VMEM((planes, points), jnp.bfloat16),
            pltpu.VMEM((2, planes * turned_pitch, lanes), jnp.float32),
            pltpu.SemaphoreType.DMA((6,)),
        ],
        compiler_params=pltpu.CompilerParams(vmem_limit_bytes=limit),
        cost_estimate=small,
        name="backward",
    )(flags, *slabs, *pieces, cas_matrix, windows)


def add(a, b):
    return (a.astype(jnp.float32) + b.astype(jnp.float32)).astype(jnp.bfloat16)


def pair_plan(orbitals, source_index):
    local_count, planes, points = orbitals.shape
    slabs = lax.axis_size("grid")
    extent = planes * slabs
    band, z = lax.axis_index("band"), lax.axis_index("grid")
    column, core = band // cores, band % cores
    quarter = points // 4
    at_home = core == holder(z)
    direct_neighbour = core == 1 - z % 2
    parity = z % 2
    inner = (z == 1) | (z == 2)
    second = inner.astype(jnp.int32)
    flags = jnp.stack([core, column, at_home, direct_neighbour, second, 1 - second]).astype(jnp.int32)
    home, direct = 2, 3

    chosen = [source_index[core] % local_count, source_index[1 - core] % local_count]
    picked, other = pick(orbitals, chosen)
    owner = source_index[core] // local_count
    slab = jnp.where(owner % cores == core, picked, swap_cores(other))
    to_near = pick(stage(orbitals, other), [1 - parity], (5, 3))

    def cut(d):
        return lax.dynamic_slice_in_dim(slab, (column ^ d) * quarter, quarter, 1)

    cuts, to_near = stage(([cut(d) for d in range(4)], to_near))
    near = [move(to_near[0], near_routes())]
    candidates = [cuts[0]] + [to_column(cuts[d], d) for d in (1, 2, 3)]
    (own_parity,) = pick(stage(orbitals, cuts), [parity])
    cas_matrix = cas_table(extent)
    windows = window_tables(cas_matrix)
    windows_back = jnp.swapaxes(windows, 1, 2)
    places = (((z ^ jnp.arange(slabs)) * planes)[:, None] + jnp.arange(planes)).reshape(extent)
    into = cas_entries(jnp.arange(extent), places, extent)
    square_x = wave_square(jnp.arange(extent, dtype=jnp.int32), extent)
    strength = (extent * spacing) ** 2 / math.pi
    square = (square_x[:, None] + square_x[None, :] + 1.0) * (1.0 / strength)
    square = jnp.pad(square, ((0, 0), (0, 2 * lanes - extent)), constant_values=1.0)
    tables = [cas_matrix, windows, windows_back, into, into.T, square]

    candidates, tables, own_parity, flags = stage((candidates, tables, own_parity, flags), near)
    cas_matrix, windows, windows_back, into, outof, square = tables
    own = lax.select_n(column ^ (owner // cores), *candidates)
    own = stage(own, tables)
    own_swapped = swap_cores(own_parity)
    own_x, own_y = to_column(own, 1), to_column(own, 2)
    neighbour = to_height(own, {0: 1, 1: 0, 2: 3, 3: 2})
    crossed = to_height(own, {1: 2, 2: 1})

    neighbour, crossed, own_x, own_y, own_swapped = stage((neighbour, crossed, own_x, own_y, own_swapped))
    neighbour_x, neighbour_y = to_column(neighbour, 1), to_column(neighbour, 2)
    crossed_2 = to_height(neighbour, {1: 2, 2: 1})
    handed = to_height(crossed, {1: 0, 2: 3})

    low = jnp.stack([own_x[:, : quarter // 2], neighbour_x[:, : quarter // 2]])
    high = jnp.stack([own_y[:, quarter // 2 :], neighbour_y[:, quarter // 2 :]])
    low, high, crossed_2, own_parity, last = stage((low, high, crossed_2, own_parity, to_near[1]), handed)
    low, high = to_column(low, 2), to_column(high, 1)
    handed_2 = to_height(crossed_2, {1: 0, 2: 3})
    near.append(move(last, near_routes()))
    far = move(own_parity, far_routes())

    across = jnp.stack([jnp.where(inner, crossed, handed), jnp.where(inner, crossed_2, handed_2)])
    across, low, high = stage((across, low, high))
    sources = [
        [own[None], own_x[None], own_y[None], low[:1], high[:1]],
        [neighbour[None], neighbour_x[None], neighbour_y[None], low[1:], high[1:]],
    ]
    across_x, across_y = to_column(across, 1), to_column(across, 2)
    near_swapped = [swap_cores(stage(near[0], across))]
    along_y = [forward(flags, 0, home, [[own_parity], [own_swapped]], sources[0], cas_matrix, windows)]

    low, high = across_x[:, :, : quarter // 2], across_y[:, :, quarter // 2 :]
    near[1] = stage(near[1], along_y)
    near_swapped.append(swap_cores(near[1]))
    low, high, near_swapped = stage((low, high, near_swapped), along_y)
    low, high = to_column(low, 2), to_column(high, 1)
    along_y.append(forward(flags, 1, direct, [near, near_swapped], sources[1], cas_matrix, windows))

    low, high, far = stage((low, high, far), along_y)
    across_source = [across, across_x, across_y, low, high]
    sources += [across_source, across_source]
    far_swapped = swap_cores(far)
    along_y_3 = forward(flags, 3, direct, [near_swapped, near], across_source, cas_matrix, windows)
    far_swapped = stage(far_swapped, along_y_3)
    given, kept, back_x = central(
        flags,
        home,
        direct,
        [*along_y, along_y_3],
        [far_swapped, far],
        sources[1],
        across_source,
        [cas_matrix, windows, windows_back, into, outof, square],
        4,
    )

    def partials(places, first, *earlier):
        slabs = stage([back_x[place // 2] for place in places], *earlier)
        groups = [sources[place] for place in places]
        return backward(flags, places, first, slabs, groups, cas_matrix, windows_back, 4)

    near = [add(k, swap_cores(g)) for g, k in zip(given, kept)]
    near = [near[0], jnp.concatenate(near[1:], axis=1)]
    near_home = [move(part, back(near_routes())) for part in near]
    given = partials([2, 0], home, near[0])
    kept = partials([0, 2], home, given[0], near_home[0])
    far = [add(k, swap_cores(g)) for k, g in zip(kept, given)]
    far_home = [move(part, back(far_routes())) for part in far]
    return put(parity, at_home, near_home, far, far_home)


def solution(mesh):
    def shards(orbitals, source_index):
        slabs, bands = mesh.shape["grid"], mesh.shape["band"]
        fits = slabs == 4 and bands == 8 and orbitals.shape[0] == 2 and source_index.shape[0] == cores
        return (pair_plan if fits else slab_plan)(orbitals, source_index)

    return jax.shard_map(
        shards,
        mesh=mesh,
        in_specs=(P("band", "grid", None), P()),
        out_specs=P("band", "grid", None),
        check_vma=False,
    )
```

```python
import functools
import math

import jax
import jax.numpy as jnp
from jax import lax
from jax.experimental import pallas as pl
from jax.experimental.pallas import tpu as pltpu
from jax.sharding import PartitionSpec as P

spacing = 0.3
cores = 2


def cas_entries(rows, columns, extent):
    products_mod = rows[:, None] * columns[None, :] % extent
    radians = products_mod.astype(jnp.float32) * (2.0 * math.pi / extent)
    return ((jnp.cos(radians) + jnp.sin(radians)) / math.sqrt(extent)).astype(jnp.bfloat16)


def cas_table(extent):
    wavenum = jnp.arange(extent, dtype=jnp.int32)
    return cas_entries(wavenum, wavenum, extent)


def wave_square(indices, extent):
    folded = jnp.minimum(indices, extent - indices).astype(jnp.float32)
    return folded * folded


def coulomb_block(extent, columns, offset):
    square_x = wave_square(jnp.arange(extent, dtype=jnp.int32), extent)
    square_y = wave_square(offset + jnp.arange(columns, dtype=jnp.int32), extent)
    total_sq = square_x[:, None, None] + square_y[None, :, None] + square_x[None, None, :]
    strength = (extent * spacing) ** 2 / math.pi
    return jnp.where(total_sq > 0, strength / (total_sq + 1.0), 0.0)


def transform(grid_data, cas_matrix, pattern):
    return jnp.einsum(pattern, grid_data, cas_matrix, preferred_element_type=jnp.float32)


def broadcast(x, axis, root):
    mine = lax.axis_index(axis) == root
    return lax.psum(jnp.where(mine, x, jnp.zeros_like(x)), axis)


def slab_potentials(pair_rho, cas_matrix, kernel_block):
    along_z = transform(pair_rho, cas_matrix, "pxyz,kz->pxyk").astype(jnp.bfloat16)
    along_y = transform(along_z, cas_matrix, "pxyz,ky->pxkz").astype(jnp.bfloat16)
    turned = lax.all_to_all(along_y, "grid", split_axis=2, concat_axis=1, tiled=True)
    scaled = (kernel_block * transform(turned, cas_matrix, "pxyz,kx->pkyz")).astype(jnp.bfloat16)
    back_x = transform(scaled, cas_matrix, "pxyz,kx->pkyz").astype(jnp.bfloat16)
    returned = lax.all_to_all(back_x, "grid", split_axis=1, concat_axis=2, tiled=True)
    again_y = transform(returned, cas_matrix, "pxyz,ky->pxkz").astype(jnp.bfloat16)
    return transform(again_y, cas_matrix, "pxyz,kz->pxyk")


def fetch_source(orbitals, which):
    local_count = orbitals.shape[0]
    local_slab = lax.dynamic_index_in_dim(orbitals, which % local_count, 0, keepdims=False)
    return broadcast(local_slab, "band", which // local_count)


def slab_plan(orbitals, source_index):
    local_count, planes, _ = orbitals.shape
    extent = planes * lax.axis_size("grid")
    orbitals = orbitals.reshape(local_count, planes, extent, extent)
    source_count = source_index.shape[0]
    cas_matrix = cas_table(extent)
    columns = extent // lax.axis_size("grid")
    kernel_block = coulomb_block(extent, columns, lax.axis_index("grid") * columns)
    fetched = [fetch_source(orbitals, source_index[number]) for number in range(source_count)]
    stacked = jnp.stack(fetched)[:, None].astype(jnp.float32)
    pair_rho = (stacked * orbitals[None].astype(jnp.float32)).astype(jnp.bfloat16)
    pair_rho = pair_rho.reshape(source_count * local_count, planes, extent, extent)
    potential = slab_potentials(pair_rho, cas_matrix, kernel_block)
    potential = potential.reshape(source_count, local_count, planes, extent, extent)
    result = (-jnp.sum(stacked * potential, axis=0)).astype(jnp.bfloat16)
    return result.reshape(local_count, planes, extent * extent)


lanes = 128
quad = 4
ring = 4
turned_pitch = 161
plane_pitch = 41


def move(x, routes):
    slabs = lax.axis_size("grid")

    def place(column, core, z):
        return (column * cores + core) * slabs + z % slabs

    return lax.ppermute(x, ("band", "grid"), [(place(*a), place(*b)) for a, b in routes])


def everywhere():
    columns = lax.axis_size("band") // cores
    return [(c, k, z) for c in range(columns) for k in range(cores) for z in range(lax.axis_size("grid"))]


def swap_cores(x):
    return move(x, [((c, k, z), (c, 1 - k, z)) for c, k, z in everywhere()])


def to_column(x, d):
    return move(x, [((c, k, z), (c ^ d, k, z)) for c, k, z in everywhere()])


def to_height(x, to):
    return move(x, [((c, k, z), (c, k, to[z])) for c, k, z in everywhere() if z in to])


def holder(z):
    return z % ring // 2


def side(core):
    return 2 * core - 1


def near_routes():
    return [((c, holder(z), z + side(k)), (c, k, z)) for c, k, z in everywhere()]


def far_routes():
    return [((c, holder(z), z + 2), (c, k, z)) for c, k, z in everywhere() if k != holder(z)]


def back(routes):
    return [(b, a) for a, b in routes]


def stage(values, *earlier):
    return lax.optimization_barrier((values, earlier))[0]


def choose(first, refs, start):
    if len(refs) == 1:
        start(refs[0])
    else:
        pl.when(first)(lambda: start(refs[0]))
        pl.when(jnp.logical_not(first))(lambda: start(refs[1]))


def start_pieces(pieces, sems):
    for number, (refs, first, to) in enumerate(pieces):
        choose(first, refs, lambda ref, to=to, number=number: pltpu.make_async_copy(ref, to, sems.at[number]).start())


def wait_pieces(pieces, sems):
    for number, (refs, _, to) in enumerate(pieces):
        pltpu.make_async_copy(refs[0], to, sems.at[number]).wait()


def source_of(refs, flags, place):
    return refs, flags[2 + place] if place > 1 else 0


def source_pieces(groups, first, source, column):
    quarter = source.shape[1] // 4
    offsets = [(column ^ e) * quarter for e in range(4)]
    offsets.append(offsets[3] + quarter // 2)
    pieces = []
    for number, offset in enumerate(offsets):
        refs = [five[number].at[which] for five, which in groups]
        to = source.at[:, pl.ds(pl.multiple_of(offset, lanes), refs[0].shape[1])]
        pieces.append((refs, first, to))
    return pieces


def split(refs, *counts):
    taken = []
    for count in counts:
        taken.append(refs[:count])
        refs = refs[count:]
    return taken


def dot(a, b):
    return jnp.dot(a, b, preferred_element_type=jnp.float32)


def both(ref, rows):
    return jnp.concatenate([ref[0, rows, :], ref[1, rows, :]], axis=1)


def beside(values):
    return jnp.concatenate(values, axis=1)


def apart(value):
    return [value[:, n : n + 2 * lanes] for n in range(0, value.shape[1], 2 * lanes)]


def put_both(ref, rows, value):
    ref[0, rows, :] = value[:, :lanes]
    ref[1, rows, :] = value[:, lanes:]


def lane_ranges(pieces):
    ranges = []
    start = 0
    for piece in pieces:
        ranges.append((start, piece.shape[1]))
        start += piece.shape[1]
    return ranges


def pick_kernel(which, source_index, orbitals, *refs):
    outs, sems = refs[:-1], refs[-1]
    chosen = which(source_index)
    parts = len(outs) // len(chosen)
    ranges = lane_ranges(outs[:parts])
    copies = []
    for n, out in enumerate(outs):
        lane = pl.ds(*ranges[n % parts])
        copies.append(pltpu.make_async_copy(orbitals.at[chosen[n // parts], :, lane], out, sems.at[n]))
    for copy in copies:
        copy.start()
    for copy in copies:
        copy.wait()


def put_kernel(count, flags, *refs):
    (out, sems), refs = refs[-2:], refs[:-2]
    near, choices = refs[:-count], refs[-count:]
    half = count // 2
    pieces = [((ref,), None, out.at[1 - flags[0], :, pl.ds(*lane)]) for ref, lane in zip(near, lane_ranges(near))]
    for n, lane in enumerate(lane_ranges(choices[:half])):
        pieces.append((choices[n::half], flags[1] == 1, out.at[flags[0], :, pl.ds(*lane)]))
    start_pieces(pieces, sems)
    wait_pieces(pieces, sems)


def transform_in(source, target, windows, cas, turned, out):
    planes, points = target.shape
    extent = cas.shape[0]
    step = 8
    block = quad * extent

    @pl.loop(0, points // block // step)
    def _(i):
        for r in range(quad):
            density = []
            for j in range(step):
                at = pl.ds(pl.multiple_of((i * step + j) * block + r * lanes, lanes), 2 * lanes)
                density.append(source[:, at].astype(jnp.float32) * target[:, at].astype(jnp.float32))
            density = jnp.concatenate(density, axis=0).astype(jnp.bfloat16)
            along_z = dot(density, windows[r])
            for j in range(step):
                y = (i * step + j) * quad + r
                put_both(turned, pl.ds(y, planes, stride=turned_pitch), along_z[j * planes : (j + 1) * planes])

    @pl.loop(0, planes // 4)
    def _(i):
        for j in range(4):
            x = i * 4 + j
            along_z = both(turned, pl.ds(x * turned_pitch, extent)).astype(jnp.bfloat16)
            put_both(out, pl.ds(x, extent, stride=plane_pitch), dot(cas[...], along_z))


def transform_x(slabs, into, outof, square):
    extent = square.shape[0]
    planes = extent // ring
    strength = (extent * spacing) ** 2 / math.pi
    rows = 8

    @pl.loop(0, extent // rows)
    def _(step):
        base = pl.multiple_of(step * rows * plane_pitch, 8)
        for i in range(rows):
            at = pl.ds(base + i * plane_pitch, planes)
            along_y = jnp.concatenate([both(slab, at) for slab in slabs], axis=0).astype(jnp.bfloat16)
            ky = step * rows + i
            folded = jnp.minimum(ky, extent - ky)
            weight = square[...] + (folded * folded).astype(jnp.float32) * (1.0 / strength)
            guess = pl.reciprocal(weight, approx=True)
            factor = guess * (2.0 - weight * guess)
            factor = jnp.where(weight > 1.25 / strength, factor, 0.0)
            scaled = (factor * dot(into[...], along_y)).astype(jnp.bfloat16)
            back_x = dot(outof[...], scaled)
            for n, slab in enumerate(slabs):
                put_both(slab, at, back_x[n * planes : (n + 1) * planes])


def transform_out(back_x, source, windows, cas, turned, outs):
    planes, points = source.shape
    extent = cas.shape[0]

    @pl.loop(0, planes // 4)
    def _(i):
        for j in range(4):
            x = i * 4 + j
            column_x = both(back_x, pl.ds(x, extent, stride=plane_pitch)).astype(jnp.bfloat16)
            put_both(turned, pl.ds(x * turned_pitch, extent), dot(cas[...], column_x))

    step = 5
    block = quad * extent
    blocks = points // block // len(outs)
    for number, out in enumerate(outs):

        @pl.loop(0, blocks // step)
        def _(i):
            first = number * blocks + i * step
            windowed = []
            for r in range(quad):
                again_y = jnp.concatenate(
                    [both(turned, pl.ds((first + j) * quad + r, planes, stride=turned_pitch)) for j in range(step)],
                    axis=0,
                ).astype(jnp.bfloat16)
                windowed.append(dot(again_y, windows[r]))
            for j in range(step):
                w = [part[j * planes : (j + 1) * planes] for part in windowed]
                potential = [w[0][:, :lanes]]
                potential += [w[r][:, lanes:] + w[r + 1][:, :lanes] for r in range(quad - 1)]
                potential = jnp.concatenate(potential + [w[-1][:, lanes:]], axis=1)
                at = pl.ds(pl.multiple_of((first + j) * block, lanes), block)
                to = pl.ds(pl.multiple_of((i * step + j) * block, lanes), block)
                out[:, to] = (-(source[:, at].astype(jnp.float32) * potential)).astype(jnp.bfloat16)


def forward_kernel(place, first, choices, count, flags, *refs):
    targets, five, (cas, windows, out, target, source, turned, sems) = split(refs, choices * count, 5, 7)
    ranges = lane_ranges(targets[:count])
    pieces = [(targets[n::count], flags[first] == 1, target.at[:, pl.ds(*lane)]) for n, lane in enumerate(ranges)]
    pieces += source_pieces([source_of(five, flags, place)], None, source, flags[1])
    start_pieces(pieces, sems)
    wait_pieces(pieces, sems)
    transform_in(source, target, windows, cas, turned, out)


def backward_kernel(places, first, parts, flags, *refs):
    slabs, groups, (cas, windows), outs, (back_x, source, turned, sems) = split(
        refs, len(places), 5 * len(places), 2, parts, 4
    )
    chosen = [source_of(five, flags, place) for five, place in zip(split(groups, *[5] * len(places)), places)]
    pieces = [(slabs, flags[first] == 1, back_x)] + source_pieces(chosen, flags[first] == 1, source, flags[1])
    start_pieces(pieces, sems)
    wait_pieces(pieces, sems)
    transform_out(back_x, source, windows, cas, turned, outs)


def central_kernel(home, direct, parts, flags, *refs):
    ready, targets, neighbour_source, across_source, tables, outs, scratch = split(refs, 3, 2, 5, 5, 6, 2 * parts + 2, 9)
    cas, windows, windows_back, into, outof, square = tables
    given, kept, (own_out, far_out) = split(outs, parts, parts, 2)
    slabs, target, source, given_source, kept_source, turned, first_sems, later_sems, out_sems = scratch
    at_direct = flags[direct] == 1
    column = flags[1]

    first = [(targets, flags[home] == 1, target)]
    first += source_pieces([source_of(across_source, flags, 2)], None, source, column)
    start_pieces(first, first_sems)
    later = [((ref,), None, slabs.at[place]) for ref, place in zip(ready, (0, 1, 3))]
    near_sources = [source_of(across_source, flags, 3), source_of(neighbour_source, flags, 1)]
    later += source_pieces(near_sources, at_direct, given_source, column)
    later += source_pieces(near_sources[::-1], at_direct, kept_source, column)
    start_pieces(later, later_sems)
    wait_pieces(first, first_sems)
    transform_in(source, target, windows, cas, turned, slabs.at[2])
    wait_pieces(later, later_sems)

    transform_x([slabs.at[place] for place in range(4)], into, outof, square)

    leave = [((slabs.at[0],), None, own_out), ((slabs.at[2],), None, far_out)]
    start_pieces(leave, out_sems)
    kept_place = jnp.where(at_direct, 1, 3)
    transform_out(slabs.at[4 - kept_place], given_source, windows_back, cas, turned, given)
    transform_out(slabs.at[kept_place], kept_source, windows_back, cas, turned, kept)
    wait_pieces(leave, out_sems)


def window_tables(cas_matrix):
    extent = cas_matrix.shape[0]
    tables = []
    for r in range(quad):
        shift = r * extent % lanes
        tables.append(jnp.pad(cas_matrix, ((shift, 2 * lanes - extent - shift), (0, 2 * lanes - extent))))
    return jnp.stack(tables)


limit = 60 * 2**20
whole = pl.BlockSpec(memory_space=pltpu.VMEM)
outside = pl.BlockSpec(memory_space=pl.ANY)
scalars = pl.BlockSpec(memory_space=pltpu.SMEM)
small = pl.CostEstimate(flops=10**6, bytes_accessed=10**4, transcendentals=0)


def pick(orbitals, source_index, which, shares=(1,)):
    _, planes, points = orbitals.shape
    unit = points // sum(shares)
    outs = [jax.ShapeDtypeStruct((planes, share * unit), orbitals.dtype) for share in shares]
    return pl.pallas_call(
        functools.partial(pick_kernel, which),
        out_shape=outs,
        in_specs=[scalars, outside],
        out_specs=[whole] * len(outs),
        scratch_shapes=[pltpu.SemaphoreType.DMA((len(outs),))],
        compiler_params=pltpu.CompilerParams(vmem_limit_bytes=limit),
        cost_estimate=small,
        name="pick",
    )(source_index, orbitals)


def put(parity, first, near, *choices):
    pieces = near + [piece for choice in choices for piece in choice]
    planes, points = near[0].shape[0], sum(piece.shape[1] for piece in near)
    return pl.pallas_call(
        functools.partial(put_kernel, 2 * len(choices[0])),
        out_shape=jax.ShapeDtypeStruct((2, planes, points), near[0].dtype),
        in_specs=[scalars] + [outside] * len(pieces),
        out_specs=whole,
        scratch_shapes=[pltpu.SemaphoreType.DMA((len(near) + len(choices[0]),))],
        compiler_params=pltpu.CompilerParams(vmem_limit_bytes=limit),
        cost_estimate=small,
        name="put",
    )(jnp.stack([parity, first.astype(parity.dtype)]).astype(jnp.int32), *pieces)


def forward(flags, place, first, targets, group, cas_matrix, windows):
    planes = group[0].shape[1]
    extent = cas_matrix.shape[0]
    points = extent * extent
    return pl.pallas_call(
        functools.partial(forward_kernel, place, first, len(targets), len(targets[0])),
        out_shape=jax.ShapeDtypeStruct((2, extent * plane_pitch, lanes), jnp.float32),
        in_specs=[scalars] + [outside] * (len(targets) * len(targets[0]) + len(group)) + [whole] * 2,
        out_specs=whole,
        scratch_shapes=[
            pltpu.VMEM((planes, points), jnp.bfloat16),
            pltpu.VMEM((planes, points), jnp.bfloat16),
            pltpu.VMEM((2, planes * turned_pitch, lanes), jnp.float32),
            pltpu.SemaphoreType.DMA((len(targets[0]) + 5,)),
        ],
        compiler_params=pltpu.CompilerParams(vmem_limit_bytes=limit),
        cost_estimate=small,
        name="forward",
    )(flags, *[piece for choice in targets for piece in choice], *group, cas_matrix, windows)


def central(flags, home, direct, ready, targets, neighbour_source, across_source, tables, parts):
    planes = across_source[0].shape[1]
    extent = tables[0].shape[0]
    points = extent * extent
    pieces = [*ready, *targets, *neighbour_source, *across_source]
    part = jax.ShapeDtypeStruct((planes, points // parts), jnp.bfloat16)
    slab = jax.ShapeDtypeStruct(ready[0].shape, jnp.float32)
    outs = pl.pallas_call(
        functools.partial(central_kernel, home, direct, parts),
        out_shape=[part] * (2 * parts) + [slab] * 2,
        in_specs=[scalars] + [outside] * len(pieces) + [whole] * len(tables),
        out_specs=[whole] * (2 * parts) + [outside] * 2,
        scratch_shapes=[
            pltpu.VMEM((ring, *slab.shape), jnp.float32),
            *[pltpu.VMEM((planes, points), jnp.bfloat16)] * 4,
            pltpu.VMEM((2, planes * turned_pitch, lanes), jnp.float32),
            pltpu.SemaphoreType.DMA((6,)),
            pltpu.SemaphoreType.DMA((13,)),
            pltpu.SemaphoreType.DMA((2,)),
        ],
        compiler_params=pltpu.CompilerParams(vmem_limit_bytes=limit),
        cost_estimate=small,
        name="central",
    )(flags, *pieces, *tables)
    return split(outs, parts, parts, 2)


def backward(flags, places, first, slabs, groups, cas_matrix, windows, parts):
    planes = groups[0][0].shape[1]
    extent = cas_matrix.shape[0]
    points = extent * extent
    pieces = [piece for group in groups for piece in group]
    return pl.pallas_call(
        functools.partial(backward_kernel, places, first, parts),
        out_shape=[jax.ShapeDtypeStruct((planes, points // parts), jnp.bfloat16)] * parts,
        in_specs=[scalars] + [outside] * (len(slabs) + len(pieces)) + [whole] * 2,
        out_specs=[whole] * parts,
        scratch_shapes=[
            pltpu.VMEM(slabs[0].shape, jnp.float32),
            pltpu.VMEM((planes, points), jnp.bfloat16),
            pltpu.VMEM((2, planes * turned_pitch, lanes), jnp.float32),
            pltpu.SemaphoreType.DMA((6,)),
        ],
        compiler_params=pltpu.CompilerParams(vmem_limit_bytes=limit),
        cost_estimate=small,
        name="backward",
    )(flags, *slabs, *pieces, cas_matrix, windows)


def add(a, b):
    return (a.astype(jnp.float32) + b.astype(jnp.float32)).astype(jnp.bfloat16)


def pair_plan(orbitals, source_index):
    local_count, planes, points = orbitals.shape
    slabs = lax.axis_size("grid")
    extent = planes * slabs
    band, z = lax.axis_index("band"), lax.axis_index("grid")
    column, core = band // cores, band % cores
    quarter = points // 4
    at_home = core == holder(z)
    direct_neighbour = core == 1 - z % 2
    parity = z % 2
    inner = (z == 1) | (z == 2)
    second = inner.astype(jnp.int32)
    flags = jnp.stack([core, column, at_home, direct_neighbour, second, 1 - second]).astype(jnp.int32)
    home, direct = 2, 3

    def candidate(of_other):
        def which(source_index):
            core = lax.rem(lax.axis_index("band"), cores)
            return [lax.rem(source_index[1 - core if of_other else core], local_count)]

        return which

    def by_parity(flip):
        return lambda _: [lax.rem(lax.axis_index("grid") + flip, 2)]

    (other,) = pick(orbitals, source_index, candidate(True))
    (picked,) = pick(stage(orbitals, other), source_index, candidate(False))
    owner = source_index[core] // local_count
    slab = jnp.where(owner % cores == core, picked, swap_cores(other))
    to_near = pick(stage(orbitals, picked), source_index, by_parity(1), (2, 2, 1, 3))

    half = quarter // 2

    def cut(d, part):
        return lax.dynamic_slice_in_dim(slab, (column ^ d) * quarter + part * half, half, 1)

    def pair(d, e, part):
        return jnp.concatenate([cut(d, part), cut(e, part)], axis=1)

    pairs, to_near = stage(([pair(1, 3, 0), pair(0, 2, 0), pair(2, 3, 1), pair(0, 1, 1)], to_near))
    near = [move(to_near[0], near_routes())]
    apart_by = column ^ (owner // cores)
    same_x, same_y = apart_by % 2 == 0, apart_by // 2 == 0
    by_x = jnp.where(same_x, pairs[1], to_column(pairs[0], 1))
    by_y = jnp.where(same_y, pairs[3], to_column(pairs[2], 2))
    by_x, by_y, near, part = stage((by_x, by_y, near, to_near[1]))
    near_swapped = [swap_cores(near[0])]
    near.append(move(part, near_routes()))
    by_x = jnp.where(same_y, by_x[:, :half], to_column(by_x[:, half:], 2))
    by_y = jnp.where(same_x, by_y[:, :half], to_column(by_y[:, half:], 1))
    (own_parity,) = pick(stage(orbitals, pairs), source_index, by_parity(0))
    cas_matrix = cas_table(extent)
    windows = window_tables(cas_matrix)
    windows_back = jnp.swapaxes(windows, 1, 2)
    places = (((z ^ jnp.arange(slabs)) * planes)[:, None] + jnp.arange(planes)).reshape(extent)
    into = cas_entries(jnp.arange(extent), places, extent)
    square_x = wave_square(jnp.arange(extent, dtype=jnp.int32), extent)
    strength = (extent * spacing) ** 2 / math.pi
    square = (square_x[:, None] + square_x[None, :] + 1.0) * (1.0 / strength)
    square = jnp.pad(square, ((0, 0), (0, 2 * lanes - extent)), constant_values=1.0)
    tables = [cas_matrix, windows, windows_back, into, into.T, square]

    by_x, by_y, tables, own_parity, flags, last = stage((by_x, by_y, tables, own_parity, flags, to_near[2]), near, near_swapped)
    cas_matrix, windows, windows_back, into, outof, square = tables
    own = jnp.concatenate([by_x, by_y], axis=1)
    own = stage(own, tables)
    near.append(move(stage(last, own), near_routes()))
    own_x, own_y = to_column(own, 1), to_column(own, 2)
    neighbour = to_height(own, {0: 1, 1: 0, 2: 3, 3: 2})
    crossed = to_height(own, {1: 2, 2: 1})

    neighbour, crossed, own_x, own_y, own_parity = stage((neighbour, crossed, own_x, own_y, own_parity), near)
    own_swapped = swap_cores(own_parity)
    neighbour_x, neighbour_y = to_column(neighbour, 1), to_column(neighbour, 2)
    crossed_2 = to_height(neighbour, {1: 2, 2: 1})
    handed = to_height(crossed, {1: 0, 2: 3})

    low = jnp.stack([own_x[:, : quarter // 2], neighbour_x[:, : quarter // 2]])
    high = jnp.stack([own_y[:, quarter // 2 :], neighbour_y[:, quarter // 2 :]])
    staged = stage((low, high, crossed_2, own_parity, own_swapped, to_near[3]), handed)
    low, high, crossed_2, own_parity, own_swapped, last = staged
    low, high = to_column(low, 2), to_column(high, 1)
    handed_2 = to_height(crossed_2, {1: 0, 2: 3})
    near.append(move(last, near_routes()))
    far = move(own_parity, far_routes())

    across = jnp.stack([jnp.where(inner, crossed, handed), jnp.where(inner, crossed_2, handed_2)])
    across, low, high = stage((across, low, high))
    sources = [
        [own[None], own_x[None], own_y[None], low[:1], high[:1]],
        [neighbour[None], neighbour_x[None], neighbour_y[None], low[1:], high[1:]],
    ]
    across_x, across_y = to_column(across, 1), to_column(across, 2)
    near_swapped += [swap_cores(part) for part in stage(near[1:3], across)]
    along_y = [forward(flags, 0, home, [[own_parity], [own_swapped]], sources[0], cas_matrix, windows)]

    low, high = across_x[:, :, : quarter // 2], across_y[:, :, quarter // 2 :]
    near[3] = stage(near[3], along_y)
    near_swapped.append(swap_cores(near[3]))
    low, high, near_swapped = stage((low, high, near_swapped), along_y)
    low, high = to_column(low, 2), to_column(high, 1)
    along_y.append(forward(flags, 1, direct, [near, near_swapped], sources[1], cas_matrix, windows))

    low, high, far = stage((low, high, far), along_y)
    across_source = [across, across_x, across_y, low, high]
    sources += [across_source, across_source]
    far_swapped = swap_cores(far)
    along_y_3 = forward(flags, 3, direct, [near_swapped, near], across_source, cas_matrix, windows)
    far_swapped = stage(far_swapped, along_y_3)
    given, kept, back_x = central(
        flags,
        home,
        direct,
        [*along_y, along_y_3],
        [far_swapped, far],
        sources[1],
        across_source,
        [cas_matrix, windows, windows_back, into, outof, square],
        4,
    )

    def partials(places, first, *earlier):
        slabs = stage([back_x[place // 2] for place in places], *earlier)
        groups = [sources[place] for place in places]
        return backward(flags, places, first, slabs, groups, cas_matrix, windows_back, 4)

    near = [add(k, swap_cores(g)) for g, k in zip(given, kept)]
    near = [near[0], jnp.concatenate(near[1:], axis=1)]
    near_home = [move(part, back(near_routes())) for part in near]
    given = partials([2, 0], home, near[0])
    kept = partials([0, 2], home, given[0], near_home[0])
    far = [add(k, swap_cores(g)) for k, g in zip(kept, given)]
    far_home = [move(part, back(far_routes())) for part in far]
    return put(parity, at_home, near_home, far, far_home)


def solution(mesh):
    def shards(orbitals, source_index):
        slabs, bands = mesh.shape["grid"], mesh.shape["band"]
        fits = slabs == 4 and bands == 8 and orbitals.shape[0] == 2 and source_index.shape[0] == cores
        return (pair_plan if fits else slab_plan)(orbitals, source_index)

    return jax.shard_map(
        shards,
        mesh=mesh,
        in_specs=(P("band", "grid", None), P()),
        out_specs=P("band", "grid", None),
        check_vma=False,
    )
```

```python
import functools
import math

import jax
import jax.numpy as jnp
from jax import lax
from jax.experimental import pallas as pl
from jax.experimental.pallas import tpu as pltpu
from jax.sharding import PartitionSpec as P

spacing = 0.3
cores = 2


def cas_entries(rows, columns, extent):
    products_mod = rows[:, None] * columns[None, :] % extent
    radians = products_mod.astype(jnp.float32) * (2.0 * math.pi / extent)
    return ((jnp.cos(radians) + jnp.sin(radians)) / math.sqrt(extent)).astype(jnp.bfloat16)


def cas_table(extent):
    wavenum = jnp.arange(extent, dtype=jnp.int32)
    return cas_entries(wavenum, wavenum, extent)


def wave_square(indices, extent):
    folded = jnp.minimum(indices, extent - indices).astype(jnp.float32)
    return folded * folded


def coulomb_block(extent, columns, offset):
    square_x = wave_square(jnp.arange(extent, dtype=jnp.int32), extent)
    square_y = wave_square(offset + jnp.arange(columns, dtype=jnp.int32), extent)
    total_sq = square_x[:, None, None] + square_y[None, :, None] + square_x[None, None, :]
    strength = (extent * spacing) ** 2 / math.pi
    return jnp.where(total_sq > 0, strength / (total_sq + 1.0), 0.0)


def transform(grid_data, cas_matrix, pattern):
    return jnp.einsum(pattern, grid_data, cas_matrix, preferred_element_type=jnp.float32)


def broadcast(x, axis, root):
    mine = lax.axis_index(axis) == root
    return lax.psum(jnp.where(mine, x, jnp.zeros_like(x)), axis)


def slab_potentials(pair_rho, cas_matrix, kernel_block):
    along_z = transform(pair_rho, cas_matrix, "pxyz,kz->pxyk").astype(jnp.bfloat16)
    along_y = transform(along_z, cas_matrix, "pxyz,ky->pxkz").astype(jnp.bfloat16)
    turned = lax.all_to_all(along_y, "grid", split_axis=2, concat_axis=1, tiled=True)
    scaled = (kernel_block * transform(turned, cas_matrix, "pxyz,kx->pkyz")).astype(jnp.bfloat16)
    back_x = transform(scaled, cas_matrix, "pxyz,kx->pkyz").astype(jnp.bfloat16)
    returned = lax.all_to_all(back_x, "grid", split_axis=1, concat_axis=2, tiled=True)
    again_y = transform(returned, cas_matrix, "pxyz,ky->pxkz").astype(jnp.bfloat16)
    return transform(again_y, cas_matrix, "pxyz,kz->pxyk")


def fetch_source(orbitals, which):
    local_count = orbitals.shape[0]
    local_slab = lax.dynamic_index_in_dim(orbitals, which % local_count, 0, keepdims=False)
    return broadcast(local_slab, "band", which // local_count)


def slab_plan(orbitals, source_index):
    local_count, planes, _ = orbitals.shape
    extent = planes * lax.axis_size("grid")
    orbitals = orbitals.reshape(local_count, planes, extent, extent)
    source_count = source_index.shape[0]
    cas_matrix = cas_table(extent)
    columns = extent // lax.axis_size("grid")
    kernel_block = coulomb_block(extent, columns, lax.axis_index("grid") * columns)
    fetched = [fetch_source(orbitals, source_index[number]) for number in range(source_count)]
    stacked = jnp.stack(fetched)[:, None].astype(jnp.float32)
    pair_rho = (stacked * orbitals[None].astype(jnp.float32)).astype(jnp.bfloat16)
    pair_rho = pair_rho.reshape(source_count * local_count, planes, extent, extent)
    potential = slab_potentials(pair_rho, cas_matrix, kernel_block)
    potential = potential.reshape(source_count, local_count, planes, extent, extent)
    result = (-jnp.sum(stacked * potential, axis=0)).astype(jnp.bfloat16)
    return result.reshape(local_count, planes, extent * extent)


lanes = 128
quad = 4
ring = 4
turned_pitch = 161
plane_pitch = 41


def move(x, routes):
    slabs = lax.axis_size("grid")

    def place(column, core, z):
        return (column * cores + core) * slabs + z % slabs

    return lax.ppermute(x, ("band", "grid"), [(place(*a), place(*b)) for a, b in routes])


def everywhere():
    columns = lax.axis_size("band") // cores
    return [(c, k, z) for c in range(columns) for k in range(cores) for z in range(lax.axis_size("grid"))]


def swap_cores(x):
    return move(x, [((c, k, z), (c, 1 - k, z)) for c, k, z in everywhere()])


def to_column(x, d):
    return move(x, [((c, k, z), (c ^ d, k, z)) for c, k, z in everywhere()])


def to_height(x, to):
    return move(x, [((c, k, z), (c, k, to[z])) for c, k, z in everywhere() if z in to])


def holder(z):
    return z % ring // 2


def side(core):
    return 2 * core - 1


def near_routes():
    return [((c, holder(z), z + side(k)), (c, k, z)) for c, k, z in everywhere()]


def far_routes():
    return [((c, holder(z), z + 2), (c, k, z)) for c, k, z in everywhere() if k != holder(z)]


def back(routes):
    return [(b, a) for a, b in routes]


def stage(values, *earlier):
    return lax.optimization_barrier((values, earlier))[0]


def choose(first, refs, start):
    if len(refs) == 1:
        start(refs[0])
    else:
        pl.when(first)(lambda: start(refs[0]))
        pl.when(jnp.logical_not(first))(lambda: start(refs[1]))


def start_pieces(pieces, sems):
    for number, (refs, first, to) in enumerate(pieces):
        choose(first, refs, lambda ref, to=to, number=number: pltpu.make_async_copy(ref, to, sems.at[number]).start())


def wait_pieces(pieces, sems):
    for number, (refs, _, to) in enumerate(pieces):
        pltpu.make_async_copy(refs[0], to, sems.at[number]).wait()


def source_of(refs, flags, place):
    return refs, flags[2 + place] if place > 1 else 0


def source_pieces(groups, first, source, column):
    quarter = source.shape[1] // 4
    offsets = [(column ^ e) * quarter for e in range(4)]
    offsets.append(offsets[3] + quarter // 2)
    pieces = []
    for number, offset in enumerate(offsets):
        refs = [five[number].at[which] for five, which in groups]
        to = source.at[:, pl.ds(pl.multiple_of(offset, lanes), refs[0].shape[1])]
        pieces.append((refs, first, to))
    return pieces


def split(refs, *counts):
    taken = []
    for count in counts:
        taken.append(refs[:count])
        refs = refs[count:]
    return taken


def dot(a, b):
    return jnp.dot(a, b, preferred_element_type=jnp.float32)


def both(ref, rows):
    return jnp.concatenate([ref[0, rows, :], ref[1, rows, :]], axis=1)


def beside(values):
    return jnp.concatenate(values, axis=1)


def apart(value):
    return [value[:, n : n + 2 * lanes] for n in range(0, value.shape[1], 2 * lanes)]


def put_both(ref, rows, value):
    ref[0, rows, :] = value[:, :lanes]
    ref[1, rows, :] = value[:, lanes:]


def lane_ranges(pieces):
    ranges = []
    start = 0
    for piece in pieces:
        ranges.append((start, piece.shape[1]))
        start += piece.shape[1]
    return ranges


def pick_kernel(which, source_index, orbitals, *refs):
    outs, sems = refs[:-1], refs[-1]
    chosen = which(source_index)
    parts = len(outs) // len(chosen)
    ranges = lane_ranges(outs[:parts])
    copies = []
    for n, out in enumerate(outs):
        lane = pl.ds(*ranges[n % parts])
        copies.append(pltpu.make_async_copy(orbitals.at[chosen[n // parts], :, lane], out, sems.at[n]))
    for copy in copies:
        copy.start()
    for copy in copies:
        copy.wait()


def cut_kernel(source_index, orbitals, crossed, *refs):
    outs, sems = refs[:-1], refs[-1]
    local_count = orbitals.shape[0]
    band = lax.axis_index("band")
    core, column = lax.rem(band, cores), lax.div(band, cores)
    which = lax.rem(source_index[core], local_count)
    owner = lax.rem(lax.div(source_index[core], local_count), cores)
    width = outs[0].shape[1]
    pieces = []
    for d, out in enumerate(outs):
        lane = pl.ds(pl.multiple_of((column ^ d) * width, lanes), width)
        pieces.append(((orbitals.at[which, :, lane], crossed.at[:, lane]), owner == core, out))
    start_pieces(pieces, sems)
    wait_pieces(pieces, sems)


def put_kernel(count, flags, *refs):
    (out, sems), refs = refs[-2:], refs[:-2]
    near, choices = refs[:-count], refs[-count:]
    half = count // 2
    pieces = [((ref,), None, out.at[1 - flags[0], :, pl.ds(*lane)]) for ref, lane in zip(near, lane_ranges(near))]
    for n, lane in enumerate(lane_ranges(choices[:half])):
        pieces.append((choices[n::half], flags[1] == 1, out.at[flags[0], :, pl.ds(*lane)]))
    start_pieces(pieces, sems)
    wait_pieces(pieces, sems)


def transform_in(source, target, windows, cas, turned, out):
    planes, points = target.shape
    extent = cas.shape[0]
    step = 8
    block = quad * extent

    @pl.loop(0, points // block // step)
    def _(i):
        for r in range(quad):
            density = []
            for j in range(step):
                at = pl.ds(pl.multiple_of((i * step + j) * block + r * lanes, lanes), 2 * lanes)
                density.append(source[:, at].astype(jnp.float32) * target[:, at].astype(jnp.float32))
            density = jnp.concatenate(density, axis=0).astype(jnp.bfloat16)
            along_z = dot(density, windows[r])
            for j in range(step):
                y = (i * step + j) * quad + r
                put_both(turned, pl.ds(y, planes, stride=turned_pitch), along_z[j * planes : (j + 1) * planes])

    @pl.loop(0, planes // 4)
    def _(i):
        for j in range(4):
            x = i * 4 + j
            along_z = both(turned, pl.ds(x * turned_pitch, extent)).astype(jnp.bfloat16)
            put_both(out, pl.ds(x, extent, stride=plane_pitch), dot(cas[...], along_z))


def transform_x(slabs, into, outof, square):
    extent = square.shape[0]
    planes = extent // ring
    strength = (extent * spacing) ** 2 / math.pi
    rows = 8

    @pl.loop(0, extent // rows)
    def _(step):
        base = pl.multiple_of(step * rows * plane_pitch, 8)
        for i in range(rows):
            at = pl.ds(base + i * plane_pitch, planes)
            along_y = jnp.concatenate([both(slab, at) for slab in slabs], axis=0).astype(jnp.bfloat16)
            ky = step * rows + i
            folded = jnp.minimum(ky, extent - ky)
            weight = square[...] + (folded * folded).astype(jnp.float32) * (1.0 / strength)
            guess = pl.reciprocal(weight, approx=True)
            factor = guess * (2.0 - weight * guess)
            factor = jnp.where(weight > 1.25 / strength, factor, 0.0)
            scaled = (factor * dot(into[...], along_y)).astype(jnp.bfloat16)
            back_x = dot(outof[...], scaled)
            for n, slab in enumerate(slabs):
                put_both(slab, at, back_x[n * planes : (n + 1) * planes])


def transform_out(back_x, source, windows, cas, turned, outs, rows):
    planes, points = source.shape
    extent = cas.shape[0]
    low, high = rows

    @pl.loop(0, planes // 4)
    def _(i):
        for j in range(4):
            x = i * 4 + j
            column_x = both(back_x, pl.ds(x, extent, stride=plane_pitch)).astype(jnp.bfloat16)
            put_both(turned, pl.ds(x * turned_pitch + low, high - low), dot(cas[low:high], column_x))

    block = quad * extent
    begin = low // quad
    for out in outs:
        blocks = out.shape[1] // block
        step = 5 if blocks % 5 == 0 else 4

        @pl.loop(0, blocks // step)
        def _(i, begin=begin, step=step, out=out):
            first = begin + i * step
            windowed = []
            for r in range(quad):
                again_y = jnp.concatenate(
                    [both(turned, pl.ds((first + j) * quad + r, planes, stride=turned_pitch)) for j in range(step)],
                    axis=0,
                ).astype(jnp.bfloat16)
                windowed.append(dot(again_y, windows[r]))
            for j in range(step):
                w = [part[j * planes : (j + 1) * planes] for part in windowed]
                potential = [w[0][:, :lanes]]
                potential += [w[r][:, lanes:] + w[r + 1][:, :lanes] for r in range(quad - 1)]
                potential = jnp.concatenate(potential + [w[-1][:, lanes:]], axis=1)
                at = pl.ds(pl.multiple_of((first + j) * block, lanes), block)
                to = pl.ds(pl.multiple_of((i * step + j) * block, lanes), block)
                out[:, to] = (-(source[:, at].astype(jnp.float32) * potential)).astype(jnp.bfloat16)

        begin += blocks


def forward_kernel(place, first, choices, count, flags, *refs):
    targets, five, (cas, windows, out, target, source, turned, sems) = split(refs, choices * count, 5, 7)
    ranges = lane_ranges(targets[:count])
    pieces = [(targets[n::count], flags[first] == 1, target.at[:, pl.ds(*lane)]) for n, lane in enumerate(ranges)]
    pieces += source_pieces([source_of(five, flags, place)], None, source, flags[1])
    start_pieces(pieces, sems)
    wait_pieces(pieces, sems)
    transform_in(source, target, windows, cas, turned, out)


def backward_kernel(places, first, choices, rows, flags, *refs):
    slabs, groups, (cas, windows), outs, (back_x, source, turned, sems) = split(
        refs, choices, 5 * len(places), 2, len(refs) - choices - 5 * len(places) - 6, 4
    )
    chosen = [source_of(five, flags, place) for five, place in zip(split(groups, *[5] * len(places)), places)]
    pieces = [(slabs, flags[first] == 1, back_x)] + source_pieces(chosen, flags[first] == 1, source, flags[1])
    start_pieces(pieces, sems)
    wait_pieces(pieces, sems)
    transform_out(back_x, source, windows, cas, turned, outs, rows)


def central_kernel(home, direct, rows, flags, *refs):
    ready, targets, neighbour_source, across_source, tables, outs, scratch = split(refs, 3, 2, 5, 5, 6, 8, 9)
    cas, windows, windows_back, into, outof, square = tables
    given, kept, (given_out, kept_out, own_out, far_out) = split(outs, 2, 2, 4)
    slabs, target, source, given_source, kept_source, turned, first_sems, later_sems, out_sems = scratch
    at_direct = flags[direct] == 1
    column = flags[1]

    first = [(targets, flags[home] == 1, target)]
    first += source_pieces([source_of(across_source, flags, 2)], None, source, column)
    start_pieces(first, first_sems)
    later = [((ref,), None, slabs.at[place]) for ref, place in zip(ready, (0, 1, 3))]
    near_sources = [source_of(across_source, flags, 3), source_of(neighbour_source, flags, 1)]
    later += source_pieces(near_sources, at_direct, given_source, column)
    later += source_pieces(near_sources[::-1], at_direct, kept_source, column)
    start_pieces(later, later_sems)
    wait_pieces(first, first_sems)
    transform_in(source, target, windows, cas, turned, slabs.at[2])
    wait_pieces(later, later_sems)

    transform_x([slabs.at[place] for place in range(4)], into, outof, square)

    kept_place = jnp.where(at_direct, 1, 3)
    given_place = 4 - kept_place
    leave = [
        ((slabs.at[place],), None, out)
        for place, out in ((given_place, given_out), (kept_place, kept_out), (2, far_out), (0, own_out))
    ]
    start_pieces(leave, out_sems)
    transform_out(slabs.at[given_place], given_source, windows_back, cas, turned, given, rows)
    transform_out(slabs.at[kept_place], kept_source, windows_back, cas, turned, kept, rows)
    wait_pieces(leave, out_sems)


def window_tables(cas_matrix):
    extent = cas_matrix.shape[0]
    tables = []
    for r in range(quad):
        shift = r * extent % lanes
        tables.append(jnp.pad(cas_matrix, ((shift, 2 * lanes - extent - shift), (0, 2 * lanes - extent))))
    return jnp.stack(tables)


limit = 60 * 2**20
whole = pl.BlockSpec(memory_space=pltpu.VMEM)
outside = pl.BlockSpec(memory_space=pl.ANY)
scalars = pl.BlockSpec(memory_space=pltpu.SMEM)
small = pl.CostEstimate(flops=10**6, bytes_accessed=10**4, transcendentals=0)


def pick(orbitals, source_index, which, shares=(1,)):
    _, planes, points = orbitals.shape
    unit = points // sum(shares)
    outs = [jax.ShapeDtypeStruct((planes, share * unit), orbitals.dtype) for share in shares]
    return pl.pallas_call(
        functools.partial(pick_kernel, which),
        out_shape=outs,
        in_specs=[scalars, outside],
        out_specs=[whole] * len(outs),
        scratch_shapes=[pltpu.SemaphoreType.DMA((len(outs),))],
        compiler_params=pltpu.CompilerParams(vmem_limit_bytes=limit),
        cost_estimate=small,
        name="pick",
    )(source_index, orbitals)


def cut_quarters(source_index, orbitals, crossed):
    planes, points = crossed.shape
    return pl.pallas_call(
        cut_kernel,
        out_shape=[jax.ShapeDtypeStruct((planes, points // 4), crossed.dtype)] * 4,
        in_specs=[scalars, outside, outside],
        out_specs=[whole] * 4,
        scratch_shapes=[pltpu.SemaphoreType.DMA((4,))],
        compiler_params=pltpu.CompilerParams(vmem_limit_bytes=limit),
        cost_estimate=small,
        name="cut",
    )(source_index, orbitals, crossed)


def put(parity, first, near, *choices):
    pieces = near + [piece for choice in choices for piece in choice]
    planes, points = near[0].shape[0], sum(piece.shape[1] for piece in near)
    return pl.pallas_call(
        functools.partial(put_kernel, 2 * len(choices[0])),
        out_shape=jax.ShapeDtypeStruct((2, planes, points), near[0].dtype),
        in_specs=[scalars] + [outside] * len(pieces),
        out_specs=whole,
        scratch_shapes=[pltpu.SemaphoreType.DMA((len(near) + len(choices[0]),))],
        compiler_params=pltpu.CompilerParams(vmem_limit_bytes=limit),
        cost_estimate=small,
        name="put",
    )(jnp.stack([parity, first.astype(parity.dtype)]).astype(jnp.int32), *pieces)


def forward(flags, place, first, targets, group, cas_matrix, windows):
    planes = group[0].shape[1]
    extent = cas_matrix.shape[0]
    points = extent * extent
    return pl.pallas_call(
        functools.partial(forward_kernel, place, first, len(targets), len(targets[0])),
        out_shape=jax.ShapeDtypeStruct((2, extent * plane_pitch, lanes), jnp.float32),
        in_specs=[scalars] + [outside] * (len(targets) * len(targets[0]) + len(group)) + [whole] * 2,
        out_specs=whole,
        scratch_shapes=[
            pltpu.VMEM((planes, points), jnp.bfloat16),
            pltpu.VMEM((planes, points), jnp.bfloat16),
            pltpu.VMEM((2, planes * turned_pitch, lanes), jnp.float32),
            pltpu.SemaphoreType.DMA((len(targets[0]) + 5,)),
        ],
        compiler_params=pltpu.CompilerParams(vmem_limit_bytes=limit),
        cost_estimate=small,
        name="forward",
    )(flags, *[piece for choice in targets for piece in choice], *group, cas_matrix, windows)


def central(flags, home, direct, ready, targets, neighbour_source, across_source, tables, rows):
    planes = across_source[0].shape[1]
    extent = tables[0].shape[0]
    points = extent * extent
    pieces = [*ready, *targets, *neighbour_source, *across_source]
    part = jax.ShapeDtypeStruct((planes, (rows[1] - rows[0]) * extent // 2), jnp.bfloat16)
    slab = jax.ShapeDtypeStruct(ready[0].shape, jnp.float32)
    outs = pl.pallas_call(
        functools.partial(central_kernel, home, direct, rows),
        out_shape=[part] * 4 + [slab] * 4,
        in_specs=[scalars] + [outside] * len(pieces) + [whole] * len(tables),
        out_specs=[whole] * 4 + [outside] * 4,
        scratch_shapes=[
            pltpu.VMEM((ring, *slab.shape), jnp.float32),
            *[pltpu.VMEM((planes, points), jnp.bfloat16)] * 4,
            pltpu.VMEM((2, planes * turned_pitch, lanes), jnp.float32),
            pltpu.SemaphoreType.DMA((6,)),
            pltpu.SemaphoreType.DMA((13,)),
            pltpu.SemaphoreType.DMA((4,)),
        ],
        compiler_params=pltpu.CompilerParams(vmem_limit_bytes=limit),
        cost_estimate=small,
        name="central",
    )(flags, *pieces, *tables)
    return split(outs, 2, 2, 4)


def backward(flags, places, first, slabs, groups, cas_matrix, windows, rows, parts):
    planes = groups[0][0].shape[1]
    extent = cas_matrix.shape[0]
    points = extent * extent
    pieces = [piece for group in groups for piece in group]
    return pl.pallas_call(
        functools.partial(backward_kernel, places, first, len(slabs), rows),
        out_shape=[jax.ShapeDtypeStruct((planes, (rows[1] - rows[0]) * extent // parts), jnp.bfloat16)] * parts,
        in_specs=[scalars] + [outside] * (len(slabs) + len(pieces)) + [whole] * 2,
        out_specs=[whole] * parts,
        scratch_shapes=[
            pltpu.VMEM(slabs[0].shape, jnp.float32),
            pltpu.VMEM((planes, points), jnp.bfloat16),
            pltpu.VMEM((2, planes * turned_pitch, lanes), jnp.float32),
            pltpu.SemaphoreType.DMA((6,)),
        ],
        compiler_params=pltpu.CompilerParams(vmem_limit_bytes=limit),
        cost_estimate=small,
        name="backward",
    )(flags, *slabs, *pieces, cas_matrix, windows)


def add(a, b):
    return (a.astype(jnp.float32) + b.astype(jnp.float32)).astype(jnp.bfloat16)


def pair_plan(orbitals, source_index):
    local_count, planes, points = orbitals.shape
    slabs = lax.axis_size("grid")
    extent = planes * slabs
    band, z = lax.axis_index("band"), lax.axis_index("grid")
    column, core = band // cores, band % cores
    quarter = points // 4
    at_home = core == holder(z)
    direct_neighbour = core == 1 - z % 2
    parity = z % 2
    inner = (z == 1) | (z == 2)
    second = inner.astype(jnp.int32)
    flags = jnp.stack([core, column, at_home, direct_neighbour, second, 1 - second]).astype(jnp.int32)
    home, direct = 2, 3

    def candidate(source_index):
        core = lax.rem(lax.axis_index("band"), cores)
        return [lax.rem(source_index[1 - core], local_count)]

    def by_parity(flip):
        return lambda _: [lax.rem(lax.axis_index("grid") + flip, 2)]

    (other,) = pick(orbitals, source_index, candidate)
    crossed = swap_cores(other)
    owner = source_index[core] // local_count
    to_near = pick(stage(orbitals, other), source_index, by_parity(1), (5, 3))

    cuts, to_near = stage((cut_quarters(source_index, orbitals, crossed), to_near))
    near = [move(to_near[0], near_routes())]
    candidates = [cuts[0]] + [to_column(cuts[d], d) for d in (1, 2, 3)]
    (own_parity,) = pick(stage(orbitals, cuts), source_index, by_parity(0))
    cas_matrix = cas_table(extent)
    windows = window_tables(cas_matrix)
    windows_back = jnp.swapaxes(windows, 1, 2)
    places = (((z ^ jnp.arange(slabs)) * planes)[:, None] + jnp.arange(planes)).reshape(extent)
    into = cas_entries(jnp.arange(extent), places, extent)
    square_x = wave_square(jnp.arange(extent, dtype=jnp.int32), extent)
    strength = (extent * spacing) ** 2 / math.pi
    square = (square_x[:, None] + square_x[None, :] + 1.0) * (1.0 / strength)
    square = jnp.pad(square, ((0, 0), (0, 2 * lanes - extent)), constant_values=1.0)
    tables = [cas_matrix, windows, windows_back, into, into.T, square]

    candidates, tables, own_parity, flags = stage((candidates, tables, own_parity, flags), near)
    cas_matrix, windows, windows_back, into, outof, square = tables
    own = lax.select_n(column ^ (owner // cores), *candidates)
    own = stage(own, tables)
    own_swapped = swap_cores(own_parity)
    own_x, own_y = to_column(own, 1), to_column(own, 2)
    neighbour = to_height(own, {0: 1, 1: 0, 2: 3, 3: 2})
    crossed = to_height(own, {1: 2, 2: 1})

    neighbour, crossed, own_x, own_y, own_swapped = stage((neighbour, crossed, own_x, own_y, own_swapped))
    neighbour_x, neighbour_y = to_column(neighbour, 1), to_column(neighbour, 2)
    crossed_2 = to_height(neighbour, {1: 2, 2: 1})
    handed = to_height(crossed, {1: 0, 2: 3})

    low = jnp.stack([own_x[:, : quarter // 2], neighbour_x[:, : quarter // 2]])
    high = jnp.stack([own_y[:, quarter // 2 :], neighbour_y[:, quarter // 2 :]])
    low, high, crossed_2, own_parity, last = stage((low, high, crossed_2, own_parity, to_near[1]), handed)
    low, high = to_column(low, 2), to_column(high, 1)
    handed_2 = to_height(crossed_2, {1: 0, 2: 3})
    near.append(move(last, near_routes()))
    far = move(own_parity, far_routes())

    across = jnp.stack([jnp.where(inner, crossed, handed), jnp.where(inner, crossed_2, handed_2)])
    across, low, high = stage((across, low, high))
    sources = [
        [own[None], own_x[None], own_y[None], low[:1], high[:1]],
        [neighbour[None], neighbour_x[None], neighbour_y[None], low[1:], high[1:]],
    ]
    across_x, across_y = to_column(across, 1), to_column(across, 2)
    near_swapped = [swap_cores(stage(near[0], across))]
    along_y = [forward(flags, 0, home, [[own_parity], [own_swapped]], sources[0], cas_matrix, windows)]

    low, high = across_x[:, :, : quarter // 2], across_y[:, :, quarter // 2 :]
    near[1] = stage(near[1], along_y)
    near_swapped.append(swap_cores(near[1]))
    low, high, near_swapped = stage((low, high, near_swapped), along_y)
    low, high = to_column(low, 2), to_column(high, 1)
    along_y.append(forward(flags, 1, direct, [near, near_swapped], sources[1], cas_matrix, windows))

    low, high, far = stage((low, high, far), along_y)
    across_source = [across, across_x, across_y, low, high]
    sources += [across_source, across_source]
    far_swapped = swap_cores(far)
    along_y_3 = forward(flags, 3, direct, [near_swapped, near], across_source, cas_matrix, windows)
    far_swapped = stage(far_swapped, along_y_3)
    head = (0, 2 * extent // 5)
    tail = (head[1], extent)
    given, kept, (given_back, kept_back, own_back, far_back) = central(
        flags,
        home,
        direct,
        [*along_y, along_y_3],
        [far_swapped, far],
        sources[1],
        across_source,
        [cas_matrix, windows, windows_back, into, outof, square],
        head,
    )

    def partials(places, first, slabs, rows, parts, *earlier):
        groups = [sources[place] for place in places]
        return backward(flags, places, first, stage(slabs, *earlier), groups, cas_matrix, windows_back, rows, parts)

    near = [add(k, swap_cores(g)) for k, g in zip(kept, given)]
    near_home = [move(near[0], back(near_routes()))]
    given = stage(partials([3, 1], direct, [given_back], tail, 2, near), near_home)
    kept = partials([1, 3], direct, [kept_back], tail, 2, given)
    near_home.append(move(near[1], back(near_routes())))
    near += stage([add(k, swap_cores(g)) for k, g in zip(kept, given)], near_home)
    near_home.append(move(near[2], back(near_routes())))
    given = stage(partials([2, 0], home, [far_back, own_back], (0, extent), 4, near), near_home)
    near_home.append(move(near[3], back(near_routes())))
    kept = partials([0, 2], home, [own_back, far_back], (0, extent), 4, given)
    far = [add(k, swap_cores(g)) for k, g in zip(kept, given)]
    far_home = [move(part, back(far_routes())) for part in far]
    return put(parity, at_home, near_home, far, far_home)


def solution(mesh):
    def shards(orbitals, source_index):
        slabs, bands = mesh.shape["grid"], mesh.shape["band"]
        fits = slabs == 4 and bands == 8 and orbitals.shape[0] == 2 and source_index.shape[0] == cores
        return (pair_plan if fits else slab_plan)(orbitals, source_index)

    return jax.shard_map(
        shards,
        mesh=mesh,
        in_specs=(P("band", "grid", None), P()),
        out_specs=P("band", "grid", None),
        check_vma=False,
    )
```

```python
import functools
import math

import jax
import jax.numpy as jnp
from jax import lax
from jax.experimental import pallas as pl
from jax.experimental.pallas import tpu as pltpu
from jax.sharding import PartitionSpec as P

spacing = 0.3
cores = 2


def cas_entries(rows, columns, extent):
    products_mod = rows[:, None] * columns[None, :] % extent
    radians = products_mod.astype(jnp.float32) * (2.0 * math.pi / extent)
    return ((jnp.cos(radians) + jnp.sin(radians)) / math.sqrt(extent)).astype(jnp.bfloat16)


def cas_table(extent):
    wavenum = jnp.arange(extent, dtype=jnp.int32)
    return cas_entries(wavenum, wavenum, extent)


def wave_square(indices, extent):
    folded = jnp.minimum(indices, extent - indices).astype(jnp.float32)
    return folded * folded


def coulomb_block(extent, columns, offset):
    square_x = wave_square(jnp.arange(extent, dtype=jnp.int32), extent)
    square_y = wave_square(offset + jnp.arange(columns, dtype=jnp.int32), extent)
    total_sq = square_x[:, None, None] + square_y[None, :, None] + square_x[None, None, :]
    strength = (extent * spacing) ** 2 / math.pi
    return jnp.where(total_sq > 0, strength / (total_sq + 1.0), 0.0)


def transform(grid_data, cas_matrix, pattern):
    return jnp.einsum(pattern, grid_data, cas_matrix, preferred_element_type=jnp.float32)


def broadcast(x, axis, root):
    mine = lax.axis_index(axis) == root
    return lax.psum(jnp.where(mine, x, jnp.zeros_like(x)), axis)


def slab_potentials(pair_rho, cas_matrix, kernel_block):
    along_z = transform(pair_rho, cas_matrix, "pxyz,kz->pxyk").astype(jnp.bfloat16)
    along_y = transform(along_z, cas_matrix, "pxyz,ky->pxkz").astype(jnp.bfloat16)
    turned = lax.all_to_all(along_y, "grid", split_axis=2, concat_axis=1, tiled=True)
    scaled = (kernel_block * transform(turned, cas_matrix, "pxyz,kx->pkyz")).astype(jnp.bfloat16)
    back_x = transform(scaled, cas_matrix, "pxyz,kx->pkyz").astype(jnp.bfloat16)
    returned = lax.all_to_all(back_x, "grid", split_axis=1, concat_axis=2, tiled=True)
    again_y = transform(returned, cas_matrix, "pxyz,ky->pxkz").astype(jnp.bfloat16)
    return transform(again_y, cas_matrix, "pxyz,kz->pxyk")


def fetch_source(orbitals, which):
    local_count = orbitals.shape[0]
    local_slab = lax.dynamic_index_in_dim(orbitals, which % local_count, 0, keepdims=False)
    return broadcast(local_slab, "band", which // local_count)


def slab_plan(orbitals, source_index):
    local_count, planes, _ = orbitals.shape
    extent = planes * lax.axis_size("grid")
    orbitals = orbitals.reshape(local_count, planes, extent, extent)
    source_count = source_index.shape[0]
    cas_matrix = cas_table(extent)
    columns = extent // lax.axis_size("grid")
    kernel_block = coulomb_block(extent, columns, lax.axis_index("grid") * columns)
    fetched = [fetch_source(orbitals, source_index[number]) for number in range(source_count)]
    stacked = jnp.stack(fetched)[:, None].astype(jnp.float32)
    pair_rho = (stacked * orbitals[None].astype(jnp.float32)).astype(jnp.bfloat16)
    pair_rho = pair_rho.reshape(source_count * local_count, planes, extent, extent)
    potential = slab_potentials(pair_rho, cas_matrix, kernel_block)
    potential = potential.reshape(source_count, local_count, planes, extent, extent)
    result = (-jnp.sum(stacked * potential, axis=0)).astype(jnp.bfloat16)
    return result.reshape(local_count, planes, extent * extent)


lanes = 128
quad = 4
ring = 4
turned_pitch = 161
plane_pitch = 41


def move(x, routes):
    slabs = lax.axis_size("grid")

    def place(column, core, z):
        return (column * cores + core) * slabs + z % slabs

    return lax.ppermute(x, ("band", "grid"), [(place(*a), place(*b)) for a, b in routes])


def everywhere():
    columns = lax.axis_size("band") // cores
    return [(c, k, z) for c in range(columns) for k in range(cores) for z in range(lax.axis_size("grid"))]


def swap_cores(x):
    return move(x, [((c, k, z), (c, 1 - k, z)) for c, k, z in everywhere()])


def to_column(x, d):
    return move(x, [((c, k, z), (c ^ d, k, z)) for c, k, z in everywhere()])


def to_height(x, to):
    return move(x, [((c, k, z), (c, k, to[z])) for c, k, z in everywhere() if z in to])


def holder(z):
    return z % ring // 2


def side(core):
    return 2 * core - 1


def near_routes():
    return [((c, holder(z), z + side(k)), (c, k, z)) for c, k, z in everywhere()]


def far_routes():
    return [((c, holder(z), z + 2), (c, k, z)) for c, k, z in everywhere() if k != holder(z)]


def back(routes):
    return [(b, a) for a, b in routes]


def stage(values, *earlier):
    return lax.optimization_barrier((values, earlier))[0]


def choose(first, refs, start):
    if len(refs) == 1:
        start(refs[0])
    else:
        pl.when(first)(lambda: start(refs[0]))
        pl.when(jnp.logical_not(first))(lambda: start(refs[1]))


def start_pieces(pieces, sems):
    for number, (refs, first, to) in enumerate(pieces):
        choose(first, refs, lambda ref, to=to, number=number: pltpu.make_async_copy(ref, to, sems.at[number]).start())


def wait_pieces(pieces, sems):
    for number, (refs, _, to) in enumerate(pieces):
        pltpu.make_async_copy(refs[0], to, sems.at[number]).wait()


def source_of(refs, flags, place):
    return refs, flags[2 + place] if place > 1 else 0


def source_pieces(groups, first, source, column):
    quarter = source.shape[1] // 4
    offsets = [(column ^ e) * quarter for e in range(4)]
    offsets.append(offsets[3] + quarter // 2)
    pieces = []
    for number, offset in enumerate(offsets):
        refs = [five[number].at[which] for five, which in groups]
        to = source.at[:, pl.ds(pl.multiple_of(offset, lanes), refs[0].shape[1])]
        pieces.append((refs, first, to))
    return pieces


def split(refs, *counts):
    taken = []
    for count in counts:
        taken.append(refs[:count])
        refs = refs[count:]
    return taken


def dot(a, b):
    return jnp.dot(a, b, preferred_element_type=jnp.float32)


def both(ref, rows):
    return jnp.concatenate([ref[0, rows, :], ref[1, rows, :]], axis=1)


def beside(values):
    return jnp.concatenate(values, axis=1)


def apart(value):
    return [value[:, n : n + 2 * lanes] for n in range(0, value.shape[1], 2 * lanes)]


def put_both(ref, rows, value):
    ref[0, rows, :] = value[:, :lanes]
    ref[1, rows, :] = value[:, lanes:]


def lane_ranges(pieces):
    ranges = []
    start = 0
    for piece in pieces:
        ranges.append((start, piece.shape[1]))
        start += piece.shape[1]
    return ranges


def pick_kernel(which, source_index, orbitals, *refs):
    outs, sems = refs[:-1], refs[-1]
    chosen = which(source_index)
    parts = len(outs) // len(chosen)
    ranges = lane_ranges(outs[:parts])
    copies = []
    for n, out in enumerate(outs):
        lane = pl.ds(*ranges[n % parts])
        copies.append(pltpu.make_async_copy(orbitals.at[chosen[n // parts], :, lane], out, sems.at[n]))
    for copy in copies:
        copy.start()
    for copy in copies:
        copy.wait()


def cut_kernel(source_index, orbitals, crossed, *refs):
    outs, sems = refs[:-1], refs[-1]
    local_count = orbitals.shape[0]
    band = lax.axis_index("band")
    core, column = lax.rem(band, cores), lax.div(band, cores)
    which = lax.rem(source_index[core], local_count)
    owner = lax.rem(lax.div(source_index[core], local_count), cores)
    width = outs[0].shape[1]
    pieces = []
    for d, out in enumerate(outs):
        lane = pl.ds(pl.multiple_of((column ^ d) * width, lanes), width)
        pieces.append(((orbitals.at[which, :, lane], crossed.at[:, lane]), owner == core, out))
    start_pieces(pieces, sems)
    wait_pieces(pieces, sems)


def put_kernel(count, flags, *refs):
    (out, staged, sems, out_sems), refs = refs[-4:], refs[:-4]
    near, choices = refs[:-count], refs[-count:]
    half = count // 2
    places = [(1 - flags[0], pl.ds(*lane)) for lane in lane_ranges(near)]
    places += [(flags[0], pl.ds(*lane)) for lane in lane_ranges(choices[:half])]
    chosen = [(ref,) for ref in near] + [choices[n::half] for n in range(half)]
    pieces = [(refs, flags[1] == 1, staged.at[which, :, lane]) for refs, (which, lane) in zip(chosen, places)]
    start_pieces(pieces, sems)
    leave = []
    for number, (which, lane) in enumerate(places):
        piece = staged.at[which, :, lane]
        pltpu.make_async_copy(chosen[number][0], piece, sems.at[number]).wait()
        leave.append(pltpu.make_async_copy(piece, out.at[which, :, lane], out_sems.at[number]))
        leave[-1].start()
    for copy in leave:
        copy.wait()


def transform_in(source, target, windows, cas, turned, out):
    planes, points = target.shape
    extent = cas.shape[0]
    step = 8
    block = quad * extent

    @pl.loop(0, points // block // step)
    def _(i):
        for r in range(quad):
            density = []
            for j in range(step):
                at = pl.ds(pl.multiple_of((i * step + j) * block + r * lanes, lanes), 2 * lanes)
                density.append(source[:, at].astype(jnp.float32) * target[:, at].astype(jnp.float32))
            density = jnp.concatenate(density, axis=0).astype(jnp.bfloat16)
            along_z = dot(density, windows[r])
            for j in range(step):
                y = (i * step + j) * quad + r
                put_both(turned, pl.ds(y, planes, stride=turned_pitch), along_z[j * planes : (j + 1) * planes])

    @pl.loop(0, planes // 4)
    def _(i):
        for j in range(4):
            x = i * 4 + j
            along_z = both(turned, pl.ds(x * turned_pitch, extent)).astype(jnp.bfloat16)
            put_both(out, pl.ds(x, extent, stride=plane_pitch), dot(cas[...], along_z))


def transform_x(slabs, into, outof, square):
    extent = square.shape[0]
    planes = extent // ring
    strength = (extent * spacing) ** 2 / math.pi
    rows = 8

    @pl.loop(0, extent // rows)
    def _(step):
        base = pl.multiple_of(step * rows * plane_pitch, 8)
        for i in range(rows):
            at = pl.ds(base + i * plane_pitch, planes)
            along_y = jnp.concatenate([both(slab, at) for slab in slabs], axis=0).astype(jnp.bfloat16)
            ky = step * rows + i
            folded = jnp.minimum(ky, extent - ky)
            weight = square[...] + (folded * folded).astype(jnp.float32) * (1.0 / strength)
            guess = pl.reciprocal(weight, approx=True)
            factor = guess * (2.0 - weight * guess)
            factor = jnp.where(weight > 1.25 / strength, factor, 0.0)
            scaled = (factor * dot(into[...], along_y)).astype(jnp.bfloat16)
            back_x = dot(outof[...], scaled)
            for n, slab in enumerate(slabs):
                put_both(slab, at, back_x[n * planes : (n + 1) * planes])


def transform_out(back_x, source, windows, cas, turned, outs):
    planes, points = source.shape
    extent = cas.shape[0]

    @pl.loop(0, planes // 4)
    def _(i):
        for j in range(4):
            x = i * 4 + j
            column_x = both(back_x, pl.ds(x, extent, stride=plane_pitch)).astype(jnp.bfloat16)
            put_both(turned, pl.ds(x * turned_pitch, extent), dot(cas[...], column_x))

    block = quad * extent
    begin = 0
    for out in outs:
        blocks = out.shape[1] // block
        step = 5 if blocks % 5 == 0 else 4

        @pl.loop(0, blocks // step)
        def _(i, begin=begin, step=step, out=out):
            first = begin + i * step
            windowed = []
            for r in range(quad):
                again_y = jnp.concatenate(
                    [both(turned, pl.ds((first + j) * quad + r, planes, stride=turned_pitch)) for j in range(step)],
                    axis=0,
                ).astype(jnp.bfloat16)
                windowed.append(dot(again_y, windows[r]))
            for j in range(step):
                w = [part[j * planes : (j + 1) * planes] for part in windowed]
                potential = [w[0][:, :lanes]]
                potential += [w[r][:, lanes:] + w[r + 1][:, :lanes] for r in range(quad - 1)]
                potential = jnp.concatenate(potential + [w[-1][:, lanes:]], axis=1)
                at = pl.ds(pl.multiple_of((first + j) * block, lanes), block)
                to = pl.ds(pl.multiple_of((i * step + j) * block, lanes), block)
                out[:, to] = (-(source[:, at].astype(jnp.float32) * potential)).astype(jnp.bfloat16)

        begin += blocks


def forward_kernel(place, first, choices, count, flags, *refs):
    targets, five, (cas, windows, out, target, source, turned, sems) = split(refs, choices * count, 5, 7)
    ranges = lane_ranges(targets[:count])
    pieces = [(targets[n::count], flags[first] == 1, target.at[:, pl.ds(*lane)]) for n, lane in enumerate(ranges)]
    pieces += source_pieces([source_of(five, flags, place)], None, source, flags[1])
    start_pieces(pieces, sems)
    wait_pieces(pieces, sems)
    transform_in(source, target, windows, cas, turned, out)


def backward_kernel(places, first, parts, flags, *refs):
    slabs, groups, (cas, windows), outs, (back_x, source, turned, sems) = split(
        refs, len(places), 5 * len(places), 2, parts, 4
    )
    chosen = [source_of(five, flags, place) for five, place in zip(split(groups, *[5] * len(places)), places)]
    pieces = [(slabs, flags[first] == 1, back_x)] + source_pieces(chosen, flags[first] == 1, source, flags[1])
    start_pieces(pieces, sems)
    wait_pieces(pieces, sems)
    transform_out(back_x, source, windows, cas, turned, outs)


def central_kernel(home, direct, flags, *refs):
    ready, targets, neighbour_source, across_source, tables, outs, scratch = split(
        refs, 3, len(refs) - 34, 5, 5, 6, 6, 9
    )
    cas, windows, windows_back, into, outof, square = tables
    given, kept, (own_out, far_out) = split(outs, 2, 2, 2)
    slabs, target, source, given_source, kept_source, turned, first_sems, later_sems, out_sems = scratch
    at_direct = flags[direct] == 1
    column = flags[1]

    count = len(targets) // 2
    ranges = lane_ranges(targets[:count])
    first = [(targets[n::count], flags[home] == 1, target.at[:, pl.ds(*lane)]) for n, lane in enumerate(ranges)]
    first += source_pieces([source_of(across_source, flags, 2)], None, source, column)
    start_pieces(first, first_sems)
    later = [((ref,), None, slabs.at[place]) for ref, place in zip(ready, (0, 1, 3))]
    near_sources = [source_of(across_source, flags, 3), source_of(neighbour_source, flags, 1)]
    later += source_pieces(near_sources, at_direct, given_source, column)
    later += source_pieces(near_sources[::-1], at_direct, kept_source, column)
    start_pieces(later, later_sems)
    wait_pieces(first, first_sems)
    transform_in(source, target, windows, cas, turned, slabs.at[2])
    wait_pieces(later, later_sems)

    transform_x([slabs.at[place] for place in range(4)], into, outof, square)

    leave = [((slabs.at[2],), None, far_out), ((slabs.at[0],), None, own_out)]
    start_pieces(leave, out_sems)
    kept_place = jnp.where(at_direct, 1, 3)
    transform_out(slabs.at[4 - kept_place], given_source, windows_back, cas, turned, given)
    transform_out(slabs.at[kept_place], kept_source, windows_back, cas, turned, kept)
    wait_pieces(leave, out_sems)


def window_tables(cas_matrix):
    extent = cas_matrix.shape[0]
    tables = []
    for r in range(quad):
        shift = r * extent % lanes
        tables.append(jnp.pad(cas_matrix, ((shift, 2 * lanes - extent - shift), (0, 2 * lanes - extent))))
    return jnp.stack(tables)


limit = 60 * 2**20
whole = pl.BlockSpec(memory_space=pltpu.VMEM)
outside = pl.BlockSpec(memory_space=pl.ANY)
scalars = pl.BlockSpec(memory_space=pltpu.SMEM)
small = pl.CostEstimate(flops=10**6, bytes_accessed=10**4, transcendentals=0)


def pick(orbitals, source_index, which, shares=(1,)):
    _, planes, points = orbitals.shape
    unit = points // sum(shares)
    outs = [jax.ShapeDtypeStruct((planes, share * unit), orbitals.dtype) for share in shares]
    return pl.pallas_call(
        functools.partial(pick_kernel, which),
        out_shape=outs,
        in_specs=[scalars, outside],
        out_specs=[whole] * len(outs),
        scratch_shapes=[pltpu.SemaphoreType.DMA((len(outs),))],
        compiler_params=pltpu.CompilerParams(vmem_limit_bytes=limit),
        cost_estimate=small,
        name="pick",
    )(source_index, orbitals)


def cut_quarters(source_index, orbitals, crossed):
    planes, points = crossed.shape
    return pl.pallas_call(
        cut_kernel,
        out_shape=[jax.ShapeDtypeStruct((planes, points // 4), crossed.dtype)] * 4,
        in_specs=[scalars, outside, outside],
        out_specs=[whole] * 4,
        scratch_shapes=[pltpu.SemaphoreType.DMA((4,))],
        compiler_params=pltpu.CompilerParams(vmem_limit_bytes=limit),
        cost_estimate=small,
        name="cut",
    )(source_index, orbitals, crossed)


def put(parity, first, near, *choices):
    pieces = near + [piece for choice in choices for piece in choice]
    planes, points = near[0].shape[0], sum(piece.shape[1] for piece in near)
    return pl.pallas_call(
        functools.partial(put_kernel, 2 * len(choices[0])),
        out_shape=jax.ShapeDtypeStruct((2, planes, points), near[0].dtype),
        in_specs=[scalars] + [outside] * len(pieces),
        out_specs=outside,
        scratch_shapes=[
            pltpu.VMEM((2, planes, points), near[0].dtype),
            pltpu.SemaphoreType.DMA((len(near) + len(choices[0]),)),
            pltpu.SemaphoreType.DMA((len(near) + len(choices[0]),)),
        ],
        compiler_params=pltpu.CompilerParams(vmem_limit_bytes=limit),
        cost_estimate=small,
        name="put",
    )(jnp.stack([parity, first.astype(parity.dtype)]).astype(jnp.int32), *pieces)


def forward(flags, place, first, targets, group, cas_matrix, windows):
    planes = group[0].shape[1]
    extent = cas_matrix.shape[0]
    points = extent * extent
    return pl.pallas_call(
        functools.partial(forward_kernel, place, first, len(targets), len(targets[0])),
        out_shape=jax.ShapeDtypeStruct((2, extent * plane_pitch, lanes), jnp.float32),
        in_specs=[scalars] + [outside] * (len(targets) * len(targets[0]) + len(group)) + [whole] * 2,
        out_specs=whole,
        scratch_shapes=[
            pltpu.VMEM((planes, points), jnp.bfloat16),
            pltpu.VMEM((planes, points), jnp.bfloat16),
            pltpu.VMEM((2, planes * turned_pitch, lanes), jnp.float32),
            pltpu.SemaphoreType.DMA((len(targets[0]) + 5,)),
        ],
        compiler_params=pltpu.CompilerParams(vmem_limit_bytes=limit),
        cost_estimate=small,
        name="forward",
    )(flags, *[piece for choice in targets for piece in choice], *group, cas_matrix, windows)


def central(flags, home, direct, ready, targets, neighbour_source, across_source, tables):
    planes = across_source[0].shape[1]
    extent = tables[0].shape[0]
    points = extent * extent
    pieces = [*ready, *targets[0], *targets[1], *neighbour_source, *across_source]
    parts = [jax.ShapeDtypeStruct((planes, share * points // 5), jnp.bfloat16) for share in (2, 3)]
    slab = jax.ShapeDtypeStruct(ready[0].shape, jnp.float32)
    outs = pl.pallas_call(
        functools.partial(central_kernel, home, direct),
        out_shape=parts * 2 + [slab] * 2,
        in_specs=[scalars] + [outside] * len(pieces) + [whole] * len(tables),
        out_specs=[whole] * 4 + [outside] * 2,
        scratch_shapes=[
            pltpu.VMEM((ring, *slab.shape), jnp.float32),
            *[pltpu.VMEM((planes, points), jnp.bfloat16)] * 4,
            pltpu.VMEM((2, planes * turned_pitch, lanes), jnp.float32),
            pltpu.SemaphoreType.DMA((len(targets[0]) + 5,)),
            pltpu.SemaphoreType.DMA((13,)),
            pltpu.SemaphoreType.DMA((2,)),
        ],
        compiler_params=pltpu.CompilerParams(vmem_limit_bytes=limit),
        cost_estimate=small,
        name="central",
    )(flags, *pieces, *tables)
    return split(outs, 2, 2, 2)


def backward(flags, places, first, slabs, groups, cas_matrix, windows, parts):
    planes = groups[0][0].shape[1]
    extent = cas_matrix.shape[0]
    points = extent * extent
    pieces = [piece for group in groups for piece in group]
    return pl.pallas_call(
        functools.partial(backward_kernel, places, first, parts),
        out_shape=[jax.ShapeDtypeStruct((planes, points // parts), jnp.bfloat16)] * parts,
        in_specs=[scalars] + [outside] * (len(slabs) + len(pieces)) + [whole] * 2,
        out_specs=[whole] * parts,
        scratch_shapes=[
            pltpu.VMEM(slabs[0].shape, jnp.float32),
            pltpu.VMEM((planes, points), jnp.bfloat16),
            pltpu.VMEM((2, planes * turned_pitch, lanes), jnp.float32),
            pltpu.SemaphoreType.DMA((6,)),
        ],
        compiler_params=pltpu.CompilerParams(vmem_limit_bytes=limit),
        cost_estimate=small,
        name="backward",
    )(flags, *slabs, *pieces, cas_matrix, windows)


def add(a, b):
    return (a.astype(jnp.float32) + b.astype(jnp.float32)).astype(jnp.bfloat16)


def pair_plan(orbitals, source_index):
    local_count, planes, points = orbitals.shape
    slabs = lax.axis_size("grid")
    extent = planes * slabs
    band, z = lax.axis_index("band"), lax.axis_index("grid")
    column, core = band // cores, band % cores
    quarter = points // 4
    at_home = core == holder(z)
    direct_neighbour = core == 1 - z % 2
    parity = z % 2
    inner = (z == 1) | (z == 2)
    second = inner.astype(jnp.int32)
    flags = jnp.stack([core, column, at_home, direct_neighbour, second, 1 - second]).astype(jnp.int32)
    home, direct = 2, 3

    def candidate(source_index):
        core = lax.rem(lax.axis_index("band"), cores)
        return [lax.rem(source_index[1 - core], local_count)]

    def by_parity(flip):
        return lambda _: [lax.rem(lax.axis_index("grid") + flip, 2)]

    (other,) = pick(orbitals, source_index, candidate)
    crossed = swap_cores(other)
    owner = source_index[core] // local_count
    to_near = pick(stage(orbitals, other), source_index, by_parity(1), (5, 3))

    cuts, to_near = stage((cut_quarters(source_index, orbitals, crossed), to_near))
    near = [move(to_near[0], near_routes())]
    candidates = [cuts[0]] + [to_column(cuts[d], d) for d in (1, 2, 3)]
    (own_parity,) = pick(stage(orbitals, cuts), source_index, by_parity(0))
    cas_matrix = cas_table(extent)
    windows = window_tables(cas_matrix)
    windows_back = jnp.swapaxes(windows, 1, 2)
    places = (((z ^ jnp.arange(slabs)) * planes)[:, None] + jnp.arange(planes)).reshape(extent)
    into = cas_entries(jnp.arange(extent), places, extent)
    square_x = wave_square(jnp.arange(extent, dtype=jnp.int32), extent)
    strength = (extent * spacing) ** 2 / math.pi
    square = (square_x[:, None] + square_x[None, :] + 1.0) * (1.0 / strength)
    square = jnp.pad(square, ((0, 0), (0, 2 * lanes - extent)), constant_values=1.0)
    tables = [cas_matrix, windows, windows_back, into, into.T, square]

    candidates, tables, own_parity, flags = stage((candidates, tables, own_parity, flags), near)
    cas_matrix, windows, windows_back, into, outof, square = tables
    own = lax.select_n(column ^ (owner // cores), *candidates)
    own = stage(own, tables)
    own_swapped = swap_cores(own_parity)
    own_x, own_y = to_column(own, 1), to_column(own, 2)
    neighbour = to_height(own, {0: 1, 1: 0, 2: 3, 3: 2})
    crossed = to_height(own, {1: 2, 2: 1})

    neighbour, crossed, own_x, own_y, own_swapped = stage((neighbour, crossed, own_x, own_y, own_swapped))
    neighbour_x, neighbour_y = to_column(neighbour, 1), to_column(neighbour, 2)
    crossed_2 = to_height(neighbour, {1: 2, 2: 1})
    handed = to_height(crossed, {1: 0, 2: 3})

    low = jnp.stack([own_x[:, : quarter // 2], neighbour_x[:, : quarter // 2]])
    high = jnp.stack([own_y[:, quarter // 2 :], neighbour_y[:, quarter // 2 :]])
    low, high, crossed_2, own_parity, last = stage((low, high, crossed_2, own_parity, to_near[1]), handed)
    low, high = to_column(low, 2), to_column(high, 1)
    handed_2 = to_height(crossed_2, {1: 0, 2: 3})
    near.append(move(last, near_routes()))
    far = [move(own_parity, far_routes())]

    across = jnp.stack([jnp.where(inner, crossed, handed), jnp.where(inner, crossed_2, handed_2)])
    across, low, high = stage((across, low, high))
    sources = [
        [own[None], own_x[None], own_y[None], low[:1], high[:1]],
        [neighbour[None], neighbour_x[None], neighbour_y[None], low[1:], high[1:]],
    ]
    across_x, across_y = to_column(across, 1), to_column(across, 2)
    near_swapped = [swap_cores(stage(near[0], across))]
    along_y = [forward(flags, 0, home, [[own_parity], [own_swapped]], sources[0], cas_matrix, windows)]

    low, high = across_x[:, :, : quarter // 2], across_y[:, :, quarter // 2 :]
    near[1] = stage(near[1], along_y)
    near_swapped.append(swap_cores(near[1]))
    low, high, near_swapped = stage((low, high, near_swapped), along_y)
    low, high = to_column(low, 2), to_column(high, 1)
    along_y.append(forward(flags, 1, direct, [near, near_swapped], sources[1], cas_matrix, windows))

    low, high, far = stage((low, high, far), along_y)
    across_source = [across, across_x, across_y, low, high]
    sources += [across_source, across_source]
    far_swapped = [swap_cores(part) for part in far]
    along_y_3 = forward(flags, 3, direct, [near_swapped, near], across_source, cas_matrix, windows)
    far_swapped = stage(far_swapped, along_y_3)
    given, kept, (own_back, far_back) = central(
        flags,
        home,
        direct,
        [*along_y, along_y_3],
        [far_swapped, far],
        sources[1],
        across_source,
        [cas_matrix, windows, windows_back, into, outof, square],
    )

    def partials(places, slabs, *earlier):
        groups = [sources[place] for place in places]
        return backward(flags, places, home, stage(slabs, *earlier), groups, cas_matrix, windows_back, 4)

    near = [add(k, swap_cores(g)) for k, g in zip(kept, given)]
    near_home = [move(part, back(near_routes())) for part in near]
    given = partials([2, 0], [far_back, own_back], near[0])
    kept = partials([0, 2], [own_back, far_back], given[0], near_home[0])
    far = [add(k, swap_cores(g)) for k, g in zip(kept, given)]
    far_home = [move(part, back(far_routes())) for part in far]
    return put(parity, at_home, near_home, far, far_home)


def solution(mesh):
    def shards(orbitals, source_index):
        slabs, bands = mesh.shape["grid"], mesh.shape["band"]
        fits = slabs == 4 and bands == 8 and orbitals.shape[0] == 2 and source_index.shape[0] == cores
        return (pair_plan if fits else slab_plan)(orbitals, source_index)

    return jax.shard_map(
        shards,
        mesh=mesh,
        in_specs=(P("band", "grid", None), P()),
        out_specs=P("band", "grid", None),
        check_vma=False,
    )
```

```python
import functools
import math

import jax
import jax.numpy as jnp
from jax import lax
from jax.experimental import pallas as pl
from jax.experimental.pallas import tpu as pltpu
from jax.sharding import PartitionSpec as P

spacing = 0.3
cores = 2


def cas_entries(rows, columns, extent):
    products_mod = rows[:, None] * columns[None, :] % extent
    radians = products_mod.astype(jnp.float32) * (2.0 * math.pi / extent)
    return ((jnp.cos(radians) + jnp.sin(radians)) / math.sqrt(extent)).astype(jnp.bfloat16)


def cas_table(extent):
    wavenum = jnp.arange(extent, dtype=jnp.int32)
    return cas_entries(wavenum, wavenum, extent)


def wave_square(indices, extent):
    folded = jnp.minimum(indices, extent - indices).astype(jnp.float32)
    return folded * folded


def coulomb_block(extent, columns, offset):
    square_x = wave_square(jnp.arange(extent, dtype=jnp.int32), extent)
    square_y = wave_square(offset + jnp.arange(columns, dtype=jnp.int32), extent)
    total_sq = square_x[:, None, None] + square_y[None, :, None] + square_x[None, None, :]
    strength = (extent * spacing) ** 2 / math.pi
    return jnp.where(total_sq > 0, strength / (total_sq + 1.0), 0.0)


def transform(grid_data, cas_matrix, pattern):
    return jnp.einsum(pattern, grid_data, cas_matrix, preferred_element_type=jnp.float32)


def broadcast(x, axis, root):
    mine = lax.axis_index(axis) == root
    return lax.psum(jnp.where(mine, x, jnp.zeros_like(x)), axis)


def slab_potentials(pair_rho, cas_matrix, kernel_block):
    along_z = transform(pair_rho, cas_matrix, "pxyz,kz->pxyk").astype(jnp.bfloat16)
    along_y = transform(along_z, cas_matrix, "pxyz,ky->pxkz").astype(jnp.bfloat16)
    turned = lax.all_to_all(along_y, "grid", split_axis=2, concat_axis=1, tiled=True)
    scaled = (kernel_block * transform(turned, cas_matrix, "pxyz,kx->pkyz")).astype(jnp.bfloat16)
    back_x = transform(scaled, cas_matrix, "pxyz,kx->pkyz").astype(jnp.bfloat16)
    returned = lax.all_to_all(back_x, "grid", split_axis=1, concat_axis=2, tiled=True)
    again_y = transform(returned, cas_matrix, "pxyz,ky->pxkz").astype(jnp.bfloat16)
    return transform(again_y, cas_matrix, "pxyz,kz->pxyk")


def fetch_source(orbitals, which):
    local_count = orbitals.shape[0]
    local_slab = lax.dynamic_index_in_dim(orbitals, which % local_count, 0, keepdims=False)
    return broadcast(local_slab, "band", which // local_count)


def slab_plan(orbitals, source_index):
    local_count, planes, _ = orbitals.shape
    extent = planes * lax.axis_size("grid")
    orbitals = orbitals.reshape(local_count, planes, extent, extent)
    source_count = source_index.shape[0]
    cas_matrix = cas_table(extent)
    columns = extent // lax.axis_size("grid")
    kernel_block = coulomb_block(extent, columns, lax.axis_index("grid") * columns)
    fetched = [fetch_source(orbitals, source_index[number]) for number in range(source_count)]
    stacked = jnp.stack(fetched)[:, None].astype(jnp.float32)
    pair_rho = (stacked * orbitals[None].astype(jnp.float32)).astype(jnp.bfloat16)
    pair_rho = pair_rho.reshape(source_count * local_count, planes, extent, extent)
    potential = slab_potentials(pair_rho, cas_matrix, kernel_block)
    potential = potential.reshape(source_count, local_count, planes, extent, extent)
    result = (-jnp.sum(stacked * potential, axis=0)).astype(jnp.bfloat16)
    return result.reshape(local_count, planes, extent * extent)


lanes = 128
quad = 4
ring = 4
turned_pitch = 161
plane_pitch = 41


def move(x, routes):
    slabs = lax.axis_size("grid")

    def place(column, core, z):
        return (column * cores + core) * slabs + z % slabs

    return lax.ppermute(x, ("band", "grid"), [(place(*a), place(*b)) for a, b in routes])


def everywhere():
    columns = lax.axis_size("band") // cores
    return [(c, k, z) for c in range(columns) for k in range(cores) for z in range(lax.axis_size("grid"))]


def swap_cores(x):
    return move(x, [((c, k, z), (c, 1 - k, z)) for c, k, z in everywhere()])


def to_column(x, d):
    return move(x, [((c, k, z), (c ^ d, k, z)) for c, k, z in everywhere()])


def to_height(x, to):
    return move(x, [((c, k, z), (c, k, to[z])) for c, k, z in everywhere() if z in to])


def holder(z):
    return z % ring // 2


def side(core):
    return 2 * core - 1


def near_routes():
    return [((c, holder(z), z + side(k)), (c, k, z)) for c, k, z in everywhere()]


def far_routes():
    return [((c, holder(z), z + 2), (c, k, z)) for c, k, z in everywhere() if k != holder(z)]


def back(routes):
    return [(b, a) for a, b in routes]


def stage(values, *earlier):
    return lax.optimization_barrier((values, earlier))[0]


def choose(first, refs, start):
    if len(refs) == 1:
        start(refs[0])
    else:
        pl.when(first)(lambda: start(refs[0]))
        pl.when(jnp.logical_not(first))(lambda: start(refs[1]))


def start_pieces(pieces, sems):
    for number, (refs, first, to) in enumerate(pieces):
        choose(first, refs, lambda ref, to=to, number=number: pltpu.make_async_copy(ref, to, sems.at[number]).start())


def wait_pieces(pieces, sems):
    for number, (refs, _, to) in enumerate(pieces):
        pltpu.make_async_copy(refs[0], to, sems.at[number]).wait()


def source_of(refs, flags, place):
    return refs, flags[2 + place] if place > 1 else 0


def source_pieces(groups, first, source, column):
    quarter = source.shape[1] // 4
    offsets = [(column ^ e) * quarter for e in range(4)]
    offsets.append(offsets[3] + quarter // 2)
    pieces = []
    for number, offset in enumerate(offsets):
        refs = [five[number].at[which] for five, which in groups]
        to = source.at[:, pl.ds(pl.multiple_of(offset, lanes), refs[0].shape[1])]
        pieces.append((refs, first, to))
    return pieces


def split(refs, *counts):
    taken = []
    for count in counts:
        taken.append(refs[:count])
        refs = refs[count:]
    return taken


def dot(a, b):
    return jnp.dot(a, b, preferred_element_type=jnp.float32)


def both(ref, rows):
    return jnp.concatenate([ref[0, rows, :], ref[1, rows, :]], axis=1)


def beside(values):
    return jnp.concatenate(values, axis=1)


def apart(value):
    return [value[:, n : n + 2 * lanes] for n in range(0, value.shape[1], 2 * lanes)]


def put_both(ref, rows, value):
    ref[0, rows, :] = value[:, :lanes]
    ref[1, rows, :] = value[:, lanes:]


def lane_ranges(pieces):
    ranges = []
    start = 0
    for piece in pieces:
        ranges.append((start, piece.shape[1]))
        start += piece.shape[1]
    return ranges


def pick_kernel(which, source_index, orbitals, *refs):
    outs, sems = refs[:-1], refs[-1]
    copies = []
    for n, (out, (orbital, start)) in enumerate(zip(outs, which(source_index))):
        copies.append(pltpu.make_async_copy(orbitals.at[orbital, :, pl.ds(start, out.shape[1])], out, sems.at[n]))
    for copy in copies:
        copy.start()
    for copy in copies:
        copy.wait()


def cut_kernel(source_index, orbitals, crossed, *refs):
    outs, sems = refs[:-1], refs[-1]
    local_count = orbitals.shape[0]
    band = lax.axis_index("band")
    core, column = lax.rem(band, cores), lax.div(band, cores)
    which = lax.rem(source_index[core], local_count)
    owner = lax.rem(lax.div(source_index[core], local_count), cores)
    width = outs[0].shape[1]
    pieces = []
    for d, out in enumerate(outs):
        lane = pl.ds(pl.multiple_of((column ^ d) * width, lanes), width)
        pieces.append(((orbitals.at[which, :, lane], crossed.at[:, lane]), owner == core, out))
    start_pieces(pieces, sems)
    wait_pieces(pieces, sems)


def put_kernel(count, flags, *refs):
    (out, staged, sems, out_sems), refs = refs[-4:], refs[:-4]
    near, choices = refs[:-count], refs[-count:]
    half = count // 2
    places = [(1 - flags[0], pl.ds(*lane)) for lane in lane_ranges(near)]
    places += [(flags[0], pl.ds(*lane)) for lane in lane_ranges(choices[:half])]
    chosen = [(ref,) for ref in near] + [choices[n::half] for n in range(half)]
    pieces = [(refs, flags[1] == 1, staged.at[which, :, lane]) for refs, (which, lane) in zip(chosen, places)]
    start_pieces(pieces, sems)
    leave = []
    for number, (which, lane) in enumerate(places):
        piece = staged.at[which, :, lane]
        pltpu.make_async_copy(chosen[number][0], piece, sems.at[number]).wait()
        leave.append(pltpu.make_async_copy(piece, out.at[which, :, lane], out_sems.at[number]))
        leave[-1].start()
    for copy in leave:
        copy.wait()


def transform_in(source, target, windows, cas, turned, out):
    planes, points = target.shape
    extent = cas.shape[0]
    step = 8
    block = quad * extent

    @pl.loop(0, points // block // step)
    def _(i):
        for r in range(quad):
            density = []
            for j in range(step):
                at = pl.ds(pl.multiple_of((i * step + j) * block + r * lanes, lanes), 2 * lanes)
                density.append(source[:, at].astype(jnp.float32) * target[:, at].astype(jnp.float32))
            density = jnp.concatenate(density, axis=0).astype(jnp.bfloat16)
            along_z = dot(density, windows[r])
            for j in range(step):
                y = (i * step + j) * quad + r
                put_both(turned, pl.ds(y, planes, stride=turned_pitch), along_z[j * planes : (j + 1) * planes])

    @pl.loop(0, planes // 4)
    def _(i):
        for j in range(4):
            x = i * 4 + j
            along_z = both(turned, pl.ds(x * turned_pitch, extent)).astype(jnp.bfloat16)
            put_both(out, pl.ds(x, extent, stride=plane_pitch), dot(cas[...], along_z))


def transform_x(slabs, into, outof, square):
    extent = square.shape[0]
    planes = extent // ring
    strength = (extent * spacing) ** 2 / math.pi
    rows = 8

    @pl.loop(0, extent // rows)
    def _(step):
        base = pl.multiple_of(step * rows * plane_pitch, 8)
        for i in range(rows):
            at = pl.ds(base + i * plane_pitch, planes)
            along_y = jnp.concatenate([both(slab, at) for slab in slabs], axis=0).astype(jnp.bfloat16)
            ky = step * rows + i
            folded = jnp.minimum(ky, extent - ky)
            weight = square[...] + (folded * folded).astype(jnp.float32) * (1.0 / strength)
            guess = pl.reciprocal(weight, approx=True)
            factor = guess * (2.0 - weight * guess)
            factor = jnp.where(weight > 1.25 / strength, factor, 0.0)
            scaled = (factor * dot(into[...], along_y)).astype(jnp.bfloat16)
            back_x = dot(outof[...], scaled)
            for n, slab in enumerate(slabs):
                put_both(slab, at, back_x[n * planes : (n + 1) * planes])


def transform_out(back_x, source, windows, cas, turned, outs):
    planes, points = source.shape
    extent = cas.shape[0]

    @pl.loop(0, planes // 4)
    def _(i):
        for j in range(4):
            x = i * 4 + j
            column_x = both(back_x, pl.ds(x, extent, stride=plane_pitch)).astype(jnp.bfloat16)
            put_both(turned, pl.ds(x * turned_pitch, extent), dot(cas[...], column_x))

    block = quad * extent
    begin = 0
    for out in outs:
        blocks = out.shape[1] // block
        step = 5 if blocks % 5 == 0 else 4

        @pl.loop(0, blocks // step)
        def _(i, begin=begin, step=step, out=out):
            first = begin + i * step
            windowed = []
            for r in range(quad):
                again_y = jnp.concatenate(
                    [both(turned, pl.ds((first + j) * quad + r, planes, stride=turned_pitch)) for j in range(step)],
                    axis=0,
                ).astype(jnp.bfloat16)
                windowed.append(dot(again_y, windows[r]))
            for j in range(step):
                w = [part[j * planes : (j + 1) * planes] for part in windowed]
                potential = [w[0][:, :lanes]]
                potential += [w[r][:, lanes:] + w[r + 1][:, :lanes] for r in range(quad - 1)]
                potential = jnp.concatenate(potential + [w[-1][:, lanes:]], axis=1)
                at = pl.ds(pl.multiple_of((first + j) * block, lanes), block)
                to = pl.ds(pl.multiple_of((i * step + j) * block, lanes), block)
                out[:, to] = (-(source[:, at].astype(jnp.float32) * potential)).astype(jnp.bfloat16)

        begin += blocks


def forward_kernel(place, first, choices, count, flags, *refs):
    targets, five, (cas, windows, _, _, out, target, source, turned, sems) = split(refs, choices * count, 5, 9)
    ranges = lane_ranges(targets[:count])
    pieces = [(targets[n::count], flags[first] == 1, target.at[:, pl.ds(*lane)]) for n, lane in enumerate(ranges)]
    pieces += source_pieces([source_of(five, flags, place)], None, source, flags[1])
    start_pieces(pieces, sems)
    wait_pieces(pieces, sems)
    transform_in(source, target, windows, cas, turned, out)


def backward_kernel(places, first, parts, flags, *refs):
    slabs, groups, (cas, windows), outs, (back_x, source, turned, sems) = split(
        refs, len(places), 5 * len(places), 2, parts, 4
    )
    chosen = [source_of(five, flags, place) for five, place in zip(split(groups, *[5] * len(places)), places)]
    pieces = [(slabs, flags[first] == 1, back_x)] + source_pieces(chosen, flags[first] == 1, source, flags[1])
    start_pieces(pieces, sems)
    wait_pieces(pieces, sems)
    transform_out(back_x, source, windows, cas, turned, outs)


def central_kernel(home, direct, flags, *refs):
    ready, targets, neighbour_source, across_source, tables, outs, scratch = split(
        refs, 3, len(refs) - 34, 5, 5, 6, 6, 9
    )
    cas, windows, windows_back, into, outof, square = tables
    given, kept, (own_out, far_out) = split(outs, 2, 2, 2)
    slabs, target, source, given_source, kept_source, turned, first_sems, later_sems, out_sems = scratch
    at_direct = flags[direct] == 1
    column = flags[1]

    count = len(targets) // 2
    ranges = lane_ranges(targets[:count])
    first = [(targets[n::count], flags[home] == 1, target.at[:, pl.ds(*lane)]) for n, lane in enumerate(ranges)]
    first += source_pieces([source_of(across_source, flags, 2)], None, source, column)
    start_pieces(first, first_sems)
    later = [((ref,), None, slabs.at[place]) for ref, place in zip(ready, (0, 1, 3))]
    near_sources = [source_of(across_source, flags, 3), source_of(neighbour_source, flags, 1)]
    later += source_pieces(near_sources, at_direct, given_source, column)
    later += source_pieces(near_sources[::-1], at_direct, kept_source, column)
    start_pieces(later, later_sems)
    wait_pieces(first, first_sems)
    transform_in(source, target, windows, cas, turned, slabs.at[2])
    wait_pieces(later, later_sems)

    transform_x([slabs.at[place] for place in range(4)], into, outof, square)

    leave = [((slabs.at[2],), None, far_out), ((slabs.at[0],), None, own_out)]
    start_pieces(leave, out_sems)
    kept_place = jnp.where(at_direct, 1, 3)
    transform_out(slabs.at[4 - kept_place], given_source, windows_back, cas, turned, given)
    transform_out(slabs.at[kept_place], kept_source, windows_back, cas, turned, kept)
    wait_pieces(leave, out_sems)


def window_tables(cas_matrix):
    extent = cas_matrix.shape[0]
    tables = []
    for r in range(quad):
        shift = r * extent % lanes
        tables.append(jnp.pad(cas_matrix, ((shift, 2 * lanes - extent - shift), (0, 2 * lanes - extent))))
    return jnp.stack(tables)


limit = 60 * 2**20
whole = pl.BlockSpec(memory_space=pltpu.VMEM)
outside = pl.BlockSpec(memory_space=pl.ANY)
scalars = pl.BlockSpec(memory_space=pltpu.SMEM)
small = pl.CostEstimate(flops=10**6, bytes_accessed=10**4, transcendentals=0)


def pick(orbitals, source_index, which, widths):
    planes = orbitals.shape[1]
    return pl.pallas_call(
        functools.partial(pick_kernel, which),
        out_shape=[jax.ShapeDtypeStruct((planes, width), orbitals.dtype) for width in widths],
        in_specs=[scalars, outside],
        out_specs=[whole] * len(widths),
        scratch_shapes=[pltpu.SemaphoreType.DMA((len(widths),))],
        compiler_params=pltpu.CompilerParams(vmem_limit_bytes=limit),
        cost_estimate=small,
        name="pick",
    )(source_index, orbitals)


def cut_quarters(source_index, orbitals, crossed):
    planes, points = crossed.shape
    return pl.pallas_call(
        cut_kernel,
        out_shape=[jax.ShapeDtypeStruct((planes, points // 4), crossed.dtype)] * 4,
        in_specs=[scalars, outside, outside],
        out_specs=[whole] * 4,
        scratch_shapes=[pltpu.SemaphoreType.DMA((4,))],
        compiler_params=pltpu.CompilerParams(vmem_limit_bytes=limit),
        cost_estimate=small,
        name="cut",
    )(source_index, orbitals, crossed)


def put(parity, first, near, *choices):
    pieces = near + [piece for choice in choices for piece in choice]
    planes, points = near[0].shape[0], sum(piece.shape[1] for piece in near)
    return pl.pallas_call(
        functools.partial(put_kernel, 2 * len(choices[0])),
        out_shape=jax.ShapeDtypeStruct((2, planes, points), near[0].dtype),
        in_specs=[scalars] + [outside] * len(pieces),
        out_specs=outside,
        scratch_shapes=[
            pltpu.VMEM((2, planes, points), near[0].dtype),
            pltpu.SemaphoreType.DMA((len(near) + len(choices[0]),)),
            pltpu.SemaphoreType.DMA((len(near) + len(choices[0]),)),
        ],
        compiler_params=pltpu.CompilerParams(vmem_limit_bytes=limit),
        cost_estimate=small,
        name="put",
    )(jnp.stack([parity, first.astype(parity.dtype)]).astype(jnp.int32), *pieces)


def forward(flags, place, first, targets, group, tables):
    planes = group[0].shape[1]
    extent = tables[0].shape[0]
    points = extent * extent
    return pl.pallas_call(
        functools.partial(forward_kernel, place, first, len(targets), len(targets[0])),
        out_shape=jax.ShapeDtypeStruct((2, extent * plane_pitch, lanes), jnp.float32),
        in_specs=[scalars] + [outside] * (len(targets) * len(targets[0]) + len(group)) + [whole] * len(tables),
        out_specs=whole,
        scratch_shapes=[
            pltpu.VMEM((planes, points), jnp.bfloat16),
            pltpu.VMEM((planes, points), jnp.bfloat16),
            pltpu.VMEM((2, planes * turned_pitch, lanes), jnp.float32),
            pltpu.SemaphoreType.DMA((len(targets[0]) + 5,)),
        ],
        compiler_params=pltpu.CompilerParams(vmem_limit_bytes=limit),
        cost_estimate=small,
        name="forward",
    )(flags, *[piece for choice in targets for piece in choice], *group, *tables)


def central(flags, home, direct, ready, targets, neighbour_source, across_source, tables):
    planes = across_source[0].shape[1]
    extent = tables[0].shape[0]
    points = extent * extent
    pieces = [*ready, *targets[0], *targets[1], *neighbour_source, *across_source]
    parts = [jax.ShapeDtypeStruct((planes, share * points // 5), jnp.bfloat16) for share in (2, 3)]
    slab = jax.ShapeDtypeStruct(ready[0].shape, jnp.float32)
    outs = pl.pallas_call(
        functools.partial(central_kernel, home, direct),
        out_shape=parts * 2 + [slab] * 2,
        in_specs=[scalars] + [outside] * len(pieces) + [whole] * len(tables),
        out_specs=[whole] * 4 + [outside] * 2,
        scratch_shapes=[
            pltpu.VMEM((ring, *slab.shape), jnp.float32),
            *[pltpu.VMEM((planes, points), jnp.bfloat16)] * 4,
            pltpu.VMEM((2, planes * turned_pitch, lanes), jnp.float32),
            pltpu.SemaphoreType.DMA((len(targets[0]) + 5,)),
            pltpu.SemaphoreType.DMA((13,)),
            pltpu.SemaphoreType.DMA((2,)),
        ],
        compiler_params=pltpu.CompilerParams(vmem_limit_bytes=limit),
        cost_estimate=small,
        name="central",
    )(flags, *pieces, *tables)
    return split(outs, 2, 2, 2)


def backward(flags, places, first, slabs, groups, cas_matrix, windows, parts):
    planes = groups[0][0].shape[1]
    extent = cas_matrix.shape[0]
    points = extent * extent
    pieces = [piece for group in groups for piece in group]
    return pl.pallas_call(
        functools.partial(backward_kernel, places, first, parts),
        out_shape=[jax.ShapeDtypeStruct((planes, points // parts), jnp.bfloat16)] * parts,
        in_specs=[scalars] + [outside] * (len(slabs) + len(pieces)) + [whole] * 2,
        out_specs=[whole] * parts,
        scratch_shapes=[
            pltpu.VMEM(slabs[0].shape, jnp.float32),
            pltpu.VMEM((planes, points), jnp.bfloat16),
            pltpu.VMEM((2, planes * turned_pitch, lanes), jnp.float32),
            pltpu.SemaphoreType.DMA((6,)),
        ],
        compiler_params=pltpu.CompilerParams(vmem_limit_bytes=limit),
        cost_estimate=small,
        name="backward",
    )(flags, *slabs, *pieces, cas_matrix, windows)


def add(a, b):
    return (a.astype(jnp.float32) + b.astype(jnp.float32)).astype(jnp.bfloat16)


def pair_plan(orbitals, source_index):
    local_count, planes, points = orbitals.shape
    slabs = lax.axis_size("grid")
    extent = planes * slabs
    band, z = lax.axis_index("band"), lax.axis_index("grid")
    column, core = band // cores, band % cores
    quarter = points // 4
    at_home = core == holder(z)
    direct_neighbour = core == 1 - z % 2
    parity = z % 2
    inner = (z == 1) | (z == 2)
    second = inner.astype(jnp.int32)
    flags = jnp.stack([core, column, at_home, direct_neighbour, second, 1 - second]).astype(jnp.int32)
    home, direct = 2, 3

    unit = points // 8

    def first_pieces(source_index):
        core = lax.rem(lax.axis_index("band"), cores)
        near_parity = lax.rem(lax.axis_index("grid") + 1, 2)
        candidate = lax.rem(source_index[1 - core], local_count)
        return [(candidate, 0)] + [(near_parity, start) for start in (0, unit, 6 * unit)]

    def own_orbital(source_index):
        return [(lax.rem(lax.axis_index("grid"), 2), 0)]

    other, *to_near = pick(orbitals, source_index, first_pieces, (points, unit, 5 * unit, 2 * unit))
    crossed = swap_cores(other)
    near = [move(to_near[0], near_routes())]
    owner = source_index[core] // local_count

    cuts, to_near = stage((cut_quarters(source_index, orbitals, crossed), to_near), near)
    near.append(move(to_near[1], near_routes()))
    candidates = [cuts[0]] + [to_column(cuts[d], d) for d in (1, 2, 3)]
    (own_parity,) = pick(stage(orbitals, cuts), source_index, own_orbital, (points,))
    cas_matrix = cas_table(extent)
    windows = window_tables(cas_matrix)
    windows_back = jnp.swapaxes(windows, 1, 2)
    places = (((z ^ jnp.arange(slabs)) * planes)[:, None] + jnp.arange(planes)).reshape(extent)
    into = cas_entries(jnp.arange(extent), places, extent)
    square_x = wave_square(jnp.arange(extent, dtype=jnp.int32), extent)
    strength = (extent * spacing) ** 2 / math.pi
    square = (square_x[:, None] + square_x[None, :] + 1.0) * (1.0 / strength)
    square = jnp.pad(square, ((0, 0), (0, 2 * lanes - extent)), constant_values=1.0)
    tables = [cas_matrix, windows, windows_back, into, into.T, square]

    candidates, tables, own_parity, flags = stage((candidates, tables, own_parity, flags), near)
    cas_matrix, windows, windows_back, into, outof, square = tables
    forward_tables = [cas_matrix, windows, into, outof]
    own = lax.select_n(column ^ (owner // cores), *candidates)
    own = stage(own, tables)
    own_swapped = swap_cores(own_parity)
    own_x, own_y = to_column(own, 1), to_column(own, 2)
    neighbour = to_height(own, {0: 1, 1: 0, 2: 3, 3: 2})
    crossed = to_height(own, {1: 2, 2: 1})

    neighbour, crossed, own_x, own_y, own_swapped = stage((neighbour, crossed, own_x, own_y, own_swapped))
    neighbour_x, neighbour_y = to_column(neighbour, 1), to_column(neighbour, 2)
    crossed_2 = to_height(neighbour, {1: 2, 2: 1})
    handed = to_height(crossed, {1: 0, 2: 3})

    low = jnp.stack([own_x[:, : quarter // 2], neighbour_x[:, : quarter // 2]])
    high = jnp.stack([own_y[:, quarter // 2 :], neighbour_y[:, quarter // 2 :]])
    low, high, crossed_2, own_parity, last = stage((low, high, crossed_2, own_parity, to_near[2]), handed)
    low, high = to_column(low, 2), to_column(high, 1)
    handed_2 = to_height(crossed_2, {1: 0, 2: 3})
    near.append(move(last, near_routes()))
    far = [move(own_parity, far_routes())]

    across = jnp.stack([jnp.where(inner, crossed, handed), jnp.where(inner, crossed_2, handed_2)])
    across, low, high = stage((across, low, high))
    sources = [
        [own[None], own_x[None], own_y[None], low[:1], high[:1]],
        [neighbour[None], neighbour_x[None], neighbour_y[None], low[1:], high[1:]],
    ]
    across_x, across_y = to_column(across, 1), to_column(across, 2)
    near_swapped = [swap_cores(part) for part in stage(near[:2], across)]
    along_y = [forward(flags, 0, home, [[own_parity], [own_swapped]], sources[0], forward_tables)]

    low, high = across_x[:, :, : quarter // 2], across_y[:, :, quarter // 2 :]
    near[2] = stage(near[2], along_y)
    near_swapped.append(swap_cores(near[2]))
    low, high, near_swapped = stage((low, high, near_swapped), along_y)
    low, high = to_column(low, 2), to_column(high, 1)
    along_y.append(forward(flags, 1, direct, [near, near_swapped], sources[1], forward_tables))

    low, high, far = stage((low, high, far), along_y)
    across_source = [across, across_x, across_y, low, high]
    sources += [across_source, across_source]
    far_swapped = [swap_cores(part) for part in far]
    along_y_3 = forward(flags, 3, direct, [near_swapped, near], across_source, forward_tables)
    far_swapped = stage(far_swapped, along_y_3)
    given, kept, (own_back, far_back) = central(
        flags,
        home,
        direct,
        [*along_y, along_y_3],
        [far_swapped, far],
        sources[1],
        across_source,
        [cas_matrix, windows, windows_back, into, outof, square],
    )

    def partials(places, slabs, *earlier):
        groups = [sources[place] for place in places]
        return backward(flags, places, home, stage(slabs, *earlier), groups, cas_matrix, windows_back, 4)

    near = [add(k, swap_cores(g)) for k, g in zip(kept, given)]
    near_home = [move(part, back(near_routes())) for part in near]
    given = partials([2, 0], [far_back, own_back], near[0])
    kept = partials([0, 2], [own_back, far_back], given[0], near_home[0])
    far = [add(k, swap_cores(g)) for k, g in zip(kept, given)]
    far_home = [move(part, back(far_routes())) for part in far]
    return put(parity, at_home, near_home, far, far_home)


def solution(mesh):
    def shards(orbitals, source_index):
        slabs, bands = mesh.shape["grid"], mesh.shape["band"]
        fits = slabs == 4 and bands == 8 and orbitals.shape[0] == 2 and source_index.shape[0] == cores
        return (pair_plan if fits else slab_plan)(orbitals, source_index)

    return jax.shard_map(
        shards,
        mesh=mesh,
        in_specs=(P("band", "grid", None), P()),
        out_specs=P("band", "grid", None),
        check_vma=False,
    )
```

```python
import functools
import math

import jax
import jax.numpy as jnp
from jax import lax
from jax.experimental import pallas as pl
from jax.experimental.pallas import tpu as pltpu
from jax.sharding import PartitionSpec as P

spacing = 0.3
cores = 2


def cas_entries(rows, columns, extent):
    products_mod = rows[:, None] * columns[None, :] % extent
    radians = products_mod.astype(jnp.float32) * (2.0 * math.pi / extent)
    return ((jnp.cos(radians) + jnp.sin(radians)) / math.sqrt(extent)).astype(jnp.bfloat16)


def cas_table(extent):
    wavenum = jnp.arange(extent, dtype=jnp.int32)
    return cas_entries(wavenum, wavenum, extent)


def wave_square(indices, extent):
    folded = jnp.minimum(indices, extent - indices).astype(jnp.float32)
    return folded * folded


def coulomb_block(extent, columns, offset):
    square_x = wave_square(jnp.arange(extent, dtype=jnp.int32), extent)
    square_y = wave_square(offset + jnp.arange(columns, dtype=jnp.int32), extent)
    total_sq = square_x[:, None, None] + square_y[None, :, None] + square_x[None, None, :]
    strength = (extent * spacing) ** 2 / math.pi
    return jnp.where(total_sq > 0, strength / (total_sq + 1.0), 0.0)


def transform(grid_data, cas_matrix, pattern):
    return jnp.einsum(pattern, grid_data, cas_matrix, preferred_element_type=jnp.float32)


def broadcast(x, axis, root):
    mine = lax.axis_index(axis) == root
    return lax.psum(jnp.where(mine, x, jnp.zeros_like(x)), axis)


def slab_potentials(pair_rho, cas_matrix, kernel_block):
    along_z = transform(pair_rho, cas_matrix, "pxyz,kz->pxyk").astype(jnp.bfloat16)
    along_y = transform(along_z, cas_matrix, "pxyz,ky->pxkz").astype(jnp.bfloat16)
    turned = lax.all_to_all(along_y, "grid", split_axis=2, concat_axis=1, tiled=True)
    scaled = (kernel_block * transform(turned, cas_matrix, "pxyz,kx->pkyz")).astype(jnp.bfloat16)
    back_x = transform(scaled, cas_matrix, "pxyz,kx->pkyz").astype(jnp.bfloat16)
    returned = lax.all_to_all(back_x, "grid", split_axis=1, concat_axis=2, tiled=True)
    again_y = transform(returned, cas_matrix, "pxyz,ky->pxkz").astype(jnp.bfloat16)
    return transform(again_y, cas_matrix, "pxyz,kz->pxyk")


def fetch_source(orbitals, which):
    local_count = orbitals.shape[0]
    local_slab = lax.dynamic_index_in_dim(orbitals, which % local_count, 0, keepdims=False)
    return broadcast(local_slab, "band", which // local_count)


def slab_plan(orbitals, source_index):
    local_count, planes, _ = orbitals.shape
    extent = planes * lax.axis_size("grid")
    orbitals = orbitals.reshape(local_count, planes, extent, extent)
    source_count = source_index.shape[0]
    cas_matrix = cas_table(extent)
    columns = extent // lax.axis_size("grid")
    kernel_block = coulomb_block(extent, columns, lax.axis_index("grid") * columns)
    fetched = [fetch_source(orbitals, source_index[number]) for number in range(source_count)]
    stacked = jnp.stack(fetched)[:, None].astype(jnp.float32)
    pair_rho = (stacked * orbitals[None].astype(jnp.float32)).astype(jnp.bfloat16)
    pair_rho = pair_rho.reshape(source_count * local_count, planes, extent, extent)
    potential = slab_potentials(pair_rho, cas_matrix, kernel_block)
    potential = potential.reshape(source_count, local_count, planes, extent, extent)
    result = (-jnp.sum(stacked * potential, axis=0)).astype(jnp.bfloat16)
    return result.reshape(local_count, planes, extent * extent)


lanes = 128
quad = 4
ring = 4
turned_pitch = 161
plane_pitch = 41


def move(x, routes):
    slabs = lax.axis_size("grid")

    def place(column, core, z):
        return (column * cores + core) * slabs + z % slabs

    return lax.ppermute(x, ("band", "grid"), [(place(*a), place(*b)) for a, b in routes])


def everywhere():
    columns = lax.axis_size("band") // cores
    return [(c, k, z) for c in range(columns) for k in range(cores) for z in range(lax.axis_size("grid"))]


def swap_cores(x):
    return move(x, [((c, k, z), (c, 1 - k, z)) for c, k, z in everywhere()])


def to_column(x, d):
    return move(x, [((c, k, z), (c ^ d, k, z)) for c, k, z in everywhere()])


def to_height(x, to):
    return move(x, [((c, k, z), (c, k, to[z])) for c, k, z in everywhere() if z in to])


def holder(z):
    return z % ring // 2


def side(core):
    return 2 * core - 1


def near_routes():
    return [((c, holder(z), z + side(k)), (c, k, z)) for c, k, z in everywhere()]


def far_routes():
    return [((c, holder(z), z + 2), (c, k, z)) for c, k, z in everywhere() if k != holder(z)]


def back(routes):
    return [(b, a) for a, b in routes]


def stage(values, *earlier):
    return lax.optimization_barrier((values, earlier))[0]


def choose(first, refs, start):
    if len(refs) == 1:
        start(refs[0])
    else:
        pl.when(first)(lambda: start(refs[0]))
        pl.when(jnp.logical_not(first))(lambda: start(refs[1]))


def start_pieces(pieces, sems):
    for number, (refs, first, to) in enumerate(pieces):
        choose(first, refs, lambda ref, to=to, number=number: pltpu.make_async_copy(ref, to, sems.at[number]).start())


def wait_pieces(pieces, sems):
    for number, (refs, _, to) in enumerate(pieces):
        pltpu.make_async_copy(refs[0], to, sems.at[number]).wait()


def source_of(refs, flags, place):
    return refs, flags[2 + place] if place > 1 else 0


def source_pieces(groups, first, source, column):
    quarter = source.shape[1] // 4
    offsets = [(column ^ e) * quarter for e in range(4)]
    offsets.append(offsets[3] + quarter // 2)
    pieces = []
    for number, offset in enumerate(offsets):
        refs = [five[number].at[which] for five, which in groups]
        to = source.at[:, pl.ds(pl.multiple_of(offset, lanes), refs[0].shape[1])]
        pieces.append((refs, first, to))
    return pieces


def split(refs, *counts):
    taken = []
    for count in counts:
        taken.append(refs[:count])
        refs = refs[count:]
    return taken


def dot(a, b):
    return jnp.dot(a, b, preferred_element_type=jnp.float32)


def both(ref, rows):
    return jnp.concatenate([ref[0, rows, :], ref[1, rows, :]], axis=1)


def beside(values):
    return jnp.concatenate(values, axis=1)


def apart(value):
    return [value[:, n : n + 2 * lanes] for n in range(0, value.shape[1], 2 * lanes)]


def put_both(ref, rows, value):
    ref[0, rows, :] = value[:, :lanes]
    ref[1, rows, :] = value[:, lanes:]


def lane_ranges(pieces):
    ranges = []
    start = 0
    for piece in pieces:
        ranges.append((start, piece.shape[1]))
        start += piece.shape[1]
    return ranges


def pick_kernel(which, source_index, orbitals, *refs):
    outs, sems = refs[:-1], refs[-1]
    copies = []
    for n, (out, (orbital, start)) in enumerate(zip(outs, which(source_index))):
        copies.append(pltpu.make_async_copy(orbitals.at[orbital, :, pl.ds(start, out.shape[1])], out, sems.at[n]))
    for copy in copies:
        copy.start()
    for copy in copies:
        copy.wait()


def cut_kernel(source_index, orbitals, crossed, *refs):
    outs, sems = refs[:-1], refs[-1]
    local_count = orbitals.shape[0]
    band = lax.axis_index("band")
    core, column = lax.rem(band, cores), lax.div(band, cores)
    which = lax.rem(source_index[core], local_count)
    owner = lax.rem(lax.div(source_index[core], local_count), cores)
    width = outs[0].shape[1]
    pieces = []
    for d, out in enumerate(outs):
        lane = pl.ds(pl.multiple_of((column ^ d) * width, lanes), width)
        pieces.append(((orbitals.at[which, :, lane], crossed.at[:, lane]), owner == core, out))
    start_pieces(pieces, sems)
    wait_pieces(pieces, sems)


def put_kernel(count, flags, *refs):
    (out, staged, sems, out_sems), refs = refs[-4:], refs[:-4]
    near, choices = refs[:-count], refs[-count:]
    half = count // 2
    places = [(1 - flags[0], pl.ds(*lane)) for lane in lane_ranges(near)]
    places += [(flags[0], pl.ds(*lane)) for lane in lane_ranges(choices[:half])]
    chosen = [(ref,) for ref in near] + [choices[n::half] for n in range(half)]
    pieces = [(refs, flags[1] == 1, staged.at[which, :, lane]) for refs, (which, lane) in zip(chosen, places)]
    start_pieces(pieces, sems)
    leave = []
    for number, (which, lane) in enumerate(places):
        piece = staged.at[which, :, lane]
        pltpu.make_async_copy(chosen[number][0], piece, sems.at[number]).wait()
        leave.append(pltpu.make_async_copy(piece, out.at[which, :, lane], out_sems.at[number]))
        leave[-1].start()
    for copy in leave:
        copy.wait()


def transform_in(source, target, windows, cas, turned, out):
    planes, points = target.shape
    extent = cas.shape[0]
    step = 8
    block = quad * extent

    @pl.loop(0, points // block // step)
    def _(i):
        for r in range(quad):
            density = []
            for j in range(step):
                at = pl.ds(pl.multiple_of((i * step + j) * block + r * lanes, lanes), 2 * lanes)
                density.append(source[:, at].astype(jnp.float32) * target[:, at].astype(jnp.float32))
            density = jnp.concatenate(density, axis=0).astype(jnp.bfloat16)
            along_z = dot(density, windows[r])
            for j in range(step):
                y = (i * step + j) * quad + r
                put_both(turned, pl.ds(y, planes, stride=turned_pitch), along_z[j * planes : (j + 1) * planes])

    @pl.loop(0, planes // 4)
    def _(i):
        for j in range(4):
            x = i * 4 + j
            along_z = both(turned, pl.ds(x * turned_pitch, extent)).astype(jnp.bfloat16)
            put_both(out, pl.ds(x, extent, stride=plane_pitch), dot(cas[...], along_z))


def transform_x(slabs, into, outof, square):
    extent = square.shape[0]
    planes = extent // ring
    strength = (extent * spacing) ** 2 / math.pi
    rows = 8

    @pl.loop(0, extent // rows)
    def _(step):
        base = pl.multiple_of(step * rows * plane_pitch, 8)
        for i in range(rows):
            at = pl.ds(base + i * plane_pitch, planes)
            along_y = jnp.concatenate([both(slab, at) for slab in slabs], axis=0).astype(jnp.bfloat16)
            ky = step * rows + i
            folded = jnp.minimum(ky, extent - ky)
            weight = square[...] + (folded * folded).astype(jnp.float32) * (1.0 / strength)
            guess = pl.reciprocal(weight, approx=True)
            factor = guess * (2.0 - weight * guess)
            factor = jnp.where(weight > 1.25 / strength, factor, 0.0)
            scaled = (factor * dot(into[...], along_y)).astype(jnp.bfloat16)
            back_x = dot(outof[...], scaled)
            for n, slab in enumerate(slabs):
                put_both(slab, at, back_x[n * planes : (n + 1) * planes])


def transform_out(back_x, source, windows, cas, turned, outs):
    planes, points = source.shape
    extent = cas.shape[0]

    @pl.loop(0, planes // 4)
    def _(i):
        for j in range(4):
            x = i * 4 + j
            column_x = both(back_x, pl.ds(x, extent, stride=plane_pitch)).astype(jnp.bfloat16)
            put_both(turned, pl.ds(x * turned_pitch, extent), dot(cas[...], column_x))

    block = quad * extent
    begin = 0
    for out in outs:
        blocks = out.shape[1] // block
        step = 5 if blocks % 5 == 0 else 4

        @pl.loop(0, blocks // step)
        def _(i, begin=begin, step=step, out=out):
            first = begin + i * step
            windowed = []
            for r in range(quad):
                again_y = jnp.concatenate(
                    [both(turned, pl.ds((first + j) * quad + r, planes, stride=turned_pitch)) for j in range(step)],
                    axis=0,
                ).astype(jnp.bfloat16)
                windowed.append(dot(again_y, windows[r]))
            for j in range(step):
                w = [part[j * planes : (j + 1) * planes] for part in windowed]
                potential = [w[0][:, :lanes]]
                potential += [w[r][:, lanes:] + w[r + 1][:, :lanes] for r in range(quad - 1)]
                potential = jnp.concatenate(potential + [w[-1][:, lanes:]], axis=1)
                at = pl.ds(pl.multiple_of((first + j) * block, lanes), block)
                to = pl.ds(pl.multiple_of((i * step + j) * block, lanes), block)
                out[:, to] = (-(source[:, at].astype(jnp.float32) * potential)).astype(jnp.bfloat16)

        begin += blocks


def forward_kernel(place, first, choices, count, flags, *refs):
    targets, five, (cas, windows, _, _, out, target, source, turned, sems) = split(refs, choices * count, 5, 9)
    ranges = lane_ranges(targets[:count])
    pieces = [(targets[n::count], flags[first] == 1, target.at[:, pl.ds(*lane)]) for n, lane in enumerate(ranges)]
    pieces += source_pieces([source_of(five, flags, place)], None, source, flags[1])
    start_pieces(pieces, sems)
    wait_pieces(pieces, sems)
    transform_in(source, target, windows, cas, turned, out)


def backward_kernel(places, first, parts, flags, *refs):
    slabs, groups, (cas, windows), outs, (back_x, source, turned, sems) = split(
        refs, len(places), 5 * len(places), 2, parts, 4
    )
    chosen = [source_of(five, flags, place) for five, place in zip(split(groups, *[5] * len(places)), places)]
    pieces = [(slabs, flags[first] == 1, back_x)] + source_pieces(chosen, flags[first] == 1, source, flags[1])
    start_pieces(pieces, sems)
    wait_pieces(pieces, sems)
    transform_out(back_x, source, windows, cas, turned, outs)


def central_kernel(home, direct, flags, *refs):
    ready, targets, neighbour_source, across_source, tables, outs, scratch = split(
        refs, 3, len(refs) - 34, 5, 5, 6, 6, 9
    )
    cas, windows, windows_back, into, outof, square = tables
    given, kept, (own_out, far_out) = split(outs, 2, 2, 2)
    slabs, target, source, given_source, kept_source, turned, first_sems, later_sems, out_sems = scratch
    at_direct = flags[direct] == 1
    column = flags[1]

    count = len(targets) // 2
    ranges = lane_ranges(targets[:count])
    first = [(targets[n::count], flags[home] == 1, target.at[:, pl.ds(*lane)]) for n, lane in enumerate(ranges)]
    first += source_pieces([source_of(across_source, flags, 2)], None, source, column)
    start_pieces(first, first_sems)
    later = [((ref,), None, slabs.at[place]) for ref, place in zip(ready, (0, 1, 3))]
    near_sources = [source_of(across_source, flags, 3), source_of(neighbour_source, flags, 1)]
    later += source_pieces(near_sources, at_direct, given_source, column)
    later += source_pieces(near_sources[::-1], at_direct, kept_source, column)
    start_pieces(later, later_sems)
    wait_pieces(first, first_sems)
    transform_in(source, target, windows, cas, turned, slabs.at[2])
    wait_pieces(later, later_sems)

    transform_x([slabs.at[place] for place in range(4)], into, outof, square)

    leave = [((slabs.at[2],), None, far_out), ((slabs.at[0],), None, own_out)]
    start_pieces(leave, out_sems)
    kept_place = jnp.where(at_direct, 1, 3)
    transform_out(slabs.at[4 - kept_place], given_source, windows_back, cas, turned, given)
    transform_out(slabs.at[kept_place], kept_source, windows_back, cas, turned, kept)
    wait_pieces(leave, out_sems)


def window_tables(cas_matrix):
    extent = cas_matrix.shape[0]
    tables = []
    for r in range(quad):
        shift = r * extent % lanes
        tables.append(jnp.pad(cas_matrix, ((shift, 2 * lanes - extent - shift), (0, 2 * lanes - extent))))
    return jnp.stack(tables)


limit = 63 * 2**20
whole = pl.BlockSpec(memory_space=pltpu.VMEM)
outside = pl.BlockSpec(memory_space=pl.ANY)
scalars = pl.BlockSpec(memory_space=pltpu.SMEM)
small = pl.CostEstimate(flops=10**6, bytes_accessed=10**4, transcendentals=0)


def pick(orbitals, source_index, which, widths):
    planes = orbitals.shape[1]
    return pl.pallas_call(
        functools.partial(pick_kernel, which),
        out_shape=[jax.ShapeDtypeStruct((planes, width), orbitals.dtype) for width in widths],
        in_specs=[scalars, outside],
        out_specs=[whole] * len(widths),
        scratch_shapes=[pltpu.SemaphoreType.DMA((len(widths),))],
        compiler_params=pltpu.CompilerParams(vmem_limit_bytes=limit),
        cost_estimate=small,
        name="pick",
    )(source_index, orbitals)


def cut_quarters(source_index, orbitals, crossed):
    planes, points = crossed.shape
    return pl.pallas_call(
        cut_kernel,
        out_shape=[jax.ShapeDtypeStruct((planes, points // 4), crossed.dtype)] * 4,
        in_specs=[scalars, outside, outside],
        out_specs=[whole] * 4,
        scratch_shapes=[pltpu.SemaphoreType.DMA((4,))],
        compiler_params=pltpu.CompilerParams(vmem_limit_bytes=limit),
        cost_estimate=small,
        name="cut",
    )(source_index, orbitals, crossed)


def put(parity, first, near, *choices):
    pieces = near + [piece for choice in choices for piece in choice]
    planes, points = near[0].shape[0], sum(piece.shape[1] for piece in near)
    return pl.pallas_call(
        functools.partial(put_kernel, 2 * len(choices[0])),
        out_shape=jax.ShapeDtypeStruct((2, planes, points), near[0].dtype),
        in_specs=[scalars] + [outside] * len(pieces),
        out_specs=outside,
        scratch_shapes=[
            pltpu.VMEM((2, planes, points), near[0].dtype),
            pltpu.SemaphoreType.DMA((len(near) + len(choices[0]),)),
            pltpu.SemaphoreType.DMA((len(near) + len(choices[0]),)),
        ],
        compiler_params=pltpu.CompilerParams(vmem_limit_bytes=limit),
        cost_estimate=small,
        name="put",
    )(jnp.stack([parity, first.astype(parity.dtype)]).astype(jnp.int32), *pieces)


def forward(flags, place, first, targets, group, tables):
    planes = group[0].shape[1]
    extent = tables[0].shape[0]
    points = extent * extent
    return pl.pallas_call(
        functools.partial(forward_kernel, place, first, len(targets), len(targets[0])),
        out_shape=jax.ShapeDtypeStruct((2, extent * plane_pitch, lanes), jnp.float32),
        in_specs=[scalars] + [outside] * (len(targets) * len(targets[0]) + len(group)) + [whole] * len(tables),
        out_specs=whole,
        scratch_shapes=[
            pltpu.VMEM((planes, points), jnp.bfloat16),
            pltpu.VMEM((planes, points), jnp.bfloat16),
            pltpu.VMEM((2, planes * turned_pitch, lanes), jnp.float32),
            pltpu.SemaphoreType.DMA((len(targets[0]) + 5,)),
        ],
        compiler_params=pltpu.CompilerParams(vmem_limit_bytes=limit),
        cost_estimate=small,
        name="forward",
    )(flags, *[piece for choice in targets for piece in choice], *group, *tables)


def central(flags, home, direct, ready, targets, neighbour_source, across_source, tables):
    planes = across_source[0].shape[1]
    extent = tables[0].shape[0]
    points = extent * extent
    pieces = [*ready, *targets[0], *targets[1], *neighbour_source, *across_source]
    parts = [jax.ShapeDtypeStruct((planes, share * points // 5), jnp.bfloat16) for share in (2, 3)]
    slab = jax.ShapeDtypeStruct(ready[0].shape, jnp.float32)
    outs = pl.pallas_call(
        functools.partial(central_kernel, home, direct),
        out_shape=parts * 2 + [slab] * 2,
        in_specs=[scalars] + [outside] * len(pieces) + [whole] * len(tables),
        out_specs=[whole] * 4 + [outside] * 2,
        scratch_shapes=[
            pltpu.VMEM((ring, *slab.shape), jnp.float32),
            *[pltpu.VMEM((planes, points), jnp.bfloat16)] * 4,
            pltpu.VMEM((2, planes * turned_pitch, lanes), jnp.float32),
            pltpu.SemaphoreType.DMA((len(targets[0]) + 5,)),
            pltpu.SemaphoreType.DMA((13,)),
            pltpu.SemaphoreType.DMA((2,)),
        ],
        compiler_params=pltpu.CompilerParams(vmem_limit_bytes=limit),
        cost_estimate=small,
        name="central",
    )(flags, *pieces, *tables)
    return split(outs, 2, 2, 2)


def backward(flags, places, first, slabs, groups, cas_matrix, windows, parts):
    planes = groups[0][0].shape[1]
    extent = cas_matrix.shape[0]
    points = extent * extent
    pieces = [piece for group in groups for piece in group]
    return pl.pallas_call(
        functools.partial(backward_kernel, places, first, parts),
        out_shape=[jax.ShapeDtypeStruct((planes, points // parts), jnp.bfloat16)] * parts,
        in_specs=[scalars] + [outside] * (len(slabs) + len(pieces)) + [whole] * 2,
        out_specs=[whole] * parts,
        scratch_shapes=[
            pltpu.VMEM(slabs[0].shape, jnp.float32),
            pltpu.VMEM((planes, points), jnp.bfloat16),
            pltpu.VMEM((2, planes * turned_pitch, lanes), jnp.float32),
            pltpu.SemaphoreType.DMA((6,)),
        ],
        compiler_params=pltpu.CompilerParams(vmem_limit_bytes=limit),
        cost_estimate=small,
        name="backward",
    )(flags, *slabs, *pieces, cas_matrix, windows)


def add(a, b):
    return (a.astype(jnp.float32) + b.astype(jnp.float32)).astype(jnp.bfloat16)


def pair_plan(orbitals, source_index):
    local_count, planes, points = orbitals.shape
    slabs = lax.axis_size("grid")
    extent = planes * slabs
    band, z = lax.axis_index("band"), lax.axis_index("grid")
    column, core = band // cores, band % cores
    quarter = points // 4
    at_home = core == holder(z)
    direct_neighbour = core == 1 - z % 2
    parity = z % 2
    inner = (z == 1) | (z == 2)
    second = inner.astype(jnp.int32)
    flags = jnp.stack([core, column, at_home, direct_neighbour, second, 1 - second]).astype(jnp.int32)
    home, direct = 2, 3

    unit = points // 8

    def first_pieces(source_index):
        core = lax.rem(lax.axis_index("band"), cores)
        near_parity = lax.rem(lax.axis_index("grid") + 1, 2)
        candidate = lax.rem(source_index[1 - core], local_count)
        return [(candidate, 0)] + [(near_parity, start) for start in (0, unit, 6 * unit)]

    def own_orbital(source_index):
        return [(lax.rem(lax.axis_index("grid"), 2), 0)]

    other, *to_near = pick(orbitals, source_index, first_pieces, (points, unit, 5 * unit, 2 * unit))
    crossed = swap_cores(other)
    near = [move(to_near[0], near_routes())]
    owner = source_index[core] // local_count

    cuts, to_near = stage((cut_quarters(source_index, orbitals, crossed), to_near), near)
    near.append(move(to_near[1], near_routes()))
    candidates = [cuts[0]] + [to_column(cuts[d], d) for d in (1, 2, 3)]
    (own_parity,) = pick(stage(orbitals, cuts), source_index, own_orbital, (points,))
    cas_matrix = cas_table(extent)
    windows = window_tables(cas_matrix)
    windows_back = jnp.swapaxes(windows, 1, 2)
    places = (((z ^ jnp.arange(slabs)) * planes)[:, None] + jnp.arange(planes)).reshape(extent)
    into = cas_entries(jnp.arange(extent), places, extent)
    square_x = wave_square(jnp.arange(extent, dtype=jnp.int32), extent)
    strength = (extent * spacing) ** 2 / math.pi
    square = (square_x[:, None] + square_x[None, :] + 1.0) * (1.0 / strength)
    square = jnp.pad(square, ((0, 0), (0, 2 * lanes - extent)), constant_values=1.0)
    tables = [cas_matrix, windows, windows_back, into, into.T, square]

    candidates, tables, own_parity, flags = stage((candidates, tables, own_parity, flags), near)
    cas_matrix, windows, windows_back, into, outof, square = tables
    forward_tables = [cas_matrix, windows, into, outof]
    own = lax.select_n(column ^ (owner // cores), *candidates)
    own = stage(own, tables)
    own_swapped = swap_cores(own_parity)
    own_x, own_y = to_column(own, 1), to_column(own, 2)
    neighbour = to_height(own, {0: 1, 1: 0, 2: 3, 3: 2})
    crossed = to_height(own, {1: 2, 2: 1})

    neighbour, crossed, own_x, own_y, own_swapped = stage((neighbour, crossed, own_x, own_y, own_swapped))
    neighbour_x, neighbour_y = to_column(neighbour, 1), to_column(neighbour, 2)
    crossed_2 = to_height(neighbour, {1: 2, 2: 1})
    handed = to_height(crossed, {1: 0, 2: 3})

    low = jnp.stack([own_x[:, : quarter // 2], neighbour_x[:, : quarter // 2]])
    high = jnp.stack([own_y[:, quarter // 2 :], neighbour_y[:, quarter // 2 :]])
    low, high, crossed_2, own_parity = stage((low, high, crossed_2, own_parity), handed)
    low, high = to_column(low, 2), to_column(high, 1)
    handed_2 = to_height(crossed_2, {1: 0, 2: 3})
    far = [move(own_parity, far_routes())]

    across = jnp.stack([jnp.where(inner, crossed, handed), jnp.where(inner, crossed_2, handed_2)])
    across, low, high, last = stage((across, low, high, to_near[2]))
    near.append(move(last, near_routes()))
    sources = [
        [own[None], own_x[None], own_y[None], low[:1], high[:1]],
        [neighbour[None], neighbour_x[None], neighbour_y[None], low[1:], high[1:]],
    ]
    across_x, across_y = to_column(across, 1), to_column(across, 2)
    near_swapped = [swap_cores(part) for part in stage(near[:2], across)]
    along_y = [forward(flags, 0, home, [[own_parity], [own_swapped]], sources[0], forward_tables)]

    low, high = across_x[:, :, : quarter // 2], across_y[:, :, quarter // 2 :]
    near[2] = stage(near[2], along_y)
    near_swapped.append(swap_cores(near[2]))
    low, high, near_swapped = stage((low, high, near_swapped), along_y)
    low, high = to_column(low, 2), to_column(high, 1)
    along_y.append(forward(flags, 1, direct, [near, near_swapped], sources[1], forward_tables))

    low, high, far = stage((low, high, far), along_y)
    across_source = [across, across_x, across_y, low, high]
    sources += [across_source, across_source]
    far_swapped = [swap_cores(part) for part in far]
    along_y_3 = forward(flags, 3, direct, [near_swapped, near], across_source, forward_tables)
    far_swapped = stage(far_swapped, along_y_3)
    given, kept, (own_back, far_back) = central(
        flags,
        home,
        direct,
        [*along_y, along_y_3],
        [far_swapped, far],
        sources[1],
        across_source,
        [cas_matrix, windows, windows_back, into, outof, square],
    )

    def partials(places, slabs, *earlier):
        groups = [sources[place] for place in places]
        return backward(flags, places, home, stage(slabs, *earlier), groups, cas_matrix, windows_back, 4)

    near = [add(k, swap_cores(g)) for k, g in zip(kept, given)]
    near_home = [move(part, back(near_routes())) for part in near]
    given = partials([2, 0], [far_back, own_back], near[0])
    kept = partials([0, 2], [own_back, far_back], given[0], near_home[0])
    far = [add(k, swap_cores(g)) for k, g in zip(kept, given)]
    far_home = [move(part, back(far_routes())) for part in far]
    return put(parity, at_home, near_home, far, far_home)


def solution(mesh):
    def shards(orbitals, source_index):
        slabs, bands = mesh.shape["grid"], mesh.shape["band"]
        fits = slabs == 4 and bands == 8 and orbitals.shape[0] == 2 and source_index.shape[0] == cores
        return (pair_plan if fits else slab_plan)(orbitals, source_index)

    return jax.shard_map(
        shards,
        mesh=mesh,
        in_specs=(P("band", "grid", None), P()),
        out_specs=P("band", "grid", None),
        check_vma=False,
    )
```

```python
import functools
import math

import jax
import jax.numpy as jnp
from jax import lax
from jax.experimental import pallas as pl
from jax.experimental.pallas import tpu as pltpu
from jax.sharding import PartitionSpec as P

spacing = 0.3
cores = 2


def cas_entries(rows, columns, extent):
    products_mod = rows[:, None] * columns[None, :] % extent
    radians = products_mod.astype(jnp.float32) * (2.0 * math.pi / extent)
    return ((jnp.cos(radians) + jnp.sin(radians)) / math.sqrt(extent)).astype(jnp.bfloat16)


def cas_table(extent):
    wavenum = jnp.arange(extent, dtype=jnp.int32)
    return cas_entries(wavenum, wavenum, extent)


def wave_square(indices, extent):
    folded = jnp.minimum(indices, extent - indices).astype(jnp.float32)
    return folded * folded


def coulomb_block(extent, columns, offset):
    square_x = wave_square(jnp.arange(extent, dtype=jnp.int32), extent)
    square_y = wave_square(offset + jnp.arange(columns, dtype=jnp.int32), extent)
    total_sq = square_x[:, None, None] + square_y[None, :, None] + square_x[None, None, :]
    strength = (extent * spacing) ** 2 / math.pi
    return jnp.where(total_sq > 0, strength / (total_sq + 1.0), 0.0)


def transform(grid_data, cas_matrix, pattern):
    return jnp.einsum(pattern, grid_data, cas_matrix, preferred_element_type=jnp.float32)


def broadcast(x, axis, root):
    mine = lax.axis_index(axis) == root
    return lax.psum(jnp.where(mine, x, jnp.zeros_like(x)), axis)


def slab_potentials(pair_rho, cas_matrix, kernel_block):
    along_z = transform(pair_rho, cas_matrix, "pxyz,kz->pxyk").astype(jnp.bfloat16)
    along_y = transform(along_z, cas_matrix, "pxyz,ky->pxkz").astype(jnp.bfloat16)
    turned = lax.all_to_all(along_y, "grid", split_axis=2, concat_axis=1, tiled=True)
    scaled = (kernel_block * transform(turned, cas_matrix, "pxyz,kx->pkyz")).astype(jnp.bfloat16)
    back_x = transform(scaled, cas_matrix, "pxyz,kx->pkyz").astype(jnp.bfloat16)
    returned = lax.all_to_all(back_x, "grid", split_axis=1, concat_axis=2, tiled=True)
    again_y = transform(returned, cas_matrix, "pxyz,ky->pxkz").astype(jnp.bfloat16)
    return transform(again_y, cas_matrix, "pxyz,kz->pxyk")


def fetch_source(orbitals, which):
    local_count = orbitals.shape[0]
    local_slab = lax.dynamic_index_in_dim(orbitals, which % local_count, 0, keepdims=False)
    return broadcast(local_slab, "band", which // local_count)


def slab_plan(orbitals, source_index):
    local_count, planes, _ = orbitals.shape
    extent = planes * lax.axis_size("grid")
    orbitals = orbitals.reshape(local_count, planes, extent, extent)
    source_count = source_index.shape[0]
    cas_matrix = cas_table(extent)
    columns = extent // lax.axis_size("grid")
    kernel_block = coulomb_block(extent, columns, lax.axis_index("grid") * columns)
    fetched = [fetch_source(orbitals, source_index[number]) for number in range(source_count)]
    stacked = jnp.stack(fetched)[:, None].astype(jnp.float32)
    pair_rho = (stacked * orbitals[None].astype(jnp.float32)).astype(jnp.bfloat16)
    pair_rho = pair_rho.reshape(source_count * local_count, planes, extent, extent)
    potential = slab_potentials(pair_rho, cas_matrix, kernel_block)
    potential = potential.reshape(source_count, local_count, planes, extent, extent)
    result = (-jnp.sum(stacked * potential, axis=0)).astype(jnp.bfloat16)
    return result.reshape(local_count, planes, extent * extent)


lanes = 128
quad = 4
ring = 4
turned_pitch = 161
plane_pitch = 41


def move(x, routes):
    slabs = lax.axis_size("grid")

    def place(column, core, z):
        return (column * cores + core) * slabs + z % slabs

    return lax.ppermute(x, ("band", "grid"), [(place(*a), place(*b)) for a, b in routes])


def everywhere():
    columns = lax.axis_size("band") // cores
    return [(c, k, z) for c in range(columns) for k in range(cores) for z in range(lax.axis_size("grid"))]


def swap_cores(x):
    return move(x, [((c, k, z), (c, 1 - k, z)) for c, k, z in everywhere()])


def to_column(x, d):
    return move(x, [((c, k, z), (c ^ d, k, z)) for c, k, z in everywhere()])


def to_height(x, to):
    return move(x, [((c, k, z), (c, k, to[z])) for c, k, z in everywhere() if z in to])


def holder(z):
    return z % ring // 2


def side(core):
    return 2 * core - 1


def near_routes():
    return [((c, holder(z), z + side(k)), (c, k, z)) for c, k, z in everywhere()]


def far_routes():
    return [((c, holder(z), z + 2), (c, k, z)) for c, k, z in everywhere() if k != holder(z)]


def far_half_routes():
    return [((c, k, z + 2), (c, k, z)) for c, k, z in everywhere()]


def back(routes):
    return [(b, a) for a, b in routes]


def stage(values, *earlier):
    return lax.optimization_barrier((values, earlier))[0]


def choose(first, refs, start):
    if len(refs) == 1:
        start(refs[0])
    else:
        pl.when(first)(lambda: start(refs[0]))
        pl.when(jnp.logical_not(first))(lambda: start(refs[1]))


def start_pieces(pieces, sems):
    for number, (refs, first, to) in enumerate(pieces):
        choose(first, refs, lambda ref, to=to, number=number: pltpu.make_async_copy(ref, to, sems.at[number]).start())


def wait_pieces(pieces, sems):
    for number, (refs, _, to) in enumerate(pieces):
        pltpu.make_async_copy(refs[0], to, sems.at[number]).wait()


def source_pieces(groups, first, source, column):
    quarter = source.shape[1] // 4
    offsets = [(column ^ e) * quarter for e in range(4)]
    offsets.append(offsets[3] + quarter // 2)
    pieces = []
    for number, offset in enumerate(offsets):
        refs = [five[number].at[0] for five in groups]
        to = source.at[:, pl.ds(pl.multiple_of(offset, lanes), refs[0].shape[1])]
        pieces.append((refs, first, to))
    return pieces


def split(refs, *counts):
    taken = []
    for count in counts:
        taken.append(refs[:count])
        refs = refs[count:]
    return taken


def dot(a, b):
    return jnp.dot(a, b, preferred_element_type=jnp.float32)


def both(ref, rows):
    return jnp.concatenate([ref[0, rows, :], ref[1, rows, :]], axis=1)


def beside(values):
    return jnp.concatenate(values, axis=1)


def apart(value):
    return [value[:, n : n + 2 * lanes] for n in range(0, value.shape[1], 2 * lanes)]


def put_both(ref, rows, value):
    ref[0, rows, :] = value[:, :lanes]
    ref[1, rows, :] = value[:, lanes:]


def lane_ranges(pieces):
    ranges = []
    start = 0
    for piece in pieces:
        ranges.append((start, piece.shape[1]))
        start += piece.shape[1]
    return ranges


def pick_kernel(which, source_index, orbitals, *refs):
    outs, sems = refs[:-1], refs[-1]
    copies = []
    for n, (out, (orbital, start)) in enumerate(zip(outs, which(source_index))):
        copies.append(pltpu.make_async_copy(orbitals.at[orbital, :, pl.ds(start, out.shape[1])], out, sems.at[n]))
    for copy in copies:
        copy.start()
    for copy in copies:
        copy.wait()


def cut_kernel(source_index, orbitals, crossed, *refs):
    outs, sems = refs[:-1], refs[-1]
    local_count = orbitals.shape[0]
    band = lax.axis_index("band")
    core, column = lax.rem(band, cores), lax.div(band, cores)
    which = lax.rem(source_index[core], local_count)
    owner = lax.rem(lax.div(source_index[core], local_count), cores)
    width = outs[0].shape[1]
    pieces = []
    for d, out in enumerate(outs):
        lane = pl.ds(pl.multiple_of((column ^ d) * width, lanes), width)
        pieces.append(((orbitals.at[which, :, lane], crossed.at[:, lane]), owner == core, out))
    start_pieces(pieces, sems)
    wait_pieces(pieces, sems)


def put_kernel(count, flags, *refs):
    (out, staged, sems, out_sems), refs = refs[-4:], refs[:-4]
    near, choices = refs[:-count], refs[-count:]
    half = count // 2
    places = [(1 - flags[0], pl.ds(*lane)) for lane in lane_ranges(near)]
    places += [(flags[0], pl.ds(*lane)) for lane in lane_ranges(choices[:half])]
    chosen = [(ref,) for ref in near] + [choices[n::half] for n in range(half)]
    pieces = [(refs, flags[1] == 1, staged.at[which, :, lane]) for refs, (which, lane) in zip(chosen, places)]
    start_pieces(pieces, sems)
    leave = []
    for number, (which, lane) in enumerate(places):
        piece = staged.at[which, :, lane]
        pltpu.make_async_copy(chosen[number][0], piece, sems.at[number]).wait()
        leave.append(pltpu.make_async_copy(piece, out.at[which, :, lane], out_sems.at[number]))
        leave[-1].start()
    for copy in leave:
        copy.wait()


def transform_in(source, target, windows, cas, turned, out):
    planes, points = target.shape
    extent = cas.shape[0]
    step = 8
    block = quad * extent

    @pl.loop(0, points // block // step)
    def _(i):
        for r in range(quad):
            density = []
            for j in range(step):
                at = pl.ds(pl.multiple_of((i * step + j) * block + r * lanes, lanes), 2 * lanes)
                density.append(source[:, at].astype(jnp.float32) * target[:, at].astype(jnp.float32))
            density = jnp.concatenate(density, axis=0).astype(jnp.bfloat16)
            along_z = dot(density, windows[r])
            for j in range(step):
                y = (i * step + j) * quad + r
                put_both(turned, pl.ds(y, planes, stride=turned_pitch), along_z[j * planes : (j + 1) * planes])

    @pl.loop(0, planes // 4)
    def _(i):
        for j in range(4):
            x = i * 4 + j
            along_z = both(turned, pl.ds(x * turned_pitch, extent)).astype(jnp.bfloat16)
            put_both(out, pl.ds(x, extent, stride=plane_pitch), dot(cas[...], along_z))


def transform_x(slabs, into, outof, square):
    extent = square.shape[0]
    planes = extent // ring
    strength = (extent * spacing) ** 2 / math.pi
    rows = 8

    @pl.loop(0, extent // rows)
    def _(step):
        base = pl.multiple_of(step * rows * plane_pitch, 8)
        for i in range(rows):
            at = pl.ds(base + i * plane_pitch, planes)
            along_y = jnp.concatenate([both(slab, at) for slab in slabs], axis=0).astype(jnp.bfloat16)
            ky = step * rows + i
            folded = jnp.minimum(ky, extent - ky)
            weight = square[...] + (folded * folded).astype(jnp.float32) * (1.0 / strength)
            guess = pl.reciprocal(weight, approx=True)
            factor = guess * (2.0 - weight * guess)
            factor = jnp.where(weight > 1.25 / strength, factor, 0.0)
            scaled = (factor * dot(into[...], along_y)).astype(jnp.bfloat16)
            back_x = dot(outof[...], scaled)
            for n, slab in enumerate(slabs):
                put_both(slab, at, back_x[n * planes : (n + 1) * planes])


def transform_out(back_x, source, windows, cas, turned, outs):
    planes, points = source.shape
    extent = cas.shape[0]

    @pl.loop(0, planes // 4)
    def _(i):
        for j in range(4):
            x = i * 4 + j
            column_x = both(back_x, pl.ds(x, extent, stride=plane_pitch)).astype(jnp.bfloat16)
            put_both(turned, pl.ds(x * turned_pitch, extent), dot(cas[...], column_x))

    block = quad * extent
    begin = 0
    for out in outs:
        blocks = out.shape[1] // block
        step = 5 if blocks % 5 == 0 else 4

        @pl.loop(0, blocks // step)
        def _(i, begin=begin, step=step, out=out):
            first = begin + i * step
            windowed = []
            for r in range(quad):
                again_y = jnp.concatenate(
                    [both(turned, pl.ds((first + j) * quad + r, planes, stride=turned_pitch)) for j in range(step)],
                    axis=0,
                ).astype(jnp.bfloat16)
                windowed.append(dot(again_y, windows[r]))
            for j in range(step):
                w = [part[j * planes : (j + 1) * planes] for part in windowed]
                potential = [w[0][:, :lanes]]
                potential += [w[r][:, lanes:] + w[r + 1][:, :lanes] for r in range(quad - 1)]
                potential = jnp.concatenate(potential + [w[-1][:, lanes:]], axis=1)
                at = pl.ds(pl.multiple_of((first + j) * block, lanes), block)
                to = pl.ds(pl.multiple_of((i * step + j) * block, lanes), block)
                out[:, to] = (-(source[:, at].astype(jnp.float32) * potential)).astype(jnp.bfloat16)

        begin += blocks


def forward_kernel(first, choices, count, flags, *refs):
    targets, five, (cas, windows, _, _, out, target, source, turned, sems) = split(refs, choices * count, 5, 9)
    ranges = lane_ranges(targets[:count])
    pieces = [(targets[n::count], flags[first] == 1, target.at[:, pl.ds(*lane)]) for n, lane in enumerate(ranges)]
    pieces += source_pieces([five], None, source, flags[1])
    start_pieces(pieces, sems)
    wait_pieces(pieces, sems)
    transform_in(source, target, windows, cas, turned, out)


def backward_kernel(first, parts, flags, *refs):
    slabs, groups, (cas, windows), outs, (back_x, source, turned, sems) = split(
        refs, 2, 10, 2, parts, 4
    )
    chosen = split(groups, 5, 5)
    pieces = [(slabs, flags[first] == 1, back_x)] + source_pieces(chosen, flags[first] == 1, source, flags[1])
    start_pieces(pieces, sems)
    wait_pieces(pieces, sems)
    transform_out(back_x, source, windows, cas, turned, outs)


def central_kernel(direct, flags, *refs):
    ready, targets, neighbour_source, second_source, third_source, tables, outs, scratch = split(
        refs, 3, 4, 5, 5, 5, 6, 6, 9
    )
    cas, windows, windows_back, into, outof, square = tables
    given, kept, (own_out, far_out) = split(outs, 2, 2, 2)
    slabs, target, source, given_source, kept_source, turned, first_sems, later_sems, out_sems = scratch
    at_direct = flags[direct] == 1
    column = flags[1]

    count = len(targets) // 2
    ranges = lane_ranges(targets[:count])
    first = [(targets[n::count], flags[0] == 1, target.at[:, pl.ds(*lane)]) for n, lane in enumerate(ranges)]
    first += source_pieces([second_source], None, source, column)
    start_pieces(first, first_sems)
    later = [((ref,), None, slabs.at[place]) for ref, place in zip(ready, (0, 1, 3))]
    near_sources = [third_source, neighbour_source]
    later += source_pieces(near_sources, at_direct, given_source, column)
    later += source_pieces(near_sources[::-1], at_direct, kept_source, column)
    start_pieces(later, later_sems)
    wait_pieces(first, first_sems)
    transform_in(source, target, windows, cas, turned, slabs.at[2])
    wait_pieces(later, later_sems)

    transform_x([slabs.at[place] for place in range(4)], into, outof, square)

    leave = [((slabs.at[2],), None, far_out), ((slabs.at[0],), None, own_out)]
    start_pieces(leave, out_sems)
    kept_place = jnp.where(at_direct, 1, 3)
    transform_out(slabs.at[4 - kept_place], given_source, windows_back, cas, turned, given)
    transform_out(slabs.at[kept_place], kept_source, windows_back, cas, turned, kept)
    wait_pieces(leave, out_sems)


def window_tables(cas_matrix):
    extent = cas_matrix.shape[0]
    tables = []
    for r in range(quad):
        shift = r * extent % lanes
        tables.append(jnp.pad(cas_matrix, ((shift, 2 * lanes - extent - shift), (0, 2 * lanes - extent))))
    return jnp.stack(tables)


limit = 63 * 2**20
whole = pl.BlockSpec(memory_space=pltpu.VMEM)
outside = pl.BlockSpec(memory_space=pl.ANY)
scalars = pl.BlockSpec(memory_space=pltpu.SMEM)
small = pl.CostEstimate(flops=10**6, bytes_accessed=10**4, transcendentals=0)


def pick(orbitals, source_index, which, widths):
    planes = orbitals.shape[1]
    return pl.pallas_call(
        functools.partial(pick_kernel, which),
        out_shape=[jax.ShapeDtypeStruct((planes, width), orbitals.dtype) for width in widths],
        in_specs=[scalars, outside],
        out_specs=[whole] * len(widths),
        scratch_shapes=[pltpu.SemaphoreType.DMA((len(widths),))],
        compiler_params=pltpu.CompilerParams(vmem_limit_bytes=limit),
        cost_estimate=small,
        name="pick",
    )(source_index, orbitals)


def cut_quarters(source_index, orbitals, crossed):
    planes, points = crossed.shape
    return pl.pallas_call(
        cut_kernel,
        out_shape=[jax.ShapeDtypeStruct((planes, points // 4), crossed.dtype)] * 4,
        in_specs=[scalars, outside, outside],
        out_specs=[whole] * 4,
        scratch_shapes=[pltpu.SemaphoreType.DMA((4,))],
        compiler_params=pltpu.CompilerParams(vmem_limit_bytes=limit),
        cost_estimate=small,
        name="cut",
    )(source_index, orbitals, crossed)


def put(parity, first, near, *choices):
    pieces = near + [piece for choice in choices for piece in choice]
    planes, points = near[0].shape[0], sum(piece.shape[1] for piece in near)
    return pl.pallas_call(
        functools.partial(put_kernel, 2 * len(choices[0])),
        out_shape=jax.ShapeDtypeStruct((2, planes, points), near[0].dtype),
        in_specs=[scalars] + [outside] * len(pieces),
        out_specs=outside,
        scratch_shapes=[
            pltpu.VMEM((2, planes, points), near[0].dtype),
            pltpu.SemaphoreType.DMA((len(near) + len(choices[0]),)),
            pltpu.SemaphoreType.DMA((len(near) + len(choices[0]),)),
        ],
        compiler_params=pltpu.CompilerParams(vmem_limit_bytes=limit),
        cost_estimate=small,
        name="put",
    )(jnp.stack([parity, first.astype(parity.dtype)]).astype(jnp.int32), *pieces)


def forward(flags, first, targets, group, tables):
    planes = group[0].shape[1]
    extent = tables[0].shape[0]
    points = extent * extent
    return pl.pallas_call(
        functools.partial(forward_kernel, first, len(targets), len(targets[0])),
        out_shape=jax.ShapeDtypeStruct((2, extent * plane_pitch, lanes), jnp.float32),
        in_specs=[scalars] + [outside] * (len(targets) * len(targets[0]) + len(group)) + [whole] * len(tables),
        out_specs=whole,
        scratch_shapes=[
            pltpu.VMEM((planes, points), jnp.bfloat16),
            pltpu.VMEM((planes, points), jnp.bfloat16),
            pltpu.VMEM((2, planes * turned_pitch, lanes), jnp.float32),
            pltpu.SemaphoreType.DMA((len(targets[0]) + 5,)),
        ],
        compiler_params=pltpu.CompilerParams(vmem_limit_bytes=limit),
        cost_estimate=small,
        name="forward",
    )(flags, *[piece for choice in targets for piece in choice], *group, *tables)


def central(flags, direct, ready, targets, neighbour_source, second_source, third_source, tables):
    planes = second_source[0].shape[1]
    extent = tables[0].shape[0]
    points = extent * extent
    pieces = [*ready, *targets[0], *targets[1], *neighbour_source, *second_source, *third_source]
    parts = [jax.ShapeDtypeStruct((planes, share * points // 5), jnp.bfloat16) for share in (2, 3)]
    slab = jax.ShapeDtypeStruct(ready[0].shape, jnp.float32)
    outs = pl.pallas_call(
        functools.partial(central_kernel, direct),
        out_shape=parts * 2 + [slab] * 2,
        in_specs=[scalars] + [outside] * len(pieces) + [whole] * len(tables),
        out_specs=[whole] * 4 + [outside] * 2,
        scratch_shapes=[
            pltpu.VMEM((ring, *slab.shape), jnp.float32),
            *[pltpu.VMEM((planes, points), jnp.bfloat16)] * 4,
            pltpu.VMEM((2, planes * turned_pitch, lanes), jnp.float32),
            pltpu.SemaphoreType.DMA((len(targets[0]) + 5,)),
            pltpu.SemaphoreType.DMA((13,)),
            pltpu.SemaphoreType.DMA((2,)),
        ],
        compiler_params=pltpu.CompilerParams(vmem_limit_bytes=limit),
        cost_estimate=small,
        name="central",
    )(flags, *pieces, *tables)
    return split(outs, 2, 2, 2)


def backward(flags, first, slabs, groups, cas_matrix, windows, parts):
    planes = groups[0][0].shape[1]
    extent = cas_matrix.shape[0]
    points = extent * extent
    pieces = [piece for group in groups for piece in group]
    return pl.pallas_call(
        functools.partial(backward_kernel, first, parts),
        out_shape=[jax.ShapeDtypeStruct((planes, points // parts), jnp.bfloat16)] * parts,
        in_specs=[scalars] + [outside] * (len(slabs) + len(pieces)) + [whole] * 2,
        out_specs=[whole] * parts,
        scratch_shapes=[
            pltpu.VMEM(slabs[0].shape, jnp.float32),
            pltpu.VMEM((planes, points), jnp.bfloat16),
            pltpu.VMEM((2, planes * turned_pitch, lanes), jnp.float32),
            pltpu.SemaphoreType.DMA((6,)),
        ],
        compiler_params=pltpu.CompilerParams(vmem_limit_bytes=limit),
        cost_estimate=small,
        name="backward",
    )(flags, *slabs, *pieces, cas_matrix, windows)


def add(a, b):
    return (a.astype(jnp.float32) + b.astype(jnp.float32)).astype(jnp.bfloat16)


def pair_plan(orbitals, source_index):
    local_count, planes, points = orbitals.shape
    slabs = lax.axis_size("grid")
    extent = planes * slabs
    band, z = lax.axis_index("band"), lax.axis_index("grid")
    column, core = band // cores, band % cores
    quarter = points // 4
    at_home = core == holder(z)
    direct_neighbour = core == 1 - z % 2
    parity = z % 2
    inner = (z == 1) | (z == 2)
    flags = jnp.stack([core, column, at_home, direct_neighbour]).astype(jnp.int32)
    home, direct = 2, 3

    unit = points // 8

    def first_pieces(source_index):
        core = lax.rem(lax.axis_index("band"), cores)
        near_parity = lax.rem(lax.axis_index("grid") + 1, 2)
        candidate = lax.rem(source_index[1 - core], local_count)
        return [(candidate, 0)] + [(near_parity, start) for start in (0, unit, 6 * unit)]

    def own_orbital(source_index):
        return [(lax.rem(lax.axis_index("grid"), 2), 0)]

    other, *to_near = pick(orbitals, source_index, first_pieces, (points, unit, 5 * unit, 2 * unit))
    crossed = swap_cores(other)
    near = [move(to_near[0], near_routes())]
    owner = source_index[core] // local_count

    cuts, to_near = stage((cut_quarters(source_index, orbitals, crossed), to_near), near)
    near.append(move(to_near[1], near_routes()))
    candidates = [cuts[0]] + [to_column(cuts[d], d) for d in (1, 2, 3)]
    (own_parity,) = pick(stage(orbitals, cuts), source_index, own_orbital, (points,))
    cas_matrix = cas_table(extent)
    windows = window_tables(cas_matrix)
    windows_back = jnp.swapaxes(windows, 1, 2)
    places = (((z ^ jnp.arange(slabs)) * planes)[:, None] + jnp.arange(planes)).reshape(extent)
    into = cas_entries(jnp.arange(extent), places, extent)
    square_x = wave_square(jnp.arange(extent, dtype=jnp.int32), extent)
    strength = (extent * spacing) ** 2 / math.pi
    square = (square_x[:, None] + square_x[None, :] + 1.0) * (1.0 / strength)
    square = jnp.pad(square, ((0, 0), (0, 2 * lanes - extent)), constant_values=1.0)
    tables = [cas_matrix, windows, windows_back, into, into.T, square]

    candidates, tables, own_parity, flags = stage((candidates, tables, own_parity, flags), near)
    cas_matrix, windows, windows_back, into, outof, square = tables
    forward_tables = [cas_matrix, windows, into, outof]
    own = lax.select_n(column ^ (owner // cores), *candidates)
    own = stage(own, tables)
    own_swapped = swap_cores(own_parity)
    own_x, own_y = to_column(own, 1), to_column(own, 2)
    neighbour = to_height(own, {0: 1, 1: 0, 2: 3, 3: 2})
    crossed = to_height(own, {1: 2, 2: 1})

    neighbour, crossed, own_x, own_y, own_swapped = stage((neighbour, crossed, own_x, own_y, own_swapped))
    neighbour_x, neighbour_y = to_column(neighbour, 1), to_column(neighbour, 2)
    near_swapped = [swap_cores(stage(near[0], neighbour))]
    crossed_2 = to_height(neighbour, {1: 2, 2: 1})
    handed = to_height(crossed, {1: 0, 2: 3})

    low = jnp.stack([own_x[:, : quarter // 2], neighbour_x[:, : quarter // 2]])
    high = jnp.stack([own_y[:, quarter // 2 :], neighbour_y[:, quarter // 2 :]])
    staged = stage((low, high, crossed_2, own_parity, own_swapped, to_near[2]), handed, near_swapped)
    low, high, crossed_2, own_parity, own_swapped, last = staged
    low, high = to_column(low, 2), to_column(high, 1)
    handed_2 = to_height(crossed_2, {1: 0, 2: 3})
    near.append(move(last, near_routes()))
    to_far = jnp.where(at_home, own_swapped, own_parity)
    far = move(lax.dynamic_slice_in_dim(to_far, core * (points // 2), points // 2, 1), far_half_routes())

    third = jnp.where(inner, crossed, handed_2)[None]
    second = jnp.where(inner, crossed_2, handed)[None]
    third, second, low, high = stage((third, second, low, high))
    sources = [
        [own[None], own_x[None], own_y[None], low[:1], high[:1]],
        [neighbour[None], neighbour_x[None], neighbour_y[None], low[1:], high[1:]],
    ]
    third_x, third_y = to_column(third, 1), to_column(third, 2)
    near_swapped.append(swap_cores(stage(near[1], third)))
    along_y = [forward(flags, home, [[own_parity], [own_swapped]], sources[0], forward_tables)]

    staged = stage((third_x, third_y, second, near_swapped, near), along_y)
    third_x, third_y, second, near_swapped, near = staged
    low, high = to_column(third_x[:, :, : quarter // 2], 2), to_column(third_y[:, :, quarter // 2 :], 1)
    second_x, second_y = to_column(second, 1), to_column(second, 2)
    near_swapped.append(swap_cores(near[2]))
    along_y.append(forward(flags, direct, [near, near_swapped], sources[1], forward_tables))

    low, high, second_x, second_y, far = stage((low, high, second_x, second_y, far), along_y)
    third_source = [third, third_x, third_y, low, high]
    low, high = to_column(second_x[:, :, : quarter // 2], 2), to_column(second_y[:, :, quarter // 2 :], 1)
    along_y_3 = forward(flags, direct, [near_swapped, near], third_source, forward_tables)
    low, high, far_swapped = stage((low, high, swap_cores(far)), along_y_3)
    second_source = [second, second_x, second_y, low, high]
    sources += [second_source, third_source]
    given, kept, (own_back, far_back) = central(
        flags,
        direct,
        [*along_y, along_y_3],
        [[far_swapped, far], [far, far_swapped]],
        sources[1],
        second_source,
        third_source,
        [cas_matrix, windows, windows_back, into, outof, square],
    )

    def partials(places, slabs, *earlier):
        groups = [sources[place] for place in places]
        return backward(flags, home, stage(slabs, *earlier), groups, cas_matrix, windows_back, 4)

    near = [add(k, swap_cores(g)) for k, g in zip(kept, given)]
    near_home = [move(part, back(near_routes())) for part in near]
    given = partials([2, 0], [far_back, own_back], near[0])
    kept = partials([0, 2], [own_back, far_back], given[0], near_home[0])
    far = [add(k, swap_cores(g)) for k, g in zip(kept, given)]
    far_home = [move(part, back(far_routes())) for part in far]
    return put(parity, at_home, near_home, far, far_home)


def solution(mesh):
    def shards(orbitals, source_index):
        slabs, bands = mesh.shape["grid"], mesh.shape["band"]
        fits = slabs == 4 and bands == 8 and orbitals.shape[0] == 2 and source_index.shape[0] == cores
        return (pair_plan if fits else slab_plan)(orbitals, source_index)

    return jax.shard_map(
        shards,
        mesh=mesh,
        in_specs=(P("band", "grid", None), P()),
        out_specs=P("band", "grid", None),
        check_vma=False,
    )
```

```python
import functools
import math

import jax
import jax.numpy as jnp
from jax import lax
from jax.experimental import pallas as pl
from jax.experimental.pallas import tpu as pltpu
from jax.sharding import PartitionSpec as P

spacing = 0.3
cores = 2


def cas_entries(rows, columns, extent):
    products_mod = rows[:, None] * columns[None, :] % extent
    radians = products_mod.astype(jnp.float32) * (2.0 * math.pi / extent)
    return ((jnp.cos(radians) + jnp.sin(radians)) / math.sqrt(extent)).astype(jnp.bfloat16)


def cas_table(extent):
    wavenum = jnp.arange(extent, dtype=jnp.int32)
    return cas_entries(wavenum, wavenum, extent)


def wave_square(indices, extent):
    folded = jnp.minimum(indices, extent - indices).astype(jnp.float32)
    return folded * folded


def coulomb_block(extent, columns, offset):
    square_x = wave_square(jnp.arange(extent, dtype=jnp.int32), extent)
    square_y = wave_square(offset + jnp.arange(columns, dtype=jnp.int32), extent)
    total_sq = square_x[:, None, None] + square_y[None, :, None] + square_x[None, None, :]
    strength = (extent * spacing) ** 2 / math.pi
    return jnp.where(total_sq > 0, strength / (total_sq + 1.0), 0.0)


def transform(grid_data, cas_matrix, pattern):
    return jnp.einsum(pattern, grid_data, cas_matrix, preferred_element_type=jnp.float32)


def broadcast(x, axis, root):
    mine = lax.axis_index(axis) == root
    return lax.psum(jnp.where(mine, x, jnp.zeros_like(x)), axis)


def slab_potentials(pair_rho, cas_matrix, kernel_block):
    along_z = transform(pair_rho, cas_matrix, "pxyz,kz->pxyk").astype(jnp.bfloat16)
    along_y = transform(along_z, cas_matrix, "pxyz,ky->pxkz").astype(jnp.bfloat16)
    turned = lax.all_to_all(along_y, "grid", split_axis=2, concat_axis=1, tiled=True)
    scaled = (kernel_block * transform(turned, cas_matrix, "pxyz,kx->pkyz")).astype(jnp.bfloat16)
    back_x = transform(scaled, cas_matrix, "pxyz,kx->pkyz").astype(jnp.bfloat16)
    returned = lax.all_to_all(back_x, "grid", split_axis=1, concat_axis=2, tiled=True)
    again_y = transform(returned, cas_matrix, "pxyz,ky->pxkz").astype(jnp.bfloat16)
    return transform(again_y, cas_matrix, "pxyz,kz->pxyk")


def fetch_source(orbitals, which):
    local_count = orbitals.shape[0]
    local_slab = lax.dynamic_index_in_dim(orbitals, which % local_count, 0, keepdims=False)
    return broadcast(local_slab, "band", which // local_count)


def slab_plan(orbitals, source_index):
    local_count, planes, _ = orbitals.shape
    extent = planes * lax.axis_size("grid")
    orbitals = orbitals.reshape(local_count, planes, extent, extent)
    source_count = source_index.shape[0]
    cas_matrix = cas_table(extent)
    columns = extent // lax.axis_size("grid")
    kernel_block = coulomb_block(extent, columns, lax.axis_index("grid") * columns)
    fetched = [fetch_source(orbitals, source_index[number]) for number in range(source_count)]
    stacked = jnp.stack(fetched)[:, None].astype(jnp.float32)
    pair_rho = (stacked * orbitals[None].astype(jnp.float32)).astype(jnp.bfloat16)
    pair_rho = pair_rho.reshape(source_count * local_count, planes, extent, extent)
    potential = slab_potentials(pair_rho, cas_matrix, kernel_block)
    potential = potential.reshape(source_count, local_count, planes, extent, extent)
    result = (-jnp.sum(stacked * potential, axis=0)).astype(jnp.bfloat16)
    return result.reshape(local_count, planes, extent * extent)


lanes = 128
quad = 4
ring = 4
turned_pitch = 161
plane_pitch = 41


def move(x, routes):
    slabs = lax.axis_size("grid")

    def place(column, core, z):
        return (column * cores + core) * slabs + z % slabs

    return lax.ppermute(x, ("band", "grid"), [(place(*a), place(*b)) for a, b in routes])


def everywhere():
    columns = lax.axis_size("band") // cores
    return [(c, k, z) for c in range(columns) for k in range(cores) for z in range(lax.axis_size("grid"))]


def swap_cores(x):
    return move(x, [((c, k, z), (c, 1 - k, z)) for c, k, z in everywhere()])


def to_column(x, d):
    return move(x, [((c, k, z), (c ^ d, k, z)) for c, k, z in everywhere()])


def to_height(x, to):
    return move(x, [((c, k, z), (c, k, to[z])) for c, k, z in everywhere() if z in to])


def holder(z):
    return z % ring // 2


def side(core):
    return 2 * core - 1


def near_routes():
    return [((c, holder(z), z + side(k)), (c, k, z)) for c, k, z in everywhere()]


def far_routes():
    return [((c, holder(z), z + 2), (c, k, z)) for c, k, z in everywhere() if k != holder(z)]


def back(routes):
    return [(b, a) for a, b in routes]


def stage(values, *earlier):
    return lax.optimization_barrier((values, earlier))[0]


def choose(first, refs, start):
    if len(refs) == 1:
        start(refs[0])
    else:
        pl.when(first)(lambda: start(refs[0]))
        pl.when(jnp.logical_not(first))(lambda: start(refs[1]))


def start_pieces(pieces, sems):
    for number, (refs, first, to) in enumerate(pieces):
        choose(first, refs, lambda ref, to=to, number=number: pltpu.make_async_copy(ref, to, sems.at[number]).start())


def wait_pieces(pieces, sems):
    for number, (refs, _, to) in enumerate(pieces):
        pltpu.make_async_copy(refs[0], to, sems.at[number]).wait()


def source_of(refs, flags, place):
    return refs, flags[2 + place] if place > 1 else 0


def source_pieces(groups, first, source, column):
    quarter = source.shape[1] // 4
    offsets = [(column ^ e) * quarter for e in range(4)]
    offsets.append(offsets[3] + quarter // 2)
    pieces = []
    for number, offset in enumerate(offsets):
        refs = [five[number].at[which] for five, which in groups]
        to = source.at[:, pl.ds(pl.multiple_of(offset, lanes), refs[0].shape[1])]
        pieces.append((refs, first, to))
    return pieces


def split(refs, *counts):
    taken = []
    for count in counts:
        taken.append(refs[:count])
        refs = refs[count:]
    return taken


def dot(a, b):
    return jnp.dot(a, b, preferred_element_type=jnp.float32)


def both(ref, rows):
    return jnp.concatenate([ref[0, rows, :], ref[1, rows, :]], axis=1)


def beside(values):
    return jnp.concatenate(values, axis=1)


def apart(value):
    return [value[:, n : n + 2 * lanes] for n in range(0, value.shape[1], 2 * lanes)]


def put_both(ref, rows, value):
    ref[0, rows, :] = value[:, :lanes]
    ref[1, rows, :] = value[:, lanes:]


def lane_ranges(pieces):
    ranges = []
    start = 0
    for piece in pieces:
        ranges.append((start, piece.shape[1]))
        start += piece.shape[1]
    return ranges


def pick_kernel(which, source_index, orbitals, *refs):
    outs, sems = refs[:-1], refs[-1]
    copies = []
    for n, (out, (orbital, start)) in enumerate(zip(outs, which(source_index))):
        copies.append(pltpu.make_async_copy(orbitals.at[orbital, :, pl.ds(start, out.shape[1])], out, sems.at[n]))
    for copy in copies:
        copy.start()
    for copy in copies:
        copy.wait()


def cut_kernel(source_index, orbitals, crossed, *refs):
    outs, sems = refs[:-1], refs[-1]
    local_count = orbitals.shape[0]
    band = lax.axis_index("band")
    core, column = lax.rem(band, cores), lax.div(band, cores)
    which = lax.rem(source_index[core], local_count)
    owner = lax.rem(lax.div(source_index[core], local_count), cores)
    width = outs[0].shape[1]
    pieces = []
    for d, out in enumerate(outs):
        lane = pl.ds(pl.multiple_of((column ^ d) * width, lanes), width)
        pieces.append(((orbitals.at[which, :, lane], crossed.at[:, lane]), owner == core, out))
    start_pieces(pieces, sems)
    wait_pieces(pieces, sems)


def put_kernel(count, flags, *refs):
    (out, staged, sems, out_sems), refs = refs[-4:], refs[:-4]
    near, choices = refs[:-count], refs[-count:]
    half = count // 2
    places = [(1 - flags[0], pl.ds(*lane)) for lane in lane_ranges(near)]
    places += [(flags[0], pl.ds(*lane)) for lane in lane_ranges(choices[:half])]
    chosen = [(ref,) for ref in near] + [choices[n::half] for n in range(half)]
    pieces = [(refs, flags[1] == 1, staged.at[which, :, lane]) for refs, (which, lane) in zip(chosen, places)]
    start_pieces(pieces, sems)
    leave = []
    for number, (which, lane) in enumerate(places):
        piece = staged.at[which, :, lane]
        pltpu.make_async_copy(chosen[number][0], piece, sems.at[number]).wait()
        leave.append(pltpu.make_async_copy(piece, out.at[which, :, lane], out_sems.at[number]))
        leave[-1].start()
    for copy in leave:
        copy.wait()


def transform_in(source, target, windows, cas, turned, out):
    planes, points = target.shape
    extent = cas.shape[0]
    step = 8
    block = quad * extent

    @pl.loop(0, points // block // step)
    def _(i):
        for r in range(quad):
            density = []
            for j in range(step):
                at = pl.ds(pl.multiple_of((i * step + j) * block + r * lanes, lanes), 2 * lanes)
                density.append(source[:, at].astype(jnp.float32) * target[:, at].astype(jnp.float32))
            density = jnp.concatenate(density, axis=0).astype(jnp.bfloat16)
            along_z = dot(density, windows[r])
            for j in range(step):
                y = (i * step + j) * quad + r
                put_both(turned, pl.ds(y, planes, stride=turned_pitch), along_z[j * planes : (j + 1) * planes])

    @pl.loop(0, planes // 4)
    def _(i):
        for j in range(4):
            x = i * 4 + j
            along_z = both(turned, pl.ds(x * turned_pitch, extent)).astype(jnp.bfloat16)
            put_both(out, pl.ds(x, extent, stride=plane_pitch), dot(cas[...], along_z))


def transform_x(slabs, into, outof, square):
    extent = square.shape[0]
    planes = extent // ring
    strength = (extent * spacing) ** 2 / math.pi
    rows = 8

    def factor_of(folded):
        weight = square[...] + (folded * folded).astype(jnp.float32) * (1.0 / strength)
        guess = pl.reciprocal(weight, approx=True)
        return guess * (2.0 - weight * guess), weight

    def transform(start, factor):
        at = pl.ds(start, planes)
        along_y = jnp.concatenate([both(slab, at) for slab in slabs], axis=0).astype(jnp.bfloat16)
        scaled = (factor * dot(into[...], along_y)).astype(jnp.bfloat16)
        back_x = dot(outof[...], scaled)
        for n, slab in enumerate(slabs):
            put_both(slab, at, back_x[n * planes : (n + 1) * planes])

    def pair(first, last, i, ky):
        factor, _ = factor_of(ky)
        transform(first + i * plane_pitch, factor)
        transform(last - i * plane_pitch, factor)

    end = extent * plane_pitch
    factor, weight = factor_of(jnp.int32(0))
    transform(0, jnp.where(weight > 1.25 / strength, factor, 0.0))
    transform(end // 2, factor_of(jnp.int32(extent // 2))[0])
    for i in range(1, rows):
        pair(0, end, i, jnp.int32(i))

    @pl.loop(1, extent // 2 // rows)
    def _(step):
        first = pl.multiple_of(step * rows * plane_pitch, 8)
        last = pl.multiple_of(end - step * rows * plane_pitch, 8)
        for i in range(rows):
            pair(first, last, i, step * rows + i)


def transform_out(back_x, source, windows, cas, turned, outs):
    planes, points = source.shape
    extent = cas.shape[0]

    @pl.loop(0, planes // 4)
    def _(i):
        for j in range(4):
            x = i * 4 + j
            column_x = both(back_x, pl.ds(x, extent, stride=plane_pitch)).astype(jnp.bfloat16)
            put_both(turned, pl.ds(x * turned_pitch, extent), dot(cas[...], column_x))

    block = quad * extent
    begin = 0
    for out in outs:
        blocks = out.shape[1] // block
        step = 5 if blocks % 5 == 0 else 4

        @pl.loop(0, blocks // step)
        def _(i, begin=begin, step=step, out=out):
            first = begin + i * step
            windowed = []
            for r in range(quad):
                again_y = jnp.concatenate(
                    [both(turned, pl.ds((first + j) * quad + r, planes, stride=turned_pitch)) for j in range(step)],
                    axis=0,
                ).astype(jnp.bfloat16)
                windowed.append(dot(again_y, windows[r]))
            for j in range(step):
                w = [part[j * planes : (j + 1) * planes] for part in windowed]
                potential = [w[0][:, :lanes]]
                potential += [w[r][:, lanes:] + w[r + 1][:, :lanes] for r in range(quad - 1)]
                potential = jnp.concatenate(potential + [w[-1][:, lanes:]], axis=1)
                at = pl.ds(pl.multiple_of((first + j) * block, lanes), block)
                to = pl.ds(pl.multiple_of((i * step + j) * block, lanes), block)
                out[:, to] = (-(source[:, at].astype(jnp.float32) * potential)).astype(jnp.bfloat16)

        begin += blocks


def forward_kernel(place, first, choices, count, flags, *refs):
    targets, five, (cas, windows, _, _, out, target, source, turned, sems) = split(refs, choices * count, 5, 9)
    ranges = lane_ranges(targets[:count])
    pieces = [(targets[n::count], flags[first] == 1, target.at[:, pl.ds(*lane)]) for n, lane in enumerate(ranges)]
    pieces += source_pieces([source_of(five, flags, place)], None, source, flags[1])
    start_pieces(pieces, sems)
    wait_pieces(pieces, sems)
    transform_in(source, target, windows, cas, turned, out)


def backward_kernel(places, first, parts, flags, *refs):
    slabs, groups, (cas, windows), outs, (back_x, source, turned, sems) = split(
        refs, len(places), 5 * len(places), 2, parts, 4
    )
    chosen = [source_of(five, flags, place) for five, place in zip(split(groups, *[5] * len(places)), places)]
    pieces = [(slabs, flags[first] == 1, back_x)] + source_pieces(chosen, flags[first] == 1, source, flags[1])
    start_pieces(pieces, sems)
    wait_pieces(pieces, sems)
    transform_out(back_x, source, windows, cas, turned, outs)


def central_kernel(home, direct, flags, *refs):
    ready, targets, neighbour_source, across_source, tables, outs, scratch = split(
        refs, 3, len(refs) - 34, 5, 5, 6, 6, 9
    )
    cas, windows, windows_back, into, outof, square = tables
    given, kept, (own_out, far_out) = split(outs, 2, 2, 2)
    slabs, target, source, given_source, kept_source, turned, first_sems, later_sems, out_sems = scratch
    at_direct = flags[direct] == 1
    column = flags[1]

    count = len(targets) // 2
    ranges = lane_ranges(targets[:count])
    first = [(targets[n::count], flags[home] == 1, target.at[:, pl.ds(*lane)]) for n, lane in enumerate(ranges)]
    first += source_pieces([source_of(across_source, flags, 2)], None, source, column)
    start_pieces(first, first_sems)
    later = [((ref,), None, slabs.at[place]) for ref, place in zip(ready, (0, 1, 3))]
    near_sources = [source_of(across_source, flags, 3), source_of(neighbour_source, flags, 1)]
    later += source_pieces(near_sources, at_direct, given_source, column)
    later += source_pieces(near_sources[::-1], at_direct, kept_source, column)
    start_pieces(later, later_sems)
    wait_pieces(first, first_sems)
    transform_in(source, target, windows, cas, turned, slabs.at[2])
    wait_pieces(later, later_sems)

    transform_x([slabs.at[place] for place in range(4)], into, outof, square)

    leave = [((slabs.at[2],), None, far_out), ((slabs.at[0],), None, own_out)]
    start_pieces(leave, out_sems)
    kept_place = jnp.where(at_direct, 1, 3)
    transform_out(slabs.at[4 - kept_place], given_source, windows_back, cas, turned, given)
    transform_out(slabs.at[kept_place], kept_source, windows_back, cas, turned, kept)
    wait_pieces(leave, out_sems)


def window_tables(cas_matrix):
    extent = cas_matrix.shape[0]
    tables = []
    for r in range(quad):
        shift = r * extent % lanes
        tables.append(jnp.pad(cas_matrix, ((shift, 2 * lanes - extent - shift), (0, 2 * lanes - extent))))
    return jnp.stack(tables)


limit = 60 * 2**20
full = 64 * 2**20
whole = pl.BlockSpec(memory_space=pltpu.VMEM)
outside = pl.BlockSpec(memory_space=pl.ANY)
scalars = pl.BlockSpec(memory_space=pltpu.SMEM)
small = pl.CostEstimate(flops=10**6, bytes_accessed=10**4, transcendentals=0)


def pick(orbitals, source_index, which, widths):
    planes = orbitals.shape[1]
    return pl.pallas_call(
        functools.partial(pick_kernel, which),
        out_shape=[jax.ShapeDtypeStruct((planes, width), orbitals.dtype) for width in widths],
        in_specs=[scalars, outside],
        out_specs=[whole] * len(widths),
        scratch_shapes=[pltpu.SemaphoreType.DMA((len(widths),))],
        compiler_params=pltpu.CompilerParams(vmem_limit_bytes=limit),
        cost_estimate=small,
        name="pick",
    )(source_index, orbitals)


def cut_quarters(source_index, orbitals, crossed):
    planes, points = crossed.shape
    return pl.pallas_call(
        cut_kernel,
        out_shape=[jax.ShapeDtypeStruct((planes, points // 4), crossed.dtype)] * 4,
        in_specs=[scalars, outside, outside],
        out_specs=[whole] * 4,
        scratch_shapes=[pltpu.SemaphoreType.DMA((4,))],
        compiler_params=pltpu.CompilerParams(vmem_limit_bytes=full),
        cost_estimate=small,
        name="cut",
    )(source_index, orbitals, crossed)


def put(parity, first, near, *choices):
    pieces = near + [piece for choice in choices for piece in choice]
    planes, points = near[0].shape[0], sum(piece.shape[1] for piece in near)
    return pl.pallas_call(
        functools.partial(put_kernel, 2 * len(choices[0])),
        out_shape=jax.ShapeDtypeStruct((2, planes, points), near[0].dtype),
        in_specs=[scalars] + [outside] * len(pieces),
        out_specs=outside,
        scratch_shapes=[
            pltpu.VMEM((2, planes, points), near[0].dtype),
            pltpu.SemaphoreType.DMA((len(near) + len(choices[0]),)),
            pltpu.SemaphoreType.DMA((len(near) + len(choices[0]),)),
        ],
        compiler_params=pltpu.CompilerParams(vmem_limit_bytes=full),
        cost_estimate=small,
        name="put",
    )(jnp.stack([parity, first.astype(parity.dtype)]).astype(jnp.int32), *pieces)


def forward(flags, place, first, targets, group, tables):
    planes = group[0].shape[1]
    extent = tables[0].shape[0]
    points = extent * extent
    return pl.pallas_call(
        functools.partial(forward_kernel, place, first, len(targets), len(targets[0])),
        out_shape=jax.ShapeDtypeStruct((2, extent * plane_pitch, lanes), jnp.float32),
        in_specs=[scalars] + [outside] * (len(targets) * len(targets[0]) + len(group)) + [whole] * len(tables),
        out_specs=whole,
        scratch_shapes=[
            pltpu.VMEM((planes, points), jnp.bfloat16),
            pltpu.VMEM((planes, points), jnp.bfloat16),
            pltpu.VMEM((2, planes * turned_pitch, lanes), jnp.float32),
            pltpu.SemaphoreType.DMA((len(targets[0]) + 5,)),
        ],
        compiler_params=pltpu.CompilerParams(vmem_limit_bytes=limit),
        cost_estimate=small,
        name="forward",
    )(flags, *[piece for choice in targets for piece in choice], *group, *tables)


def central(flags, home, direct, ready, targets, neighbour_source, across_source, tables):
    planes = across_source[0].shape[1]
    extent = tables[0].shape[0]
    points = extent * extent
    pieces = [*ready, *targets[0], *targets[1], *neighbour_source, *across_source]
    parts = [jax.ShapeDtypeStruct((planes, share * points // 5), jnp.bfloat16) for share in (2, 3)]
    slab = jax.ShapeDtypeStruct(ready[0].shape, jnp.float32)
    outs = pl.pallas_call(
        functools.partial(central_kernel, home, direct),
        out_shape=parts * 2 + [slab] * 2,
        in_specs=[scalars] + [outside] * len(pieces) + [whole] * len(tables),
        out_specs=[whole] * 4 + [outside] * 2,
        scratch_shapes=[
            pltpu.VMEM((ring, *slab.shape), jnp.float32),
            *[pltpu.VMEM((planes, points), jnp.bfloat16)] * 4,
            pltpu.VMEM((2, planes * turned_pitch, lanes), jnp.float32),
            pltpu.SemaphoreType.DMA((len(targets[0]) + 5,)),
            pltpu.SemaphoreType.DMA((13,)),
            pltpu.SemaphoreType.DMA((2,)),
        ],
        compiler_params=pltpu.CompilerParams(vmem_limit_bytes=full),
        cost_estimate=small,
        name="central",
    )(flags, *pieces, *tables)
    return split(outs, 2, 2, 2)


def backward(flags, places, first, slabs, groups, cas_matrix, windows, parts):
    planes = groups[0][0].shape[1]
    extent = cas_matrix.shape[0]
    points = extent * extent
    pieces = [piece for group in groups for piece in group]
    return pl.pallas_call(
        functools.partial(backward_kernel, places, first, parts),
        out_shape=[jax.ShapeDtypeStruct((planes, points // parts), jnp.bfloat16)] * parts,
        in_specs=[scalars] + [outside] * (len(slabs) + len(pieces)) + [whole] * 2,
        out_specs=[whole] * parts,
        scratch_shapes=[
            pltpu.VMEM(slabs[0].shape, jnp.float32),
            pltpu.VMEM((planes, points), jnp.bfloat16),
            pltpu.VMEM((2, planes * turned_pitch, lanes), jnp.float32),
            pltpu.SemaphoreType.DMA((6,)),
        ],
        compiler_params=pltpu.CompilerParams(vmem_limit_bytes=limit),
        cost_estimate=small,
        name="backward",
    )(flags, *slabs, *pieces, cas_matrix, windows)


def add(a, b):
    return (a.astype(jnp.float32) + b.astype(jnp.float32)).astype(jnp.bfloat16)


def pair_plan(orbitals, source_index):
    local_count, planes, points = orbitals.shape
    slabs = lax.axis_size("grid")
    extent = planes * slabs
    band, z = lax.axis_index("band"), lax.axis_index("grid")
    column, core = band // cores, band % cores
    quarter = points // 4
    at_home = core == holder(z)
    direct_neighbour = core == 1 - z % 2
    parity = z % 2
    inner = (z == 1) | (z == 2)
    second = inner.astype(jnp.int32)
    flags = jnp.stack([core, column, at_home, direct_neighbour, second, 1 - second]).astype(jnp.int32)
    home, direct = 2, 3

    unit = points // 8

    def first_pieces(source_index):
        core = lax.rem(lax.axis_index("band"), cores)
        near_parity = lax.rem(lax.axis_index("grid") + 1, 2)
        candidate = lax.rem(source_index[1 - core], local_count)
        return [(candidate, 0)] + [(near_parity, start) for start in (0, unit, 6 * unit)]

    def own_orbital(source_index):
        return [(lax.rem(lax.axis_index("grid"), 2), 0)]

    other, *to_near = pick(orbitals, source_index, first_pieces, (points, unit, 5 * unit, 2 * unit))
    crossed = swap_cores(other)
    near = [move(to_near[0], near_routes())]
    owner = source_index[core] // local_count

    cuts, to_near = stage((cut_quarters(source_index, orbitals, crossed), to_near), near)
    near.append(move(to_near[1], near_routes()))
    candidates = [cuts[0]] + [to_column(cuts[d], d) for d in (1, 2, 3)]
    (own_parity,) = pick(stage(orbitals, cuts), source_index, own_orbital, (points,))
    cas_matrix = cas_table(extent)
    windows = window_tables(cas_matrix)
    windows_back = jnp.swapaxes(windows, 1, 2)
    places = (((z ^ jnp.arange(slabs)) * planes)[:, None] + jnp.arange(planes)).reshape(extent)
    into = cas_entries(jnp.arange(extent), places, extent)
    square_x = wave_square(jnp.arange(extent, dtype=jnp.int32), extent)
    strength = (extent * spacing) ** 2 / math.pi
    square = (square_x[:, None] + square_x[None, :] + 1.0) * (1.0 / strength)
    square = jnp.pad(square, ((0, 0), (0, 2 * lanes - extent)), constant_values=1.0)
    tables = [cas_matrix, windows, windows_back, into, into.T, square]

    candidates, tables, own_parity, flags = stage((candidates, tables, own_parity, flags), near)
    cas_matrix, windows, windows_back, into, outof, square = tables
    forward_tables = [cas_matrix, windows, into, outof]
    own = lax.select_n(column ^ (owner // cores), *candidates)
    own = stage(own, tables)
    own_swapped = swap_cores(own_parity)
    own_x, own_y = to_column(own, 1), to_column(own, 2)
    neighbour = to_height(own, {0: 1, 1: 0, 2: 3, 3: 2})
    crossed = to_height(own, {1: 2, 2: 1})

    neighbour, crossed, own_x, own_y, own_swapped = stage((neighbour, crossed, own_x, own_y, own_swapped))
    neighbour_x, neighbour_y = to_column(neighbour, 1), to_column(neighbour, 2)
    crossed_2 = to_height(neighbour, {1: 2, 2: 1})
    handed = to_height(crossed, {1: 0, 2: 3})

    low = jnp.stack([own_x[:, : quarter // 2], neighbour_x[:, : quarter // 2]])
    high = jnp.stack([own_y[:, quarter // 2 :], neighbour_y[:, quarter // 2 :]])
    low, high, crossed_2, own_parity, last = stage((low, high, crossed_2, own_parity, to_near[2]), handed)
    low, high = to_column(low, 2), to_column(high, 1)
    handed_2 = to_height(crossed_2, {1: 0, 2: 3})
    near.append(move(last, near_routes()))
    far = [move(own_parity, far_routes())]

    across = jnp.stack([jnp.where(inner, crossed, handed), jnp.where(inner, crossed_2, handed_2)])
    across, low, high = stage((across, low, high))
    sources = [
        [own[None], own_x[None], own_y[None], low[:1], high[:1]],
        [neighbour[None], neighbour_x[None], neighbour_y[None], low[1:], high[1:]],
    ]
    across_x, across_y = to_column(across, 1), to_column(across, 2)
    near_swapped = [swap_cores(part) for part in stage(near[:2], across)]
    along_y = [forward(flags, 0, home, [[own_parity], [own_swapped]], sources[0], forward_tables)]

    low, high = across_x[:, :, : quarter // 2], across_y[:, :, quarter // 2 :]
    near[2] = stage(near[2], along_y)
    near_swapped.append(swap_cores(near[2]))
    low, high, near_swapped = stage((low, high, near_swapped), along_y)
    low, high = to_column(low, 2), to_column(high, 1)
    along_y.append(forward(flags, 1, direct, [near, near_swapped], sources[1], forward_tables))

    low, high, far = stage((low, high, far), along_y)
    across_source = [across, across_x, across_y, low, high]
    sources += [across_source, across_source]
    far_swapped = [swap_cores(part) for part in far]
    along_y_3 = forward(flags, 3, direct, [near_swapped, near], across_source, forward_tables)
    far_swapped = stage(far_swapped, along_y_3)
    given, kept, (own_back, far_back) = central(
        flags,
        home,
        direct,
        [*along_y, along_y_3],
        [far_swapped, far],
        sources[1],
        across_source,
        [cas_matrix, windows, windows_back, into, outof, square],
    )

    def partials(places, slabs, *earlier):
        groups = [sources[place] for place in places]
        return backward(flags, places, home, stage(slabs, *earlier), groups, cas_matrix, windows_back, 4)

    near = [add(k, swap_cores(g)) for k, g in zip(kept, given)]
    near_home = [move(part, back(near_routes())) for part in near]
    given = partials([2, 0], [far_back, own_back], near[0])
    kept = partials([0, 2], [own_back, far_back], given[0], near_home[0])
    far = [add(k, swap_cores(g)) for k, g in zip(kept, given)]
    far_home = [move(part, back(far_routes())) for part in far]
    return put(parity, at_home, near_home, far, far_home)


def solution(mesh):
    def shards(orbitals, source_index):
        slabs, bands = mesh.shape["grid"], mesh.shape["band"]
        fits = slabs == 4 and bands == 8 and orbitals.shape[0] == 2 and source_index.shape[0] == cores
        return (pair_plan if fits else slab_plan)(orbitals, source_index)

    return jax.shard_map(
        shards,
        mesh=mesh,
        in_specs=(P("band", "grid", None), P()),
        out_specs=P("band", "grid", None),
        check_vma=False,
    )
```

```python
import functools
import math

import jax
import jax.numpy as jnp
from jax import lax
from jax.experimental import pallas as pl
from jax.experimental.pallas import tpu as pltpu
from jax.sharding import PartitionSpec as P

spacing = 0.3
cores = 2


def cas_entries(rows, columns, extent):
    products_mod = rows[:, None] * columns[None, :] % extent
    radians = products_mod.astype(jnp.float32) * (2.0 * math.pi / extent)
    return ((jnp.cos(radians) + jnp.sin(radians)) / math.sqrt(extent)).astype(jnp.bfloat16)


def cas_table(extent):
    wavenum = jnp.arange(extent, dtype=jnp.int32)
    return cas_entries(wavenum, wavenum, extent)


def wave_square(indices, extent):
    folded = jnp.minimum(indices, extent - indices).astype(jnp.float32)
    return folded * folded


def coulomb_block(extent, columns, offset):
    square_x = wave_square(jnp.arange(extent, dtype=jnp.int32), extent)
    square_y = wave_square(offset + jnp.arange(columns, dtype=jnp.int32), extent)
    total_sq = square_x[:, None, None] + square_y[None, :, None] + square_x[None, None, :]
    strength = (extent * spacing) ** 2 / math.pi
    return jnp.where(total_sq > 0, strength / (total_sq + 1.0), 0.0)


def transform(grid_data, cas_matrix, pattern):
    return jnp.einsum(pattern, grid_data, cas_matrix, preferred_element_type=jnp.float32)


def broadcast(x, axis, root):
    mine = lax.axis_index(axis) == root
    return lax.psum(jnp.where(mine, x, jnp.zeros_like(x)), axis)


def slab_potentials(pair_rho, cas_matrix, kernel_block):
    along_z = transform(pair_rho, cas_matrix, "pxyz,kz->pxyk").astype(jnp.bfloat16)
    along_y = transform(along_z, cas_matrix, "pxyz,ky->pxkz").astype(jnp.bfloat16)
    turned = lax.all_to_all(along_y, "grid", split_axis=2, concat_axis=1, tiled=True)
    scaled = (kernel_block * transform(turned, cas_matrix, "pxyz,kx->pkyz")).astype(jnp.bfloat16)
    back_x = transform(scaled, cas_matrix, "pxyz,kx->pkyz").astype(jnp.bfloat16)
    returned = lax.all_to_all(back_x, "grid", split_axis=1, concat_axis=2, tiled=True)
    again_y = transform(returned, cas_matrix, "pxyz,ky->pxkz").astype(jnp.bfloat16)
    return transform(again_y, cas_matrix, "pxyz,kz->pxyk")


def fetch_source(orbitals, which):
    local_count = orbitals.shape[0]
    local_slab = lax.dynamic_index_in_dim(orbitals, which % local_count, 0, keepdims=False)
    return broadcast(local_slab, "band", which // local_count)


def slab_plan(orbitals, source_index):
    local_count, planes, _ = orbitals.shape
    extent = planes * lax.axis_size("grid")
    orbitals = orbitals.reshape(local_count, planes, extent, extent)
    source_count = source_index.shape[0]
    cas_matrix = cas_table(extent)
    columns = extent // lax.axis_size("grid")
    kernel_block = coulomb_block(extent, columns, lax.axis_index("grid") * columns)
    fetched = [fetch_source(orbitals, source_index[number]) for number in range(source_count)]
    stacked = jnp.stack(fetched)[:, None].astype(jnp.float32)
    pair_rho = (stacked * orbitals[None].astype(jnp.float32)).astype(jnp.bfloat16)
    pair_rho = pair_rho.reshape(source_count * local_count, planes, extent, extent)
    potential = slab_potentials(pair_rho, cas_matrix, kernel_block)
    potential = potential.reshape(source_count, local_count, planes, extent, extent)
    result = (-jnp.sum(stacked * potential, axis=0)).astype(jnp.bfloat16)
    return result.reshape(local_count, planes, extent * extent)


lanes = 128
quad = 4
ring = 4
turned_pitch = 161
plane_pitch = 41


def move(x, routes):
    slabs = lax.axis_size("grid")

    def place(column, core, z):
        return (column * cores + core) * slabs + z % slabs

    return lax.ppermute(x, ("band", "grid"), [(place(*a), place(*b)) for a, b in routes])


def everywhere():
    columns = lax.axis_size("band") // cores
    return [(c, k, z) for c in range(columns) for k in range(cores) for z in range(lax.axis_size("grid"))]


def swap_cores(x):
    return move(x, [((c, k, z), (c, 1 - k, z)) for c, k, z in everywhere()])


def to_column(x, d):
    return move(x, [((c, k, z), (c ^ d, k, z)) for c, k, z in everywhere()])


def to_height(x, to):
    return move(x, [((c, k, z), (c, k, to[z])) for c, k, z in everywhere() if z in to])


def holder(z):
    return z % ring // 2


def side(core):
    return 2 * core - 1


def near_routes():
    return [((c, holder(z), z + side(k)), (c, k, z)) for c, k, z in everywhere()]


def far_routes():
    return [((c, holder(z), z + 2), (c, k, z)) for c, k, z in everywhere() if k != holder(z)]


def back(routes):
    return [(b, a) for a, b in routes]


def stage(values, *earlier):
    return lax.optimization_barrier((values, earlier))[0]


def choose(first, refs, start):
    if len(refs) == 1:
        start(refs[0])
    else:
        pl.when(first)(lambda: start(refs[0]))
        pl.when(jnp.logical_not(first))(lambda: start(refs[1]))


def start_pieces(pieces, sems):
    for number, (refs, first, to) in enumerate(pieces):
        choose(first, refs, lambda ref, to=to, number=number: pltpu.make_async_copy(ref, to, sems.at[number]).start())


def wait_pieces(pieces, sems):
    for number, (refs, _, to) in enumerate(pieces):
        pltpu.make_async_copy(refs[0], to, sems.at[number]).wait()


def source_of(refs, flags, place):
    return refs, flags[2 + place] if place > 1 else 0


def source_pieces(groups, first, source, column):
    quarter = source.shape[1] // 4
    offsets = [(column ^ e) * quarter for e in range(4)]
    offsets.append(offsets[3] + quarter // 2)
    pieces = []
    for number, offset in enumerate(offsets):
        refs = [five[number].at[which] for five, which in groups]
        to = source.at[:, pl.ds(pl.multiple_of(offset, lanes), refs[0].shape[1])]
        pieces.append((refs, first, to))
    return pieces


def split(refs, *counts):
    taken = []
    for count in counts:
        taken.append(refs[:count])
        refs = refs[count:]
    return taken


def dot(a, b):
    return jnp.dot(a, b, preferred_element_type=jnp.float32)


def both(ref, rows):
    return jnp.concatenate([ref[0, rows, :], ref[1, rows, :]], axis=1)


def beside(values):
    return jnp.concatenate(values, axis=1)


def apart(value):
    return [value[:, n : n + 2 * lanes] for n in range(0, value.shape[1], 2 * lanes)]


def put_both(ref, rows, value):
    ref[0, rows, :] = value[:, :lanes]
    ref[1, rows, :] = value[:, lanes:]


def lane_ranges(pieces):
    ranges = []
    start = 0
    for piece in pieces:
        ranges.append((start, piece.shape[1]))
        start += piece.shape[1]
    return ranges


def pick_kernel(which, source_index, orbitals, *refs):
    outs, sems = refs[:-1], refs[-1]
    copies = []
    for n, (out, (orbital, start)) in enumerate(zip(outs, which(source_index))):
        copies.append(pltpu.make_async_copy(orbitals.at[orbital, :, pl.ds(start, out.shape[1])], out, sems.at[n]))
    for copy in copies:
        copy.start()
    for copy in copies:
        copy.wait()


def cut_kernel(source_index, orbitals, crossed, *refs):
    outs, sems = refs[:-1], refs[-1]
    local_count = orbitals.shape[0]
    band = lax.axis_index("band")
    core, column = lax.rem(band, cores), lax.div(band, cores)
    which = lax.rem(source_index[core], local_count)
    owner = lax.rem(lax.div(source_index[core], local_count), cores)
    width = outs[0].shape[1]
    pieces = []
    for d, out in enumerate(outs):
        lane = pl.ds(pl.multiple_of((column ^ d) * width, lanes), width)
        pieces.append(((orbitals.at[which, :, lane], crossed.at[:, lane]), owner == core, out))
    start_pieces(pieces, sems)
    wait_pieces(pieces, sems)


def put_kernel(choices, aliased, flags, *refs):
    (out, staged, sems, out_sems), refs = refs[-4:], refs[aliased:-4]
    count = len(refs) // choices
    places = [pl.ds(*lane) for lane in lane_ranges(refs[:count])]
    chosen = [refs[n::count] for n in range(count)]
    start_pieces([(refs, flags[1] == 1, staged.at[:, lane]) for refs, lane in zip(chosen, places)], sems)
    leave = []
    for number, lane in enumerate(places):
        piece = staged.at[:, lane]
        pltpu.make_async_copy(chosen[number][0], piece, sems.at[number]).wait()
        leave.append(pltpu.make_async_copy(piece, out.at[flags[0], :, lane], out_sems.at[number]))
        leave[-1].start()
    for copy in leave:
        copy.wait()


def transform_in(source, target, windows, cas, turned, out):
    planes, points = target.shape
    extent = cas.shape[0]
    step = 10
    block = quad * extent

    @pl.loop(0, points // block // step)
    def _(i):
        for r in range(quad):
            density = []
            for j in range(step):
                at = pl.ds(pl.multiple_of((i * step + j) * block + r * lanes, lanes), 2 * lanes)
                density.append(source[:, at].astype(jnp.float32) * target[:, at].astype(jnp.float32))
            density = jnp.concatenate(density, axis=0).astype(jnp.bfloat16)
            along_z = dot(density, windows[r])
            for j in range(step):
                y = (i * step + j) * quad + r
                put_both(turned, pl.ds(y, planes, stride=turned_pitch), along_z[j * planes : (j + 1) * planes])

    @pl.loop(0, planes // 8)
    def _(i):
        for j in range(8):
            x = i * 8 + j
            along_z = both(turned, pl.ds(x * turned_pitch, extent)).astype(jnp.bfloat16)
            put_both(out, pl.ds(x, extent, stride=plane_pitch), dot(cas[...], along_z))


def transform_x(slabs, into, outof, square):
    extent = square.shape[0]
    planes = extent // ring
    strength = (extent * spacing) ** 2 / math.pi
    rows = 16

    @pl.loop(0, extent // rows)
    def _(step):
        base = pl.multiple_of(step * rows * plane_pitch, 8)
        for i in range(rows):
            at = pl.ds(base + i * plane_pitch, planes)
            along_y = jnp.concatenate([both(slab, at) for slab in slabs], axis=0).astype(jnp.bfloat16)
            ky = step * rows + i
            folded = jnp.minimum(ky, extent - ky)
            weight = square[...] + (folded * folded).astype(jnp.float32) * (1.0 / strength)
            guess = pl.reciprocal(weight, approx=True)
            factor = guess * (2.0 - weight * guess)
            factor = jnp.where(weight > 1.25 / strength, factor, 0.0)
            scaled = (factor * dot(into[...], along_y)).astype(jnp.bfloat16)
            back_x = dot(outof[...], scaled)
            for n, slab in enumerate(slabs):
                put_both(slab, at, back_x[n * planes : (n + 1) * planes])


def transform_out(back_x, source, windows, cas, turned, outs):
    planes, points = source.shape
    extent = cas.shape[0]

    @pl.loop(0, planes // 8)
    def _(i):
        for j in range(8):
            x = i * 8 + j
            column_x = both(back_x, pl.ds(x, extent, stride=plane_pitch)).astype(jnp.bfloat16)
            put_both(turned, pl.ds(x * turned_pitch, extent), dot(cas[...], column_x))

    block = quad * extent
    begin = 0
    for out in outs:
        blocks = out.shape[1] // block
        step = 5 if blocks % 5 == 0 else 4

        @pl.loop(0, blocks // step)
        def _(i, begin=begin, step=step, out=out):
            first = begin + i * step
            windowed = []
            for r in range(quad):
                again_y = jnp.concatenate(
                    [both(turned, pl.ds((first + j) * quad + r, planes, stride=turned_pitch)) for j in range(step)],
                    axis=0,
                ).astype(jnp.bfloat16)
                windowed.append(dot(again_y, windows[r]))
            for j in range(step):
                w = [part[j * planes : (j + 1) * planes] for part in windowed]
                potential = [w[0][:, :lanes]]
                potential += [w[r][:, lanes:] + w[r + 1][:, :lanes] for r in range(quad - 1)]
                potential = jnp.concatenate(potential + [w[-1][:, lanes:]], axis=1)
                at = pl.ds(pl.multiple_of((first + j) * block, lanes), block)
                to = pl.ds(pl.multiple_of((i * step + j) * block, lanes), block)
                out[:, to] = (-(source[:, at].astype(jnp.float32) * potential)).astype(jnp.bfloat16)

        begin += blocks


def forward_kernel(place, first, choices, count, flags, *refs):
    targets, five, (cas, windows, _, _, out, target, source, turned, sems) = split(refs, choices * count, 5, 9)
    ranges = lane_ranges(targets[:count])
    pieces = [(targets[n::count], flags[first] == 1, target.at[:, pl.ds(*lane)]) for n, lane in enumerate(ranges)]
    pieces += source_pieces([source_of(five, flags, place)], None, source, flags[1])
    start_pieces(pieces, sems)
    wait_pieces(pieces, sems)
    transform_in(source, target, windows, cas, turned, out)


def backward_kernel(places, first, parts, flags, *refs):
    slabs, groups, (cas, windows), outs, (back_x, source, turned, sems) = split(
        refs, len(places), 5 * len(places), 2, parts, 4
    )
    chosen = [source_of(five, flags, place) for five, place in zip(split(groups, *[5] * len(places)), places)]
    pieces = [(slabs, flags[first] == 1, back_x)] + source_pieces(chosen, flags[first] == 1, source, flags[1])
    start_pieces(pieces, sems)
    wait_pieces(pieces, sems)
    transform_out(back_x, source, windows, cas, turned, outs)


def central_kernel(home, direct, flags, *refs):
    ready, targets, neighbour_source, across_source, tables, outs, scratch = split(
        refs, 3, len(refs) - 34, 5, 5, 6, 6, 9
    )
    cas, windows, windows_back, into, outof, square = tables
    given, kept, (own_out, far_out) = split(outs, 2, 2, 2)
    slabs, target, source, given_source, kept_source, turned, first_sems, later_sems, out_sems = scratch
    at_direct = flags[direct] == 1
    column = flags[1]

    count = len(targets) // 2
    ranges = lane_ranges(targets[:count])
    first = [(targets[n::count], flags[home] == 1, target.at[:, pl.ds(*lane)]) for n, lane in enumerate(ranges)]
    first += source_pieces([source_of(across_source, flags, 2)], None, source, column)
    start_pieces(first, first_sems)
    later = [((ref,), None, slabs.at[place]) for ref, place in zip(ready, (0, 1, 3))]
    near_sources = [source_of(across_source, flags, 3), source_of(neighbour_source, flags, 1)]
    later += source_pieces(near_sources, at_direct, given_source, column)
    later += source_pieces(near_sources[::-1], at_direct, kept_source, column)
    start_pieces(later, later_sems)
    wait_pieces(first, first_sems)
    transform_in(source, target, windows, cas, turned, slabs.at[2])
    wait_pieces(later, later_sems)

    transform_x([slabs.at[place] for place in range(4)], into, outof, square)

    leave = [((slabs.at[2],), None, far_out), ((slabs.at[0],), None, own_out)]
    start_pieces(leave, out_sems)
    kept_place = jnp.where(at_direct, 1, 3)
    transform_out(slabs.at[4 - kept_place], given_source, windows_back, cas, turned, given)
    transform_out(slabs.at[kept_place], kept_source, windows_back, cas, turned, kept)
    wait_pieces(leave, out_sems)


def window_tables(cas_matrix):
    extent = cas_matrix.shape[0]
    tables = []
    for r in range(quad):
        shift = r * extent % lanes
        tables.append(jnp.pad(cas_matrix, ((shift, 2 * lanes - extent - shift), (0, 2 * lanes - extent))))
    return jnp.stack(tables)


limit = 60 * 2**20
full = 64 * 2**20
whole = pl.BlockSpec(memory_space=pltpu.VMEM)
outside = pl.BlockSpec(memory_space=pl.ANY)
scalars = pl.BlockSpec(memory_space=pltpu.SMEM)
small = pl.CostEstimate(flops=10**6, bytes_accessed=10**4, transcendentals=0)


def pick(orbitals, source_index, which, widths):
    planes = orbitals.shape[1]
    return pl.pallas_call(
        functools.partial(pick_kernel, which),
        out_shape=[jax.ShapeDtypeStruct((planes, width), orbitals.dtype) for width in widths],
        in_specs=[scalars, outside],
        out_specs=[whole] * len(widths),
        scratch_shapes=[pltpu.SemaphoreType.DMA((len(widths),))],
        compiler_params=pltpu.CompilerParams(vmem_limit_bytes=limit),
        cost_estimate=small,
        name="pick",
    )(source_index, orbitals)


def cut_quarters(source_index, orbitals, crossed):
    planes, points = crossed.shape
    return pl.pallas_call(
        cut_kernel,
        out_shape=[jax.ShapeDtypeStruct((planes, points // 4), crossed.dtype)] * 4,
        in_specs=[scalars, outside, outside],
        out_specs=[whole] * 4,
        scratch_shapes=[pltpu.SemaphoreType.DMA((4,))],
        compiler_params=pltpu.CompilerParams(vmem_limit_bytes=full),
        cost_estimate=small,
        name="cut",
    )(source_index, orbitals, crossed)


def put(which, first, choices, result=None):
    pieces = [piece for choice in choices for piece in choice]
    count = len(choices[0])
    planes, points = pieces[0].shape[0], sum(piece.shape[1] for piece in choices[0])
    before = [] if result is None else [result]
    return pl.pallas_call(
        functools.partial(put_kernel, len(choices), len(before)),
        out_shape=jax.ShapeDtypeStruct((2, planes, points), pieces[0].dtype),
        in_specs=[scalars] + [outside] * (len(before) + len(pieces)),
        out_specs=outside,
        scratch_shapes=[
            pltpu.VMEM((planes, points), pieces[0].dtype),
            pltpu.SemaphoreType.DMA((count,)),
            pltpu.SemaphoreType.DMA((count,)),
        ],
        input_output_aliases={1: 0} if before else {},
        compiler_params=pltpu.CompilerParams(vmem_limit_bytes=full),
        cost_estimate=small,
        name="put",
    )(jnp.stack([which, first.astype(which.dtype)]).astype(jnp.int32), *before, *pieces)


def forward(flags, place, first, targets, group, tables):
    planes = group[0].shape[1]
    extent = tables[0].shape[0]
    points = extent * extent
    return pl.pallas_call(
        functools.partial(forward_kernel, place, first, len(targets), len(targets[0])),
        out_shape=jax.ShapeDtypeStruct((2, extent * plane_pitch, lanes), jnp.float32),
        in_specs=[scalars] + [outside] * (len(targets) * len(targets[0]) + len(group)) + [whole] * len(tables),
        out_specs=whole,
        scratch_shapes=[
            pltpu.VMEM((planes, points), jnp.bfloat16),
            pltpu.VMEM((planes, points), jnp.bfloat16),
            pltpu.VMEM((2, planes * turned_pitch, lanes), jnp.float32),
            pltpu.SemaphoreType.DMA((len(targets[0]) + 5,)),
        ],
        compiler_params=pltpu.CompilerParams(vmem_limit_bytes=limit),
        cost_estimate=small,
        name="forward",
    )(flags, *[piece for choice in targets for piece in choice], *group, *tables)


def central(flags, home, direct, ready, targets, neighbour_source, across_source, tables):
    planes = across_source[0].shape[1]
    extent = tables[0].shape[0]
    points = extent * extent
    pieces = [*ready, *targets[0], *targets[1], *neighbour_source, *across_source]
    parts = [jax.ShapeDtypeStruct((planes, share * points // 5), jnp.bfloat16) for share in (2, 3)]
    slab = jax.ShapeDtypeStruct(ready[0].shape, jnp.float32)
    outs = pl.pallas_call(
        functools.partial(central_kernel, home, direct),
        out_shape=parts * 2 + [slab] * 2,
        in_specs=[scalars] + [outside] * len(pieces) + [whole] * len(tables),
        out_specs=[whole] * 4 + [outside] * 2,
        scratch_shapes=[
            pltpu.VMEM((ring, *slab.shape), jnp.float32),
            *[pltpu.VMEM((planes, points), jnp.bfloat16)] * 4,
            pltpu.VMEM((2, planes * turned_pitch, lanes), jnp.float32),
            pltpu.SemaphoreType.DMA((len(targets[0]) + 5,)),
            pltpu.SemaphoreType.DMA((13,)),
            pltpu.SemaphoreType.DMA((2,)),
        ],
        compiler_params=pltpu.CompilerParams(vmem_limit_bytes=full),
        cost_estimate=small,
        name="central",
    )(flags, *pieces, *tables)
    return split(outs, 2, 2, 2)


def backward(flags, places, first, slabs, groups, cas_matrix, windows, parts):
    planes = groups[0][0].shape[1]
    extent = cas_matrix.shape[0]
    points = extent * extent
    pieces = [piece for group in groups for piece in group]
    return pl.pallas_call(
        functools.partial(backward_kernel, places, first, parts),
        out_shape=[jax.ShapeDtypeStruct((planes, points // parts), jnp.bfloat16)] * parts,
        in_specs=[scalars] + [outside] * (len(slabs) + len(pieces)) + [whole] * 2,
        out_specs=[whole] * parts,
        scratch_shapes=[
            pltpu.VMEM(slabs[0].shape, jnp.float32),
            pltpu.VMEM((planes, points), jnp.bfloat16),
            pltpu.VMEM((2, planes * turned_pitch, lanes), jnp.float32),
            pltpu.SemaphoreType.DMA((6,)),
        ],
        compiler_params=pltpu.CompilerParams(vmem_limit_bytes=limit),
        cost_estimate=small,
        name="backward",
    )(flags, *slabs, *pieces, cas_matrix, windows)


def add(a, b):
    return (a.astype(jnp.float32) + b.astype(jnp.float32)).astype(jnp.bfloat16)


def pair_plan(orbitals, source_index):
    local_count, planes, points = orbitals.shape
    slabs = lax.axis_size("grid")
    extent = planes * slabs
    band, z = lax.axis_index("band"), lax.axis_index("grid")
    column, core = band // cores, band % cores
    quarter = points // 4
    at_home = core == holder(z)
    direct_neighbour = core == 1 - z % 2
    parity = z % 2
    inner = (z == 1) | (z == 2)
    second = inner.astype(jnp.int32)
    flags = jnp.stack([core, column, at_home, direct_neighbour, second, 1 - second]).astype(jnp.int32)
    home, direct = 2, 3

    unit = points // 8

    def first_pieces(source_index):
        core = lax.rem(lax.axis_index("band"), cores)
        near_parity = lax.rem(lax.axis_index("grid") + 1, 2)
        candidate = lax.rem(source_index[1 - core], local_count)
        return [(candidate, 0)] + [(near_parity, start) for start in (0, unit, 6 * unit)]

    def own_orbital(source_index):
        return [(lax.rem(lax.axis_index("grid"), 2), 0)]

    other, *to_near = pick(orbitals, source_index, first_pieces, (points, unit, 5 * unit, 2 * unit))
    crossed = swap_cores(other)
    near = [move(to_near[0], near_routes())]
    owner = source_index[core] // local_count

    cuts, to_near = stage((cut_quarters(source_index, orbitals, crossed), to_near), near)
    near.append(move(to_near[1], near_routes()))
    candidates = [cuts[0]] + [to_column(cuts[d], d) for d in (1, 2, 3)]
    (own_parity,) = pick(stage(orbitals, cuts), source_index, own_orbital, (points,))
    cas_matrix = cas_table(extent)
    windows = window_tables(cas_matrix)
    windows_back = jnp.swapaxes(windows, 1, 2)
    places = (((z ^ jnp.arange(slabs)) * planes)[:, None] + jnp.arange(planes)).reshape(extent)
    into = cas_entries(jnp.arange(extent), places, extent)
    square_x = wave_square(jnp.arange(extent, dtype=jnp.int32), extent)
    strength = (extent * spacing) ** 2 / math.pi
    square = (square_x[:, None] + square_x[None, :] + 1.0) * (1.0 / strength)
    square = jnp.pad(square, ((0, 0), (0, 2 * lanes - extent)), constant_values=1.0)
    tables = [cas_matrix, windows, windows_back, into, into.T, square]

    candidates, tables, own_parity, flags = stage((candidates, tables, own_parity, flags), near)
    cas_matrix, windows, windows_back, into, outof, square = tables
    forward_tables = [cas_matrix, windows, into, outof]
    own = lax.select_n(column ^ (owner // cores), *candidates)
    own = stage(own, tables)
    own_swapped = swap_cores(own_parity)
    own_x, own_y = to_column(own, 1), to_column(own, 2)
    neighbour = to_height(own, {0: 1, 1: 0, 2: 3, 3: 2})
    crossed = to_height(own, {1: 2, 2: 1})

    neighbour, crossed, own_x, own_y, own_swapped = stage((neighbour, crossed, own_x, own_y, own_swapped))
    neighbour_x, neighbour_y = to_column(neighbour, 1), to_column(neighbour, 2)
    crossed_2 = to_height(neighbour, {1: 2, 2: 1})
    handed = to_height(crossed, {1: 0, 2: 3})

    low = jnp.stack([own_x[:, : quarter // 2], neighbour_x[:, : quarter // 2]])
    high = jnp.stack([own_y[:, quarter // 2 :], neighbour_y[:, quarter // 2 :]])
    low, high, crossed_2, own_parity, last = stage((low, high, crossed_2, own_parity, to_near[2]), handed)
    low, high = to_column(low, 2), to_column(high, 1)
    handed_2 = to_height(crossed_2, {1: 0, 2: 3})
    near.append(move(last, near_routes()))
    far = [move(own_parity, far_routes())]

    across = jnp.stack([jnp.where(inner, crossed, handed), jnp.where(inner, crossed_2, handed_2)])
    across, low, high = stage((across, low, high))
    sources = [
        [own[None], own_x[None], own_y[None], low[:1], high[:1]],
        [neighbour[None], neighbour_x[None], neighbour_y[None], low[1:], high[1:]],
    ]
    across_x, across_y = to_column(across, 1), to_column(across, 2)
    near_swapped = [swap_cores(part) for part in stage(near[:2], across)]
    along_y = [forward(flags, 0, home, [[own_parity], [own_swapped]], sources[0], forward_tables)]

    low, high = across_x[:, :, : quarter // 2], across_y[:, :, quarter // 2 :]
    near[2] = stage(near[2], along_y)
    near_swapped.append(swap_cores(near[2]))
    low, high, near_swapped = stage((low, high, near_swapped), along_y)
    low, high = to_column(low, 2), to_column(high, 1)
    along_y.append(forward(flags, 1, direct, [near, near_swapped], sources[1], forward_tables))

    low, high, far = stage((low, high, far), along_y)
    across_source = [across, across_x, across_y, low, high]
    sources += [across_source, across_source]
    far_swapped = [swap_cores(part) for part in far]
    along_y_3 = forward(flags, 3, direct, [near_swapped, near], across_source, forward_tables)
    far_swapped = stage(far_swapped, along_y_3)
    given, kept, (own_back, far_back) = central(
        flags,
        home,
        direct,
        [*along_y, along_y_3],
        [far_swapped, far],
        sources[1],
        across_source,
        [cas_matrix, windows, windows_back, into, outof, square],
    )

    def partials(places, slabs, *earlier):
        groups = [sources[place] for place in places]
        return backward(flags, places, home, stage(slabs, *earlier), groups, cas_matrix, windows_back, 4)

    near = [add(k, swap_cores(g)) for k, g in zip(kept, given)]
    near_home = [move(part, back(near_routes())) for part in near]
    given = partials([2, 0], [far_back, own_back], near[0])
    kept = partials([0, 2], [own_back, far_back], given[0], near_home[0])
    far = [add(k, swap_cores(g)) for k, g in zip(kept, given)]
    far_home = [move(part, back(far_routes())) for part in far]
    result = put(1 - parity, at_home, [near_home])
    result, far_home = stage((result, far_home))
    return put(parity, at_home, [far, far_home], result)


def solution(mesh):
    def shards(orbitals, source_index):
        slabs, bands = mesh.shape["grid"], mesh.shape["band"]
        fits = slabs == 4 and bands == 8 and orbitals.shape[0] == 2 and source_index.shape[0] == cores
        return (pair_plan if fits else slab_plan)(orbitals, source_index)

    return jax.shard_map(
        shards,
        mesh=mesh,
        in_specs=(P("band", "grid", None), P()),
        out_specs=P("band", "grid", None),
        check_vma=False,
    )
```

```python
import functools
import math

import jax
import jax.numpy as jnp
from jax import lax
from jax.experimental import pallas as pl
from jax.experimental.pallas import tpu as pltpu
from jax.sharding import PartitionSpec as P

spacing = 0.3
cores = 2


def cas_entries(rows, columns, extent):
    products_mod = rows[:, None] * columns[None, :] % extent
    radians = products_mod.astype(jnp.float32) * (2.0 * math.pi / extent)
    return ((jnp.cos(radians) + jnp.sin(radians)) / math.sqrt(extent)).astype(jnp.bfloat16)


def cas_table(extent):
    wavenum = jnp.arange(extent, dtype=jnp.int32)
    return cas_entries(wavenum, wavenum, extent)


def wave_square(indices, extent):
    folded = jnp.minimum(indices, extent - indices).astype(jnp.float32)
    return folded * folded


def coulomb_block(extent, columns, offset):
    square_x = wave_square(jnp.arange(extent, dtype=jnp.int32), extent)
    square_y = wave_square(offset + jnp.arange(columns, dtype=jnp.int32), extent)
    total_sq = square_x[:, None, None] + square_y[None, :, None] + square_x[None, None, :]
    strength = (extent * spacing) ** 2 / math.pi
    return jnp.where(total_sq > 0, strength / (total_sq + 1.0), 0.0)


def transform(grid_data, cas_matrix, pattern):
    return jnp.einsum(pattern, grid_data, cas_matrix, preferred_element_type=jnp.float32)


def broadcast(x, axis, root):
    mine = lax.axis_index(axis) == root
    return lax.psum(jnp.where(mine, x, jnp.zeros_like(x)), axis)


def slab_potentials(pair_rho, cas_matrix, kernel_block):
    along_z = transform(pair_rho, cas_matrix, "pxyz,kz->pxyk").astype(jnp.bfloat16)
    along_y = transform(along_z, cas_matrix, "pxyz,ky->pxkz").astype(jnp.bfloat16)
    turned = lax.all_to_all(along_y, "grid", split_axis=2, concat_axis=1, tiled=True)
    scaled = (kernel_block * transform(turned, cas_matrix, "pxyz,kx->pkyz")).astype(jnp.bfloat16)
    back_x = transform(scaled, cas_matrix, "pxyz,kx->pkyz").astype(jnp.bfloat16)
    returned = lax.all_to_all(back_x, "grid", split_axis=1, concat_axis=2, tiled=True)
    again_y = transform(returned, cas_matrix, "pxyz,ky->pxkz").astype(jnp.bfloat16)
    return transform(again_y, cas_matrix, "pxyz,kz->pxyk")


def fetch_source(orbitals, which):
    local_count = orbitals.shape[0]
    local_slab = lax.dynamic_index_in_dim(orbitals, which % local_count, 0, keepdims=False)
    return broadcast(local_slab, "band", which // local_count)


def slab_plan(orbitals, source_index):
    local_count, planes, _ = orbitals.shape
    extent = planes * lax.axis_size("grid")
    orbitals = orbitals.reshape(local_count, planes, extent, extent)
    source_count = source_index.shape[0]
    cas_matrix = cas_table(extent)
    columns = extent // lax.axis_size("grid")
    kernel_block = coulomb_block(extent, columns, lax.axis_index("grid") * columns)
    fetched = [fetch_source(orbitals, source_index[number]) for number in range(source_count)]
    stacked = jnp.stack(fetched)[:, None].astype(jnp.float32)
    pair_rho = (stacked * orbitals[None].astype(jnp.float32)).astype(jnp.bfloat16)
    pair_rho = pair_rho.reshape(source_count * local_count, planes, extent, extent)
    potential = slab_potentials(pair_rho, cas_matrix, kernel_block)
    potential = potential.reshape(source_count, local_count, planes, extent, extent)
    result = (-jnp.sum(stacked * potential, axis=0)).astype(jnp.bfloat16)
    return result.reshape(local_count, planes, extent * extent)


lanes = 128
quad = 4
ring = 4
turned_pitch = 161
plane_pitch = 41


def move(x, routes):
    slabs = lax.axis_size("grid")

    def place(column, core, z):
        return (column * cores + core) * slabs + z % slabs

    return lax.ppermute(x, ("band", "grid"), [(place(*a), place(*b)) for a, b in routes])


def everywhere():
    columns = lax.axis_size("band") // cores
    return [(c, k, z) for c in range(columns) for k in range(cores) for z in range(lax.axis_size("grid"))]


def swap_cores(x):
    return move(x, [((c, k, z), (c, 1 - k, z)) for c, k, z in everywhere()])


def to_column(x, d):
    return move(x, [((c, k, z), (c ^ d, k, z)) for c, k, z in everywhere()])


def to_height(x, to):
    return move(x, [((c, k, z), (c, k, to[z])) for c, k, z in everywhere() if z in to])


def holder(z):
    return z % ring // 2


def side(core):
    return 2 * core - 1


def near_routes():
    return [((c, holder(z), z + side(k)), (c, k, z)) for c, k, z in everywhere()]


def far_routes():
    return [((c, holder(z), z + 2), (c, k, z)) for c, k, z in everywhere() if k != holder(z)]


def back(routes):
    return [(b, a) for a, b in routes]


def stage(values, *earlier):
    return lax.optimization_barrier((values, earlier))[0]


def choose(first, refs, start):
    if len(refs) == 1:
        start(refs[0])
    else:
        pl.when(first)(lambda: start(refs[0]))
        pl.when(jnp.logical_not(first))(lambda: start(refs[1]))


def start_pieces(pieces, sems):
    for number, (refs, first, to) in enumerate(pieces):
        choose(first, refs, lambda ref, to=to, number=number: pltpu.make_async_copy(ref, to, sems.at[number]).start())


def wait_pieces(pieces, sems):
    for number, (refs, _, to) in enumerate(pieces):
        pltpu.make_async_copy(refs[0], to, sems.at[number]).wait()


def source_of(refs, flags, place):
    return refs, flags[2 + place] if place > 1 else 0


def source_pieces(groups, first, source, column):
    quarter = source.shape[1] // 4
    offsets = [(column ^ e) * quarter for e in range(4)]
    offsets.append(offsets[3] + quarter // 2)
    pieces = []
    for number, offset in enumerate(offsets):
        refs = [five[number].at[which] for five, which in groups]
        to = source.at[:, pl.ds(pl.multiple_of(offset, lanes), refs[0].shape[1])]
        pieces.append((refs, first, to))
    return pieces


def split(refs, *counts):
    taken = []
    for count in counts:
        taken.append(refs[:count])
        refs = refs[count:]
    return taken


def dot(a, b):
    return jnp.dot(a, b, preferred_element_type=jnp.float32)


def both(ref, rows):
    return jnp.concatenate([ref[0, rows, :], ref[1, rows, :]], axis=1)


def beside(values):
    return jnp.concatenate(values, axis=1)


def apart(value):
    return [value[:, n : n + 2 * lanes] for n in range(0, value.shape[1], 2 * lanes)]


def put_both(ref, rows, value):
    ref[0, rows, :] = value[:, :lanes]
    ref[1, rows, :] = value[:, lanes:]


def lane_ranges(pieces):
    ranges = []
    start = 0
    for piece in pieces:
        ranges.append((start, piece.shape[1]))
        start += piece.shape[1]
    return ranges


def pick_kernel(which, source_index, orbitals, *refs):
    outs, sems = refs[:-1], refs[-1]
    copies = []
    for n, (out, (orbital, start)) in enumerate(zip(outs, which(source_index))):
        copies.append(pltpu.make_async_copy(orbitals.at[orbital, :, pl.ds(start, out.shape[1])], out, sems.at[n]))
    for copy in copies:
        copy.start()
    for copy in copies:
        copy.wait()


def cut_kernel(source_index, orbitals, crossed, *refs):
    outs, sems = refs[:-1], refs[-1]
    local_count = orbitals.shape[0]
    band = lax.axis_index("band")
    core, column = lax.rem(band, cores), lax.div(band, cores)
    which = lax.rem(source_index[core], local_count)
    owner = lax.rem(lax.div(source_index[core], local_count), cores)
    width = outs[0].shape[1]
    pieces = []
    for d, out in enumerate(outs):
        lane = pl.ds(pl.multiple_of((column ^ d) * width, lanes), width)
        pieces.append(((orbitals.at[which, :, lane], crossed.at[:, lane]), owner == core, out))
    start_pieces(pieces, sems)
    wait_pieces(pieces, sems)


def put_kernel(choices, aliased, flags, *refs):
    (out, staged, sems, out_sems), refs = refs[-4:], refs[aliased:-4]
    count = len(refs) // choices
    places = [pl.ds(*lane) for lane in lane_ranges(refs[:count])]
    chosen = [refs[n::count] for n in range(count)]
    start_pieces([(refs, flags[1] == 1, staged.at[:, lane]) for refs, lane in zip(chosen, places)], sems)
    leave = []
    for number, lane in enumerate(places):
        piece = staged.at[:, lane]
        pltpu.make_async_copy(chosen[number][0], piece, sems.at[number]).wait()
        leave.append(pltpu.make_async_copy(piece, out.at[flags[0], :, lane], out_sems.at[number]))
        leave[-1].start()
    for copy in leave:
        copy.wait()


def transform_in(source, target, windows, cas, turned, out):
    planes, points = target.shape
    extent = cas.shape[0]
    step = 20
    block = quad * extent

    @pl.loop(0, points // block // step)
    def _(i):
        for r in range(quad):
            density = []
            for j in range(step):
                at = pl.ds(pl.multiple_of((i * step + j) * block + r * lanes, lanes), 2 * lanes)
                density.append(source[:, at].astype(jnp.float32) * target[:, at].astype(jnp.float32))
            density = jnp.concatenate(density, axis=0).astype(jnp.bfloat16)
            along_z = dot(density, windows[r])
            for j in range(step):
                y = (i * step + j) * quad + r
                put_both(turned, pl.ds(y, planes, stride=turned_pitch), along_z[j * planes : (j + 1) * planes])

    @pl.loop(0, planes // 20)
    def _(i):
        for j in range(20):
            x = i * 20 + j
            along_z = both(turned, pl.ds(x * turned_pitch, extent)).astype(jnp.bfloat16)
            put_both(out, pl.ds(x, extent, stride=plane_pitch), dot(cas[...], along_z))


def transform_x(slabs, into, outof, square):
    extent = square.shape[0]
    planes = extent // ring
    strength = (extent * spacing) ** 2 / math.pi
    rows = 32

    @pl.loop(0, extent // rows)
    def _(step):
        base = pl.multiple_of(step * rows * plane_pitch, 8)
        for i in range(rows):
            at = pl.ds(base + i * plane_pitch, planes)
            along_y = jnp.concatenate([both(slab, at) for slab in slabs], axis=0).astype(jnp.bfloat16)
            ky = step * rows + i
            folded = jnp.minimum(ky, extent - ky)
            weight = square[...] + (folded * folded).astype(jnp.float32) * (1.0 / strength)
            guess = pl.reciprocal(weight, approx=True)
            factor = guess * (2.0 - weight * guess)
            factor = jnp.where(weight > 1.25 / strength, factor, 0.0)
            scaled = (factor * dot(into[...], along_y)).astype(jnp.bfloat16)
            back_x = dot(outof[...], scaled)
            for n, slab in enumerate(slabs):
                put_both(slab, at, back_x[n * planes : (n + 1) * planes])


def transform_out(back_x, source, windows, cas, turned, outs):
    planes, points = source.shape
    extent = cas.shape[0]

    @pl.loop(0, planes // 20)
    def _(i):
        for j in range(20):
            x = i * 20 + j
            column_x = both(back_x, pl.ds(x, extent, stride=plane_pitch)).astype(jnp.bfloat16)
            put_both(turned, pl.ds(x * turned_pitch, extent), dot(cas[...], column_x))

    block = quad * extent
    begin = 0
    for out in outs:
        blocks = out.shape[1] // block
        step = 10 if blocks % 10 == 0 else 8

        @pl.loop(0, blocks // step)
        def _(i, begin=begin, step=step, out=out):
            first = begin + i * step
            windowed = []
            for r in range(quad):
                again_y = jnp.concatenate(
                    [both(turned, pl.ds((first + j) * quad + r, planes, stride=turned_pitch)) for j in range(step)],
                    axis=0,
                ).astype(jnp.bfloat16)
                windowed.append(dot(again_y, windows[r]))
            for j in range(step):
                w = [part[j * planes : (j + 1) * planes] for part in windowed]
                potential = [w[0][:, :lanes]]
                potential += [w[r][:, lanes:] + w[r + 1][:, :lanes] for r in range(quad - 1)]
                potential = jnp.concatenate(potential + [w[-1][:, lanes:]], axis=1)
                at = pl.ds(pl.multiple_of((first + j) * block, lanes), block)
                to = pl.ds(pl.multiple_of((i * step + j) * block, lanes), block)
                out[:, to] = (-(source[:, at].astype(jnp.float32) * potential)).astype(jnp.bfloat16)

        begin += blocks


def forward_kernel(place, first, choices, count, flags, *refs):
    targets, five, (cas, windows, _, _, out, target, source, turned, sems) = split(refs, choices * count, 5, 9)
    ranges = lane_ranges(targets[:count])
    pieces = [(targets[n::count], flags[first] == 1, target.at[:, pl.ds(*lane)]) for n, lane in enumerate(ranges)]
    pieces += source_pieces([source_of(five, flags, place)], None, source, flags[1])
    start_pieces(pieces, sems)
    wait_pieces(pieces, sems)
    transform_in(source, target, windows, cas, turned, out)


def backward_kernel(places, first, parts, flags, *refs):
    slabs, groups, (cas, windows), outs, (back_x, source, turned, sems) = split(
        refs, len(places), 5 * len(places), 2, parts, 4
    )
    chosen = [source_of(five, flags, place) for five, place in zip(split(groups, *[5] * len(places)), places)]
    pieces = [(slabs, flags[first] == 1, back_x)] + source_pieces(chosen, flags[first] == 1, source, flags[1])
    start_pieces(pieces, sems)
    wait_pieces(pieces, sems)
    transform_out(back_x, source, windows, cas, turned, outs)


def central_kernel(home, direct, flags, *refs):
    ready, targets, neighbour_source, across_source, tables, outs, scratch = split(
        refs, 3, len(refs) - 34, 5, 5, 6, 6, 9
    )
    cas, windows, windows_back, into, outof, square = tables
    given, kept, (own_out, far_out) = split(outs, 2, 2, 2)
    slabs, target, source, given_source, kept_source, turned, first_sems, later_sems, out_sems = scratch
    at_direct = flags[direct] == 1
    column = flags[1]

    count = len(targets) // 2
    ranges = lane_ranges(targets[:count])
    first = [(targets[n::count], flags[home] == 1, target.at[:, pl.ds(*lane)]) for n, lane in enumerate(ranges)]
    first += source_pieces([source_of(across_source, flags, 2)], None, source, column)
    start_pieces(first, first_sems)
    later = [((ref,), None, slabs.at[place]) for ref, place in zip(ready, (0, 1, 3))]
    near_sources = [source_of(across_source, flags, 3), source_of(neighbour_source, flags, 1)]
    later += source_pieces(near_sources, at_direct, given_source, column)
    later += source_pieces(near_sources[::-1], at_direct, kept_source, column)
    start_pieces(later, later_sems)
    wait_pieces(first, first_sems)
    transform_in(source, target, windows, cas, turned, slabs.at[2])
    wait_pieces(later, later_sems)

    transform_x([slabs.at[place] for place in range(4)], into, outof, square)

    leave = [((slabs.at[2],), None, far_out), ((slabs.at[0],), None, own_out)]
    start_pieces(leave, out_sems)
    kept_place = jnp.where(at_direct, 1, 3)
    transform_out(slabs.at[4 - kept_place], given_source, windows_back, cas, turned, given)
    transform_out(slabs.at[kept_place], kept_source, windows_back, cas, turned, kept)
    wait_pieces(leave, out_sems)


def window_tables(cas_matrix):
    extent = cas_matrix.shape[0]
    tables = []
    for r in range(quad):
        shift = r * extent % lanes
        tables.append(jnp.pad(cas_matrix, ((shift, 2 * lanes - extent - shift), (0, 2 * lanes - extent))))
    return jnp.stack(tables)


limit = 60 * 2**20
full = 64 * 2**20
whole = pl.BlockSpec(memory_space=pltpu.VMEM)
outside = pl.BlockSpec(memory_space=pl.ANY)
scalars = pl.BlockSpec(memory_space=pltpu.SMEM)
small = pl.CostEstimate(flops=10**6, bytes_accessed=10**4, transcendentals=0)


def pick(orbitals, source_index, which, widths):
    planes = orbitals.shape[1]
    return pl.pallas_call(
        functools.partial(pick_kernel, which),
        out_shape=[jax.ShapeDtypeStruct((planes, width), orbitals.dtype) for width in widths],
        in_specs=[scalars, outside],
        out_specs=[whole] * len(widths),
        scratch_shapes=[pltpu.SemaphoreType.DMA((len(widths),))],
        compiler_params=pltpu.CompilerParams(vmem_limit_bytes=limit),
        cost_estimate=small,
        name="pick",
    )(source_index, orbitals)


def cut_quarters(source_index, orbitals, crossed):
    planes, points = crossed.shape
    return pl.pallas_call(
        cut_kernel,
        out_shape=[jax.ShapeDtypeStruct((planes, points // 4), crossed.dtype)] * 4,
        in_specs=[scalars, outside, outside],
        out_specs=[whole] * 4,
        scratch_shapes=[pltpu.SemaphoreType.DMA((4,))],
        compiler_params=pltpu.CompilerParams(vmem_limit_bytes=full),
        cost_estimate=small,
        name="cut",
    )(source_index, orbitals, crossed)


def put(which, first, choices, result=None):
    pieces = [piece for choice in choices for piece in choice]
    count = len(choices[0])
    planes, points = pieces[0].shape[0], sum(piece.shape[1] for piece in choices[0])
    before = [] if result is None else [result]
    return pl.pallas_call(
        functools.partial(put_kernel, len(choices), len(before)),
        out_shape=jax.ShapeDtypeStruct((2, planes, points), pieces[0].dtype),
        in_specs=[scalars] + [outside] * (len(before) + len(pieces)),
        out_specs=outside,
        scratch_shapes=[
            pltpu.VMEM((planes, points), pieces[0].dtype),
            pltpu.SemaphoreType.DMA((count,)),
            pltpu.SemaphoreType.DMA((count,)),
        ],
        input_output_aliases={1: 0} if before else {},
        compiler_params=pltpu.CompilerParams(vmem_limit_bytes=full),
        cost_estimate=small,
        name="put",
    )(jnp.stack([which, first.astype(which.dtype)]).astype(jnp.int32), *before, *pieces)


def forward(flags, place, first, targets, group, tables):
    planes = group[0].shape[1]
    extent = tables[0].shape[0]
    points = extent * extent
    return pl.pallas_call(
        functools.partial(forward_kernel, place, first, len(targets), len(targets[0])),
        out_shape=jax.ShapeDtypeStruct((2, extent * plane_pitch, lanes), jnp.float32),
        in_specs=[scalars] + [outside] * (len(targets) * len(targets[0]) + len(group)) + [whole] * len(tables),
        out_specs=whole,
        scratch_shapes=[
            pltpu.VMEM((planes, points), jnp.bfloat16),
            pltpu.VMEM((planes, points), jnp.bfloat16),
            pltpu.VMEM((2, planes * turned_pitch, lanes), jnp.float32),
            pltpu.SemaphoreType.DMA((len(targets[0]) + 5,)),
        ],
        compiler_params=pltpu.CompilerParams(vmem_limit_bytes=limit),
        cost_estimate=small,
        name="forward",
    )(flags, *[piece for choice in targets for piece in choice], *group, *tables)


def central(flags, home, direct, ready, targets, neighbour_source, across_source, tables):
    planes = across_source[0].shape[1]
    extent = tables[0].shape[0]
    points = extent * extent
    pieces = [*ready, *targets[0], *targets[1], *neighbour_source, *across_source]
    parts = [jax.ShapeDtypeStruct((planes, share * points // 5), jnp.bfloat16) for share in (2, 3)]
    slab = jax.ShapeDtypeStruct(ready[0].shape, jnp.float32)
    outs = pl.pallas_call(
        functools.partial(central_kernel, home, direct),
        out_shape=parts * 2 + [slab] * 2,
        in_specs=[scalars] + [outside] * len(pieces) + [whole] * len(tables),
        out_specs=[whole] * 4 + [outside] * 2,
        scratch_shapes=[
            pltpu.VMEM((ring, *slab.shape), jnp.float32),
            *[pltpu.VMEM((planes, points), jnp.bfloat16)] * 4,
            pltpu.VMEM((2, planes * turned_pitch, lanes), jnp.float32),
            pltpu.SemaphoreType.DMA((len(targets[0]) + 5,)),
            pltpu.SemaphoreType.DMA((13,)),
            pltpu.SemaphoreType.DMA((2,)),
        ],
        compiler_params=pltpu.CompilerParams(vmem_limit_bytes=full),
        cost_estimate=small,
        name="central",
    )(flags, *pieces, *tables)
    return split(outs, 2, 2, 2)


def backward(flags, places, first, slabs, groups, cas_matrix, windows, parts):
    planes = groups[0][0].shape[1]
    extent = cas_matrix.shape[0]
    points = extent * extent
    pieces = [piece for group in groups for piece in group]
    return pl.pallas_call(
        functools.partial(backward_kernel, places, first, parts),
        out_shape=[jax.ShapeDtypeStruct((planes, points // parts), jnp.bfloat16)] * parts,
        in_specs=[scalars] + [outside] * (len(slabs) + len(pieces)) + [whole] * 2,
        out_specs=[whole] * parts,
        scratch_shapes=[
            pltpu.VMEM(slabs[0].shape, jnp.float32),
            pltpu.VMEM((planes, points), jnp.bfloat16),
            pltpu.VMEM((2, planes * turned_pitch, lanes), jnp.float32),
            pltpu.SemaphoreType.DMA((6,)),
        ],
        compiler_params=pltpu.CompilerParams(vmem_limit_bytes=limit),
        cost_estimate=small,
        name="backward",
    )(flags, *slabs, *pieces, cas_matrix, windows)


def add(a, b):
    return (a.astype(jnp.float32) + b.astype(jnp.float32)).astype(jnp.bfloat16)


def pair_plan(orbitals, source_index):
    local_count, planes, points = orbitals.shape
    slabs = lax.axis_size("grid")
    extent = planes * slabs
    band, z = lax.axis_index("band"), lax.axis_index("grid")
    column, core = band // cores, band % cores
    quarter = points // 4
    at_home = core == holder(z)
    direct_neighbour = core == 1 - z % 2
    parity = z % 2
    inner = (z == 1) | (z == 2)
    second = inner.astype(jnp.int32)
    flags = jnp.stack([core, column, at_home, direct_neighbour, second, 1 - second]).astype(jnp.int32)
    home, direct = 2, 3

    unit = points // 8

    def first_pieces(source_index):
        core = lax.rem(lax.axis_index("band"), cores)
        near_parity = lax.rem(lax.axis_index("grid") + 1, 2)
        candidate = lax.rem(source_index[1 - core], local_count)
        return [(candidate, 0)] + [(near_parity, start) for start in (0, unit, 6 * unit)]

    def own_orbital(source_index):
        return [(lax.rem(lax.axis_index("grid"), 2), 0)]

    other, *to_near = pick(orbitals, source_index, first_pieces, (points, unit, 5 * unit, 2 * unit))
    crossed = swap_cores(other)
    near = [move(to_near[0], near_routes())]
    owner = source_index[core] // local_count

    cuts, to_near = stage((cut_quarters(source_index, orbitals, crossed), to_near), near)
    near.append(move(to_near[1], near_routes()))
    candidates = [cuts[0]] + [to_column(cuts[d], d) for d in (1, 2, 3)]
    (own_parity,) = pick(stage(orbitals, cuts), source_index, own_orbital, (points,))
    cas_matrix = cas_table(extent)
    windows = window_tables(cas_matrix)
    windows_back = jnp.swapaxes(windows, 1, 2)
    places = (((z ^ jnp.arange(slabs)) * planes)[:, None] + jnp.arange(planes)).reshape(extent)
    into = cas_entries(jnp.arange(extent), places, extent)
    square_x = wave_square(jnp.arange(extent, dtype=jnp.int32), extent)
    strength = (extent * spacing) ** 2 / math.pi
    square = (square_x[:, None] + square_x[None, :] + 1.0) * (1.0 / strength)
    square = jnp.pad(square, ((0, 0), (0, 2 * lanes - extent)), constant_values=1.0)
    tables = [cas_matrix, windows, windows_back, into, into.T, square]

    candidates, tables, own_parity, flags = stage((candidates, tables, own_parity, flags), near)
    cas_matrix, windows, windows_back, into, outof, square = tables
    forward_tables = [cas_matrix, windows, into, outof]
    own = lax.select_n(column ^ (owner // cores), *candidates)
    own = stage(own, tables)
    own_swapped = swap_cores(own_parity)
    own_x, own_y = to_column(own, 1), to_column(own, 2)
    neighbour = to_height(own, {0: 1, 1: 0, 2: 3, 3: 2})
    crossed = to_height(own, {1: 2, 2: 1})

    neighbour, crossed, own_x, own_y, own_swapped = stage((neighbour, crossed, own_x, own_y, own_swapped))
    neighbour_x, neighbour_y = to_column(neighbour, 1), to_column(neighbour, 2)
    crossed_2 = to_height(neighbour, {1: 2, 2: 1})
    handed = to_height(crossed, {1: 0, 2: 3})

    low = jnp.stack([own_x[:, : quarter // 2], neighbour_x[:, : quarter // 2]])
    high = jnp.stack([own_y[:, quarter // 2 :], neighbour_y[:, quarter // 2 :]])
    low, high, crossed_2, own_parity, last = stage((low, high, crossed_2, own_parity, to_near[2]), handed)
    low, high = to_column(low, 2), to_column(high, 1)
    handed_2 = to_height(crossed_2, {1: 0, 2: 3})
    near.append(move(last, near_routes()))
    far = [move(own_parity, far_routes())]

    across = jnp.stack([jnp.where(inner, crossed, handed), jnp.where(inner, crossed_2, handed_2)])
    across, low, high = stage((across, low, high))
    sources = [
        [own[None], own_x[None], own_y[None], low[:1], high[:1]],
        [neighbour[None], neighbour_x[None], neighbour_y[None], low[1:], high[1:]],
    ]
    across_x, across_y = to_column(across, 1), to_column(across, 2)
    near_swapped = [swap_cores(part) for part in stage(near[:2], across)]
    along_y = [forward(flags, 0, home, [[own_parity], [own_swapped]], sources[0], forward_tables)]

    low, high = across_x[:, :, : quarter // 2], across_y[:, :, quarter // 2 :]
    near[2] = stage(near[2], along_y)
    near_swapped.append(swap_cores(near[2]))
    low, high, near_swapped = stage((low, high, near_swapped), along_y)
    low, high = to_column(low, 2), to_column(high, 1)
    along_y.append(forward(flags, 1, direct, [near, near_swapped], sources[1], forward_tables))

    low, high, far = stage((low, high, far), along_y)
    across_source = [across, across_x, across_y, low, high]
    sources += [across_source, across_source]
    far_swapped = [swap_cores(part) for part in far]
    along_y_3 = forward(flags, 3, direct, [near_swapped, near], across_source, forward_tables)
    far_swapped = stage(far_swapped, along_y_3)
    given, kept, (own_back, far_back) = central(
        flags,
        home,
        direct,
        [*along_y, along_y_3],
        [far_swapped, far],
        sources[1],
        across_source,
        [cas_matrix, windows, windows_back, into, outof, square],
    )

    def partials(places, slabs, *earlier):
        groups = [sources[place] for place in places]
        return backward(flags, places, home, stage(slabs, *earlier), groups, cas_matrix, windows_back, 4)

    near = [add(k, swap_cores(g)) for k, g in zip(kept, given)]
    near_home = [move(part, back(near_routes())) for part in near]
    given = partials([2, 0], [far_back, own_back], near[0])
    kept = partials([0, 2], [own_back, far_back], given[0], near_home[0])
    far = [add(k, swap_cores(g)) for k, g in zip(kept, given)]
    far_home = [move(part, back(far_routes())) for part in far]
    result = put(1 - parity, at_home, [near_home])
    result, far_home = stage((result, far_home))
    return put(parity, at_home, [far, far_home], result)


def solution(mesh):
    def shards(orbitals, source_index):
        slabs, bands = mesh.shape["grid"], mesh.shape["band"]
        fits = slabs == 4 and bands == 8 and orbitals.shape[0] == 2 and source_index.shape[0] == cores
        return (pair_plan if fits else slab_plan)(orbitals, source_index)

    return jax.shard_map(
        shards,
        mesh=mesh,
        in_specs=(P("band", "grid", None), P()),
        out_specs=P("band", "grid", None),
        check_vma=False,
    )
```

```python
import functools
import math

import jax
import jax.numpy as jnp
from jax import lax
from jax.experimental import pallas as pl
from jax.experimental.pallas import tpu as pltpu
from jax.sharding import PartitionSpec as P

spacing = 0.3
cores = 2


def cas_entries(rows, columns, extent):
    products_mod = rows[:, None] * columns[None, :] % extent
    radians = products_mod.astype(jnp.float32) * (2.0 * math.pi / extent)
    return ((jnp.cos(radians) + jnp.sin(radians)) / math.sqrt(extent)).astype(jnp.bfloat16)


def cas_table(extent):
    wavenum = jnp.arange(extent, dtype=jnp.int32)
    return cas_entries(wavenum, wavenum, extent)


def wave_square(indices, extent):
    folded = jnp.minimum(indices, extent - indices).astype(jnp.float32)
    return folded * folded


def coulomb_block(extent, columns, offset):
    square_x = wave_square(jnp.arange(extent, dtype=jnp.int32), extent)
    square_y = wave_square(offset + jnp.arange(columns, dtype=jnp.int32), extent)
    total_sq = square_x[:, None, None] + square_y[None, :, None] + square_x[None, None, :]
    strength = (extent * spacing) ** 2 / math.pi
    return jnp.where(total_sq > 0, strength / (total_sq + 1.0), 0.0)


def transform(grid_data, cas_matrix, pattern):
    return jnp.einsum(pattern, grid_data, cas_matrix, preferred_element_type=jnp.float32)


def broadcast(x, axis, root):
    mine = lax.axis_index(axis) == root
    return lax.psum(jnp.where(mine, x, jnp.zeros_like(x)), axis)


def slab_potentials(pair_rho, cas_matrix, kernel_block):
    along_z = transform(pair_rho, cas_matrix, "pxyz,kz->pxyk").astype(jnp.bfloat16)
    along_y = transform(along_z, cas_matrix, "pxyz,ky->pxkz").astype(jnp.bfloat16)
    turned = lax.all_to_all(along_y, "grid", split_axis=2, concat_axis=1, tiled=True)
    scaled = (kernel_block * transform(turned, cas_matrix, "pxyz,kx->pkyz")).astype(jnp.bfloat16)
    back_x = transform(scaled, cas_matrix, "pxyz,kx->pkyz").astype(jnp.bfloat16)
    returned = lax.all_to_all(back_x, "grid", split_axis=1, concat_axis=2, tiled=True)
    again_y = transform(returned, cas_matrix, "pxyz,ky->pxkz").astype(jnp.bfloat16)
    return transform(again_y, cas_matrix, "pxyz,kz->pxyk")


def fetch_source(orbitals, which):
    local_count = orbitals.shape[0]
    local_slab = lax.dynamic_index_in_dim(orbitals, which % local_count, 0, keepdims=False)
    return broadcast(local_slab, "band", which // local_count)


def slab_plan(orbitals, source_index):
    local_count, planes, _ = orbitals.shape
    extent = planes * lax.axis_size("grid")
    orbitals = orbitals.reshape(local_count, planes, extent, extent)
    source_count = source_index.shape[0]
    cas_matrix = cas_table(extent)
    columns = extent // lax.axis_size("grid")
    kernel_block = coulomb_block(extent, columns, lax.axis_index("grid") * columns)
    fetched = [fetch_source(orbitals, source_index[number]) for number in range(source_count)]
    stacked = jnp.stack(fetched)[:, None].astype(jnp.float32)
    pair_rho = (stacked * orbitals[None].astype(jnp.float32)).astype(jnp.bfloat16)
    pair_rho = pair_rho.reshape(source_count * local_count, planes, extent, extent)
    potential = slab_potentials(pair_rho, cas_matrix, kernel_block)
    potential = potential.reshape(source_count, local_count, planes, extent, extent)
    result = (-jnp.sum(stacked * potential, axis=0)).astype(jnp.bfloat16)
    return result.reshape(local_count, planes, extent * extent)


lanes = 128
quad = 4
ring = 4
turned_pitch = 161
plane_pitch = 41


def move(x, routes):
    slabs = lax.axis_size("grid")

    def place(column, core, z):
        return (column * cores + core) * slabs + z % slabs

    return lax.ppermute(x, ("band", "grid"), [(place(*a), place(*b)) for a, b in routes])


def everywhere():
    columns = lax.axis_size("band") // cores
    return [(c, k, z) for c in range(columns) for k in range(cores) for z in range(lax.axis_size("grid"))]


def swap_cores(x):
    return move(x, [((c, k, z), (c, 1 - k, z)) for c, k, z in everywhere()])


def to_column(x, d):
    return move(x, [((c, k, z), (c ^ d, k, z)) for c, k, z in everywhere()])


def to_height(x, to):
    return move(x, [((c, k, z), (c, k, to[z])) for c, k, z in everywhere() if z in to])


def holder(z):
    return z % ring // 2


def side(core):
    return 2 * core - 1


def near_routes():
    return [((c, holder(z), z + side(k)), (c, k, z)) for c, k, z in everywhere()]


def far_routes():
    return [((c, holder(z), z + 2), (c, k, z)) for c, k, z in everywhere() if k != holder(z)]


def back(routes):
    return [(b, a) for a, b in routes]


def stage(values, *earlier):
    return lax.optimization_barrier((values, earlier))[0]


def choose(first, refs, start):
    if len(refs) == 1:
        start(refs[0])
    else:
        pl.when(first)(lambda: start(refs[0]))
        pl.when(jnp.logical_not(first))(lambda: start(refs[1]))


def start_pieces(pieces, sems):
    for number, (refs, first, to) in enumerate(pieces):
        choose(first, refs, lambda ref, to=to, number=number: pltpu.make_async_copy(ref, to, sems.at[number]).start())


def wait_pieces(pieces, sems):
    for number, (refs, _, to) in enumerate(pieces):
        pltpu.make_async_copy(refs[0], to, sems.at[number]).wait()


def source_of(refs, flags, place):
    return refs, flags[2 + place] if place > 1 else 0


def source_pieces(groups, first, source, column):
    quarter = source.shape[1] // 4
    offsets = [(column ^ e) * quarter for e in range(4)]
    offsets.append(offsets[3] + quarter // 2)
    pieces = []
    for number, offset in enumerate(offsets):
        refs = [five[number].at[which] for five, which in groups]
        to = source.at[:, pl.ds(pl.multiple_of(offset, lanes), refs[0].shape[1])]
        pieces.append((refs, first, to))
    return pieces


def split(refs, *counts):
    taken = []
    for count in counts:
        taken.append(refs[:count])
        refs = refs[count:]
    return taken


def dot(a, b):
    return jnp.dot(a, b, preferred_element_type=jnp.float32)


def both(ref, rows):
    return jnp.concatenate([ref[0, rows, :], ref[1, rows, :]], axis=1)


def beside(values):
    return jnp.concatenate(values, axis=1)


def apart(value):
    return [value[:, n : n + 2 * lanes] for n in range(0, value.shape[1], 2 * lanes)]


def put_both(ref, rows, value):
    ref[0, rows, :] = value[:, :lanes]
    ref[1, rows, :] = value[:, lanes:]


def lane_ranges(pieces):
    ranges = []
    start = 0
    for piece in pieces:
        ranges.append((start, piece.shape[1]))
        start += piece.shape[1]
    return ranges


def pick_kernel(which, source_index, orbitals, *refs):
    outs, sems = refs[:-1], refs[-1]
    copies = []
    for n, (out, (orbital, start)) in enumerate(zip(outs, which(source_index))):
        copies.append(pltpu.make_async_copy(orbitals.at[orbital, :, pl.ds(start, out.shape[1])], out, sems.at[n]))
    for copy in copies:
        copy.start()
    for copy in copies:
        copy.wait()


def cut_kernel(source_index, orbitals, crossed, *refs):
    outs, sems = refs[:-1], refs[-1]
    local_count = orbitals.shape[0]
    band = lax.axis_index("band")
    core, column = lax.rem(band, cores), lax.div(band, cores)
    which = lax.rem(source_index[core], local_count)
    owner = lax.rem(lax.div(source_index[core], local_count), cores)
    width = outs[0].shape[1]
    pieces = []
    for d, out in enumerate(outs):
        lane = pl.ds(pl.multiple_of((column ^ d) * width, lanes), width)
        pieces.append(((orbitals.at[which, :, lane], crossed.at[:, lane]), owner == core, out))
    start_pieces(pieces, sems)
    wait_pieces(pieces, sems)


def put_kernel(choices, aliased, flags, *refs):
    (out, staged, sems, out_sems), refs = refs[-4:], refs[aliased:-4]
    count = len(refs) // choices
    places = [pl.ds(*lane) for lane in lane_ranges(refs[:count])]
    chosen = [refs[n::count] for n in range(count)]
    start_pieces([(refs, flags[1] == 1, staged.at[:, lane]) for refs, lane in zip(chosen, places)], sems)
    leave = []
    for number, lane in enumerate(places):
        piece = staged.at[:, lane]
        pltpu.make_async_copy(chosen[number][0], piece, sems.at[number]).wait()
        leave.append(pltpu.make_async_copy(piece, out.at[flags[0], :, lane], out_sems.at[number]))
        leave[-1].start()
    for copy in leave:
        copy.wait()


def transform_in(source, target, windows, cas, turned, out):
    planes, points = target.shape
    extent = cas.shape[0]
    step = 20
    block = quad * extent

    @pl.loop(0, points // block // step)
    def _(i):
        for r in range(quad):
            density = []
            for j in range(step):
                at = pl.ds(pl.multiple_of((i * step + j) * block + r * lanes, lanes), 2 * lanes)
                density.append(source[:, at].astype(jnp.float32) * target[:, at].astype(jnp.float32))
            density = jnp.concatenate(density, axis=0).astype(jnp.bfloat16)
            along_z = dot(density, windows[r])
            for j in range(step):
                y = (i * step + j) * quad + r
                put_both(turned, pl.ds(y, planes, stride=turned_pitch), along_z[j * planes : (j + 1) * planes])

    @pl.loop(0, planes // 40)
    def _(i):
        for j in range(40):
            x = i * 40 + j
            along_z = both(turned, pl.ds(x * turned_pitch, extent)).astype(jnp.bfloat16)
            put_both(out, pl.ds(x, extent, stride=plane_pitch), dot(cas[...], along_z))


def transform_x(slabs, into, outof, square):
    extent = square.shape[0]
    planes = extent // ring
    strength = (extent * spacing) ** 2 / math.pi
    rows = 40

    @pl.loop(0, extent // rows)
    def _(step):
        base = pl.multiple_of(step * rows * plane_pitch, 8)
        for i in range(rows):
            at = pl.ds(base + i * plane_pitch, planes)
            along_y = jnp.concatenate([both(slab, at) for slab in slabs], axis=0).astype(jnp.bfloat16)
            ky = step * rows + i
            folded = jnp.minimum(ky, extent - ky)
            weight = square[...] + (folded * folded).astype(jnp.float32) * (1.0 / strength)
            guess = pl.reciprocal(weight, approx=True)
            factor = guess * (2.0 - weight * guess)
            factor = jnp.where(weight > 1.25 / strength, factor, 0.0)
            scaled = (factor * dot(into[...], along_y)).astype(jnp.bfloat16)
            back_x = dot(outof[...], scaled)
            for n, slab in enumerate(slabs):
                put_both(slab, at, back_x[n * planes : (n + 1) * planes])


def transform_out(back_x, source, windows, cas, turned, outs):
    planes, points = source.shape
    extent = cas.shape[0]

    @pl.loop(0, planes // 40)
    def _(i):
        for j in range(40):
            x = i * 40 + j
            column_x = both(back_x, pl.ds(x, extent, stride=plane_pitch)).astype(jnp.bfloat16)
            put_both(turned, pl.ds(x * turned_pitch, extent), dot(cas[...], column_x))

    block = quad * extent
    begin = 0
    for out in outs:
        blocks = out.shape[1] // block
        step = 10 if blocks % 10 == 0 else 8

        @pl.loop(0, blocks // step)
        def _(i, begin=begin, step=step, out=out):
            first = begin + i * step
            windowed = []
            for r in range(quad):
                again_y = jnp.concatenate(
                    [both(turned, pl.ds((first + j) * quad + r, planes, stride=turned_pitch)) for j in range(step)],
                    axis=0,
                ).astype(jnp.bfloat16)
                windowed.append(dot(again_y, windows[r]))
            for j in range(step):
                w = [part[j * planes : (j + 1) * planes] for part in windowed]
                potential = [w[0][:, :lanes]]
                potential += [w[r][:, lanes:] + w[r + 1][:, :lanes] for r in range(quad - 1)]
                potential = jnp.concatenate(potential + [w[-1][:, lanes:]], axis=1)
                at = pl.ds(pl.multiple_of((first + j) * block, lanes), block)
                to = pl.ds(pl.multiple_of((i * step + j) * block, lanes), block)
                out[:, to] = (-(source[:, at].astype(jnp.float32) * potential)).astype(jnp.bfloat16)

        begin += blocks


def forward_kernel(place, first, choices, count, flags, *refs):
    targets, five, (cas, windows, _, _, out, target, source, turned, sems) = split(refs, choices * count, 5, 9)
    ranges = lane_ranges(targets[:count])
    pieces = [(targets[n::count], flags[first] == 1, target.at[:, pl.ds(*lane)]) for n, lane in enumerate(ranges)]
    pieces += source_pieces([source_of(five, flags, place)], None, source, flags[1])
    start_pieces(pieces, sems)
    wait_pieces(pieces, sems)
    transform_in(source, target, windows, cas, turned, out)


def backward_kernel(places, first, parts, flags, *refs):
    slabs, groups, (cas, windows), outs, (back_x, source, turned, sems) = split(
        refs, len(places), 5 * len(places), 2, parts, 4
    )
    chosen = [source_of(five, flags, place) for five, place in zip(split(groups, *[5] * len(places)), places)]
    pieces = [(slabs, flags[first] == 1, back_x)] + source_pieces(chosen, flags[first] == 1, source, flags[1])
    start_pieces(pieces, sems)
    wait_pieces(pieces, sems)
    transform_out(back_x, source, windows, cas, turned, outs)


def central_kernel(home, direct, flags, *refs):
    ready, targets, neighbour_source, across_source, tables, outs, scratch = split(
        refs, 3, len(refs) - 34, 5, 5, 6, 6, 9
    )
    cas, windows, windows_back, into, outof, square = tables
    given, kept, (own_out, far_out) = split(outs, 2, 2, 2)
    slabs, target, source, given_source, kept_source, turned, first_sems, later_sems, out_sems = scratch
    at_direct = flags[direct] == 1
    column = flags[1]

    count = len(targets) // 2
    ranges = lane_ranges(targets[:count])
    first = [(targets[n::count], flags[home] == 1, target.at[:, pl.ds(*lane)]) for n, lane in enumerate(ranges)]
    first += source_pieces([source_of(across_source, flags, 2)], None, source, column)
    start_pieces(first, first_sems)
    later = [((ref,), None, slabs.at[place]) for ref, place in zip(ready, (0, 1, 3))]
    near_sources = [source_of(across_source, flags, 3), source_of(neighbour_source, flags, 1)]
    later += source_pieces(near_sources, at_direct, given_source, column)
    later += source_pieces(near_sources[::-1], at_direct, kept_source, column)
    start_pieces(later, later_sems)
    wait_pieces(first, first_sems)
    transform_in(source, target, windows, cas, turned, slabs.at[2])
    wait_pieces(later, later_sems)

    transform_x([slabs.at[place] for place in range(4)], into, outof, square)

    leave = [((slabs.at[2],), None, far_out), ((slabs.at[0],), None, own_out)]
    start_pieces(leave, out_sems)
    kept_place = jnp.where(at_direct, 1, 3)
    transform_out(slabs.at[4 - kept_place], given_source, windows_back, cas, turned, given)
    transform_out(slabs.at[kept_place], kept_source, windows_back, cas, turned, kept)
    wait_pieces(leave, out_sems)


def window_tables(cas_matrix):
    extent = cas_matrix.shape[0]
    tables = []
    for r in range(quad):
        shift = r * extent % lanes
        tables.append(jnp.pad(cas_matrix, ((shift, 2 * lanes - extent - shift), (0, 2 * lanes - extent))))
    return jnp.stack(tables)


limit = 60 * 2**20
full = 64 * 2**20
whole = pl.BlockSpec(memory_space=pltpu.VMEM)
outside = pl.BlockSpec(memory_space=pl.ANY)
scalars = pl.BlockSpec(memory_space=pltpu.SMEM)
small = pl.CostEstimate(flops=10**6, bytes_accessed=10**4, transcendentals=0)


def pick(orbitals, source_index, which, widths):
    planes = orbitals.shape[1]
    return pl.pallas_call(
        functools.partial(pick_kernel, which),
        out_shape=[jax.ShapeDtypeStruct((planes, width), orbitals.dtype) for width in widths],
        in_specs=[scalars, outside],
        out_specs=[whole] * len(widths),
        scratch_shapes=[pltpu.SemaphoreType.DMA((len(widths),))],
        compiler_params=pltpu.CompilerParams(vmem_limit_bytes=limit),
        cost_estimate=small,
        name="pick",
    )(source_index, orbitals)


def cut_quarters(source_index, orbitals, crossed):
    planes, points = crossed.shape
    return pl.pallas_call(
        cut_kernel,
        out_shape=[jax.ShapeDtypeStruct((planes, points // 4), crossed.dtype)] * 4,
        in_specs=[scalars, outside, outside],
        out_specs=[whole] * 4,
        scratch_shapes=[pltpu.SemaphoreType.DMA((4,))],
        compiler_params=pltpu.CompilerParams(vmem_limit_bytes=full),
        cost_estimate=small,
        name="cut",
    )(source_index, orbitals, crossed)


def put(which, first, choices, result=None):
    pieces = [piece for choice in choices for piece in choice]
    count = len(choices[0])
    planes, points = pieces[0].shape[0], sum(piece.shape[1] for piece in choices[0])
    before = [] if result is None else [result]
    return pl.pallas_call(
        functools.partial(put_kernel, len(choices), len(before)),
        out_shape=jax.ShapeDtypeStruct((2, planes, points), pieces[0].dtype),
        in_specs=[scalars] + [outside] * (len(before) + len(pieces)),
        out_specs=outside,
        scratch_shapes=[
            pltpu.VMEM((planes, points), pieces[0].dtype),
            pltpu.SemaphoreType.DMA((count,)),
            pltpu.SemaphoreType.DMA((count,)),
        ],
        input_output_aliases={1: 0} if before else {},
        compiler_params=pltpu.CompilerParams(vmem_limit_bytes=full),
        cost_estimate=small,
        name="put",
    )(jnp.stack([which, first.astype(which.dtype)]).astype(jnp.int32), *before, *pieces)


def forward(flags, place, first, targets, group, tables):
    planes = group[0].shape[1]
    extent = tables[0].shape[0]
    points = extent * extent
    return pl.pallas_call(
        functools.partial(forward_kernel, place, first, len(targets), len(targets[0])),
        out_shape=jax.ShapeDtypeStruct((2, extent * plane_pitch, lanes), jnp.float32),
        in_specs=[scalars] + [outside] * (len(targets) * len(targets[0]) + len(group)) + [whole] * len(tables),
        out_specs=whole,
        scratch_shapes=[
            pltpu.VMEM((planes, points), jnp.bfloat16),
            pltpu.VMEM((planes, points), jnp.bfloat16),
            pltpu.VMEM((2, planes * turned_pitch, lanes), jnp.float32),
            pltpu.SemaphoreType.DMA((len(targets[0]) + 5,)),
        ],
        compiler_params=pltpu.CompilerParams(vmem_limit_bytes=limit),
        cost_estimate=small,
        name="forward",
    )(flags, *[piece for choice in targets for piece in choice], *group, *tables)


def central(flags, home, direct, ready, targets, neighbour_source, across_source, tables):
    planes = across_source[0].shape[1]
    extent = tables[0].shape[0]
    points = extent * extent
    pieces = [*ready, *targets[0], *targets[1], *neighbour_source, *across_source]
    parts = [jax.ShapeDtypeStruct((planes, share * points // 5), jnp.bfloat16) for share in (2, 3)]
    slab = jax.ShapeDtypeStruct(ready[0].shape, jnp.float32)
    outs = pl.pallas_call(
        functools.partial(central_kernel, home, direct),
        out_shape=parts * 2 + [slab] * 2,
        in_specs=[scalars] + [outside] * len(pieces) + [whole] * len(tables),
        out_specs=[whole] * 4 + [outside] * 2,
        scratch_shapes=[
            pltpu.VMEM((ring, *slab.shape), jnp.float32),
            *[pltpu.VMEM((planes, points), jnp.bfloat16)] * 4,
            pltpu.VMEM((2, planes * turned_pitch, lanes), jnp.float32),
            pltpu.SemaphoreType.DMA((len(targets[0]) + 5,)),
            pltpu.SemaphoreType.DMA((13,)),
            pltpu.SemaphoreType.DMA((2,)),
        ],
        compiler_params=pltpu.CompilerParams(vmem_limit_bytes=full),
        cost_estimate=small,
        name="central",
    )(flags, *pieces, *tables)
    return split(outs, 2, 2, 2)


def backward(flags, places, first, slabs, groups, cas_matrix, windows, parts):
    planes = groups[0][0].shape[1]
    extent = cas_matrix.shape[0]
    points = extent * extent
    pieces = [piece for group in groups for piece in group]
    return pl.pallas_call(
        functools.partial(backward_kernel, places, first, parts),
        out_shape=[jax.ShapeDtypeStruct((planes, points // parts), jnp.bfloat16)] * parts,
        in_specs=[scalars] + [outside] * (len(slabs) + len(pieces)) + [whole] * 2,
        out_specs=[whole] * parts,
        scratch_shapes=[
            pltpu.VMEM(slabs[0].shape, jnp.float32),
            pltpu.VMEM((planes, points), jnp.bfloat16),
            pltpu.VMEM((2, planes * turned_pitch, lanes), jnp.float32),
            pltpu.SemaphoreType.DMA((6,)),
        ],
        compiler_params=pltpu.CompilerParams(vmem_limit_bytes=limit),
        cost_estimate=small,
        name="backward",
    )(flags, *slabs, *pieces, cas_matrix, windows)


def add(a, b):
    return (a.astype(jnp.float32) + b.astype(jnp.float32)).astype(jnp.bfloat16)


def pair_plan(orbitals, source_index):
    local_count, planes, points = orbitals.shape
    slabs = lax.axis_size("grid")
    extent = planes * slabs
    band, z = lax.axis_index("band"), lax.axis_index("grid")
    column, core = band // cores, band % cores
    quarter = points // 4
    at_home = core == holder(z)
    direct_neighbour = core == 1 - z % 2
    parity = z % 2
    inner = (z == 1) | (z == 2)
    second = inner.astype(jnp.int32)
    flags = jnp.stack([core, column, at_home, direct_neighbour, second, 1 - second]).astype(jnp.int32)
    home, direct = 2, 3

    unit = points // 8

    def first_pieces(source_index):
        core = lax.rem(lax.axis_index("band"), cores)
        near_parity = lax.rem(lax.axis_index("grid") + 1, 2)
        candidate = lax.rem(source_index[1 - core], local_count)
        return [(candidate, 0)] + [(near_parity, start) for start in (0, unit, 6 * unit)]

    def own_orbital(source_index):
        return [(lax.rem(lax.axis_index("grid"), 2), 0)]

    other, *to_near = pick(orbitals, source_index, first_pieces, (points, unit, 5 * unit, 2 * unit))
    crossed = swap_cores(other)
    near = [move(to_near[0], near_routes())]
    owner = source_index[core] // local_count

    cuts, to_near = stage((cut_quarters(source_index, orbitals, crossed), to_near), near)
    near.append(move(to_near[1], near_routes()))
    candidates = [cuts[0]] + [to_column(cuts[d], d) for d in (1, 2, 3)]
    (own_parity,) = pick(stage(orbitals, cuts), source_index, own_orbital, (points,))
    cas_matrix = cas_table(extent)
    windows = window_tables(cas_matrix)
    windows_back = jnp.swapaxes(windows, 1, 2)
    places = (((z ^ jnp.arange(slabs)) * planes)[:, None] + jnp.arange(planes)).reshape(extent)
    into = cas_entries(jnp.arange(extent), places, extent)
    square_x = wave_square(jnp.arange(extent, dtype=jnp.int32), extent)
    strength = (extent * spacing) ** 2 / math.pi
    square = (square_x[:, None] + square_x[None, :] + 1.0) * (1.0 / strength)
    square = jnp.pad(square, ((0, 0), (0, 2 * lanes - extent)), constant_values=1.0)
    tables = [cas_matrix, windows, windows_back, into, into.T, square]

    candidates, tables, own_parity, flags = stage((candidates, tables, own_parity, flags), near)
    cas_matrix, windows, windows_back, into, outof, square = tables
    forward_tables = [cas_matrix, windows, into, outof]
    own = lax.select_n(column ^ (owner // cores), *candidates)
    own = stage(own, tables)
    own_swapped = swap_cores(own_parity)
    own_x, own_y = to_column(own, 1), to_column(own, 2)
    neighbour = to_height(own, {0: 1, 1: 0, 2: 3, 3: 2})
    crossed = to_height(own, {1: 2, 2: 1})

    neighbour, crossed, own_x, own_y, own_swapped = stage((neighbour, crossed, own_x, own_y, own_swapped))
    neighbour_x, neighbour_y = to_column(neighbour, 1), to_column(neighbour, 2)
    crossed_2 = to_height(neighbour, {1: 2, 2: 1})
    handed = to_height(crossed, {1: 0, 2: 3})

    low = jnp.stack([own_x[:, : quarter // 2], neighbour_x[:, : quarter // 2]])
    high = jnp.stack([own_y[:, quarter // 2 :], neighbour_y[:, quarter // 2 :]])
    low, high, crossed_2, own_parity, last = stage((low, high, crossed_2, own_parity, to_near[2]), handed)
    low, high = to_column(low, 2), to_column(high, 1)
    handed_2 = to_height(crossed_2, {1: 0, 2: 3})
    near.append(move(last, near_routes()))
    far = [move(own_parity, far_routes())]

    across = jnp.stack([jnp.where(inner, crossed, handed), jnp.where(inner, crossed_2, handed_2)])
    across, low, high = stage((across, low, high))
    sources = [
        [own[None], own_x[None], own_y[None], low[:1], high[:1]],
        [neighbour[None], neighbour_x[None], neighbour_y[None], low[1:], high[1:]],
    ]
    across_x, across_y = to_column(across, 1), to_column(across, 2)
    near_swapped = [swap_cores(part) for part in stage(near[:2], across)]
    along_y = [forward(flags, 0, home, [[own_parity], [own_swapped]], sources[0], forward_tables)]

    low, high = across_x[:, :, : quarter // 2], across_y[:, :, quarter // 2 :]
    near[2] = stage(near[2], along_y)
    near_swapped.append(swap_cores(near[2]))
    low, high, near_swapped = stage((low, high, near_swapped), along_y)
    low, high = to_column(low, 2), to_column(high, 1)
    along_y.append(forward(flags, 1, direct, [near, near_swapped], sources[1], forward_tables))

    low, high, far = stage((low, high, far), along_y)
    across_source = [across, across_x, across_y, low, high]
    sources += [across_source, across_source]
    far_swapped = [swap_cores(part) for part in far]
    along_y_3 = forward(flags, 3, direct, [near_swapped, near], across_source, forward_tables)
    far_swapped = stage(far_swapped, along_y_3)
    given, kept, (own_back, far_back) = central(
        flags,
        home,
        direct,
        [*along_y, along_y_3],
        [far_swapped, far],
        sources[1],
        across_source,
        [cas_matrix, windows, windows_back, into, outof, square],
    )

    def partials(places, slabs, *earlier):
        groups = [sources[place] for place in places]
        return backward(flags, places, home, stage(slabs, *earlier), groups, cas_matrix, windows_back, 4)

    near = [add(k, swap_cores(g)) for k, g in zip(kept, given)]
    near_home = [move(part, back(near_routes())) for part in near]
    given = partials([2, 0], [far_back, own_back], near[0])
    kept = partials([0, 2], [own_back, far_back], given[0], near_home[0])
    far = [add(k, swap_cores(g)) for k, g in zip(kept, given)]
    far_home = [move(part, back(far_routes())) for part in far]
    result = put(1 - parity, at_home, [near_home])
    result, far_home = stage((result, far_home))
    return put(parity, at_home, [far, far_home], result)


def solution(mesh):
    def shards(orbitals, source_index):
        slabs, bands = mesh.shape["grid"], mesh.shape["band"]
        fits = slabs == 4 and bands == 8 and orbitals.shape[0] == 2 and source_index.shape[0] == cores
        return (pair_plan if fits else slab_plan)(orbitals, source_index)

    return jax.shard_map(
        shards,
        mesh=mesh,
        in_specs=(P("band", "grid", None), P()),
        out_specs=P("band", "grid", None),
        check_vma=False,
    )
```
